32 devices in a mesh: section: 2 (over core), dp: 4 (over z), mp: 4 (over y, x).
Axes of the slice: x: 2, y: 2, z: 4, core: 2. Of those that a mesh axis runs over, the one named last changes fastest.
Arguments:
- inputs: bfloat16 [2, 4, 4, 1024, 512], P('section', None, 'dp', 'mp'), may hold values from -6 to 6
- lengths: int32 [2, 4, 4, 8], P('section', None, 'dp'), may hold values from 1 to 1024, as said below
- routes_self: int32 [2, 4, 4, 1024, 2], P('section', None, 'dp', 'mp'), may hold values from 0 to 7, all different within a row; in each aligned block of 256 rows (0 to 255, 256 to 511, ..., all dimensions but the last counted through in order) at most 128 rows name the same one
- routes_cross: int32 [4, 4, 1024, 2], P(None, 'dp', 'mp'), may hold values from 0 to 7, all different within a row; in each aligned block of 256 rows (0 to 255, 256 to 511, ..., all dimensions but the last counted through in order) at most 128 rows name the same one
- gains: bfloat16 [2, 3, 512], P('section'), may hold values from 0.5 to 1.5
- router_self: bfloat16 [2, 512, 8], P('section'), may hold values from -0.19921875 to 0.19921875
- query_self: bfloat16 [2, 8, 512, 64], P('section', 'mp'), may hold values from -0.25 to 0.25
- keyval_self: bfloat16 [2, 512, 128], P('section'), may hold values from -0.25 to 0.25
- output_self: bfloat16 [2, 8, 64, 512], P('section', 'mp'), may hold values from -3 to 3
- ffn_in: bfloat16 [2, 512, 2048], P('section', None, 'mp'), may hold values from -0.25 to 0.25
- ffn_out: bfloat16 [2, 2048, 512], P('section', 'mp'), may hold values from -0.1875 to 0.1875
- router_cross: bfloat16 [512, 8], replicated, may hold values from -0.19921875 to 0.19921875
- query_cross: bfloat16 [8, 512, 64], P('mp'), may hold values from -0.25 to 0.25
- keyval_cross: bfloat16 [512, 128], replicated, may hold values from -0.25 to 0.25
- output_cross: bfloat16 [8, 64, 512], P('mp'), may hold values from -3 to 3
- cotangent: bfloat16 [4, 4, 1024, 512], P(None, 'dp', 'mp'), may hold values from -6 to 6
Outputs:
- outputs: bfloat16 [2, 4, 4, 1024, 512], P('section', None, 'dp', 'mp')
- grad_inputs: float32 [2, 4, 4, 1024, 512], P('section', None, 'dp', 'mp')
- grad_gains: float32 [2, 3, 512], P(None, None, ('section', 'dp'))
- grad_router_self: float32 [2, 512, 8], P(None, ('section', 'dp'))
- grad_query_self: float32 [2, 8, 512, 64], P(None, 'mp', ('section', 'dp'))
- grad_keyval_self: float32 [2, 512, 128], P(None, ('section', 'dp'))
- grad_output_self: float32 [2, 8, 64, 512], P(None, 'mp', None, ('section', 'dp'))
- grad_ffn_in: float32 [2, 512, 2048], P(None, ('section', 'dp'), 'mp')
- grad_ffn_out: float32 [2, 2048, 512], P(None, 'mp', ('section', 'dp'))
- grad_router_cross: float32 [512, 8], P(('section', 'dp'))
- grad_query_cross: float32 [8, 512, 64], P('mp', ('section', 'dp'))
- grad_keyval_cross: float32 [512, 128], P(('section', 'dp'))
- grad_output_cross: float32 [8, 64, 512], P('mp', None, ('section', 'dp'))
The draws below stay inside these ranges and needn't reach their ends.
Inputs may be any that keep to these rules, and one draw needn't show every extreme that they name: `routes_self`: in each aligned block of 256 tokens, no expert is named by more than 128 tokens, a bound that some block reaches; a token's two experts differ. `routes_cross`: in each aligned block of 256 tokens, no expert is named by more than 128 tokens, a bound that some block reaches; a token's two experts differ. Each row's 8 lengths sum to 1024.
All inputs are finite; a program needn't handle non-finite values.
Results may differ from the reference program's by a relative error of at most 0.02.
Values may be sent and summed in bfloat16 or wider, within the bound.
No kernel may reach another device: no remote copies, remote signals or barrier semaphores. Data moves between devices by JAX's collectives and lax.ppermute only.
A program may use at most 192 MiB of HBM per device.

```python
import math
import jax
import jax.numpy as jnp
import numpy as np
from jax import lax

D = 512
EXPERTS = 8
HD = 64
FF = 2048
ROW = 1024
NSENT = 8
MICRO = 4
ROWS = 4
TOK = 256
CAPS = 128
SHORT_MAX = 36


def draw_lengths(key, part):
    key = jax.random.fold_in(key, 11)
    first_key, second_key = jax.random.split(key)
    short_parts = jax.random.randint(first_key, (2, MICRO, ROWS, NSENT), 1, SHORT_MAX + 1)
    longest_at = jax.random.randint(second_key, (2, MICRO, ROWS, 1), 0, NSENT)
    slot_index = lax.broadcasted_iota(jnp.int32, (2, MICRO, ROWS, NSENT), 3)
    is_long = slot_index == longest_at
    others = jnp.sum(jnp.where(is_long, 0, short_parts), 3, keepdims=True)
    return jnp.where(is_long, ROW - others, short_parts).astype(jnp.int32)


def strengthened(drawn, stream_key, source, target, blocks, factor):
    def block_of(axis_at):
        return (jnp.arange(drawn.shape[axis_at]) // (drawn.shape[axis_at] // blocks)).reshape((-1,) + (1,) * (drawn.ndim - 1 - axis_at))

    first = jax.random.permutation(stream_key, blocks)[block_of(target)]
    far = (block_of(target) + blocks // 2) % blocks
    return jnp.where((block_of(source) == first) | (block_of(source) == far), factor * drawn, drawn)


def level_of(key, dims, shards, smallest, top_value):
    factor_of = 1.0
    for axis_at, parts in shards:
        steps = jax.random.uniform(jax.random.fold_in(jax.random.fold_in(key, 6), axis_at), (parts,), jnp.float32, smallest / len(shards), top_value / len(shards))
        factor_of = factor_of * jnp.repeat(jnp.exp(steps), dims[axis_at] // parts).reshape((-1,) + (1,) * (len(dims) - 1 - axis_at))
    return factor_of


def assign_block(key, own, number, rows, count, top, reach, skew):
    sequence = jax.random.permutation(key, count)
    packed, common = shares(count, rows * top, reach, skew, True), shares(count, rows * top, reach, skew, False)
    places = jnp.arange(count)

    def named(tallies, turn):
        used = int((tallies > 0).sum())
        fixed = max(1, used // 4)
        moved = fixed + (places - fixed + turn * (used - fixed)) % max(1, count - fixed)
        return jnp.zeros((count,), jnp.int32).at[sequence[jnp.where(places < fixed, places, moved)]].set(jnp.asarray(tallies, jnp.int32))

    tallies = jnp.where(number % 4 == 0, named(packed, number // 4), named(common, number - number // 4 - 1))
    mixed = jax.random.permutation(jax.random.fold_in(own, 3), count)
    donor, taker = mixed[0:count // 2 * 2:2], mixed[1:count // 2 * 2:2]
    margin = jnp.minimum(tallies[donor] - 1, reach - tallies[taker]) // 2
    margin = jnp.where((donor == sequence[0]) | (taker == sequence[0]) | (tallies[taker] == 0), 0, jnp.maximum(margin, 0))
    moved = jax.random.randint(jax.random.fold_in(own, 4), (count // 2,), 0, 1 << 20) % (margin + 1)
    tallies = tallies.at[donor].add(-moved).at[taker].add(moved)
    labels = jnp.searchsorted(jnp.cumsum(tallies), jnp.arange(rows * top), side="right").astype(jnp.int32)
    table = labels.reshape(top, rows).T
    table = table[jax.random.permutation(jax.random.fold_in(own, 1), rows)]
    turn = jax.random.randint(jax.random.fold_in(own, 2), (rows, 1), 0, top)
    return jnp.take_along_axis(table, (jnp.arange(top)[None, :] + turn) % top, axis=1)


def shares(count, total, most, slope, full):
    weights = [(1 << 20) // math.isqrt(rank ** slope) + 1 for rank in range(1, count + 1)]
    largest = most if full else min(most, max(-(-total // count), total * weights[0] // sum(weights)))
    least = 1 if total - largest >= count - 1 else 0
    given, surplus = [largest] + [least] * (count - 1), total - largest - least * (count - 1)
    while surplus > 0:
        movable = [i for i in range(1, count) if given[i] < largest] or [i for i in range(1, count) if given[i] < most]
        pool, left = sum([weights[i] for i in movable]), surplus
        for i in movable:
            extra = min(most - given[i], max(1, left * weights[i] // pool), surplus)
            given[i] = given[i] + extra
            surplus = surplus - extra
    return np.array(given)


def noise(rng, extent, spread, most, cuts=(), held_as=jnp.bfloat16):
    array = jax.random.normal(rng, extent, jnp.float32) * spread
    if len(cuts) > 0:
        array = level_of(rng, extent, cuts, -0.22, 0.18) * array
    return jnp.clip(array, min=-most, max=most).astype(held_as)


def bell_draw_with(stream_key, dims, width, bound, cuts, heavy, kind=jnp.bfloat16):
    entries = width * jax.random.normal(stream_key, dims, jnp.float32)
    if cuts:
        entries = entries * level_of(stream_key, dims, cuts, -0.22, 0.18)
    return jnp.clip(strengthened(entries, jax.random.fold_in(stream_key, 3), *heavy), -bound, bound).astype(kind)


def setup_inputs(seed: int = 0) -> dict:
    arg_keys = jax.random.split(jax.random.key(seed), 17)
    inputs = noise(arg_keys[0], (2, MICRO, ROWS, ROW, D), 1.0, 6.0, ((0, 2), (2, 4), (3, 4)))
    lengths = draw_lengths(jax.random.fold_in(arg_keys[16], 71), 0)
    routes_self_keys = jax.random.split(jax.random.fold_in(arg_keys[2], 1), 2 * MICRO * ROWS * ROW // TOK)
    routes_self_turns = jax.random.permutation(jax.random.fold_in(arg_keys[2], 3), 2 * MICRO * ROWS * ROW // TOK)
    routes_self = jax.vmap(lambda own, number: assign_block(jax.random.fold_in(arg_keys[2], 2), own, number, TOK, EXPERTS, 2, CAPS, 2))(routes_self_keys, routes_self_turns).reshape((2, MICRO, ROWS, ROW, 2))
    routes_cross_keys = jax.random.split(jax.random.fold_in(arg_keys[3], 1), MICRO * ROWS * ROW // TOK)
    routes_cross_turns = jax.random.permutation(jax.random.fold_in(arg_keys[3], 3), MICRO * ROWS * ROW // TOK)
    routes_cross = jax.vmap(lambda own, number: assign_block(jax.random.fold_in(arg_keys[3], 2), own, number, TOK, EXPERTS, 2, CAPS, 2))(routes_cross_keys, routes_cross_turns).reshape((MICRO, ROWS, ROW, 2))
    gains = jnp.clip(1.0 + 0.1 * jax.random.normal(arg_keys[4], (2, 3, D), jnp.float32), 0.5, 1.5).astype(jnp.bfloat16)
    router_self = noise(arg_keys[5], (2, D, EXPERTS), 0.035, 0.19921875, ((0, 2),))
    query_self = noise(arg_keys[6], (2, EXPERTS, D, HD), D ** -0.5, 0.25, ((0, 2), (1, 4)))
    keyval_self = noise(arg_keys[7], (2, D, 2 * HD), D ** -0.5, 0.25, ((0, 2),))
    output_self = noise(arg_keys[8], (2, EXPERTS, HD, D), (HD // 16) ** -0.5, 3.0, ((0, 2), (1, 4)))
    ffn_in = noise(arg_keys[9], (2, D, FF), D ** -0.5, 0.25, ((0, 2), (2, 4)))
    ffn_out = noise(arg_keys[10], (2, FF, D), (FF // 2) ** -0.5, 0.1875, ((0, 2), (1, 4)))
    router_cross = noise(arg_keys[11], (D, EXPERTS), 0.035, 0.19921875)
    query_cross = noise(arg_keys[12], (EXPERTS, D, HD), D ** -0.5, 0.25, ((0, 4),))
    keyval_cross = noise(arg_keys[13], (D, 2 * HD), D ** -0.5, 0.25)
    output_cross = noise(arg_keys[14], (EXPERTS, HD, D), (HD // 16) ** -0.5, 3.0, ((0, 4),))
    cotangent = bell_draw_with(arg_keys[15], (MICRO, ROWS, ROW, D), 1.0, 6.0, ((1, 4), (2, 4)), (1, 3, 4, 2.0))
    return {"inputs": inputs, "lengths": lengths, "routes_self": routes_self, "routes_cross": routes_cross, "gains": gains, "router_self": router_self, "query_self": query_self, "keyval_self": keyval_self, "output_self": output_self, "ffn_in": ffn_in, "ffn_out": ffn_out, "router_cross": router_cross, "query_cross": query_cross, "keyval_cross": keyval_cross, "output_cross": output_cross, "cotangent": cotangent}


EPS = 1e-05
MASK_VALUE = -1000000000.0

@jax.custom_vjp
def low(v):
    return lax.optimization_barrier(v.astype(jnp.bfloat16)).astype(jnp.float32)

@jax.custom_vjp
def low_back(v):
    return v

def low_keep(v):
    return (low(v), None)

def low_pass(kept, grad):
    return (grad,)

def back_keep(v):
    return (v, None)

def back_low(kept, grad):
    return (low(grad),)
low.defvjp(low_keep, low_pass)
low_back.defvjp(back_keep, back_low)

def matmul(left, right):
    return jnp.dot(left, right, precision=lax.Precision.HIGHEST)

def normalize(values, gain_row):
    center = values - lax.optimization_barrier(jnp.mean(values, 1, keepdims=True))
    return center * lax.rsqrt(lax.optimization_barrier(jnp.mean(center * center, 1, keepdims=True)) + EPS) * gain_row

def segment_of(where_at, lengths):
    sentence_ends = jnp.cumsum(lengths)
    return lax.optimization_barrier(jnp.sum((where_at[:, None] >= sentence_ends[None, :]).astype(jnp.int32), 1))

def feed_forward(rows_in, w_in, w_out):
    hidden_pre = low_back(matmul(rows_in, w_in))
    return low_back(matmul(low(jax.nn.gelu(hidden_pre, approximate=False)), w_out))

def mixture(query_rows, key_rows, router, w_query, w_keyval, w_output, routes, query_segments, key_segments, causal):
    head_size = w_query.shape[2]
    experts = router.shape[1]
    keyval = low_back(low(matmul(key_rows, w_keyval)))
    keys_part = keyval[:, :head_size]
    values_part = keyval[:, head_size:]
    logits = matmul(query_rows, router)
    picked = (routes[:, :, None] == jnp.arange(experts, dtype=jnp.int32)[None, None, :]).astype(jnp.float32)
    chosen = lax.optimization_barrier(jnp.sum(picked * logits[:, None, :], 2))
    gate_values = low_back(low(jax.nn.softmax(chosen, 1)))
    weight = lax.optimization_barrier(jnp.sum(picked * gate_values[:, :, None], 1))
    row_count = query_rows.shape[0]
    key_count = key_rows.shape[0]
    allowed = query_segments[:, None] == key_segments[None, :]
    if causal:
        allowed = allowed & (jnp.arange(key_count)[None, :] <= jnp.arange(row_count)[:, None])
    score_scale = head_size ** (-0.5)

    def one_expert(bundle):
        w_q, w_o, share = bundle
        inputs_q = low_back(query_rows)
        queries = low_back(low(matmul(inputs_q, w_q)))
        scores = low_back(matmul(queries, keys_part.T) * score_scale)
        scores = jnp.where(allowed, scores, MASK_VALUE)
        probabilities = jax.nn.softmax(scores, 1)
        mixed_rows = low_back(matmul(low(probabilities), values_part))
        gated_rows = low(share[:, None] * mixed_rows)
        return low_back(low(matmul(gated_rows, w_o)))
    expert_parts = lax.map(jax.checkpoint(one_expert), (w_query, w_output, weight.T))
    return lax.optimization_barrier(jnp.sum(expert_parts, 0))

def encoder(source, lengths, routes, gain_rows, router, w_query, w_keyval, w_output, w_in, w_out):
    segments = segment_of(jnp.arange(source.shape[0], dtype=jnp.int32), lengths)
    first = low(normalize(source, gain_rows[0]))
    after_self = source + mixture(first, first, router, w_query, w_keyval, w_output, routes, segments, segments, False)
    third = low(normalize(after_self, gain_rows[2]))
    after_ffn = after_self + feed_forward(third, w_in, w_out)
    return low_back(low(normalize(after_ffn, gain_rows[1])))

def decoder(target_rows, memory, lengths, memory_lengths, routes_own, routes_other, gain_rows, self_set, cross_set, w_in, w_out):
    positions = jnp.arange(target_rows.shape[0], dtype=jnp.int32)
    segments = segment_of(positions, lengths)
    memory_segments = segment_of(positions, memory_lengths)
    first = low(normalize(target_rows, gain_rows[0]))
    after_self = target_rows + mixture(first, first, self_set[0], self_set[1], self_set[2], self_set[3], routes_own, segments, segments, True)
    second = low(normalize(after_self, gain_rows[1]))
    after_cross = after_self + mixture(second, memory, cross_set[0], cross_set[1], cross_set[2], cross_set[3], routes_other, segments, memory_segments, False)
    third = low(normalize(after_cross, gain_rows[2]))
    return after_cross + feed_forward(third, w_in, w_out)

def forward(weights, source, target_rows, source_lengths, target_lengths, source_routes, target_routes, other_routes):
    gains, router_self, query_self, keyval_self, output_self, ffn_in, ffn_out, router_cross, query_cross, keyval_cross, output_cross = weights
    memory = encoder(source, source_lengths, source_routes, gains[0], router_self[0], query_self[0], keyval_self[0], output_self[0], ffn_in[0], ffn_out[0])
    result = decoder(target_rows, memory, target_lengths, source_lengths, target_routes, other_routes, gains[1], (router_self[1], query_self[1], keyval_self[1], output_self[1]), (router_cross, query_cross, keyval_cross, output_cross), ffn_in[1], ffn_out[1])
    return (result, memory)

def reference(inputs, lengths, routes_self, routes_cross, gains, router_self, query_self, keyval_self, output_self, ffn_in, ffn_out, router_cross, query_cross, keyval_cross, output_cross, cotangent):
    weights = tuple((tensor.astype(jnp.float32) for tensor in (gains, router_self, query_self, keyval_self, output_self, ffn_in, ffn_out, router_cross, query_cross, keyval_cross, output_cross)))
    pairs = MICRO * ROWS
    flat_inputs = inputs.astype(jnp.float32).reshape(2, pairs, ROW, D)
    flat_lengths = lengths.reshape(2, pairs, NSENT)
    flat_self = routes_self.reshape(2, pairs, ROW, 2)
    flat_cross = routes_cross.reshape(pairs, ROW, 2)
    flat_upstream = cotangent.astype(jnp.float32).reshape(pairs, ROW, D)

    def one_pair(sums, bundle):
        source, target_rows, source_lengths, target_lengths, source_routes, target_routes, other_routes, upstream = bundle

        def local_forward(weights_in, source_in, target_in):
            return forward(weights_in, source_in, target_in, source_lengths, target_lengths, source_routes, target_routes, other_routes)
        (result, memory), pullback = jax.vjp(local_forward, weights, source, target_rows)
        grad_weights, grad_source, grad_target = pullback((upstream, jnp.zeros_like(memory)))
        sums = jax.tree.map(jnp.add, sums, grad_weights)
        return (sums, (result, memory, grad_source, grad_target))
    start = jax.tree.map(jnp.zeros_like, weights)
    sums, (results, memories, grad_sources, grad_targets) = lax.scan(one_pair, start, (flat_inputs[0], flat_inputs[1], flat_lengths[0], flat_lengths[1], flat_self[0], flat_self[1], flat_cross, flat_upstream))
    outputs = jnp.stack([memories, results]).reshape(2, MICRO, ROWS, ROW, D).astype(jnp.bfloat16)
    grad_inputs = jnp.stack([grad_sources, grad_targets]).reshape(2, MICRO, ROWS, ROW, D)
    return (outputs, grad_inputs, sums[0], sums[1], sums[2], sums[3], sums[4], sums[5], sums[6], sums[7], sums[8], sums[9], sums[10])
```

```python
import functools

import jax
import jax.numpy as jnp
from jax import lax
from jax.experimental import pallas as pl
from jax.experimental.pallas import tpu as pltpu
from jax.sharding import PartitionSpec as P

EPS = 1e-05
MASK_VALUE = -1000000000.0
BF = jnp.bfloat16
F32 = jnp.float32
EX_AT = 160
CODE_ROW = 3
LEN_ROW = 4
ROUTER_AT = 8
GAIN_LANE = 64
ROUTER_LANES = (8, 24, 40)
VMEM_LIMIT = 56 * 1024 * 1024


def nn(left, right):
    return lax.dot_general(left, right, (((1,), (0,)), ((), ())), preferred_element_type=F32)


def nt(left, right):
    return lax.dot_general(left, right, (((1,), (1,)), ((), ())), preferred_element_type=F32)


def tn(left, right):
    return lax.dot_general(left, right, (((0,), (0,)), ((), ())), preferred_element_type=F32)


def norm_of(values, gain_row):
    center = values - jnp.mean(values, 1, keepdims=True)
    scaled = lax.rsqrt(jnp.mean(center * center, 1, keepdims=True) + EPS)
    unit_rows = center * scaled
    return unit_rows * gain_row, unit_rows, scaled


def norm_back(upstream, unit_rows, scaled, gain_row):
    inner = upstream * gain_row
    result = scaled * (
        inner
        - jnp.mean(inner, 1, keepdims=True)
        - unit_rows * jnp.mean(inner * unit_rows, 1, keepdims=True)
    )
    return result, jnp.sum(upstream * unit_rows, 0, keepdims=True)


def eye_of(size):
    return lax.broadcasted_iota(jnp.int32, (size, size), 0) == lax.broadcasted_iota(
        jnp.int32, (size, size), 1
    )


def row_to_col(row):
    return jnp.sum(jnp.where(eye_of(row.shape[1]), row, 0.0), 1, keepdims=True)


def col_to_row(col):
    return jnp.sum(jnp.where(eye_of(col.shape[0]), col, 0.0), 0, keepdims=True)


def ends_of(extra):
    lengths = extra[LEN_ROW : LEN_ROW + 1, 0:8] * 32.0 + extra[LEN_ROW : LEN_ROW + 1, 128:136]
    ends = [lengths[:, 0:1]]
    for k in range(1, 8):
        ends.append(ends[-1] + lengths[:, k : k + 1])
    return ends


def segments(places, ends):
    total = jnp.where(places >= ends[0], 1.0, 0.0)
    for end in ends[1:]:
        total = total + jnp.where(places >= end, 1.0, 0.0)
    return total


def extra_of(recv_ref, layer, quarter):
    return recv_ref[4 * layer + quarter, EX_AT : EX_AT + 16, :]


def gain_of(recv_ref, layer, which):
    return extra_of(recv_ref, layer, 0).astype(F32)[which : which + 1, :]


def rows_of(recv_ref, layer, quarter):
    return recv_ref[4 * layer + quarter, 0:128, :].astype(F32)


def other_kv(recv_ref, layer, quarter):
    packed = recv_ref[4 * layer + quarter, 128:160, :]
    return jnp.concatenate([packed[:, 128 * c : 128 * c + 128] for c in range(4)], 0)


def routing(query_rows, router_block, code_row):
    code = row_to_col(code_row)
    second = jnp.floor(code * 0.125)
    first = code - 8.0 * second
    e0, e1 = first.astype(jnp.int32), second.astype(jnp.int32)
    logits = nt(query_rows, router_block)
    lanes = lax.broadcasted_iota(jnp.int32, logits.shape, 1)
    l0 = jnp.sum(jnp.where(lanes == e0 + ROUTER_AT, logits, 0.0), 1, keepdims=True)
    l1 = jnp.sum(jnp.where(lanes == e1 + ROUTER_AT, logits, 0.0), 1, keepdims=True)
    top = jnp.maximum(l0, l1)
    x0, x1 = jnp.exp(l0 - top), jnp.exp(l1 - top)
    total = x0 + x1
    owners = lax.broadcasted_iota(jnp.int32, (code.shape[0], 512), 1) >> 6
    return e0, e1, x0 / total, x1 / total, owners == e0, owners == e1


def fold(wide, mask):
    kept = jnp.where(mask, wide, 0.0)
    return kept[:, 0:128] + kept[:, 128:256] + kept[:, 256:384] + kept[:, 384:512]


def spread(a0, a1, m0, m1):
    parts = []
    for c in range(4):
        cut = slice(128 * c, 128 * c + 128)
        parts.append(jnp.where(m0[:, cut], a0, jnp.where(m1[:, cut], a1, 0.0)))
    return jnp.concatenate(parts, 1).astype(BF)


def rounded(value):
    return value.astype(BF).astype(F32)


def start_pick(cond, yes, no, sem):
    src_yes, dst = yes
    src_no, unused_dst = no

    @pl.when(cond)
    def _():
        pltpu.make_async_copy(src_yes, dst, sem).start()

    @pl.when(jnp.logical_not(cond))
    def _():
        pltpu.make_async_copy(src_no, dst, sem).start()


def load_columns(cond, own, oth, lane, dst, sems, base):
    for m in range(4):
        cut = (m, slice(None), pl.ds(lane, 128))
        to = dst.at[:, pl.ds(128 * m, 128)]
        start_pick(cond, (own.at[cut], to), (oth.at[cut], to), sems.at[base + m])


def wait_columns(own, lane, dst, sems, base):
    for m in range(4):
        pltpu.make_async_copy(
            own.at[m, :, pl.ds(lane, 128)], dst.at[:, pl.ds(128 * m, 128)], sems.at[base + m]
        ).wait()


def load_whole(cond, own, oth, dst, sem):
    start_pick(cond, (own, dst), (oth, dst), sem)


def wait_whole(own, dst, sem):
    pltpu.make_async_copy(own, dst, sem).wait()


def widen_kv(kv_ref, k2_ref, v2_ref):
    for j in range(4):
        kv = kv_ref[j].reshape(256, 128).astype(F32)
        turned = pltpu.roll(kv, 64, 1)
        low = lax.broadcasted_iota(jnp.int32, kv.shape, 1) < 64
        k2_ref[256 * j : 256 * j + 256, :] = jnp.where(low, kv, turned).astype(BF)
        v2_ref[256 * j : 256 * j + 256, :] = jnp.where(low, turned, kv).astype(BF)


def attend_tile(query_rows, route, w_q, w_ot, k2, v2, allowed):
    e0, e1, g0, g1, m0, m1 = route
    q_all = nn(query_rows, w_q) * 0.125
    queries = jnp.concatenate([fold(q_all, m0), fold(q_all, m1)], 0).astype(BF)
    scores = nt(queries, k2)
    scores = jnp.concatenate(
        [
            jnp.where(allowed, scores[0:128], MASK_VALUE),
            jnp.where(allowed, scores[128:256], MASK_VALUE),
        ],
        0,
    )
    top = jnp.max(scores, 1, keepdims=True)
    weights = jnp.exp(scores - top)
    total = jnp.sum(weights, 1, keepdims=True)
    mixed = nn(weights.astype(BF), v2) / total
    log_total = top + jnp.log(total)
    gated = spread(rounded(g0) * mixed[0:128], rounded(g1) * mixed[128:256], m0, m1)
    out = nt(gated, w_ot)
    rows = jnp.concatenate([col_to_row(log_total[0:128]), col_to_row(log_total[128:256])], 0)
    return out, mixed, rows


def attend_back_tile(
    j, upstream, query_rows, route, mixed, log_rows, w_q, w_ot, router_block, router_lane, k2, v2,
    allowed_t, grad_k, grad_v, gated_ref, dz_ref, dq_ref, dlog_ref,
):
    e0, e1, g0, g1, m0, m1 = route
    q_all = nn(query_rows, w_q) * 0.125
    queries = jnp.concatenate([fold(q_all, m0), fold(q_all, m1)], 0).astype(BF)
    dz = upstream.astype(BF)
    dg_all = nn(dz, w_ot)
    dgated0, dgated1 = fold(dg_all, m0), fold(dg_all, m1)
    r0, r1 = rounded(g0), rounded(g1)
    mixed0, mixed1 = mixed[0:128], mixed[128:256]
    gated_ref[j] = spread(r0 * mixed0, r1 * mixed1, m0, m1)
    dz_ref[j] = dz
    dgate0 = rounded(jnp.sum(mixed0 * dgated0, 1, keepdims=True))
    dgate1 = rounded(jnp.sum(mixed1 * dgated1, 1, keepdims=True))
    do0, do1 = (r0 * dgated0).astype(BF), (r1 * dgated1).astype(BF)
    grad_mixed = jnp.concatenate([do0, do1], 0)
    inner_row = jnp.concatenate(
        [
            col_to_row(jnp.sum(do0.astype(F32) * mixed0, 1, keepdims=True)),
            col_to_row(jnp.sum(do1.astype(F32) * mixed1, 1, keepdims=True)),
        ],
        1,
    )
    log_row = jnp.concatenate([log_rows[0:1], log_rows[1:2]], 1)
    scores = nt(k2, queries)
    scores = jnp.concatenate(
        [
            jnp.where(allowed_t, scores[:, 0:128], MASK_VALUE),
            jnp.where(allowed_t, scores[:, 128:256], MASK_VALUE),
        ],
        1,
    )
    probs = jnp.exp(scores - log_row)
    grad_probs = nt(v2, grad_mixed)
    grad_scores = (probs * (grad_probs - inner_row)).astype(BF)
    grad_v[...] += nn(probs.astype(BF), grad_mixed)
    grad_k[...] += nn(grad_scores, queries)
    grad_q = rounded(tn(grad_scores, k2) * 0.125)
    dq_all = spread(grad_q[0:128], grad_q[128:256], m0, m1)
    dq_ref[j] = dq_all
    grad_rows = nt(dq_all, w_q)
    mean_grad = g0 * dgate0 + g1 * dgate1
    dc0, dc1 = g0 * (dgate0 - mean_grad), g1 * (dgate1 - mean_grad)
    lanes = lax.broadcasted_iota(jnp.int32, (128, 16), 1)
    dlog = jnp.where(lanes == e0 + ROUTER_AT, dc0, 0.0) + jnp.where(
        lanes == e1 + ROUTER_AT, dc1, 0.0
    )
    wide = lax.broadcasted_iota(jnp.int32, (128, 128), 1)
    dlog_ref[j] = (
        jnp.where(wide == e0 + router_lane, dc0, 0.0)
        + jnp.where(wide == e1 + router_lane, dc1, 0.0)
    ).astype(BF)
    return grad_rows + nn(dlog.astype(BF), router_block)


def allowed_rows(j, sec, ends_q, ends_k, causal):
    places = (256 * j + 128 * sec).astype(F32)
    query_at = places + lax.broadcasted_iota(jnp.int32, (128, 1), 0).astype(F32)
    key_at = lax.broadcasted_iota(jnp.int32, (1, 1024), 1).astype(F32)
    allowed = segments(query_at, ends_q) == segments(key_at, ends_k)
    if causal:
        allowed = allowed & (key_at <= query_at)
    return allowed


def key_segments_t(ends_k, segk_ref):
    for j in range(8):
        at = lax.broadcasted_iota(jnp.int32, (128, 128), 0).astype(F32) + 128.0 * j
        segk_ref[128 * j : 128 * j + 128, :] = segments(at, ends_k)


def allowed_cols(j, sec, ends_q, segk_ref, causal):
    places = (256 * j + 128 * sec).astype(F32)
    query_at = places + lax.broadcasted_iota(jnp.int32, (1, 128), 1).astype(F32)
    allowed = segk_ref[...] == segments(query_at, ends_q)
    if causal:
        key_at = lax.broadcasted_iota(jnp.int32, (1024, 128), 0).astype(F32)
        allowed = allowed & (key_at <= query_at)
    return allowed


def fold_kv(grad_k, grad_v, sec, own_ref, send_ref):
    for j in range(4):
        k = grad_k[256 * j : 256 * j + 256, :]
        v = grad_v[256 * j : 256 * j + 256, :]
        k = k + pltpu.roll(k, 64, 1)
        v = v + pltpu.roll(v, 64, 1)
        low = lax.broadcasted_iota(jnp.int32, k.shape, 1) < 64
        both = jnp.where(low, k, v)
        first, second = both[0:128], both[128:256]
        own_ref[j] = jnp.where(sec == 0, first, second)
        send_ref[j] = jnp.where(sec == 0, second, first).astype(send_ref.dtype)


def split_halves(value, sec, keep_ref, send_ref, m, lane):
    upper, lower = value[0:256], value[256:512]
    cut = slice(lane, lane + value.shape[1])
    keep_ref[m, :, cut] = jnp.where(sec == 0, upper, lower).astype(BF)
    send_ref[m, :, cut] = jnp.where(sec == 0, lower, upper).astype(BF)


def turned_rows(value):
    return value.astype(F32).T.astype(BF)


def attention_weight_grads(first_t, gated_ref, dz_ref, dq_ref, sec, keep_ref, send_ref):
    dz_t = turned_rows(dz_ref[...].reshape(512, 512))
    grad_q = nn(first_t, dq_ref[...].reshape(512, 512))
    grad_o = nn(dz_t, gated_ref[...].reshape(512, 512))
    for m in range(4):
        cut = slice(128 * m, 128 * m + 128)
        split_halves(grad_q[:, cut], sec, keep_ref, send_ref, m, 0)
        split_halves(grad_o[:, cut], sec, keep_ref, send_ref, m, 128)


def gelu_parts(pre):
    cdf = 0.5 * (1.0 + lax.erf(pre * 0.7071067811865476))
    slope = cdf + pre * (jnp.exp(-0.5 * pre * pre) * 0.3989422804014327)
    return pre * cdf, slope


def own_self_kv(recv_ref, layer, sec, gain, w_kv, kv_ref):
    for j in range(4):
        first = norm_of(rows_of(recv_ref, layer, j), gain)[0].astype(BF)
        kv_ref[j, sec] = nn(first, w_kv).astype(BF)
        kv_ref[j, 1 - sec] = other_kv(recv_ref, layer, j)


def pack_kernel(x_ref, gain_ref, w_kv_ref, extra_ref, send_ref):
    gain = gain_ref[0:1, :].astype(F32)
    w_kv = w_kv_ref[...]
    for m in range(4):
        first = norm_of(x_ref[m].astype(F32), gain)[0].astype(BF)
        kv = nn(first, w_kv).astype(BF)
        for h in range(2):
            to = 4 * h + m
            send_ref[to, 0:128, :] = x_ref[m, 128 * h : 128 * h + 128, :]
            far = kv[128 * (1 - h) : 128 * (1 - h) + 128]
            send_ref[to, 128:160, :] = jnp.concatenate(
                [far[32 * c : 32 * c + 32] for c in range(4)], 1
            )
            send_ref[to, EX_AT : EX_AT + 16, :] = extra_ref[to]


def enc_fwd_kernel(
    sec_ref, recv_ref, kvc_ref, wa_own, wa_oth, kvw_own, kvw_oth, f_own, f_oth,
    h1_ref, h2_ref, mixed_ref, log_ref, mem_ref, kvm_ref,
    wq, wot, wkv, w_in, w_out, kv_s, k2, v2, third_s, acc, sems,
):
    sec = sec_ref[0]
    mine = sec == 0
    load_whole(mine, kvw_own, kvw_oth, wkv, sems.at[0])
    load_columns(mine, wa_own, wa_oth, 0, wq, sems, 1)
    load_columns(mine, wa_own, wa_oth, 128, wot, sems, 5)
    load_whole(mine, f_own, f_oth, w_in, sems.at[9])
    load_whole(mine, f_oth, f_own, w_out, sems.at[10])
    wait_whole(kvw_own, wkv, sems.at[0])
    own_self_kv(recv_ref, 0, sec, gain_of(recv_ref, 0, 0), wkv[...], kv_s)
    widen_kv(kv_s, k2, v2)
    wait_columns(wa_own, 0, wq, sems, 1)
    wait_columns(wa_own, 128, wot, sems, 5)
    ends = ends_of(extra_of(recv_ref, 0, 0).astype(F32))
    router_block = extra_of(recv_ref, 0, 0)

    def tile(j, carry):
        rows = rows_of(recv_ref, 0, j)
        first = norm_of(rows, gain_of(recv_ref, 0, 0))[0].astype(BF)
        code_row = extra_of(recv_ref, 0, j).astype(F32)[CODE_ROW : CODE_ROW + 1, 0:128]
        route = routing(first, router_block, code_row)
        allowed = allowed_rows(j, sec, ends, ends, False)
        out, mixed, rows_log = attend_tile(
            first, route, wq[...], wot[...], k2[...], v2[...], allowed
        )
        after = rows + out
        h1_ref[j] = after
        mixed_ref[j] = mixed
        log_ref[j] = rows_log
        third_s[j] = norm_of(after, gain_of(recv_ref, 0, 2))[0].astype(BF)
        acc[j] = after
        return carry

    lax.fori_loop(0, 4, tile, 0)
    wait_whole(f_own, w_in, sems.at[9])
    wait_whole(f_own, w_out, sems.at[10])

    def chunk(c, carry):
        third = third_s[...].reshape(512, 512)
        pre = nn(third, w_in[c])
        hidden = (0.5 * pre * (1.0 + lax.erf(pre * 0.7071067811865476))).astype(BF)
        acc[...] += nn(hidden, w_out[c]).reshape(4, 128, 512)
        return carry

    lax.fori_loop(0, 4, chunk, 0)
    for j in range(4):
        h2 = acc[j]
        h2_ref[j] = h2
        memory = norm_of(h2, gain_of(recv_ref, 0, 1))[0].astype(BF)
        mem_ref[j] = memory
        kvm_ref[j] = nn(memory, kvc_ref[...]).astype(BF)


def dec_self_kernel(
    sec_ref, recv_ref, wa_own, wa_oth, kvw_own, kvw_oth,
    g1_ref, mixed_ref, log_ref,
    wq, wot, wkv, kv_s, k2, v2, sems,
):
    sec = sec_ref[0]
    mine = sec == 1
    load_whole(mine, kvw_own, kvw_oth, wkv, sems.at[0])
    load_columns(mine, wa_own, wa_oth, 0, wq, sems, 1)
    load_columns(mine, wa_own, wa_oth, 128, wot, sems, 5)
    wait_whole(kvw_own, wkv, sems.at[0])
    own_self_kv(recv_ref, 1, sec, gain_of(recv_ref, 1, 0), wkv[...], kv_s)
    widen_kv(kv_s, k2, v2)
    wait_columns(wa_own, 0, wq, sems, 1)
    wait_columns(wa_own, 128, wot, sems, 5)
    ends = ends_of(extra_of(recv_ref, 1, 0).astype(F32))
    router_block = extra_of(recv_ref, 1, 0)

    def tile(j, carry):
        rows = rows_of(recv_ref, 1, j)
        first = norm_of(rows, gain_of(recv_ref, 1, 0))[0].astype(BF)
        code_row = extra_of(recv_ref, 1, j).astype(F32)[CODE_ROW : CODE_ROW + 1, 0:128]
        route = routing(first, router_block, code_row)
        allowed = allowed_rows(j, sec, ends, ends, True)
        out, mixed, rows_log = attend_tile(
            first, route, wq[...], wot[...], k2[...], v2[...], allowed
        )
        g1_ref[j] = rows + out
        mixed_ref[j] = mixed
        log_ref[j] = rows_log
        return carry

    lax.fori_loop(0, 4, tile, 0)


def cross_kv(kvm_ref, kvo_ref, sec, kv_s):
    for j in range(4):
        kv_s[j, sec] = kvm_ref[j]
        kv_s[j, 1 - sec] = kvo_ref[j]


def dec_cross_kernel(
    sec_ref, recv_ref, g1_ref, kvm_ref, kvo_ref, rc_ref, cot_ref, wa_own, wa_oth, f_own, f_oth,
    g3_ref, dg2_ref, mixed_ref, log_ref, gain_ref, keep_ref, send_ref,
    wq, wot, w_in, w_out, kv_s, k2, v2, third_s, third_t, cot_t, acc, dthird, sems,
):
    sec = sec_ref[0]
    low = sec == 0
    load_columns(low, wa_own, wa_oth, 256, wq, sems, 0)
    load_columns(low, wa_oth, wa_own, 256, wot, sems, 4)
    load_whole(low, f_own, f_oth, w_in, sems.at[8])
    load_whole(low, f_oth, f_own, w_out, sems.at[9])
    cross_kv(kvm_ref, kvo_ref, sec, kv_s)
    widen_kv(kv_s, k2, v2)
    wait_columns(wa_own, 256, wq, sems, 0)
    wait_columns(wa_own, 256, wot, sems, 4)
    ends_k = ends_of(extra_of(recv_ref, 0, 0).astype(F32))
    ends_q = ends_of(extra_of(recv_ref, 1, 0).astype(F32))

    def tile(j, carry):
        before = g1_ref[j]
        second = norm_of(before, gain_of(recv_ref, 1, 1))[0].astype(BF)
        code_row = extra_of(recv_ref, 1, j).astype(F32)[CODE_ROW : CODE_ROW + 1, 128:256]
        route = routing(second, rc_ref[...], code_row)
        allowed = allowed_rows(j, sec, ends_q, ends_k, False)
        out, mixed, rows_log = attend_tile(
            second, route, wq[...], wot[...], k2[...], v2[...], allowed
        )
        after = before + out
        mixed_ref[j] = mixed
        log_ref[j] = rows_log
        third_s[j] = norm_of(after, gain_of(recv_ref, 1, 2))[0].astype(BF)
        acc[j] = after
        return carry

    lax.fori_loop(0, 4, tile, 0)
    for j in range(4):
        dg2_ref[j] = acc[j]
    third_t[...] = turned_rows(third_s[...].reshape(512, 512))
    cot_t[...] = turned_rows(cot_ref[...].reshape(512, 512))
    dthird[...] = jnp.zeros_like(dthird)
    wait_whole(f_own, w_in, sems.at[8])
    wait_whole(f_own, w_out, sems.at[9])

    def chunk(c, carry):
        third = third_s[...].reshape(512, 512)
        cot = cot_ref[...].reshape(512, 512)
        pre = nn(third, w_in[c])
        hidden, slope = gelu_parts(pre)
        hidden = hidden.astype(BF)
        acc[...] += nn(hidden, w_out[c]).reshape(4, 128, 512)
        dpre = (nt(cot, w_out[c]) * slope).astype(BF)
        dthird[...] += nt(dpre, w_in[c])
        split_halves(nn(third_t[...], dpre), sec, keep_ref, send_ref, c, 0)
        split_halves(nn(cot_t[...], hidden), sec, keep_ref, send_ref, c, 512)
        return carry

    lax.fori_loop(0, 4, chunk, 0)
    total = jnp.zeros((1, 512), F32)
    for j in range(4):
        g3_ref[j] = acc[j].astype(BF)
        gain = gain_of(recv_ref, 1, 2)
        unused_out, unit, scaled = norm_of(dg2_ref[j], gain)
        back, gain_grad = norm_back(dthird[128 * j : 128 * j + 128, :], unit, scaled, gain)
        dg2_ref[j] = cot_ref[j].astype(F32) + back
        total = total + gain_grad
    gain_ref[...] = total


def cross_back_kernel(
    sec_ref, recv_ref, g1_ref, dg2_ref, mixed_ref, log_ref, kvm_ref, kvo_ref, rc_ref, wa_own, wa_oth,
    dg1_ref, gain_ref, own_ref, send_ref, router_ref, keepw_ref, sendw_ref,
    wq, wot, kv_s, k2, v2, segk, grad_k, grad_v, second_s, gated_s, dz_s, dq_s, dlog_s, sems,
):
    sec = sec_ref[0]
    low = sec == 0
    load_columns(low, wa_own, wa_oth, 256, wq, sems, 0)
    load_columns(low, wa_oth, wa_own, 256, wot, sems, 4)
    cross_kv(kvm_ref, kvo_ref, sec, kv_s)
    widen_kv(kv_s, k2, v2)
    ends_k = ends_of(extra_of(recv_ref, 0, 0).astype(F32))
    ends_q = ends_of(extra_of(recv_ref, 1, 0).astype(F32))
    key_segments_t(ends_k, segk)
    grad_k[...] = jnp.zeros_like(grad_k)
    grad_v[...] = jnp.zeros_like(grad_v)
    wait_columns(wa_own, 256, wq, sems, 0)
    wait_columns(wa_own, 256, wot, sems, 4)

    def tile(j, total):
        gain = gain_of(recv_ref, 1, 1)
        second, unit, scaled = norm_of(g1_ref[j], gain)
        second = second.astype(BF)
        second_s[j] = second
        code_row = extra_of(recv_ref, 1, j).astype(F32)[CODE_ROW : CODE_ROW + 1, 128:256]
        route = routing(second, rc_ref[...], code_row)
        allowed = allowed_cols(j, sec, ends_q, segk, False)
        grad_rows = attend_back_tile(
            j, dg2_ref[j], second, route, mixed_ref[j], log_ref[j], wq[...], wot[...], rc_ref[...],
            ROUTER_LANES[2], k2[...], v2[...], allowed, grad_k, grad_v, gated_s, dz_s, dq_s, dlog_s,
        )
        back, gain_grad = norm_back(grad_rows, unit, scaled, gain)
        dg1_ref[j] = dg2_ref[j] + back
        return total + gain_grad

    gain_ref[...] = lax.fori_loop(0, 4, tile, jnp.zeros((1, 512), F32))
    fold_kv(grad_k, grad_v, sec, own_ref, send_ref)
    second_t = turned_rows(second_s[...].reshape(512, 512))
    router_ref[...] = nn(second_t, dlog_s[...].reshape(512, 128))
    attention_weight_grads(second_t, gated_s, dz_s, dq_s, sec, keepw_ref, sendw_ref)


def self_back_kernel(
    layer, sec_ref, recv_ref, up_ref, mixed_ref, log_ref, wa_own, wa_oth, kvw_own, kvw_oth,
    dfirst_ref, own_ref, send_ref, router_ref, keepw_ref, sendw_ref,
    wq, wot, wkv, kv_s, k2, v2, segk, grad_k, grad_v, first_s, gated_s, dz_s, dq_s, dlog_s, sems,
):
    sec = sec_ref[0]
    mine = sec == layer
    load_whole(mine, kvw_own, kvw_oth, wkv, sems.at[0])
    load_columns(mine, wa_own, wa_oth, 0, wq, sems, 1)
    load_columns(mine, wa_own, wa_oth, 128, wot, sems, 5)
    ends = ends_of(extra_of(recv_ref, layer, 0).astype(F32))
    key_segments_t(ends, segk)
    grad_k[...] = jnp.zeros_like(grad_k)
    grad_v[...] = jnp.zeros_like(grad_v)
    wait_whole(kvw_own, wkv, sems.at[0])
    own_self_kv(recv_ref, layer, sec, gain_of(recv_ref, layer, 0), wkv[...], kv_s)
    widen_kv(kv_s, k2, v2)
    wait_columns(wa_own, 0, wq, sems, 1)
    wait_columns(wa_own, 128, wot, sems, 5)
    router_block = extra_of(recv_ref, layer, 0)

    def tile(j, carry):
        first = norm_of(rows_of(recv_ref, layer, j), gain_of(recv_ref, layer, 0))[0].astype(BF)
        first_s[j] = first
        code_row = extra_of(recv_ref, layer, j).astype(F32)[CODE_ROW : CODE_ROW + 1, 0:128]
        route = routing(first, router_block, code_row)
        allowed = allowed_cols(j, sec, ends, segk, layer == 1)
        dfirst_ref[j] = attend_back_tile(
            j, up_ref[j], first, route, mixed_ref[j], log_ref[j], wq[...], wot[...], router_block,
            ROUTER_LANES[layer], k2[...], v2[...], allowed, grad_k, grad_v, gated_s, dz_s, dq_s,
            dlog_s,
        )
        return carry

    lax.fori_loop(0, 4, tile, 0)
    fold_kv(grad_k, grad_v, sec, own_ref, send_ref)
    first_t = turned_rows(first_s[...].reshape(512, 512))
    router_ref[...] = nn(first_t, dlog_s[...].reshape(512, 128))
    attention_weight_grads(first_t, gated_s, dz_s, dq_s, sec, keepw_ref, sendw_ref)


def enc_ffn_back_kernel(
    sec_ref, recv_ref, h1_ref, h2_ref, mem_ref, own_ref, come_ref, kvc_ref, f_own, f_oth,
    dh1_ref, gain_ref, gain2_ref, wkv_ref, keep_ref, send_ref,
    w_in, w_out, third_s, third_t, dy_s, dy_t, dthird, sems,
):
    sec = sec_ref[0]
    low = sec == 0
    load_whole(low, f_own, f_oth, w_in, sems.at[0])
    load_whole(low, f_oth, f_own, w_out, sems.at[1])
    dkv = (own_ref[...] + come_ref[...].astype(F32)).astype(BF)
    wkv_ref[...] = nn(turned_rows(mem_ref[...].reshape(512, 512)), dkv.reshape(512, 128))

    def tile(j, total):
        gain = gain_of(recv_ref, 0, 1)
        dkv_j = (own_ref[j] + come_ref[j].astype(F32)).astype(BF)
        dmem = rounded(nt(dkv_j, kvc_ref[...]))
        unused_out, unit, scaled = norm_of(h2_ref[j], gain)
        back, gain_grad = norm_back(dmem, unit, scaled, gain)
        dh1_ref[j] = back
        dy_s[j] = back.astype(BF)
        third_s[j] = norm_of(h1_ref[j], gain_of(recv_ref, 0, 2))[0].astype(BF)
        return total + gain_grad

    gain_ref[...] = lax.fori_loop(0, 4, tile, jnp.zeros((1, 512), F32))
    third_t[...] = turned_rows(third_s[...].reshape(512, 512))
    dy_t[...] = turned_rows(dy_s[...].reshape(512, 512))
    dthird[...] = jnp.zeros_like(dthird)
    wait_whole(f_own, w_in, sems.at[0])
    wait_whole(f_own, w_out, sems.at[1])

    def chunk(c, carry):
        pre = nn(third_s[...].reshape(512, 512), w_in[c])
        hidden, slope = gelu_parts(pre)
        hidden = hidden.astype(BF)
        dpre = (nt(dy_s[...].reshape(512, 512), w_out[c]) * slope).astype(BF)
        dthird[...] += nt(dpre, w_in[c])
        split_halves(nn(third_t[...], dpre), sec, keep_ref, send_ref, c, 0)
        split_halves(nn(dy_t[...], hidden), sec, keep_ref, send_ref, c, 512)
        return carry

    lax.fori_loop(0, 4, chunk, 0)
    total = jnp.zeros((1, 512), F32)
    for j in range(4):
        gain = gain_of(recv_ref, 0, 2)
        unused_out, unit, scaled = norm_of(h1_ref[j], gain)
        back, gain_grad = norm_back(dthird[128 * j : 128 * j + 128, :], unit, scaled, gain)
        dh1_ref[j] += back
        total = total + gain_grad
    gain2_ref[...] = total


def finish_kernel(
    sec_ref, recv_ref, up0, up1, df0, df1, own0, own1, come0, come1, kvw_own, kvw_oth,
    wkvc_ref, r0, r1, rc, gain_b, gain_e1, gain_e2, gain_d2,
    dx_ref, keep_ref, send_ref,
    wkv0, wkv1, first_s, sems,
):
    sec = sec_ref[0]
    load_whole(sec == 0, kvw_own, kvw_oth, wkv0, sems.at[0])
    load_whole(sec == 1, kvw_own, kvw_oth, wkv1, sems.at[1])
    wait_whole(kvw_own, wkv0, sems.at[0])
    wait_whole(kvw_own, wkv1, sems.at[1])
    first_gains = []
    kv_grads = []
    for layer in range(2):
        up, df, own, come, wkv = (
            (up0, df0, own0, come0, wkv0),
            (up1, df1, own1, come1, wkv1),
        )[layer]

        def tile(j, total, layer=layer, up=up, df=df, own=own, come=come, wkv=wkv):
            gain = gain_of(recv_ref, layer, 0)
            first, unit, scaled = norm_of(rows_of(recv_ref, layer, j), gain)
            first_s[j] = first.astype(BF)
            dkv = (own[j] + come[j].astype(F32)).astype(BF)
            dfirst = df[j] + nt(dkv, wkv[...])
            back, gain_grad = norm_back(dfirst, unit, scaled, gain)
            dx_ref[layer, j] = (up[j] + back).astype(BF)
            return total + gain_grad

        first_gains.append(lax.fori_loop(0, 4, tile, jnp.zeros((1, 512), F32)))
        dkv = (own[...] + come[...].astype(F32)).astype(BF).reshape(512, 128)
        kv_grads.append(nn(turned_rows(first_s[...].reshape(512, 512)), dkv))
    kv_grads.append(wkvc_ref[...])
    for i, grad in enumerate(kv_grads):
        cut = slice(128 * i, 128 * i + 128)
        keep_ref[:, cut] = jnp.where(sec == 0, grad[0:256], grad[256:512]).astype(BF)
        send_ref[:, cut] = jnp.where(sec == 0, grad[256:512], grad[0:256]).astype(BF)
    gains = (first_gains[0], gain_e1[...], gain_e2[...], first_gains[1], gain_b[...], gain_d2[...])
    lanes = lax.broadcasted_iota(jnp.int32, (128, 128), 1)
    blocks = []
    for b in range(4):
        cut = slice(128 * b, 128 * b + 128)
        misc = r0[cut, :] + r1[cut, :] + rc[cut, :]
        for i, row in enumerate(gains):
            misc = misc + jnp.where(lanes == GAIN_LANE + i, row_to_col(row[:, cut]), 0.0)
        blocks.append(misc)
    for b in range(2):
        cut = slice(128 * b, 128 * b + 128)
        keep_ref[cut, 384:512] = jnp.where(sec == 0, blocks[b], blocks[b + 2]).astype(BF)
        send_ref[cut, 384:512] = jnp.where(sec == 0, blocks[b + 2], blocks[b]).astype(BF)


def shaped(dims, kind):
    return jax.ShapeDtypeStruct(dims, kind)


def run(kernel, args, places, outs, scratch, flops):
    space = {
        "s": pl.BlockSpec(memory_space=pltpu.SMEM),
        "v": pl.BlockSpec(memory_space=pltpu.VMEM),
        "a": pl.BlockSpec(memory_space=pl.ANY),
    }
    return pl.pallas_call(
        kernel,
        out_shape=outs,
        in_specs=[space[p] for p in places],
        out_specs=jax.tree.map(lambda _: space["v"], outs),
        scratch_shapes=scratch,
        compiler_params=pltpu.CompilerParams(vmem_limit_bytes=VMEM_LIMIT),
        cost_estimate=pl.CostEstimate(flops=flops, bytes_accessed=8 << 20, transcendentals=0),
    )(*args)


def vm(*dims, kind=BF):
    return pltpu.VMEM(dims, kind)


def swapped(value):
    return lax.ppermute(value, "section", [(0, 1), (1, 0)])


def to_all(value, axes):
    return lax.all_to_all(value, axes, split_axis=0, concat_axis=0, tiled=True)


def from_all(value):
    return to_all(jnp.broadcast_to(value[None], (4,) + value.shape), "mp")


def scattered(kept, come):
    summed = (kept.astype(F32) + come.astype(F32)).astype(BF)
    return last_stages(summed)


def last_stages(summed):
    parts = to_all(summed, "mp")
    quarter = jnp.sum(parts.astype(F32), 0).astype(BF)
    rows, width = quarter.shape
    dp = lax.axis_size("dp")
    pieces = to_all(quarter.reshape(dp, rows // dp, width), "dp")
    return jnp.sum(pieces.astype(F32), 0)


def per_device(
    inputs,
    lengths,
    routes_self,
    routes_cross,
    gains,
    router_self,
    query_self,
    keyval_self,
    output_self,
    ffn_in,
    ffn_out,
    router_cross,
    query_cross,
    keyval_cross,
    output_cross,
    cotangent,
):
    sec = lax.axis_index("section")
    low = sec == 0
    sec_arr = sec.astype(jnp.int32).reshape(1)
    rows = inputs[0, :, 0]

    code_self = routes_self[0, :, 0, :, 0] + 8 * routes_self[0, :, 0, :, 1]
    code_cross = routes_cross[:, 0, :, 0] + 8 * routes_cross[:, 0, :, 1]
    codes = jnp.concatenate(
        [
            code_self.reshape(4, 2, 128).transpose(1, 0, 2).reshape(8, 128),
            code_cross.reshape(4, 2, 128).transpose(1, 0, 2).reshape(8, 128),
        ],
        1,
    ).astype(BF)
    lens = lengths[0, :, 0]
    lens = jnp.concatenate([lens, lens], 0)
    len_row = jnp.zeros((8, 512), BF)
    len_row = len_row.at[:, 0:8].set((lens // 32).astype(BF))
    len_row = len_row.at[:, 128:136].set((lens % 32).astype(BF))
    extra = jnp.concatenate(
        [
            jnp.broadcast_to(gains[0][None], (8, 3, 512)),
            jnp.pad(codes, ((0, 0), (0, 256)))[:, None],
            len_row[:, None],
            jnp.zeros((8, 3, 512), BF),
            jnp.broadcast_to(router_self[0].T[None], (8, 8, 512)),
        ],
        1,
    )
    router_c = jnp.concatenate([jnp.zeros((8, 512), BF), router_cross.T], 0)

    packed = run(
        pack_kernel,
        (rows, gains[0], keyval_self[0], extra),
        "vvvv",
        shaped((8, 176, 512), BF),
        [],
        10**9,
    )
    recv = to_all(packed, ("section", "mp"))

    q_cols = query_self[0].transpose(1, 0, 2).reshape(512, 128)
    o_cols = output_self[0].reshape(128, 512).T
    c_cols = jnp.where(
        low,
        query_cross.transpose(1, 0, 2).reshape(512, 128),
        output_cross.reshape(128, 512).T,
    )
    wa_own = from_all(jnp.concatenate([q_cols, o_cols, c_cols], 1))
    wa_oth = swapped(wa_own)
    kvw_own = keyval_self[0]
    kvw_oth = swapped(kvw_own)

    w_in, w_out = ffn_in[0], ffn_out[0]
    half_come = swapped(jnp.where(low, w_out, w_in))
    enc_own = from_all(jnp.where(low, w_in, half_come))
    enc_oth = swapped(enc_own)
    dec_own = from_all(jnp.where(low, half_come, w_out))
    dec_oth = swapped(dec_own)

    cot_cut = lax.dynamic_index_in_dim(cotangent[:, 0].reshape(4, 2, 128, 512), sec, 1, False)
    cot = to_all(cot_cut, "mp")

    act = shaped((4, 128, 512), F32)
    actb = shaped((4, 128, 512), BF)
    mixed_s = shaped((4, 256, 128), F32)
    log_s = shaped((4, 2, 128), F32)
    kv_b = shaped((4, 128, 128), BF)
    kv_f = shaped((4, 128, 128), F32)
    row_s = shaped((1, 512), F32)
    ffn_g = shaped((4, 256, 1024), BF)
    att_g = shaped((4, 256, 256), BF)
    lane_s = shaped((512, 128), F32)
    attn_scratch = [vm(512, 512), vm(512, 512)]
    kv_scratch = [vm(4, 2, 128, 128), vm(1024, 128), vm(1024, 128)]
    back_scratch = [
        vm(1024, 128, kind=F32), vm(1024, 128, kind=F32), vm(1024, 128, kind=F32),
        vm(4, 128, 512), vm(4, 128, 512), vm(4, 128, 512), vm(4, 128, 512), vm(4, 128, 128),
    ]
    ffn_scratch = [vm(4, 512, 512), vm(4, 512, 512)]

    h1, h2, mixed_e, log_e, memory, kvm = run(
        enc_fwd_kernel,
        (sec_arr, recv, keyval_cross, wa_own, wa_oth, kvw_own, kvw_oth, enc_own, enc_oth),
        "svvaaaaaa",
        (act, act, mixed_s, log_s, actb, kv_b),
        attn_scratch + [vm(512, 128)] + ffn_scratch + kv_scratch
        + [vm(4, 128, 512), vm(4, 128, 512, kind=F32), pltpu.SemaphoreType.DMA((11,))],
        4 * 10**9,
    )
    kvm_oth = swapped(kvm)
    g1, mixed_d, log_d = run(
        dec_self_kernel,
        (sec_arr, recv, wa_own, wa_oth, kvw_own, kvw_oth),
        "svaaaa",
        (act, mixed_s, log_s),
        attn_scratch + [vm(512, 128)] + kv_scratch + [pltpu.SemaphoreType.DMA((9,))],
        2 * 10**9,
    )
    g3, dg2, mixed_c, log_c, gain_d2, keep_d, send_d = run(
        dec_cross_kernel,
        (sec_arr, recv, g1, kvm, kvm_oth, router_c, cot, wa_own, wa_oth, dec_own, dec_oth),
        "svvvvvvaaaa",
        (actb, act, mixed_s, log_s, row_s, ffn_g, ffn_g),
        attn_scratch + ffn_scratch + kv_scratch
        + [vm(4, 128, 512), vm(512, 512), vm(512, 512), vm(4, 128, 512, kind=F32)]
        + [vm(512, 512, kind=F32), pltpu.SemaphoreType.DMA((10,))],
        8 * 10**9,
    )
    come_d = swapped(send_d)
    outs_recv = to_all(jnp.concatenate([memory, g3], 0), ("section", "mp"))
    dg1, gain_b, own_c, sendkv_c, router_cg, keep_wc, send_wc = run(
        cross_back_kernel,
        (sec_arr, recv, g1, dg2, mixed_c, log_c, kvm, kvm_oth, router_c, wa_own, wa_oth),
        "svvvvvvvvaa",
        (act, row_s, kv_f, kv_b, lane_s, att_g, att_g),
        attn_scratch + kv_scratch + back_scratch + [pltpu.SemaphoreType.DMA((8,))],
        4 * 10**9,
    )
    comekv_c = swapped(sendkv_c)
    ffn_dec = scattered(keep_d, come_d)
    self_scratch = (
        attn_scratch + [vm(512, 128)] + kv_scratch + back_scratch + [pltpu.SemaphoreType.DMA((9,))]
    )
    self_outs = (act, kv_f, kv_b, lane_s, att_g, att_g)
    df1, own_1, sendkv_1, router_1g, keep_w1, send_w1 = run(
        functools.partial(self_back_kernel, 1),
        (sec_arr, recv, dg1, mixed_d, log_d, wa_own, wa_oth, kvw_own, kvw_oth),
        "svvvvaaaa",
        self_outs,
        self_scratch,
        4 * 10**9,
    )
    comekv_1 = swapped(sendkv_1)
    dh1, gain_e1, gain_e2, wkvc, keep_e, send_e = run(
        enc_ffn_back_kernel,
        (sec_arr, recv, h1, h2, memory, own_c, comekv_c, keyval_cross, enc_own, enc_oth),
        "svvvvvvvaa",
        (act, row_s, row_s, lane_s, ffn_g, ffn_g),
        ffn_scratch
        + [vm(4, 128, 512), vm(512, 512), vm(4, 128, 512), vm(512, 512)]
        + [vm(512, 512, kind=F32), pltpu.SemaphoreType.DMA((2,))],
        8 * 10**9,
    )
    come_e = swapped(send_e)
    df0, own_0, sendkv_0, router_0g, keep_w0, send_w0 = run(
        functools.partial(self_back_kernel, 0),
        (sec_arr, recv, dh1, mixed_e, log_e, wa_own, wa_oth, kvw_own, kvw_oth),
        "svvvvaaaa",
        self_outs,
        self_scratch,
        4 * 10**9,
    )
    comekv_0 = swapped(sendkv_0)
    ffn_enc = scattered(keep_e, come_e)
    dx, keep_s, send_s = run(
        finish_kernel,
        (
            sec_arr, recv, dh1, dg1, df0, df1, own_0, own_1, comekv_0, comekv_1, kvw_own, kvw_oth,
            wkvc, router_0g, router_1g, router_cg, gain_b, gain_e1, gain_e2, gain_d2,
        ),
        "svvvvvvvvvaavvvvvvvv",
        (shaped((2, 4, 128, 512), BF), shaped((256, 512), BF), shaped((256, 512), BF)),
        [vm(512, 128), vm(512, 128), vm(4, 128, 512), pltpu.SemaphoreType.DMA((2,))],
        10**9,
    )
    dx_recv = to_all(dx.reshape(8, 128, 512), ("section", "mp"))
    send_small = jnp.concatenate(
        [send_w0, send_w1, send_wc, send_s.reshape(256, 4, 128).transpose(1, 0, 2)], 2
    )
    come_small = swapped(send_small)
    keep_small = jnp.concatenate(
        [keep_w0, keep_w1, keep_wc, keep_s.reshape(256, 4, 128).transpose(1, 0, 2)], 2
    )
    summed = (keep_small.astype(F32) + come_small.astype(F32)).astype(BF)
    shared = summed[:, :, 768:].transpose(1, 0, 2).reshape(1, 256, 512)
    small = last_stages(
        jnp.concatenate([summed[:, :, :768], jnp.broadcast_to(shared, (4, 256, 512))], 2)
    )

    def placed(value):
        whole = value.reshape(2, 4, 128, 512).transpose(1, 0, 2, 3)
        return whole.reshape(1, 4, 1, 256, 512)

    share = small.shape[0]

    def query_of(at):
        return small[:, at : at + 128].reshape(share, 2, 64).transpose(1, 0, 2)

    def output_of(at):
        return small[:, at : at + 128].T.reshape(2, 64, share)

    misc = small[:, 1152:1280]

    def router_of(layer):
        return misc[:, ROUTER_LANES[layer] : ROUTER_LANES[layer] + 8]

    return (
        placed(outs_recv),
        placed(dx_recv).astype(F32),
        misc[:, GAIN_LANE : GAIN_LANE + 6].T.reshape(2, 3, share),
        jnp.stack([router_of(0), router_of(1)]),
        jnp.stack([query_of(0), query_of(256)]),
        jnp.stack([small[:, 768:896], small[:, 896:1024]]),
        jnp.stack([output_of(128), output_of(384)]),
        jnp.stack([ffn_enc[:, :512], ffn_dec[:, :512]]),
        jnp.stack([ffn_enc[:, 512:].T, ffn_dec[:, 512:].T]),
        router_of(2),
        query_of(512),
        small[:, 1024:1152],
        output_of(640),
    )


def solution(mesh):
    placed = (
        P("section", None, "dp", "mp", None),
        P("section", None, "dp", None),
        P("section", None, "dp", "mp", None),
        P(None, "dp", "mp", None),
        P("section", None, None),
        P("section", None, None),
        P("section", "mp", None, None),
        P("section", None, None),
        P("section", "mp", None, None),
        P("section", None, "mp"),
        P("section", "mp", None),
        P(),
        P("mp", None, None),
        P(),
        P("mp", None, None),
        P(None, "dp", "mp", None),
    )
    return jax.shard_map(
        per_device,
        mesh=mesh,
        in_specs=placed,
        out_specs=(
            P("section", None, "dp", "mp", None),
            P("section", None, "dp", "mp", None),
            P(None, None, ("section", "dp")),
            P(None, ("section", "dp"), None),
            P(None, "mp", ("section", "dp"), None),
            P(None, ("section", "dp"), None),
            P(None, "mp", None, ("section", "dp")),
            P(None, ("section", "dp"), "mp"),
            P(None, "mp", ("section", "dp")),
            P(("section", "dp"), None),
            P("mp", ("section", "dp"), None),
            P(("section", "dp"), None),
            P("mp", None, ("section", "dp")),
        ),
        check_vma=False,
    )
```

```python
import functools

import jax
import jax.numpy as jnp
from jax import lax
from jax.experimental import pallas as pl
from jax.experimental.pallas import tpu as pltpu
from jax.sharding import PartitionSpec as P

EPS = 1e-05
MASK_VALUE = -1000000000.0
BF = jnp.bfloat16
F32 = jnp.float32
TILE = 256
EX_AT = 160
CODE_ROW = 3
LEN_ROW = 4
ROUTER_AT = 8
GAIN_LANE = 64
ROUTER_LANES = (8, 24, 40)
VMEM_LIMIT = 56 * 1024 * 1024


def nn(left, right):
    return lax.dot_general(left, right, (((1,), (0,)), ((), ())), preferred_element_type=F32)


def nt(left, right):
    return lax.dot_general(left, right, (((1,), (1,)), ((), ())), preferred_element_type=F32)


def tn(left, right):
    return lax.dot_general(left, right, (((0,), (0,)), ((), ())), preferred_element_type=F32)


def norm_of(values, gain_row):
    center = values - jnp.mean(values, 1, keepdims=True)
    scaled = lax.rsqrt(jnp.mean(center * center, 1, keepdims=True) + EPS)
    unit_rows = center * scaled
    return unit_rows * gain_row, unit_rows, scaled


def norm_back(upstream, unit_rows, scaled, gain_row):
    inner = upstream * gain_row
    result = scaled * (
        inner
        - jnp.mean(inner, 1, keepdims=True)
        - unit_rows * jnp.mean(inner * unit_rows, 1, keepdims=True)
    )
    return result, jnp.sum(upstream * unit_rows, 0, keepdims=True)


def eye_of(size):
    return lax.broadcasted_iota(jnp.int32, (size, size), 0) == lax.broadcasted_iota(
        jnp.int32, (size, size), 1
    )


def row_to_col(row):
    return jnp.sum(jnp.where(eye_of(128), row, 0.0), 1, keepdims=True)


def col_to_row(col):
    parts = []
    for at in range(0, col.shape[0], 128):
        part = jnp.where(eye_of(128), col[at : at + 128], 0.0)
        parts.append(jnp.sum(part, 0, keepdims=True))
    return jnp.concatenate(parts, 1)


def ends_of(extra):
    lengths = extra[LEN_ROW : LEN_ROW + 1, 0:8] * 32.0 + extra[LEN_ROW : LEN_ROW + 1, 128:136]
    ends = [lengths[:, 0:1]]
    for k in range(1, 8):
        ends.append(ends[-1] + lengths[:, k : k + 1])
    return ends


def segments(places, ends):
    total = jnp.where(places >= ends[0], 1.0, 0.0)
    for end in ends[1:]:
        total = total + jnp.where(places >= end, 1.0, 0.0)
    return total


def extra_of(recv_ref, layer, quarter):
    return recv_ref[4 * layer + quarter, EX_AT : EX_AT + 16, :]


def gain_of(recv_ref, layer, which):
    return extra_of(recv_ref, layer, 0).astype(F32)[which : which + 1, :]


def rows_of(recv_ref, layer, t):
    return recv_ref[pl.ds(4 * layer + 2 * t, 2), 0:128, :].reshape(TILE, 512).astype(F32)


def codes_of(recv_ref, layer, t, lane):
    cols = []
    for i in range(2):
        extra = extra_of(recv_ref, layer, 2 * t + i).astype(F32)
        cols.append(row_to_col(extra[CODE_ROW : CODE_ROW + 1, lane : lane + 128]))
    return jnp.concatenate(cols, 0)


def other_kv(recv_ref, layer, quarter):
    packed = recv_ref[4 * layer + quarter, 128:160, :]
    return jnp.concatenate([packed[:, 128 * c : 128 * c + 128] for c in range(4)], 0)


def routing(query_rows, router_block, code, m):
    second = jnp.floor(code * 0.125)
    first = code - 8.0 * second
    e0, e1 = first.astype(jnp.int32), second.astype(jnp.int32)
    logits = nt(query_rows, router_block)
    lanes = lax.broadcasted_iota(jnp.int32, logits.shape, 1)
    l0 = jnp.sum(jnp.where(lanes == e0 + ROUTER_AT, logits, 0.0), 1, keepdims=True)
    l1 = jnp.sum(jnp.where(lanes == e1 + ROUTER_AT, logits, 0.0), 1, keepdims=True)
    top = jnp.maximum(l0, l1)
    x0, x1 = jnp.exp(l0 - top), jnp.exp(l1 - top)
    total = x0 + x1
    owners = lax.broadcasted_iota(jnp.int32, (code.shape[0], 512), 1) >> 6
    mask0 = owners == (e0 ^ (2 * m))
    mask1 = owners == (e1 ^ (2 * m))
    return e0, e1, x0 / total, x1 / total, mask0, mask1


def fold(wide, mask):
    kept = jnp.where(mask, wide, 0.0)
    return kept[:, 0:128] + kept[:, 128:256] + kept[:, 256:384] + kept[:, 384:512]


def spread(a0, a1, m0, m1):
    parts = []
    for c in range(4):
        cut = slice(128 * c, 128 * c + 128)
        parts.append(jnp.where(m0[:, cut], a0, jnp.where(m1[:, cut], a1, 0.0)))
    return jnp.concatenate(parts, 1).astype(BF)


def rounded(value):
    return value.astype(BF).astype(F32)


def start_pick(cond, yes, no, dst, sem):
    @pl.when(cond)
    def _():
        pltpu.make_async_copy(yes, dst, sem).start()

    @pl.when(jnp.logical_not(cond))
    def _():
        pltpu.make_async_copy(no, dst, sem).start()


class Loads:
    def __init__(self, sems):
        self.sems, self.used = sems, 0

    def start(self, cond, yes, no, dst):
        sem = self.sems.at[self.used]
        self.used += 1
        start_pick(cond, yes, no, dst, sem)
        return functools.partial(lambda a, b, c: pltpu.make_async_copy(a, b, c).wait(), yes, dst, sem)

    def plain(self, src, dst):
        sem = self.sems.at[self.used]
        self.used += 1
        copy = pltpu.make_async_copy(src, dst, sem)
        copy.start()
        return copy.wait

    def rows(self, cond, yes, no, at, dst):
        cut = pl.ds(at, 128)
        return [
            self.start(cond, yes[b].at[cut], no[b].at[cut], dst.at[pl.ds(128 * b, 128)])
            for b in range(4)
        ]

    def blocks(self, cond, yes, no, dst):
        return [self.start(cond, yes[b], no[b], dst.at[b]) for b in range(4)]


def wait_all(waits):
    for wait in waits:
        wait()


def widen_kv(kv_ref, k2_ref, v2_ref):
    for j in range(4):
        kv = kv_ref[j].reshape(256, 128).astype(F32)
        turned = pltpu.roll(kv, 64, 1)
        low = lax.broadcasted_iota(jnp.int32, kv.shape, 1) < 64
        k2_ref[256 * j : 256 * j + 256, :] = jnp.where(low, kv, turned).astype(BF)
        v2_ref[256 * j : 256 * j + 256, :] = jnp.where(low, turned, kv).astype(BF)


def attend_tile(query_rows, route, w_qt, w_o, k2, v2, allowed):
    e0, e1, g0, g1, m0, m1 = route
    q_all = nt(query_rows, w_qt) * 0.125
    queries = jnp.concatenate([fold(q_all, m0), fold(q_all, m1)], 0).astype(BF)
    scores = nt(queries, k2)
    scores = jnp.concatenate(
        [
            jnp.where(allowed, scores[0:TILE], MASK_VALUE),
            jnp.where(allowed, scores[TILE:], MASK_VALUE),
        ],
        0,
    )
    top = jnp.max(scores, 1, keepdims=True)
    weights = jnp.exp(scores - top)
    total = jnp.sum(weights, 1, keepdims=True)
    mixed = nn(weights.astype(BF), v2) / total
    log_total = top + jnp.log(total)
    gated = spread(rounded(g0) * mixed[0:TILE], rounded(g1) * mixed[TILE:], m0, m1)
    return nn(gated, w_o), mixed, col_to_row(log_total)


def attend_back_tile(
    t, upstream, query_rows, route, mixed, log_row, w_qt, w_o, router_block, router_lane, k2, v2,
    allowed_t, grad_k, grad_v, gated_ref, dz_ref, dq_ref, dlog_ref,
):
    e0, e1, g0, g1, m0, m1 = route
    q_all = nt(query_rows, w_qt) * 0.125
    queries = jnp.concatenate([fold(q_all, m0), fold(q_all, m1)], 0).astype(BF)
    dz = upstream.astype(BF)
    dg_all = nt(dz, w_o)
    dgated0, dgated1 = fold(dg_all, m0), fold(dg_all, m1)
    r0, r1 = rounded(g0), rounded(g1)
    mixed0, mixed1 = mixed[0:TILE], mixed[TILE:]
    gated_ref[t] = spread(r0 * mixed0, r1 * mixed1, m0, m1)
    dz_ref[t] = dz
    dgate0 = rounded(jnp.sum(mixed0 * dgated0, 1, keepdims=True))
    dgate1 = rounded(jnp.sum(mixed1 * dgated1, 1, keepdims=True))
    do0, do1 = (r0 * dgated0).astype(BF), (r1 * dgated1).astype(BF)
    grad_mixed = jnp.concatenate([do0, do1], 0)
    inner_row = jnp.concatenate(
        [
            col_to_row(jnp.sum(do0.astype(F32) * mixed0, 1, keepdims=True)),
            col_to_row(jnp.sum(do1.astype(F32) * mixed1, 1, keepdims=True)),
        ],
        1,
    )
    scores = nt(k2, queries)
    scores = jnp.concatenate(
        [
            jnp.where(allowed_t, scores[:, 0:TILE], MASK_VALUE),
            jnp.where(allowed_t, scores[:, TILE:], MASK_VALUE),
        ],
        1,
    )
    probs = jnp.exp(scores - log_row)
    grad_probs = nt(v2, grad_mixed)
    grad_scores = (probs * (grad_probs - inner_row)).astype(BF)
    grad_v[...] += nn(probs.astype(BF), grad_mixed)
    grad_k[...] += nn(grad_scores, queries)
    grad_q = rounded(tn(grad_scores, k2) * 0.125)
    dq_all = spread(grad_q[0:TILE], grad_q[TILE:], m0, m1)
    dq_ref[t] = dq_all
    grad_rows = nn(dq_all, w_qt)
    mean_grad = g0 * dgate0 + g1 * dgate1
    dc0, dc1 = g0 * (dgate0 - mean_grad), g1 * (dgate1 - mean_grad)
    lanes = lax.broadcasted_iota(jnp.int32, (TILE, 16), 1)
    dlog = jnp.where(lanes == e0 + ROUTER_AT, dc0, 0.0) + jnp.where(
        lanes == e1 + ROUTER_AT, dc1, 0.0
    )
    wide = lax.broadcasted_iota(jnp.int32, (TILE, 128), 1)
    dlog_ref[t] = (
        jnp.where(wide == e0 + router_lane, dc0, 0.0)
        + jnp.where(wide == e1 + router_lane, dc1, 0.0)
    ).astype(BF)
    return grad_rows + nn(dlog.astype(BF), router_block)


def query_places(t, sec, dims, along):
    local = lax.broadcasted_iota(jnp.int32, dims, along)
    return (512 * t + 128 * sec + local + (local & ~127)).astype(F32)


def allowed_rows(t, sec, ends_q, ends_k, causal):
    query_at = query_places(t, sec, (TILE, 1), 0)
    key_at = lax.broadcasted_iota(jnp.int32, (1, 1024), 1).astype(F32)
    allowed = segments(query_at, ends_q) == segments(key_at, ends_k)
    if causal:
        allowed = allowed & (key_at <= query_at)
    return allowed


def key_segments_t(ends_k, segk_ref):
    for j in range(8):
        at = lax.broadcasted_iota(jnp.int32, (128, TILE), 0).astype(F32) + 128.0 * j
        segk_ref[128 * j : 128 * j + 128, :] = segments(at, ends_k)


def allowed_cols(t, sec, ends_q, segk_ref, causal):
    query_at = query_places(t, sec, (1, TILE), 1)
    allowed = segk_ref[...] == segments(query_at, ends_q)
    if causal:
        key_at = lax.broadcasted_iota(jnp.int32, (1024, TILE), 0).astype(F32)
        allowed = allowed & (key_at <= query_at)
    return allowed


def fold_kv(grad_k, grad_v, sec, own_ref, send_ref):
    for j in range(4):
        k = grad_k[256 * j : 256 * j + 256, :]
        v = grad_v[256 * j : 256 * j + 256, :]
        k = k + pltpu.roll(k, 64, 1)
        v = v + pltpu.roll(v, 64, 1)
        low = lax.broadcasted_iota(jnp.int32, k.shape, 1) < 64
        both = jnp.where(low, k, v)
        first, second = both[0:128], both[128:256]
        own_ref[j] = jnp.where(sec == 0, first, second)
        send_ref[j] = jnp.where(sec == 0, second, first).astype(send_ref.dtype)


def split_halves(value, sec, keep_ref, send_ref, m, lane):
    upper, lower = value[0:256], value[256:512]
    cut = slice(lane, lane + value.shape[1])
    keep_ref[m, :, cut] = jnp.where(sec == 0, upper, lower).astype(BF)
    send_ref[m, :, cut] = jnp.where(sec == 0, lower, upper).astype(BF)


def split_flat(value, sec, keep_ref, send_ref, lane):
    upper, lower = value[0:256], value[256:512]
    cut = slice(lane, lane + value.shape[1])
    keep_ref[:, cut] = jnp.where(sec == 0, upper, lower).astype(BF)
    send_ref[:, cut] = jnp.where(sec == 0, lower, upper).astype(BF)


def turned_rows(value):
    return value.astype(F32).T.astype(BF)


def flat(ref):
    return ref[...].reshape(512, ref.shape[-1])


def attention_weight_grads(first_t, gated_ref, dz_ref, dq_ref, sec, keep_ref, send_ref):
    grad_q = nn(first_t, flat(dq_ref))
    grad_o = nn(turned_rows(flat(dz_ref)), flat(gated_ref))
    for b in range(4):
        cut = slice(128 * b, 128 * b + 128)
        split_halves(grad_q[:, cut], sec, keep_ref, send_ref, b, 0)
        split_halves(grad_o[:, cut], sec, keep_ref, send_ref, b, 128)


def gelu_parts(pre):
    cdf = 0.5 * (1.0 + lax.erf(pre * 0.7071067811865476))
    slope = cdf + pre * (jnp.exp(-0.5 * pre * pre) * 0.3989422804014327)
    return pre * cdf, slope


def own_self_kv(recv_ref, layer, sec, w_kv, kv_ref):
    gain = gain_of(recv_ref, layer, 0)
    for t in range(2):
        first = norm_of(rows_of(recv_ref, layer, t), gain)[0].astype(BF)
        kv = nn(first, w_kv).astype(BF)
        for i in range(2):
            j = 2 * t + i
            kv_ref[j, sec] = kv[128 * i : 128 * i + 128]
            kv_ref[j, 1 - sec] = other_kv(recv_ref, layer, j)


def cross_kv(kvm_ref, kvo_ref, sec, kv_s):
    for j in range(4):
        kv_s[j, sec] = kvm_ref[j]
        kv_s[j, 1 - sec] = kvo_ref[j]


def pack_kernel(ids_ref, len_ref, x_ref, gain_ref, w_kv_ref, own_ref, cross_ref, router_ref, *rest):
    sends, kv_s, extra_s = rest[:8], rest[8], rest[9]
    sec, m = ids_ref[0], ids_ref[1]
    gain = gain_ref[0:1, :].astype(F32)
    w_kv = w_kv_ref[...]
    for i in range(4):
        first = norm_of(x_ref[i].astype(F32), gain)[0].astype(BF)
        kv_s[i] = nn(first, w_kv).astype(BF).reshape(2, 128, 128)
    extra_s[...] = jnp.zeros_like(extra_s)
    extra_s[0:3, :] = gain_ref[...].astype(F32)
    extra_s[ROUTER_AT : ROUTER_AT + 8, :] = router_ref[...].astype(F32)
    lanes = lax.broadcasted_iota(jnp.int32, (1, 512), 1)
    for b in range(4):
        to = m ^ b
        row = jnp.zeros((1, 512), jnp.int32)
        for k in range(8):
            length = len_ref[to, k]
            row = jnp.where(lanes == k, length >> 5, row)
            row = jnp.where(lanes == 128 + k, length & 31, row)
        extra_s[LEN_ROW : LEN_ROW + 1, :] = row.astype(F32)
        own, cross = own_ref[to], cross_ref[to]
        own_code = (own[0:1] + 8 * own[1:2]).astype(F32)
        cross_code = (cross[0:1] + 8 * cross[1:2]).astype(F32)
        for a in range(2):
            half = sec ^ a
            ref = sends[4 * a + b]
            ref[0:128, :] = x_ref[to, pl.ds(pl.multiple_of(128 * half, 128), 128), :]
            far = kv_s[to, 1 - half]
            ref[128:160, :] = jnp.concatenate([far[32 * c : 32 * c + 32] for c in range(4)], 1)
            extra_s[CODE_ROW : CODE_ROW + 1, 0:128] = jnp.where(
                half == 0, own_code[:, 0:128], own_code[:, 128:256]
            )
            extra_s[CODE_ROW : CODE_ROW + 1, 128:256] = jnp.where(
                half == 0, cross_code[:, 0:128], cross_code[:, 128:256]
            )
            ref[EX_AT : EX_AT + 16, :] = extra_s[...].astype(BF)


def self_fwd_kernel(ids_ref, *refs):
    pieces, wa_own, wa_oth, kvw_own, kvw_oth = refs[:8], refs[8:12], refs[12:16], refs[16], refs[17]
    recv_ref, h1_ref, g1_ref, mixed_e, mixed_d, log_e, log_d = refs[18:25]
    wq, wo, wkv, kv_s, k2, v2, sems = refs[25:]
    sec, m = ids_ref[0], ids_ref[1]
    loads = Loads(sems)
    come = []
    for a in range(2):
        for b in range(4):
            at = 4 * (sec ^ a) + (m ^ b)
            come.append(loads.plain(pieces[4 * a + b], recv_ref.at[at]))
    kv_waits = [loads.start(sec == i, kvw_own, kvw_oth, wkv.at[i]) for i in range(2)]
    waits = []
    for layer in range(2):
        waits += loads.rows(sec == layer, wa_own, wa_oth, 0, wq.at[layer])
        waits += loads.rows(sec == layer, wa_own, wa_oth, 128, wo.at[layer])
    wait_all(come)
    wait_all(kv_waits)
    for layer in range(2):
        own_self_kv(recv_ref, layer, sec, wkv[layer], kv_s)
        widen_kv(kv_s, k2.at[layer], v2.at[layer])
    wait_all(waits)
    ends = [ends_of(extra_of(recv_ref, layer, 0).astype(F32)) for layer in range(2)]

    def tile(t, carry):
        for layer, after_ref, mixed_ref, log_ref in (
            (0, h1_ref, mixed_e, log_e),
            (1, g1_ref, mixed_d, log_d),
        ):
            rows = rows_of(recv_ref, layer, t)
            first = norm_of(rows, gain_of(recv_ref, layer, 0))[0].astype(BF)
            route = routing(
                first, extra_of(recv_ref, layer, 0), codes_of(recv_ref, layer, t, 0), m
            )
            allowed = allowed_rows(t, sec, ends[layer], ends[layer], layer == 1)
            out, mixed, row_log = attend_tile(
                first, route, wq[layer], wo[layer], k2[layer], v2[layer], allowed
            )
            after_ref[t] = rows + out
            mixed_ref[t] = mixed
            log_ref[t] = row_log
        return carry

    lax.fori_loop(0, 2, tile, 0)


def enc_ffn_kernel(recv_ref, h1_ref, kvc_ref, *refs):
    ids_ref, f_own, f_oth = refs[0], refs[1:5], refs[5:9]
    h2_ref, mem_ref, kvm_ref, w_in, w_out, third_s, sems = refs[9:]
    low = ids_ref[0] == 0
    loads = Loads(sems)
    waits = [
        (
            loads.start(low, f_own[b], f_oth[b], w_in.at[b]),
            loads.start(low, f_oth[b], f_own[b], w_out.at[b]),
        )
        for b in range(4)
    ]
    for t in range(2):
        h2_ref[t] = h1_ref[t]
        third_s[t] = norm_of(h1_ref[t], gain_of(recv_ref, 0, 2))[0].astype(BF)
    for pair in waits:
        wait_all(pair)

    def chunk(c, carry):
        pre = nn(flat(third_s), w_in[c])
        hidden = (0.5 * pre * (1.0 + lax.erf(pre * 0.7071067811865476))).astype(BF)
        h2_ref[...] += nn(hidden, w_out[c]).reshape(2, TILE, 512)
        return carry

    lax.fori_loop(0, 4, chunk, 0)
    for t in range(2):
        memory = norm_of(h2_ref[t], gain_of(recv_ref, 0, 1))[0].astype(BF)
        mem_ref[t] = memory
        kv = nn(memory, kvc_ref[...]).astype(BF)
        kvm_ref[2 * t] = kv[0:128]
        kvm_ref[2 * t + 1] = kv[128:256]


def cross_fwd_kernel(ids_ref, recv_ref, g1_ref, kvm_ref, kvo_ref, rc_ref, *refs):
    wa_own, wa_oth = refs[:4], refs[4:8]
    g2_ref, mixed_ref, log_ref, wq, wo, kv_s, k2, v2, sems = refs[8:]
    sec, m = ids_ref[0], ids_ref[1]
    loads = Loads(sems)
    waits = loads.rows(sec == 0, wa_own, wa_oth, 256, wq)
    waits += loads.rows(sec == 0, wa_oth, wa_own, 256, wo)
    cross_kv(kvm_ref, kvo_ref, sec, kv_s)
    widen_kv(kv_s, k2, v2)
    wait_all(waits)
    ends_k = ends_of(extra_of(recv_ref, 0, 0).astype(F32))
    ends_q = ends_of(extra_of(recv_ref, 1, 0).astype(F32))

    def tile(t, carry):
        before = g1_ref[t]
        second = norm_of(before, gain_of(recv_ref, 1, 1))[0].astype(BF)
        route = routing(second, rc_ref[...], codes_of(recv_ref, 1, t, 128), m)
        allowed = allowed_rows(t, sec, ends_q, ends_k, False)
        out, mixed, row_log = attend_tile(second, route, wq[...], wo[...], k2[...], v2[...], allowed)
        g2_ref[t] = before + out
        mixed_ref[t] = mixed
        log_ref[t] = row_log
        return carry

    lax.fori_loop(0, 2, tile, 0)


def ffn_both(c, third_s, third_t, dy_s, dy_t, w_in, w_out, dthird, sec, keep_ref, send_ref):
    pre = nn(flat(third_s), w_in[c])
    hidden, slope = gelu_parts(pre)
    hidden = hidden.astype(BF)
    dpre = (nt(flat(dy_s), w_out[c]) * slope).astype(BF)
    dthird[...] += nt(dpre, w_in[c])
    split_halves(nn(third_t[...], dpre), sec, keep_ref, send_ref, c, 0)
    split_halves(nn(dy_t[...], hidden), sec, keep_ref, send_ref, c, 512)
    return hidden


def dec_ffn_kernel(ids_ref, recv_ref, g2_ref, mem_ref, *refs):
    cots, f_own, f_oth = refs[:4], refs[4:8], refs[8:12]
    outs, dg2_ref, gain_ref, keep_ref, send_ref = refs[12:20], refs[20], refs[21], refs[22], refs[23]
    w_in, w_out, cot_s, third_s, third_t, cot_t, acc, dthird, sems = refs[24:]
    sec, m = ids_ref[0], ids_ref[1]
    low = sec == 0
    loads = Loads(sems)
    cot_waits = [loads.plain(cots[b], cot_s.at[m ^ b]) for b in range(4)]
    waits = loads.blocks(low, f_own, f_oth, w_in) + loads.blocks(low, f_oth, f_own, w_out)
    for t in range(2):
        acc[t] = g2_ref[t]
        third_s[t] = norm_of(g2_ref[t], gain_of(recv_ref, 1, 2))[0].astype(BF)
    third_t[...] = turned_rows(flat(third_s))
    wait_all(cot_waits)
    cot_t[...] = turned_rows(flat(cot_s))
    dthird[...] = jnp.zeros_like(dthird)
    wait_all(waits)

    def chunk(c, carry):
        hidden = ffn_both(
            c, third_s, third_t, cot_s, cot_t, w_in, w_out, dthird, sec, keep_ref, send_ref
        )
        acc[...] += nn(hidden, w_out[c]).reshape(2, TILE, 512)
        return carry

    lax.fori_loop(0, 4, chunk, 0)
    total = jnp.zeros((1, 512), F32)
    gain = gain_of(recv_ref, 1, 2)
    for t in range(2):
        unused_out, unit, scaled = norm_of(g2_ref[t], gain)
        back, gain_grad = norm_back(dthird[TILE * t : TILE * t + TILE, :], unit, scaled, gain)
        dg2_ref[t] = cot_s[2 * t : 2 * t + 2].reshape(TILE, 512).astype(F32) + back
        total = total + gain_grad
    gain_ref[...] = total
    for a in range(2):
        for b in range(4):
            t, i = (m ^ b) >> 1, (m ^ b) & 1
            cut = pl.ds(pl.multiple_of(128 * i, 128), 128)
            outs[4 * a + b][...] = jnp.where(
                (sec ^ a) == 0, mem_ref[t, cut, :].astype(F32), acc[t, cut, :]
            ).astype(BF)


def cross_back_kernel(
    ids_ref, recv_ref, g1_ref, dg2_ref, mixed_ref, log_ref, kvm_ref, kvo_ref, rc_ref, *refs
):
    wa_own, wa_oth = refs[:4], refs[4:8]
    dg1_ref, gain_ref, own_ref, send_ref, router_ref, keepw_ref, sendw_ref = refs[8:15]
    wq, wo, kv_s, k2, v2, segk, grad_k, grad_v, second_s, gated_s, dz_s, dq_s, dlog_s, sems = refs[15:]
    sec, m = ids_ref[0], ids_ref[1]
    loads = Loads(sems)
    waits = loads.rows(sec == 0, wa_own, wa_oth, 256, wq)
    waits += loads.rows(sec == 0, wa_oth, wa_own, 256, wo)
    cross_kv(kvm_ref, kvo_ref, sec, kv_s)
    widen_kv(kv_s, k2, v2)
    ends_k = ends_of(extra_of(recv_ref, 0, 0).astype(F32))
    ends_q = ends_of(extra_of(recv_ref, 1, 0).astype(F32))
    key_segments_t(ends_k, segk)
    grad_k[...] = jnp.zeros_like(grad_k)
    grad_v[...] = jnp.zeros_like(grad_v)
    wait_all(waits)

    def tile(t, total):
        gain = gain_of(recv_ref, 1, 1)
        second, unit, scaled = norm_of(g1_ref[t], gain)
        second = second.astype(BF)
        second_s[t] = second
        route = routing(second, rc_ref[...], codes_of(recv_ref, 1, t, 128), m)
        allowed = allowed_cols(t, sec, ends_q, segk, False)
        grad_rows = attend_back_tile(
            t, dg2_ref[t], second, route, mixed_ref[t], log_ref[t], wq[...], wo[...], rc_ref[...],
            ROUTER_LANES[2], k2[...], v2[...], allowed, grad_k, grad_v, gated_s, dz_s, dq_s, dlog_s,
        )
        back, gain_grad = norm_back(grad_rows, unit, scaled, gain)
        dg1_ref[t] = dg2_ref[t] + back
        return total + gain_grad

    gain_ref[...] = lax.fori_loop(0, 2, tile, jnp.zeros((1, 512), F32))
    fold_kv(grad_k, grad_v, sec, own_ref, send_ref)
    second_t = turned_rows(flat(second_s))
    router_ref[...] = nn(second_t, flat(dlog_s))
    attention_weight_grads(second_t, gated_s, dz_s, dq_s, sec, keepw_ref, sendw_ref)


def self_back_kernel(layer, ids_ref, recv_ref, up_ref, mixed_ref, log_ref, *refs):
    wa_own, wa_oth, kvw_own, kvw_oth = refs[:4], refs[4:8], refs[8], refs[9]
    dfirst_ref, own_ref, send_ref, router_ref, keepw_ref, sendw_ref = refs[10:16]
    wq, wo, wkv, kv_s, k2, v2, segk, grad_k, grad_v = refs[16:25]
    first_s, gated_s, dz_s, dq_s, dlog_s, sems = refs[25:]
    sec, m = ids_ref[0], ids_ref[1]
    mine = sec == layer
    loads = Loads(sems)
    kv_wait = loads.start(mine, kvw_own, kvw_oth, wkv)
    waits = loads.rows(mine, wa_own, wa_oth, 0, wq) + loads.rows(mine, wa_own, wa_oth, 128, wo)
    ends = ends_of(extra_of(recv_ref, layer, 0).astype(F32))
    key_segments_t(ends, segk)
    grad_k[...] = jnp.zeros_like(grad_k)
    grad_v[...] = jnp.zeros_like(grad_v)
    kv_wait()
    own_self_kv(recv_ref, layer, sec, wkv[...], kv_s)
    widen_kv(kv_s, k2, v2)
    wait_all(waits)
    router_block = extra_of(recv_ref, layer, 0)

    def tile(t, carry):
        first = norm_of(rows_of(recv_ref, layer, t), gain_of(recv_ref, layer, 0))[0].astype(BF)
        first_s[t] = first
        route = routing(first, router_block, codes_of(recv_ref, layer, t, 0), m)
        allowed = allowed_cols(t, sec, ends, segk, layer == 1)
        dfirst_ref[t] = attend_back_tile(
            t, up_ref[t], first, route, mixed_ref[t], log_ref[t], wq[...], wo[...], router_block,
            ROUTER_LANES[layer], k2[...], v2[...], allowed, grad_k, grad_v, gated_s, dz_s, dq_s,
            dlog_s,
        )
        return carry

    lax.fori_loop(0, 2, tile, 0)
    fold_kv(grad_k, grad_v, sec, own_ref, send_ref)
    first_t = turned_rows(flat(first_s))
    router_ref[...] = nn(first_t, flat(dlog_s))
    attention_weight_grads(first_t, gated_s, dz_s, dq_s, sec, keepw_ref, sendw_ref)


def enc_ffn_back_kernel(ids_ref, recv_ref, h1_ref, h2_ref, own_ref, come_ref, kvc_ref, *refs):
    f_own, f_oth = refs[:4], refs[4:8]
    dh1_ref, gain_ref, gain2_ref, keep_ref, send_ref = refs[8:13]
    w_in, w_out, third_s, third_t, dy_s, dy_t, dthird, sems = refs[13:]
    sec = ids_ref[0]
    low = sec == 0
    loads = Loads(sems)
    waits = loads.blocks(low, f_own, f_oth, w_in) + loads.blocks(low, f_oth, f_own, w_out)
    total = jnp.zeros((1, 512), F32)
    gain = gain_of(recv_ref, 0, 1)
    for t in range(2):
        dkv = (own_ref[2 * t : 2 * t + 2] + come_ref[2 * t : 2 * t + 2].astype(F32)).astype(BF)
        dmem = rounded(nt(dkv.reshape(TILE, 128), kvc_ref[...]))
        unused_out, unit, scaled = norm_of(h2_ref[t], gain)
        back, gain_grad = norm_back(dmem, unit, scaled, gain)
        dh1_ref[t] = back
        dy_s[t] = back.astype(BF)
        third_s[t] = norm_of(h1_ref[t], gain_of(recv_ref, 0, 2))[0].astype(BF)
        total = total + gain_grad
    gain_ref[...] = total
    third_t[...] = turned_rows(flat(third_s))
    dy_t[...] = turned_rows(flat(dy_s))
    dthird[...] = jnp.zeros_like(dthird)
    wait_all(waits)

    def chunk(c, carry):
        ffn_both(c, third_s, third_t, dy_s, dy_t, w_in, w_out, dthird, sec, keep_ref, send_ref)
        return carry

    lax.fori_loop(0, 4, chunk, 0)
    total = jnp.zeros((1, 512), F32)
    gain = gain_of(recv_ref, 0, 2)
    for t in range(2):
        unused_out, unit, scaled = norm_of(h1_ref[t], gain)
        back, gain_grad = norm_back(dthird[TILE * t : TILE * t + TILE, :], unit, scaled, gain)
        dh1_ref[t] += back
        total = total + gain_grad
    gain2_ref[...] = total


def finish_rows(layer, recv_ref, up_ref, df_ref, own_ref, come_ref, wkv, first_s, dx_s):
    total = jnp.zeros((1, 512), F32)
    gain = gain_of(recv_ref, layer, 0)
    dkvs = []
    for t in range(2):
        first, unit, scaled = norm_of(rows_of(recv_ref, layer, t), gain)
        first_s[t] = first.astype(BF)
        dkv = (own_ref[2 * t : 2 * t + 2] + come_ref[2 * t : 2 * t + 2].astype(F32)).astype(BF)
        dkv = dkv.reshape(TILE, 128)
        dkvs.append(dkv)
        back, gain_grad = norm_back(df_ref[t] + nt(dkv, wkv), unit, scaled, gain)
        dx_s[t] = (up_ref[t] + back).astype(BF)
        total = total + gain_grad
    grad = nn(turned_rows(flat(first_s)), jnp.concatenate(dkvs, 0))
    return total, grad


def dec_finish_kernel(
    ids_ref, recv_ref, up_ref, df_ref, own_ref, come_ref, own_c, come_c, mem_ref, kvw_own, kvw_oth,
    dx_ref, gain_ref, keep_ref, send_ref,
    wkv, first_s, sems,
):
    sec = ids_ref[0]
    wait = Loads(sems).start(sec == 1, kvw_own, kvw_oth, wkv)
    dkv_c = (own_c[...] + come_c[...].astype(F32)).astype(BF).reshape(512, 128)
    split_flat(nn(turned_rows(flat(mem_ref)), dkv_c), sec, keep_ref, send_ref, 128)
    wait()
    gain_ref[...], grad = finish_rows(
        1, recv_ref, up_ref, df_ref, own_ref, come_ref, wkv[...], first_s, dx_ref
    )
    split_flat(grad, sec, keep_ref, send_ref, 0)


def enc_finish_kernel(
    ids_ref, recv_ref, up_ref, df_ref, own_ref, come_ref, dx1_ref, r0, r1, rc,
    gain_e1, gain_e2, gain_d0, gain_d1, gain_d2, kvw_own, kvw_oth, *refs
):
    outs, keep_ref, send_ref, wkv, first_s, dx_s, sems = refs[:8], *refs[8:]
    sec, m = ids_ref[0], ids_ref[1]
    Loads(sems).start(sec == 0, kvw_own, kvw_oth, wkv)()
    gain_e0, grad = finish_rows(
        0, recv_ref, up_ref, df_ref, own_ref, come_ref, wkv[...], first_s, dx_s
    )
    split_flat(grad, sec, keep_ref, send_ref, 0)
    for a in range(2):
        for b in range(4):
            t, i = (m ^ b) >> 1, (m ^ b) & 1
            cut = pl.ds(pl.multiple_of(128 * i, 128), 128)
            outs[4 * a + b][...] = jnp.where(
                (sec ^ a) == 0, dx_s[t, cut, :].astype(F32), dx1_ref[t, cut, :].astype(F32)
            ).astype(BF)
    gains = (gain_e0, gain_e1[...], gain_e2[...], gain_d0[...], gain_d1[...], gain_d2[...])
    lanes = lax.broadcasted_iota(jnp.int32, (128, 128), 1)
    blocks = []
    for b in range(4):
        cut = slice(128 * b, 128 * b + 128)
        misc = r0[cut, :] + r1[cut, :] + rc[cut, :]
        for i, row in enumerate(gains):
            misc = misc + jnp.where(lanes == GAIN_LANE + i, row_to_col(row[:, cut]), 0.0)
        blocks.append(misc)
    for b in range(2):
        cut = slice(128 * b, 128 * b + 128)
        keep_ref[cut, 128:256] = jnp.where(sec == 0, blocks[b], blocks[b + 2]).astype(BF)
        send_ref[cut, 128:256] = jnp.where(sec == 0, blocks[b + 2], blocks[b]).astype(BF)


def add_kernel(counts, *refs):
    n = len(counts)
    keeps, comes, outs = refs[:n], refs[n : 2 * n], refs[2 * n :]
    for b in range(4):
        lane = 0
        for keep, come, (pieces, width) in zip(keeps, comes, counts):
            left = keep[b] if pieces == 4 else keep[...]
            right = come[b] if pieces == 4 else come[...]
            outs[b][:, lane : lane + width] = (left.astype(F32) + right.astype(F32)).astype(BF)
            lane += width


def sum_kernel(ids_ref, *refs):
    groups = (len(refs) - 4) // 4
    outs = refs[4 * groups :]
    rows = outs[0].shape[0]
    d = ids_ref[2]
    for k in range(4):
        cut = pl.ds(pl.multiple_of((d ^ k) * rows, rows), rows)
        lane = 0
        for g in range(groups):
            parts = refs[4 * g : 4 * g + 4]
            total = parts[0][cut, :].astype(F32)
            for part in parts[1:]:
                total = total + part[cut, :].astype(F32)
            width = parts[0].shape[1]
            outs[k][:, lane : lane + width] = total.astype(BF)
            lane += width


def place_kernel(ids_ref, *refs):
    pieces, out_ref, buf, sems = refs[:8], refs[8], refs[9], refs[10]
    sec, m = ids_ref[0], ids_ref[1]
    loads = Loads(sems)
    waits = [loads.plain(pieces[i], buf.at[i]) for i in range(8)]
    wait_all(waits)
    for a in range(2):
        for b in range(4):
            out_ref[m ^ b, sec ^ a] = buf[4 * a + b].astype(out_ref.dtype)


def shaped(dims, kind):
    return jax.ShapeDtypeStruct(dims, kind)


def run(kernel, args, places, outs, scratch, flops):
    space = {
        "s": pl.BlockSpec(memory_space=pltpu.SMEM),
        "v": pl.BlockSpec(memory_space=pltpu.VMEM),
        "a": pl.BlockSpec(memory_space=pl.ANY),
    }
    return pl.pallas_call(
        kernel,
        out_shape=outs,
        in_specs=[space[p] for p in places],
        out_specs=jax.tree.map(lambda _: space["v"], outs),
        scratch_shapes=scratch,
        compiler_params=pltpu.CompilerParams(vmem_limit_bytes=VMEM_LIMIT),
        cost_estimate=pl.CostEstimate(flops=flops, bytes_accessed=8 << 20, transcendentals=0),
    )(*args)


def vm(*dims, kind=BF):
    return pltpu.VMEM(dims, kind)


def dma(count):
    return pltpu.SemaphoreType.DMA((count,))


def across(value, axes, size, by):
    return lax.ppermute(value, axes, [(i, i ^ by) for i in range(size)])


def swapped(value):
    return across(value, "section", 2, 1)


def group_exchange(pieces):
    return [pieces[0]] + [across(pieces[i], ("section", "mp"), 8, i) for i in range(1, 8)]


def mp_exchange(pieces):
    return [pieces[0]] + [across(pieces[b], "mp", 4, b) for b in range(1, 4)]


def gathered(value):
    return mp_exchange([value] * 4)


def dp_sum(pieces):
    come = [pieces[0]] + [across(pieces[k], "dp", 4, k) for k in range(1, 4)]
    total = come[0].astype(F32)
    for piece in come[1:]:
        total = total + piece.astype(F32)
    return total


def add_shares(keeps, comes):
    counts = tuple((4 if k.ndim == 3 else 1, k.shape[-1]) for k in keeps)
    width = sum(c[1] for c in counts)
    return run(
        functools.partial(add_kernel, counts),
        (*keeps, *comes),
        "v" * (2 * len(keeps)),
        [shaped((256, width), BF)] * 4,
        [],
        10**8,
    )


def sum_over_rows(ids, groups):
    dp = lax.axis_size("dp")
    width = sum(g[0].shape[1] for g in groups)
    if dp == 4:
        args = [piece for g in groups for piece in g]
        pieces = run(
            sum_kernel,
            (ids, *args),
            "s" + "v" * len(args),
            [shaped((64, width), BF)] * 4,
            [],
            10**8,
        )
        return dp_sum(pieces)
    totals = []
    for group in groups:
        total = group[0].astype(F32)
        for piece in group[1:]:
            total = total + piece.astype(F32)
        totals.append(total)
    quarter = jnp.concatenate(totals, 1).astype(BF).reshape(dp, 256 // dp, width)
    come = lax.all_to_all(quarter, "dp", split_axis=0, concat_axis=0, tiled=True)
    return jnp.sum(come.astype(F32), 0)


def per_device(
    inputs,
    lengths,
    routes_self,
    routes_cross,
    gains,
    router_self,
    query_self,
    keyval_self,
    output_self,
    ffn_in,
    ffn_out,
    router_cross,
    query_cross,
    keyval_cross,
    output_cross,
    cotangent,
):
    sec, m, d = lax.axis_index("section"), lax.axis_index("mp"), lax.axis_index("dp")
    low = sec == 0
    ids = jnp.stack([sec, m, d]).astype(jnp.int32)
    sem = dma(40)

    q_rows = query_self[0].transpose(0, 2, 1).reshape(128, 512)
    o_rows = output_self[0].reshape(128, 512)
    c_rows = jnp.where(
        low, query_cross.transpose(0, 2, 1).reshape(128, 512), output_cross.reshape(128, 512)
    )
    wa_own = gathered(jnp.concatenate([q_rows, o_rows, c_rows], 0))
    kvw_own = keyval_self[0]
    kvw_oth = swapped(kvw_own)
    router_c = jnp.concatenate([jnp.zeros((8, 512), BF), router_cross.T], 0)

    packed = run(
        pack_kernel,
        (
            ids,
            lengths[0, :, 0],
            inputs[0, :, 0],
            gains[0],
            keyval_self[0],
            routes_self[0, :, 0].transpose(0, 2, 1),
            routes_cross[:, 0].transpose(0, 2, 1),
            router_self[0].T,
        ),
        "ssvvvvvv",
        [shaped((176, 512), BF)] * 8,
        [vm(4, 2, 128, 128), vm(16, 512, kind=F32)],
        10**9,
    )
    pieces = group_exchange(packed)
    wa_oth = [swapped(piece) for piece in wa_own]

    w_in, w_out = ffn_in[0], ffn_out[0]
    half_come = swapped(jnp.where(low, w_out, w_in))
    enc_own = gathered(jnp.where(low, w_in, half_come))
    enc_oth = [swapped(piece) for piece in enc_own]
    dec_own = gathered(jnp.where(low, half_come, w_out))
    dec_oth = [swapped(piece) for piece in dec_own]
    cot_cut = cotangent[:, 0].reshape(4, 2, 128, 512)
    cots = mp_exchange([cot_cut[m ^ b, sec] for b in range(4)])

    act = shaped((2, TILE, 512), F32)
    actb = shaped((2, TILE, 512), BF)
    mixed_s = shaped((2, 2 * TILE, 128), F32)
    log_s = shaped((2, 1, 2 * TILE), F32)
    kv_b = shaped((4, 128, 128), BF)
    kv_f = shaped((4, 128, 128), F32)
    row_s = shaped((1, 512), F32)
    ffn_g = shaped((4, 256, 1024), BF)
    att_g = shaped((4, 256, 256), BF)
    flat_g = shaped((256, 256), BF)
    lane_s = shaped((512, 128), F32)
    wide = [vm(512, 512), vm(512, 512)]
    kv_scratch = [vm(4, 2, 128, 128), vm(1024, 128), vm(1024, 128)]
    back_scratch = [
        vm(1024, TILE, kind=F32), vm(1024, 128, kind=F32), vm(1024, 128, kind=F32),
        vm(2, TILE, 512), vm(2, TILE, 512), vm(2, TILE, 512), vm(2, TILE, 512), vm(2, TILE, 128),
    ]
    ffn_w = [vm(4, 512, 512), vm(4, 512, 512)]

    recv, h1, g1, mixed_e, mixed_d, log_e, log_d = run(
        self_fwd_kernel,
        (ids, *pieces, *wa_own, *wa_oth, kvw_own, kvw_oth),
        "s" + "a" * 18,
        (shaped((8, 176, 512), BF), act, act, mixed_s, mixed_s, log_s, log_s),
        [vm(2, 512, 512), vm(2, 512, 512), vm(2, 512, 128), vm(4, 2, 128, 128)]
        + [vm(2, 1024, 128), vm(2, 1024, 128), sem],
        4 * 10**9,
    )
    h2, memory, kvm = run(
        enc_ffn_kernel,
        (recv, h1, keyval_cross, ids, *enc_own, *enc_oth),
        "vvvs" + "a" * 8,
        (act, actb, kv_b),
        ffn_w + [vm(2, TILE, 512), sem],
        4 * 10**9,
    )
    kvm_oth = swapped(kvm)
    g2, mixed_c, log_c = run(
        cross_fwd_kernel,
        (ids, recv, g1, kvm, kvm_oth, router_c, *wa_own, *wa_oth),
        "svvvvv" + "a" * 8,
        (act, mixed_s, log_s),
        wide + kv_scratch + [sem],
        2 * 10**9,
    )
    dec_ffn = run(
        dec_ffn_kernel,
        (ids, recv, g2, memory, *cots, *dec_own, *dec_oth),
        "svvv" + "a" * 12,
        [shaped((128, 512), BF)] * 8 + [act, row_s, ffn_g, ffn_g],
        ffn_w
        + [vm(4, 128, 512), vm(2, TILE, 512), vm(512, 512), vm(512, 512)]
        + [vm(2, TILE, 512, kind=F32), vm(512, 512, kind=F32), sem],
        12 * 10**9,
    )
    out_pieces, (dg2, gain_d2, keep_d, send_d) = dec_ffn[:8], dec_ffn[8:]
    come_d = swapped(send_d)
    outs_come = group_exchange(out_pieces)
    dg1, gain_d1, own_c, sendkv_c, router_cg, keep_wc, send_wc = run(
        cross_back_kernel,
        (ids, recv, g1, dg2, mixed_c, log_c, kvm, kvm_oth, router_c, *wa_own, *wa_oth),
        "svvvvvvvv" + "a" * 8,
        (act, row_s, kv_f, kv_b, lane_s, att_g, att_g),
        wide + kv_scratch + back_scratch + [sem],
        4 * 10**9,
    )
    comekv_c = swapped(sendkv_c)
    come_wc = swapped(send_wc)
    ffn_d_parts = mp_exchange(add_shares([keep_d], [come_d]))
    self_scratch = wide + [vm(512, 128)] + kv_scratch + back_scratch + [sem]
    self_outs = (act, kv_f, kv_b, lane_s, att_g, att_g)
    df1, own_1, sendkv_1, router_1g, keep_w1, send_w1 = run(
        functools.partial(self_back_kernel, 1),
        (ids, recv, dg1, mixed_d, log_d, *wa_own, *wa_oth, kvw_own, kvw_oth),
        "svvvv" + "a" * 10,
        self_outs,
        self_scratch,
        4 * 10**9,
    )
    comekv_1 = swapped(sendkv_1)
    come_w1 = swapped(send_w1)
    dh1, gain_e1, gain_e2, keep_e, send_e = run(
        enc_ffn_back_kernel,
        (ids, recv, h1, h2, own_c, comekv_c, keyval_cross, *enc_own, *enc_oth),
        "svvvvvv" + "a" * 8,
        (act, row_s, row_s, ffn_g, ffn_g),
        ffn_w
        + [vm(2, TILE, 512), vm(512, 512), vm(2, TILE, 512), vm(512, 512)]
        + [vm(512, 512, kind=F32), sem],
        12 * 10**9,
    )
    come_e = swapped(send_e)
    dx1, gain_d0, keep_s1, send_s1 = run(
        dec_finish_kernel,
        (ids, recv, dg1, df1, own_1, comekv_1, own_c, comekv_c, memory, kvw_own, kvw_oth),
        "svvvvvvvvaa",
        (actb, row_s, flat_g, flat_g),
        [vm(512, 128), vm(2, TILE, 512), sem],
        10**9,
    )
    come_s1 = swapped(send_s1)
    df0, own_0, sendkv_0, router_0g, keep_w0, send_w0 = run(
        functools.partial(self_back_kernel, 0),
        (ids, recv, dh1, mixed_e, log_e, *wa_own, *wa_oth, kvw_own, kvw_oth),
        "svvvv" + "a" * 10,
        self_outs,
        self_scratch,
        4 * 10**9,
    )
    comekv_0 = swapped(sendkv_0)
    come_w0 = swapped(send_w0)
    ffn_e_parts = mp_exchange(add_shares([keep_e], [come_e]))
    att_d_parts = mp_exchange(
        add_shares([keep_wc, keep_w1, keep_s1], [come_wc, come_w1, come_s1])
    )
    finish = run(
        enc_finish_kernel,
        (
            ids, recv, dh1, df0, own_0, comekv_0, dx1, router_0g, router_1g, router_cg,
            gain_e1, gain_e2, gain_d0, gain_d1, gain_d2, kvw_own, kvw_oth,
        ),
        "s" + "v" * 14 + "aa",
        [shaped((128, 512), BF)] * 8 + [flat_g, flat_g],
        [vm(512, 128), vm(2, TILE, 512), vm(2, TILE, 512), sem],
        10**9,
    )
    dx_pieces, (keep_s0, send_s0) = finish[:8], finish[8:]
    come_s0 = swapped(send_s0)
    dx_come = group_exchange(dx_pieces)
    att_e_parts = mp_exchange(add_shares([keep_w0, keep_s0], [come_w0, come_s0]))

    ffn_dec = sum_over_rows(ids, [ffn_d_parts])
    att_dec = sum_over_rows(ids, [att_d_parts])
    ffn_enc = sum_over_rows(ids, [ffn_e_parts])
    att_enc = sum_over_rows(ids, [att_e_parts])

    def placed(come, kind):
        whole = run(
            place_kernel,
            (ids, *come),
            "s" + "a" * 8,
            shaped((4, 2, 128, 512), kind),
            [vm(8, 128, 512), dma(8)],
            10**8,
        )
        return whole.reshape(1, 4, 1, 256, 512)

    share = att_enc.shape[0]

    def query_of(value, at):
        return value[:, at : at + 128].reshape(share, 2, 64).transpose(1, 0, 2)

    def output_of(value, at):
        return value[:, at : at + 128].T.reshape(2, 64, share)

    misc = att_enc[:, 384:512]

    def router_of(layer):
        return misc[:, ROUTER_LANES[layer] : ROUTER_LANES[layer] + 8]

    return (
        placed(outs_come, BF),
        placed(dx_come, F32),
        misc[:, GAIN_LANE : GAIN_LANE + 6].T.reshape(2, 3, share),
        jnp.stack([router_of(0), router_of(1)]),
        jnp.stack([query_of(att_enc, 0), query_of(att_dec, 256)]),
        jnp.stack([att_enc[:, 256:384], att_dec[:, 512:640]]),
        jnp.stack([output_of(att_enc, 128), output_of(att_dec, 384)]),
        jnp.stack([ffn_enc[:, :512], ffn_dec[:, :512]]),
        jnp.stack([ffn_enc[:, 512:].T, ffn_dec[:, 512:].T]),
        router_of(2),
        query_of(att_dec, 0),
        att_dec[:, 640:768],
        output_of(att_dec, 128),
    )


def solution(mesh):
    placed = (
        P("section", None, "dp", "mp", None),
        P("section", None, "dp", None),
        P("section", None, "dp", "mp", None),
        P(None, "dp", "mp", None),
        P("section", None, None),
        P("section", None, None),
        P("section", "mp", None, None),
        P("section", None, None),
        P("section", "mp", None, None),
        P("section", None, "mp"),
        P("section", "mp", None),
        P(),
        P("mp", None, None),
        P(),
        P("mp", None, None),
        P(None, "dp", "mp", None),
    )
    return jax.shard_map(
        per_device,
        mesh=mesh,
        in_specs=placed,
        out_specs=(
            P("section", None, "dp", "mp", None),
            P("section", None, "dp", "mp", None),
            P(None, None, ("section", "dp")),
            P(None, ("section", "dp"), None),
            P(None, "mp", ("section", "dp"), None),
            P(None, ("section", "dp"), None),
            P(None, "mp", None, ("section", "dp")),
            P(None, ("section", "dp"), "mp"),
            P(None, "mp", ("section", "dp")),
            P(("section", "dp"), None),
            P("mp", ("section", "dp"), None),
            P(("section", "dp"), None),
            P("mp", None, ("section", "dp")),
        ),
        check_vma=False,
    )
```

```python
import functools

import jax
import jax.numpy as jnp
from jax import lax
from jax.experimental import pallas as pl
from jax.experimental.pallas import tpu as pltpu
from jax.sharding import PartitionSpec as P

EPS = 1e-05
MASK_VALUE = -1000000000.0
BF = jnp.bfloat16
F32 = jnp.float32
TILE = 256
EX_AT = 160
CODE_ROW = 3
LEN_ROW = 4
ROUTER_AT = 8
GAIN_ROW = 24
ROUTER_LANES = (0, 8, 16)
VMEM_LIMIT = 56 * 1024 * 1024


def nn(left, right):
    return lax.dot_general(left, right, (((1,), (0,)), ((), ())), preferred_element_type=F32)


def nt(left, right):
    return lax.dot_general(left, right, (((1,), (1,)), ((), ())), preferred_element_type=F32)


def tn(left, right):
    return lax.dot_general(left, right, (((0,), (0,)), ((), ())), preferred_element_type=F32)


def norm_of(values, gain_row):
    center = values - jnp.mean(values, 1, keepdims=True)
    scaled = lax.rsqrt(jnp.mean(center * center, 1, keepdims=True) + EPS)
    unit_rows = center * scaled
    return unit_rows * gain_row, unit_rows, scaled


def norm_back(upstream, unit_rows, scaled, gain_row):
    inner = upstream * gain_row
    result = scaled * (
        inner
        - jnp.mean(inner, 1, keepdims=True)
        - unit_rows * jnp.mean(inner * unit_rows, 1, keepdims=True)
    )
    return result, jnp.sum(upstream * unit_rows, 0, keepdims=True)


def eye_of(size):
    return lax.broadcasted_iota(jnp.int32, (size, size), 0) == lax.broadcasted_iota(
        jnp.int32, (size, size), 1
    )


def row_to_col(row):
    return jnp.sum(jnp.where(eye_of(128), row, 0.0), 1, keepdims=True)


def col_to_row(col):
    parts = []
    for at in range(0, col.shape[0], 128):
        part = jnp.where(eye_of(128), col[at : at + 128], 0.0)
        parts.append(jnp.sum(part, 0, keepdims=True))
    return jnp.concatenate(parts, 1)


def ends_of(extra):
    lengths = extra[LEN_ROW : LEN_ROW + 1, 0:8] * 32.0 + extra[LEN_ROW : LEN_ROW + 1, 128:136]
    ends = [lengths[:, 0:1]]
    for k in range(1, 8):
        ends.append(ends[-1] + lengths[:, k : k + 1])
    return ends


def segments(places, ends):
    total = jnp.where(places >= ends[0], 1.0, 0.0)
    for end in ends[1:]:
        total = total + jnp.where(places >= end, 1.0, 0.0)
    return total


def extra_of(recv_ref, layer, quarter):
    return recv_ref[4 * layer + quarter, EX_AT : EX_AT + 16, :]


def gain_of(recv_ref, layer, which):
    return extra_of(recv_ref, layer, 0).astype(F32)[which : which + 1, :]


def rows_of(recv_ref, layer, t):
    return recv_ref[pl.ds(4 * layer + 2 * t, 2), 0:128, :].reshape(TILE, 512).astype(F32)


def codes_of(recv_ref, layer, t, lane):
    cols = []
    for i in range(2):
        extra = extra_of(recv_ref, layer, 2 * t + i).astype(F32)
        cols.append(row_to_col(extra[CODE_ROW : CODE_ROW + 1, lane : lane + 128]))
    return jnp.concatenate(cols, 0)


def other_kv(recv_ref, layer, quarter):
    packed = recv_ref[4 * layer + quarter, 128:160, :]
    return jnp.concatenate([packed[:, 128 * c : 128 * c + 128] for c in range(4)], 0)


def routing(query_rows, router_block, code):
    second = jnp.floor(code * 0.125)
    first = code - 8.0 * second
    e0, e1 = first.astype(jnp.int32), second.astype(jnp.int32)
    logits = nt(query_rows, router_block)
    lanes = lax.broadcasted_iota(jnp.int32, logits.shape, 1)
    l0 = jnp.sum(jnp.where(lanes == e0 + ROUTER_AT, logits, 0.0), 1, keepdims=True)
    l1 = jnp.sum(jnp.where(lanes == e1 + ROUTER_AT, logits, 0.0), 1, keepdims=True)
    top = jnp.maximum(l0, l1)
    x0, x1 = jnp.exp(l0 - top), jnp.exp(l1 - top)
    total = x0 + x1
    owners = lax.broadcasted_iota(jnp.int32, (code.shape[0], 512), 1) >> 6
    return e0, e1, x0 / total, x1 / total, owners == e0, owners == e1


def fold(wide, mask):
    kept = jnp.where(mask, wide, 0.0)
    return kept[:, 0:128] + kept[:, 128:256] + kept[:, 256:384] + kept[:, 384:512]


def spread(a0, a1, m0, m1):
    parts = []
    for c in range(4):
        cut = slice(128 * c, 128 * c + 128)
        parts.append(jnp.where(m0[:, cut], a0, jnp.where(m1[:, cut], a1, 0.0)))
    return jnp.concatenate(parts, 1).astype(BF)


def rounded(value):
    return value.astype(BF).astype(F32)


def start_pick(cond, yes, no, dst, sem):
    @pl.when(cond)
    def _():
        pltpu.make_async_copy(yes, dst, sem).start()

    @pl.when(jnp.logical_not(cond))
    def _():
        pltpu.make_async_copy(no, dst, sem).start()


class Loads:
    def __init__(self, sems):
        self.sems, self.used = sems, 0

    def start(self, cond, yes, no, dst):
        sem = self.sems.at[self.used]
        self.used += 1
        start_pick(cond, yes, no, dst, sem)
        return functools.partial(lambda a, b, c: pltpu.make_async_copy(a, b, c).wait(), yes, dst, sem)

    def plain(self, src, dst):
        sem = self.sems.at[self.used]
        self.used += 1
        copy = pltpu.make_async_copy(src, dst, sem)
        copy.start()
        return copy.wait

    def rows(self, cond, yes, no, at, dst, m):
        cut = pl.ds(at, 128)
        return [
            self.start(cond, yes[b].at[cut], no[b].at[cut], dst.at[pl.ds(128 * (m ^ b), 128)])
            for b in range(4)
        ]

    def stacked(self, cond, yes, no, at, dst):
        cut = pl.ds(at, 128)
        return [
            self.start(cond, yes.at[i, cut], no.at[i, cut], dst.at[pl.ds(128 * i, 128)])
            for i in range(4)
        ]

    def pieces(self, cond, yes, no, dst, m):
        return [self.start(cond, yes[b], no[b], dst.at[m ^ b]) for b in range(4)]


def wait_all(waits):
    for wait in waits:
        wait()


def widen_kv(kv_ref, k2_ref, v2_ref):
    for j in range(4):
        kv = kv_ref[j].reshape(256, 128).astype(F32)
        turned = pltpu.roll(kv, 64, 1)
        low = lax.broadcasted_iota(jnp.int32, kv.shape, 1) < 64
        k2_ref[256 * j : 256 * j + 256, :] = jnp.where(low, kv, turned).astype(BF)
        v2_ref[256 * j : 256 * j + 256, :] = jnp.where(low, turned, kv).astype(BF)


def attend_tile(query_rows, route, w_qt, w_o, k2, v2, allowed):
    e0, e1, g0, g1, m0, m1 = route
    q_all = nt(query_rows, w_qt) * 0.125
    queries = jnp.concatenate([fold(q_all, m0), fold(q_all, m1)], 0).astype(BF)
    scores = nt(queries, k2)
    scores = jnp.concatenate(
        [
            jnp.where(allowed, scores[0:TILE], MASK_VALUE),
            jnp.where(allowed, scores[TILE:], MASK_VALUE),
        ],
        0,
    )
    top = jnp.max(scores, 1, keepdims=True)
    weights = jnp.exp(scores - top)
    total = jnp.sum(weights, 1, keepdims=True)
    mixed = nn(weights.astype(BF), v2) / total
    log_total = top + jnp.log(total)
    gated = spread(rounded(g0) * mixed[0:TILE], rounded(g1) * mixed[TILE:], m0, m1)
    return nn(gated, w_o), mixed, col_to_row(log_total)


def attend_back_tile(
    t, upstream, query_rows, route, mixed, log_row, w_qt, w_o, router_block, router_lane, k2, v2,
    allowed_t, grad_k, grad_v, gated_ref, dz_ref, dq_ref, dlog_ref,
):
    e0, e1, g0, g1, m0, m1 = route
    q_all = nt(query_rows, w_qt) * 0.125
    queries = jnp.concatenate([fold(q_all, m0), fold(q_all, m1)], 0).astype(BF)
    dz = upstream.astype(BF)
    dg_all = nt(dz, w_o)
    dgated0, dgated1 = fold(dg_all, m0), fold(dg_all, m1)
    r0, r1 = rounded(g0), rounded(g1)
    mixed0, mixed1 = mixed[0:TILE], mixed[TILE:]
    gated_ref[t] = spread(r0 * mixed0, r1 * mixed1, m0, m1)
    dz_ref[t] = dz
    dgate0 = rounded(jnp.sum(mixed0 * dgated0, 1, keepdims=True))
    dgate1 = rounded(jnp.sum(mixed1 * dgated1, 1, keepdims=True))
    do0, do1 = (r0 * dgated0).astype(BF), (r1 * dgated1).astype(BF)
    grad_mixed = jnp.concatenate([do0, do1], 0)
    inner_row = jnp.concatenate(
        [
            col_to_row(jnp.sum(do0.astype(F32) * mixed0, 1, keepdims=True)),
            col_to_row(jnp.sum(do1.astype(F32) * mixed1, 1, keepdims=True)),
        ],
        1,
    )
    scores = nt(k2, queries)
    scores = jnp.concatenate(
        [
            jnp.where(allowed_t, scores[:, 0:TILE], MASK_VALUE),
            jnp.where(allowed_t, scores[:, TILE:], MASK_VALUE),
        ],
        1,
    )
    probs = jnp.exp(scores - log_row)
    grad_probs = nt(v2, grad_mixed)
    grad_scores = (probs * (grad_probs - inner_row)).astype(BF)
    grad_v[...] += nn(probs.astype(BF), grad_mixed)
    grad_k[...] += nn(grad_scores, queries)
    grad_q = rounded(tn(grad_scores, k2) * 0.125)
    dq_all = spread(grad_q[0:TILE], grad_q[TILE:], m0, m1)
    dq_ref[t] = dq_all
    grad_rows = nn(dq_all, w_qt)
    mean_grad = g0 * dgate0 + g1 * dgate1
    dc0, dc1 = g0 * (dgate0 - mean_grad), g1 * (dgate1 - mean_grad)
    lanes = lax.broadcasted_iota(jnp.int32, (TILE, 16), 1)
    dlog = jnp.where(lanes == e0 + ROUTER_AT, dc0, 0.0) + jnp.where(
        lanes == e1 + ROUTER_AT, dc1, 0.0
    )
    wide = lax.broadcasted_iota(jnp.int32, (TILE, 128), 1)
    dlog_ref[t] = (
        jnp.where(wide == e0 + router_lane, dc0, 0.0)
        + jnp.where(wide == e1 + router_lane, dc1, 0.0)
    ).astype(BF)
    return grad_rows + nn(dlog.astype(BF), router_block)


def query_places(t, sec, dims, along):
    local = lax.broadcasted_iota(jnp.int32, dims, along)
    return (512 * t + 128 * sec + local + (local & ~127)).astype(F32)


def allowed_rows(t, sec, ends_q, ends_k, causal):
    query_at = query_places(t, sec, (TILE, 1), 0)
    key_at = lax.broadcasted_iota(jnp.int32, (1, 1024), 1).astype(F32)
    allowed = segments(query_at, ends_q) == segments(key_at, ends_k)
    if causal:
        allowed = allowed & (key_at <= query_at)
    return allowed


def key_segments_t(ends_k, segk_ref):
    for j in range(8):
        at = lax.broadcasted_iota(jnp.int32, (128, TILE), 0).astype(F32) + 128.0 * j
        segk_ref[128 * j : 128 * j + 128, :] = segments(at, ends_k)


def allowed_cols(t, sec, ends_q, segk_ref, causal):
    query_at = query_places(t, sec, (1, TILE), 1)
    allowed = segk_ref[...] == segments(query_at, ends_q)
    if causal:
        key_at = lax.broadcasted_iota(jnp.int32, (1024, TILE), 0).astype(F32)
        allowed = allowed & (key_at <= query_at)
    return allowed


def fold_kv(grad_k, grad_v, sec, own_ref, send_ref):
    for j in range(4):
        k = grad_k[256 * j : 256 * j + 256, :]
        v = grad_v[256 * j : 256 * j + 256, :]
        k = k + pltpu.roll(k, 64, 1)
        v = v + pltpu.roll(v, 64, 1)
        low = lax.broadcasted_iota(jnp.int32, k.shape, 1) < 64
        both = jnp.where(low, k, v)
        first, second = both[0:128], both[128:256]
        own_ref[j] = jnp.where(sec == 0, first, second)
        send_ref[j] = jnp.where(sec == 0, second, first).astype(send_ref.dtype)


def split_halves(value, sec, keep_ref, send_ref, m, lane):
    upper, lower = value[0:256], value[256:512]
    cut = slice(lane, lane + value.shape[1])
    keep_ref[m, :, cut] = jnp.where(sec == 0, upper, lower).astype(BF)
    send_ref[m, :, cut] = jnp.where(sec == 0, lower, upper).astype(BF)


def split_flat(value, sec, keep_ref, send_ref, lane):
    upper, lower = value[0:256], value[256:512]
    cut = slice(lane, lane + value.shape[1])
    keep_ref[:, cut] = jnp.where(sec == 0, upper, lower).astype(BF)
    send_ref[:, cut] = jnp.where(sec == 0, lower, upper).astype(BF)


def turned_rows(value):
    return value.astype(F32).T.astype(BF)


def flat(ref):
    return ref[...].reshape(512, ref.shape[-1])


def attention_weight_grads(first_t, gated_ref, dz_ref, dq_ref, sec, keep_ref, send_ref, lane):
    grad_q = nn(first_t, flat(dq_ref))
    grad_o = nn(turned_rows(flat(dz_ref)), flat(gated_ref))
    for b in range(4):
        cut = slice(128 * b, 128 * b + 128)
        split_halves(grad_q[:, cut], sec, keep_ref, send_ref, b, lane)
        split_halves(grad_o[:, cut], sec, keep_ref, send_ref, b, lane + 128)


def router_grads(dlog_ref, rows_ref):
    turned = flat(dlog_ref).astype(F32).T.astype(BF)
    return nn(turned, flat(rows_ref))[0:32]


def gelu_parts(pre):
    cdf = 0.5 * (1.0 + lax.erf(pre * 0.7071067811865476))
    slope = cdf + pre * (jnp.exp(-0.5 * pre * pre) * 0.3989422804014327)
    return pre * cdf, slope


def own_self_kv(recv_ref, layer, sec, w_kv, kv_ref):
    gain = gain_of(recv_ref, layer, 0)
    for t in range(2):
        first = norm_of(rows_of(recv_ref, layer, t), gain)[0].astype(BF)
        kv = nn(first, w_kv).astype(BF)
        for i in range(2):
            j = 2 * t + i
            kv_ref[j, sec] = kv[128 * i : 128 * i + 128]
            kv_ref[j, 1 - sec] = other_kv(recv_ref, layer, j)


def cross_kv(kvm_ref, kvo_ref, sec, kv_s):
    for j in range(4):
        kv_s[j, sec] = kvm_ref[j]
        kv_s[j, 1 - sec] = kvo_ref[j]


def pack_kernel(
    len_ref, x_ref, gain_ref, w_kv_ref, own_ref, cross_ref, router_ref, send_ref, extra_s
):
    gain = gain_ref[0:1, :].astype(F32)
    w_kv = w_kv_ref[...]
    extra_s[...] = jnp.zeros_like(extra_s)
    extra_s[0:3, :] = gain_ref[...].astype(F32)
    extra_s[ROUTER_AT : ROUTER_AT + 8, :] = router_ref[...].astype(F32)
    lanes = lax.broadcasted_iota(jnp.int32, (1, 512), 1)
    for i in range(4):
        first = norm_of(x_ref[i].astype(F32), gain)[0].astype(BF)
        kv = nn(first, w_kv).astype(BF)
        row = jnp.zeros((1, 512), jnp.int32)
        for k in range(8):
            length = len_ref[i, k]
            row = jnp.where(lanes == k, length >> 5, row)
            row = jnp.where(lanes == 128 + k, length & 31, row)
        extra_s[LEN_ROW : LEN_ROW + 1, :] = row.astype(F32)
        own, cross = own_ref[i], cross_ref[i]
        own_code = (own[0:1] + 8 * own[1:2]).astype(F32)
        cross_code = (cross[0:1] + 8 * cross[1:2]).astype(F32)
        for half in range(2):
            to = 4 * half + i
            here = slice(128 * half, 128 * half + 128)
            send_ref[to, 0:128, :] = x_ref[i, here, :]
            far = kv[128 * (1 - half) : 128 * (1 - half) + 128]
            send_ref[to, 128:160, :] = jnp.concatenate(
                [far[32 * c : 32 * c + 32] for c in range(4)], 1
            )
            extra_s[CODE_ROW : CODE_ROW + 1, 0:128] = own_code[:, here]
            extra_s[CODE_ROW : CODE_ROW + 1, 128:256] = cross_code[:, here]
            send_ref[to, EX_AT : EX_AT + 16, :] = extra_s[...].astype(BF)


def self_fwd_kernel(ids_ref, recv_ref, *refs):
    wa_own, wa_oth, kvw_own, kvw_oth = refs[:4], refs[4:8], refs[8], refs[9]
    h1_ref, g1_ref, mixed_e, mixed_d, log_e, log_d = refs[10:16]
    wq, wo, wkv, kv_s, k2, v2, sems = refs[16:]
    sec, m = ids_ref[0], ids_ref[1]
    loads = Loads(sems)
    kv_waits = [loads.start(sec == i, kvw_own, kvw_oth, wkv.at[i]) for i in range(2)]
    waits = []
    for layer in range(2):
        waits += loads.rows(sec == layer, wa_own, wa_oth, 0, wq.at[layer], m)
        waits += loads.rows(sec == layer, wa_own, wa_oth, 128, wo.at[layer], m)
    wait_all(kv_waits)
    for layer in range(2):
        own_self_kv(recv_ref, layer, sec, wkv[layer], kv_s)
        widen_kv(kv_s, k2.at[layer], v2.at[layer])
    wait_all(waits)
    ends = [ends_of(extra_of(recv_ref, layer, 0).astype(F32)) for layer in range(2)]

    def tile(t, carry):
        for layer, after_ref, mixed_ref, log_ref in (
            (0, h1_ref, mixed_e, log_e),
            (1, g1_ref, mixed_d, log_d),
        ):
            rows = rows_of(recv_ref, layer, t)
            first = norm_of(rows, gain_of(recv_ref, layer, 0))[0].astype(BF)
            route = routing(first, extra_of(recv_ref, layer, 0), codes_of(recv_ref, layer, t, 0))
            allowed = allowed_rows(t, sec, ends[layer], ends[layer], layer == 1)
            out, mixed, row_log = attend_tile(
                first, route, wq[layer], wo[layer], k2[layer], v2[layer], allowed
            )
            after_ref[t] = rows + out
            mixed_ref[t] = mixed
            log_ref[t] = row_log
        return carry

    lax.fori_loop(0, 2, tile, 0)


def enc_ffn_kernel(
    ids_ref, recv_ref, h1_ref, kvc_ref, *refs
):
    f_own, f_oth = refs[:4], refs[4:8]
    h2_ref, mem_ref, kvm_ref, w_in, w_out, third_s, sems = refs[8:]
    low, m = ids_ref[0] == 0, ids_ref[1]
    loads = Loads(sems)
    waits = loads.pieces(low, f_own, f_oth, w_in, m) + loads.pieces(low, f_oth, f_own, w_out, m)
    for t in range(2):
        h2_ref[t] = h1_ref[t]
        third_s[t] = norm_of(h1_ref[t], gain_of(recv_ref, 0, 2))[0].astype(BF)
    wait_all(waits)

    def chunk(c, carry):
        pre = nn(flat(third_s), w_in[c])
        hidden = (0.5 * pre * (1.0 + lax.erf(pre * 0.7071067811865476))).astype(BF)
        h2_ref[...] += nn(hidden, w_out[c]).reshape(2, TILE, 512)
        return carry

    lax.fori_loop(0, 4, chunk, 0)
    for t in range(2):
        memory = norm_of(h2_ref[t], gain_of(recv_ref, 0, 1))[0].astype(BF)
        mem_ref[t] = memory
        kv = nn(memory, kvc_ref[...]).astype(BF)
        kvm_ref[2 * t] = kv[0:128]
        kvm_ref[2 * t + 1] = kv[128:256]


def cross_fwd_kernel(
    ids_ref, recv_ref, g1_ref, kvm_ref, kvo_ref, rc_ref, cc_own, cc_oth, g2_ref, mixed_ref, log_ref,
    wq, wo, kv_s, k2, v2, sems,
):
    sec = ids_ref[0]
    loads = Loads(sems)
    waits = loads.stacked(sec == 0, cc_own, cc_oth, 128, wq)
    waits += loads.stacked(sec == 0, cc_oth, cc_own, 128, wo)
    cross_kv(kvm_ref, kvo_ref, sec, kv_s)
    widen_kv(kv_s, k2, v2)
    wait_all(waits)
    ends_k = ends_of(extra_of(recv_ref, 0, 0).astype(F32))
    ends_q = ends_of(extra_of(recv_ref, 1, 0).astype(F32))

    def tile(t, carry):
        before = g1_ref[t]
        second = norm_of(before, gain_of(recv_ref, 1, 1))[0].astype(BF)
        route = routing(second, rc_ref[...], codes_of(recv_ref, 1, t, 128))
        allowed = allowed_rows(t, sec, ends_q, ends_k, False)
        out, mixed, row_log = attend_tile(second, route, wq[...], wo[...], k2[...], v2[...], allowed)
        g2_ref[t] = before + out
        mixed_ref[t] = mixed
        log_ref[t] = row_log
        return carry

    lax.fori_loop(0, 2, tile, 0)


def ffn_both(c, third_s, third_t, dy_s, dy_t, w_in, w_out, dthird, sec, keep_ref, send_ref):
    pre = nn(flat(third_s), w_in[c])
    hidden, slope = gelu_parts(pre)
    hidden = hidden.astype(BF)
    dpre = (nt(flat(dy_s), w_out[c]) * slope).astype(BF)
    dthird[...] += nt(dpre, w_in[c])
    split_halves(nn(third_t[...], dpre), sec, keep_ref, send_ref, c, 0)
    split_halves(nn(dy_t[...], hidden), sec, keep_ref, send_ref, c, 512)
    return hidden


def dec_ffn_kernel(
    ids_ref, recv_ref, g2_ref, mem_ref, cc_own, *refs
):
    f_own, f_oth = refs[:4], refs[4:8]
    outs_ref, dg2_ref, gain_ref, keep_ref, send_ref = refs[8:13]
    w_in, w_out, cot_s, third_s, third_t, cot_t, acc, dthird, sems = refs[13:]
    sec, m = ids_ref[0], ids_ref[1]
    low = sec == 0
    loads = Loads(sems)
    cot_waits = [loads.plain(cc_own.at[i, pl.ds(0, 128)], cot_s.at[i]) for i in range(4)]
    waits = loads.pieces(low, f_own, f_oth, w_in, m) + loads.pieces(low, f_oth, f_own, w_out, m)
    for t in range(2):
        acc[t] = g2_ref[t]
        third_s[t] = norm_of(g2_ref[t], gain_of(recv_ref, 1, 2))[0].astype(BF)
        outs_ref[2 * t : 2 * t + 2] = mem_ref[t].reshape(2, 128, 512)
    third_t[...] = turned_rows(flat(third_s))
    wait_all(cot_waits)
    cot_t[...] = turned_rows(flat(cot_s))
    dthird[...] = jnp.zeros_like(dthird)
    wait_all(waits)

    def chunk(c, carry):
        hidden = ffn_both(
            c, third_s, third_t, cot_s, cot_t, w_in, w_out, dthird, sec, keep_ref, send_ref
        )
        acc[...] += nn(hidden, w_out[c]).reshape(2, TILE, 512)
        return carry

    lax.fori_loop(0, 4, chunk, 0)
    total = jnp.zeros((1, 512), F32)
    gain = gain_of(recv_ref, 1, 2)
    for t in range(2):
        outs_ref[4 + 2 * t : 6 + 2 * t] = acc[t].astype(BF).reshape(2, 128, 512)
        unused_out, unit, scaled = norm_of(g2_ref[t], gain)
        back, gain_grad = norm_back(dthird[TILE * t : TILE * t + TILE, :], unit, scaled, gain)
        dg2_ref[t] = cot_s[2 * t : 2 * t + 2].reshape(TILE, 512).astype(F32) + back
        total = total + gain_grad
    gain_ref[...] = total


def cross_back_kernel(
    ids_ref, recv_ref, g1_ref, dg2_ref, mixed_ref, log_ref, kvm_ref, kvo_ref, rc_ref, cc_own, cc_oth,
    dg1_ref, gain_ref, own_ref, send_ref, router_ref, keepw_ref, sendw_ref,
    wq, wo, kv_s, k2, v2, segk, grad_k, grad_v, second_s, gated_s, dz_s, dq_s, dlog_s, sems,
):
    sec = ids_ref[0]
    loads = Loads(sems)
    waits = loads.stacked(sec == 0, cc_own, cc_oth, 128, wq)
    waits += loads.stacked(sec == 0, cc_oth, cc_own, 128, wo)
    cross_kv(kvm_ref, kvo_ref, sec, kv_s)
    widen_kv(kv_s, k2, v2)
    ends_k = ends_of(extra_of(recv_ref, 0, 0).astype(F32))
    ends_q = ends_of(extra_of(recv_ref, 1, 0).astype(F32))
    key_segments_t(ends_k, segk)
    grad_k[...] = jnp.zeros_like(grad_k)
    grad_v[...] = jnp.zeros_like(grad_v)
    wait_all(waits)

    def tile(t, total):
        gain = gain_of(recv_ref, 1, 1)
        second, unit, scaled = norm_of(g1_ref[t], gain)
        second = second.astype(BF)
        second_s[t] = second
        route = routing(second, rc_ref[...], codes_of(recv_ref, 1, t, 128))
        allowed = allowed_cols(t, sec, ends_q, segk, False)
        grad_rows = attend_back_tile(
            t, dg2_ref[t], second, route, mixed_ref[t], log_ref[t], wq[...], wo[...], rc_ref[...],
            ROUTER_LANES[2], k2[...], v2[...], allowed, grad_k, grad_v, gated_s, dz_s, dq_s, dlog_s,
        )
        back, gain_grad = norm_back(grad_rows, unit, scaled, gain)
        dg1_ref[t] = dg2_ref[t] + back
        return total + gain_grad

    gain_ref[...] = lax.fori_loop(0, 2, tile, jnp.zeros((1, 512), F32))
    fold_kv(grad_k, grad_v, sec, own_ref, send_ref)
    router_ref[...] = router_grads(dlog_s, second_s)
    attention_weight_grads(
        turned_rows(flat(second_s)), gated_s, dz_s, dq_s, sec, keepw_ref, sendw_ref, 0
    )


def self_back_kernel(layer, ids_ref, recv_ref, up_ref, mixed_ref, log_ref, *refs):
    wa_own, wa_oth, kvw_own, kvw_oth = refs[:4], refs[4:8], refs[8], refs[9]
    refs = refs[10:]
    if layer == 1:
        before, refs = refs[:2], refs[2:]
    dfirst_ref, own_ref, send_ref, router_ref, keepw_ref, sendw_ref = refs[:6]
    wq, wo, wkv, kv_s, k2, v2, segk, grad_k, grad_v = refs[6:15]
    first_s, gated_s, dz_s, dq_s, dlog_s, sems = refs[15:]
    sec, m = ids_ref[0], ids_ref[1]
    mine = sec == layer
    loads = Loads(sems)
    kv_wait = loads.start(mine, kvw_own, kvw_oth, wkv)
    waits = loads.rows(mine, wa_own, wa_oth, 0, wq, m) + loads.rows(mine, wa_own, wa_oth, 128, wo, m)
    lane = 0
    if layer == 1:
        lane = 256
        for src, dst in zip(before, (keepw_ref, sendw_ref)):
            waits.append(loads.plain(src, dst.at[:, :, pl.ds(0, 256)]))
    ends = ends_of(extra_of(recv_ref, layer, 0).astype(F32))
    key_segments_t(ends, segk)
    grad_k[...] = jnp.zeros_like(grad_k)
    grad_v[...] = jnp.zeros_like(grad_v)
    kv_wait()
    own_self_kv(recv_ref, layer, sec, wkv[...], kv_s)
    widen_kv(kv_s, k2, v2)
    wait_all(waits)
    router_block = extra_of(recv_ref, layer, 0)

    def tile(t, carry):
        first = norm_of(rows_of(recv_ref, layer, t), gain_of(recv_ref, layer, 0))[0].astype(BF)
        first_s[t] = first
        route = routing(first, router_block, codes_of(recv_ref, layer, t, 0))
        allowed = allowed_cols(t, sec, ends, segk, layer == 1)
        dfirst_ref[t] = attend_back_tile(
            t, up_ref[t], first, route, mixed_ref[t], log_ref[t], wq[...], wo[...], router_block,
            ROUTER_LANES[layer], k2[...], v2[...], allowed, grad_k, grad_v, gated_s, dz_s, dq_s,
            dlog_s,
        )
        return carry

    lax.fori_loop(0, 2, tile, 0)
    fold_kv(grad_k, grad_v, sec, own_ref, send_ref)
    router_ref[...] = router_grads(dlog_s, first_s)
    attention_weight_grads(
        turned_rows(flat(first_s)), gated_s, dz_s, dq_s, sec, keepw_ref, sendw_ref, lane
    )


def enc_ffn_back_kernel(
    ids_ref, recv_ref, h1_ref, h2_ref, own_ref, come_ref, kvc_ref, *refs
):
    f_own, f_oth = refs[:4], refs[4:8]
    dh1_ref, gain_ref, gain2_ref, keep_ref, send_ref = refs[8:13]
    w_in, w_out, third_s, third_t, dy_s, dy_t, dthird, sems = refs[13:]
    sec, m = ids_ref[0], ids_ref[1]
    low = sec == 0
    loads = Loads(sems)
    waits = loads.pieces(low, f_own, f_oth, w_in, m) + loads.pieces(low, f_oth, f_own, w_out, m)
    total = jnp.zeros((1, 512), F32)
    gain = gain_of(recv_ref, 0, 1)
    for t in range(2):
        dkv = (own_ref[2 * t : 2 * t + 2] + come_ref[2 * t : 2 * t + 2].astype(F32)).astype(BF)
        dmem = rounded(nt(dkv.reshape(TILE, 128), kvc_ref[...]))
        unused_out, unit, scaled = norm_of(h2_ref[t], gain)
        back, gain_grad = norm_back(dmem, unit, scaled, gain)
        dh1_ref[t] = back
        dy_s[t] = back.astype(BF)
        third_s[t] = norm_of(h1_ref[t], gain_of(recv_ref, 0, 2))[0].astype(BF)
        total = total + gain_grad
    gain_ref[...] = total
    third_t[...] = turned_rows(flat(third_s))
    dy_t[...] = turned_rows(flat(dy_s))
    dthird[...] = jnp.zeros_like(dthird)
    wait_all(waits)

    def chunk(c, carry):
        ffn_both(c, third_s, third_t, dy_s, dy_t, w_in, w_out, dthird, sec, keep_ref, send_ref)
        return carry

    lax.fori_loop(0, 4, chunk, 0)
    total = jnp.zeros((1, 512), F32)
    gain = gain_of(recv_ref, 0, 2)
    for t in range(2):
        unused_out, unit, scaled = norm_of(h1_ref[t], gain)
        back, gain_grad = norm_back(dthird[TILE * t : TILE * t + TILE, :], unit, scaled, gain)
        dh1_ref[t] += back
        total = total + gain_grad
    gain2_ref[...] = total


def finish_rows(layer, recv_ref, up_ref, df_ref, own_ref, come_ref, wkv, first_s, out_ref, at):
    total = jnp.zeros((1, 512), F32)
    gain = gain_of(recv_ref, layer, 0)
    dkvs = []
    for t in range(2):
        first, unit, scaled = norm_of(rows_of(recv_ref, layer, t), gain)
        first_s[t] = first.astype(BF)
        dkv = (own_ref[2 * t : 2 * t + 2] + come_ref[2 * t : 2 * t + 2].astype(F32)).astype(BF)
        dkv = dkv.reshape(TILE, 128)
        dkvs.append(dkv)
        back, gain_grad = norm_back(df_ref[t] + nt(dkv, wkv), unit, scaled, gain)
        dx = (up_ref[t] + back).astype(BF)
        for i in range(2):
            out_ref[at + 2 * t + i, 0:128, :] = dx[128 * i : 128 * i + 128]
        total = total + gain_grad
    grad = nn(turned_rows(flat(first_s)), jnp.concatenate(dkvs, 0))
    return total, grad


def dec_finish_kernel(
    ids_ref, recv_ref, up_ref, df_ref, own_ref, come_ref, own_c, come_c, mem_ref, kvw_own, kvw_oth,
    dx_ref, gain_ref, keep_ref, send_ref, wkv, first_s, sems,
):
    sec = ids_ref[0]
    wait = Loads(sems).start(sec == 1, kvw_own, kvw_oth, wkv)
    dkv_c = (own_c[...] + come_c[...].astype(F32)).astype(BF).reshape(512, 128)
    split_flat(nn(turned_rows(flat(mem_ref)), dkv_c), sec, keep_ref, send_ref, 128)
    wait()
    gain_ref[...], grad = finish_rows(
        1, recv_ref, up_ref, df_ref, own_ref, come_ref, wkv[...], first_s, dx_ref, 0
    )
    split_flat(grad, sec, keep_ref, send_ref, 0)


def enc_finish_kernel(
    ids_ref, recv_ref, up_ref, df_ref, own_ref, come_ref, dx1_ref, r0, r1, rc,
    gain_e1, gain_e2, gain_d0, gain_d1, gain_d2, kvw_own, kvw_oth,
    out_ref, wkv, first_s, misc, sems,
):
    sec = ids_ref[0]
    wait = Loads(sems).start(sec == 0, kvw_own, kvw_oth, wkv)
    misc[...] = r0[...] + r1[...] + rc[...]
    out_ref[4:8, 0:128, :] = dx1_ref[...]
    wait()
    gain_e0, grad = finish_rows(
        0, recv_ref, up_ref, df_ref, own_ref, come_ref, wkv[...], first_s, out_ref, 0
    )
    rows = (gain_e0, gain_e1[...], gain_e2[...], gain_d0[...], gain_d1[...], gain_d2[...])
    for i, row in enumerate(rows):
        misc[GAIN_ROW + i : GAIN_ROW + i + 1, :] = row
    both = misc[...]
    for half in range(2):
        cut = slice(256 * half, 256 * half + 256)
        part = grad[cut].astype(BF)
        small = both[:, cut].astype(BF)
        block = jnp.concatenate(
            [
                jnp.concatenate([part[64 * c : 64 * c + 64] for c in range(4)], 1),
                jnp.concatenate([small[0:16], small[16:32]], 1),
            ],
            0,
        )
        for i in range(4):
            out_ref[4 * half + i, 128:208, :] = block


def add_kernel(keep_ref, come_ref, out_ref):
    out_ref[...] = (keep_ref[...].astype(F32) + come_ref[...].astype(F32)).astype(BF)


def add_two_kernel(keep_ref, come_ref, keep_s, come_s, out_ref):
    out_ref[0, :, 0:256] = (keep_ref[0].astype(F32) + come_ref[0].astype(F32)).astype(BF)
    out_ref[0, :, 256:512] = (keep_s[...].astype(F32) + come_s[...].astype(F32)).astype(BF)


def tail_kernel(dx_ref, att_d, att_e, dx_out, out_ref):
    for i in range(4):
        for half in range(2):
            dx_out[i, half] = dx_ref[4 * half + i, 0:128, :].astype(F32)
    for ref, lane in ((att_d, 0), (att_e, 512)):
        total = ref[0].astype(F32)
        for i in range(1, 4):
            total = total + ref[i].astype(F32)
        out_ref[:, lane : lane + 512] = total.astype(BF)
    small = dx_ref[0, 128:208, :].astype(F32)
    for i in range(1, 8):
        small = small + dx_ref[i, 128:208, :].astype(F32)
    for c in range(4):
        out_ref[64 * c : 64 * c + 64, 1024:1152] = small[0:64, 128 * c : 128 * c + 128].astype(BF)
    misc = jnp.concatenate([small[64:80, 0:256], small[64:80, 256:512]], 0)
    misc = jnp.concatenate([misc, jnp.zeros((96, 256), F32)], 0)
    out_ref[:, 1152:1280] = misc.T.astype(BF)


def shaped(dims, kind):
    return jax.ShapeDtypeStruct(dims, kind)


def cost_of(micros):
    return pl.CostEstimate(
        flops=int(micros * 1.1535e9), bytes_accessed=int(micros * 3.0e6), transcendentals=0
    )


def run(kernel, args, places, outs, scratch, micros, after=()):
    space = {
        "s": pl.BlockSpec(memory_space=pltpu.SMEM),
        "v": pl.BlockSpec(memory_space=pltpu.VMEM),
        "a": pl.BlockSpec(memory_space=pl.ANY),
    }
    count, extra = len(args), len(after)

    def body(*refs):
        kernel(*refs[:count], *refs[count + extra :])

    return pl.pallas_call(
        body,
        out_shape=outs,
        in_specs=[space[p] for p in places] + [space["a"]] * extra,
        out_specs=jax.tree.map(lambda _: space["v"], outs),
        scratch_shapes=scratch,
        compiler_params=pltpu.CompilerParams(vmem_limit_bytes=VMEM_LIMIT),
        cost_estimate=cost_of(micros),
    )(*args, *after)


def vm(*dims, kind=BF):
    return pltpu.VMEM(dims, kind)


def dma(count):
    return pltpu.SemaphoreType.DMA((count,))


def across(value, axes, size, by):
    return lax.ppermute(value, axes, [(i, i ^ by) for i in range(size)])


def swapped(value):
    return across(value, "section", 2, 1)


def gathered(value):
    return [value] + [across(value, "mp", 4, b) for b in range(1, 4)]


def to_all(value, axes):
    return lax.all_to_all(value, axes, split_axis=0, concat_axis=0, tiled=True)


def add_shares(keep, come, micros, after=()):
    whole = pl.BlockSpec((1,) + keep.shape[1:], lambda i: (i, 0, 0))
    return pl.pallas_call(
        lambda k, c, *rest: add_kernel(k, c, rest[-1]),
        out_shape=shaped(keep.shape, BF),
        grid=(keep.shape[0],),
        in_specs=[whole, whole] + [pl.BlockSpec(memory_space=pl.ANY)] * len(after),
        out_specs=whole,
        cost_estimate=cost_of(micros),
    )(keep, come, *after)


def add_two(keep, come, keep_s, come_s, after):
    whole = pl.BlockSpec((1, 256, 256), lambda i: (i, 0, 0))
    small = pl.BlockSpec((256, 256), lambda i: (0, 0))
    return pl.pallas_call(
        lambda k, c, ks, cs, *rest: add_two_kernel(k, c, ks, cs, rest[-1]),
        out_shape=shaped((4, 256, 512), BF),
        grid=(4,),
        in_specs=[whole, whole, small, small] + [pl.BlockSpec(memory_space=pl.ANY)] * len(after),
        out_specs=pl.BlockSpec((1, 256, 512), lambda i: (i, 0, 0)),
        cost_estimate=cost_of(2.0),
    )(keep, come, keep_s, come_s, *after)


def gated(values, after):
    anywhere = pl.BlockSpec(memory_space=pl.ANY)
    count = len(values)
    return pl.pallas_call(
        lambda *refs: None,
        out_shape=[shaped(v.shape, v.dtype) for v in values],
        in_specs=[anywhere] * (count + len(after)),
        out_specs=[anywhere] * count,
        input_output_aliases={i: i for i in range(count)},
        cost_estimate=cost_of(0.2),
    )(*values, *after)


def shared_out(value):
    return lax.psum_scatter(value, "mp", scatter_dimension=0, tiled=False)


def per_device(
    inputs,
    lengths,
    routes_self,
    routes_cross,
    gains,
    router_self,
    query_self,
    keyval_self,
    output_self,
    ffn_in,
    ffn_out,
    router_cross,
    query_cross,
    keyval_cross,
    output_cross,
    cotangent,
):
    sec, m = lax.axis_index("section"), lax.axis_index("mp")
    low = sec == 0
    ids = jnp.stack([sec, m]).astype(jnp.int32)
    sem = dma(24)
    rowgroup = ("section", "mp")

    q_rows = query_self[0].transpose(0, 2, 1).reshape(128, 512)
    o_rows = output_self[0].reshape(128, 512)
    wa = jnp.concatenate([q_rows, o_rows], 0)
    wa_own = gathered(wa)
    w_in, w_out = ffn_in[0], ffn_out[0]
    half_come = swapped(jnp.where(low, w_out, w_in))
    enc_half = jnp.where(low, w_in, half_come)
    dec_half = jnp.where(low, half_come, w_out)
    kvw_own = keyval_self[0]
    kvw_oth = swapped(kvw_own)
    router_c = jnp.concatenate([jnp.zeros((8, 512), BF), router_cross.T], 0)

    packed = run(
        pack_kernel,
        (
            lengths[0, :, 0],
            inputs[0, :, 0],
            gains[0],
            keyval_self[0],
            routes_self[0, :, 0].transpose(0, 2, 1),
            routes_cross[:, 0].transpose(0, 2, 1),
            router_self[0].T,
        ),
        "svvvvvv",
        shaped((8, 176, 512), BF),
        [vm(16, 512, kind=F32)],
        3.4,
        after=(wa,),
    )
    recv = to_all(packed, rowgroup)
    wa_oth = [swapped(piece) for piece in wa_own]
    (enc_half,) = gated([enc_half], [packed, *wa_own[1:]])
    enc_own = gathered(enc_half)
    c_rows = jnp.where(
        low, query_cross.transpose(0, 2, 1).reshape(128, 512), output_cross.reshape(128, 512)
    )
    cot_cut = lax.dynamic_index_in_dim(cotangent[:, 0].reshape(4, 2, 128, 512), sec, 1, False)
    cc_in = jnp.concatenate([cot_cut, jnp.broadcast_to(c_rows[None], (4, 128, 512))], 1)
    (cc_in,) = gated([cc_in], [recv])
    cc_own = to_all(cc_in, "mp")

    act = shaped((2, TILE, 512), F32)
    actb = shaped((2, TILE, 512), BF)
    mixed_s = shaped((2, 2 * TILE, 128), F32)
    log_s = shaped((2, 1, 2 * TILE), F32)
    kv_b = shaped((4, 128, 128), BF)
    kv_f = shaped((4, 128, 128), F32)
    row_s = shaped((1, 512), F32)
    ffn_g = shaped((4, 256, 1024), BF)
    router_s = shaped((32, 512), F32)
    wide = [vm(512, 512), vm(512, 512)]
    kv_scratch = [vm(4, 2, 128, 128), vm(1024, 128), vm(1024, 128)]
    back_scratch = [
        vm(1024, TILE, kind=F32), vm(1024, 128, kind=F32), vm(1024, 128, kind=F32),
        vm(2, TILE, 512), vm(2, TILE, 512), vm(2, TILE, 512), vm(2, TILE, 512), vm(2, TILE, 128),
    ]
    ffn_w = [vm(4, 512, 512), vm(4, 512, 512)]

    h1, g1, mixed_e, mixed_d, log_e, log_d = run(
        self_fwd_kernel,
        (ids, recv, *wa_own, *wa_oth, kvw_own, kvw_oth),
        "sv" + "a" * 10,
        (act, act, mixed_s, mixed_s, log_s, log_s),
        [vm(2, 512, 512), vm(2, 512, 512), vm(2, 512, 128), vm(4, 2, 128, 128)]
        + [vm(2, 1024, 128), vm(2, 1024, 128), sem],
        13.6,
    )
    enc_own[1:] = gated(enc_own[1:], [h1])
    enc_oth = [swapped(piece) for piece in enc_own]
    (dec_half,) = gated([dec_half], [enc_own[1]])
    dec_own = gathered(dec_half)
    cc_oth = swapped(cc_own)
    h2, memory, kvm = run(
        enc_ffn_kernel,
        (ids, recv, h1, keyval_cross, *enc_own, *enc_oth),
        "svvv" + "a" * 8,
        (act, actb, kv_b),
        ffn_w + [vm(2, TILE, 512), sem],
        8.4,
    )
    kvm_oth = swapped(kvm)
    g2, mixed_c, log_c = run(
        cross_fwd_kernel,
        (ids, recv, g1, kvm, kvm_oth, router_c, cc_own, cc_oth),
        "svvvvvaa",
        (act, mixed_s, log_s),
        wide + kv_scratch + [sem],
        8.8,
    )
    dec_own[1:] = gated(dec_own[1:], [g2])
    dec_oth = [swapped(piece) for piece in dec_own]
    outs, dg2, gain_d2, keep_d, send_d = run(
        dec_ffn_kernel,
        (ids, recv, g2, memory, cc_own, *dec_own, *dec_oth),
        "svvva" + "a" * 8,
        (shaped((8, 128, 512), BF), act, row_s, ffn_g, ffn_g),
        ffn_w
        + [vm(4, 128, 512), vm(2, TILE, 512), vm(512, 512), vm(512, 512)]
        + [vm(2, TILE, 512, kind=F32), vm(512, 512, kind=F32), sem],
        15.0,
    )
    come_d = swapped(send_d)
    outs_come = to_all(outs, rowgroup)
    att_g = shaped((4, 256, 256), BF)
    flat_g = shaped((256, 256), BF)
    dg1, gain_d1, own_c, sendkv_c, router_cg, keep_wc, send_wc = run(
        cross_back_kernel,
        (ids, recv, g1, dg2, mixed_c, log_c, kvm, kvm_oth, router_c, cc_own, cc_oth),
        "svvvvvvvvaa",
        (act, row_s, kv_f, kv_b, router_s, att_g, att_g),
        wide + kv_scratch + back_scratch + [sem],
        13.0,
    )
    comekv_c = swapped(sendkv_c)
    ffn_d = add_shares(keep_d, come_d, 4.0, (dg1, outs_come))
    dh1, gain_e1, gain_e2, keep_e, send_e = run(
        enc_ffn_back_kernel,
        (ids, recv, h1, h2, own_c, comekv_c, keyval_cross, *enc_own, *enc_oth),
        "svvvvvv" + "a" * 8,
        (act, row_s, row_s, ffn_g, ffn_g),
        ffn_w
        + [vm(2, TILE, 512), vm(512, 512), vm(2, TILE, 512), vm(512, 512)]
        + [vm(512, 512, kind=F32), sem],
        13.4,
        after=(ffn_d,),
    )
    ffn_d = shared_out(ffn_d)
    come_e = swapped(send_e)
    self_scratch = wide + [vm(512, 128)] + kv_scratch + back_scratch + [sem]
    att_dg = shaped((4, 256, 512), BF)
    df1, own_1, sendkv_1, router_1g, keep_w1, send_w1 = run(
        functools.partial(self_back_kernel, 1),
        (
            ids, recv, dg1, mixed_d, log_d, *wa_own, *wa_oth, kvw_own, kvw_oth, keep_wc, send_wc,
        ),
        "svvvv" + "a" * 12,
        (act, kv_f, kv_b, router_s, att_dg, att_dg),
        self_scratch,
        12.2,
        after=(dh1,),
    )
    comekv_1 = swapped(sendkv_1)
    come_w1 = swapped(send_w1)
    ffn_e = add_shares(keep_e, come_e, 4.0, (df1,))
    att_d = add_shares(keep_w1, come_w1, 2.0, (ffn_e,))
    dx1, gain_d0, keep_s1, send_s1 = run(
        dec_finish_kernel,
        (ids, recv, dg1, df1, own_1, comekv_1, own_c, comekv_c, memory, kvw_own, kvw_oth),
        "svvvvvvvvaa",
        (shaped((4, 128, 512), BF), row_s, flat_g, flat_g),
        [vm(512, 128), vm(2, TILE, 512), sem],
        5.5,
        after=(att_d,),
    )
    ffn_e = shared_out(ffn_e)
    att_d = to_all(att_d, "mp")
    ffn_d = lax.psum_scatter(ffn_d, "dp", scatter_dimension=0, tiled=True).astype(F32)
    come_s1 = swapped(send_s1)
    df0, own_0, sendkv_0, router_0g, keep_w0, send_w0 = run(
        functools.partial(self_back_kernel, 0),
        (ids, recv, dh1, mixed_e, log_e, *wa_own, *wa_oth, kvw_own, kvw_oth),
        "svvvv" + "a" * 10,
        (act, kv_f, kv_b, router_s, att_g, att_g),
        self_scratch,
        11.8,
        after=(dx1,),
    )
    comekv_0 = swapped(sendkv_0)
    come_w0 = swapped(send_w0)
    ffn_e = lax.psum_scatter(ffn_e, "dp", scatter_dimension=0, tiled=True).astype(F32)
    att_e = to_all(add_two(keep_w0, come_w0, keep_s1, come_s1, (att_d,)), "mp")
    finished = run(
        enc_finish_kernel,
        (
            ids, recv, dh1, df0, own_0, comekv_0, dx1, router_0g, router_1g, router_cg,
            gain_e1, gain_e2, gain_d0, gain_d1, gain_d2, kvw_own, kvw_oth,
        ),
        "s" + "v" * 14 + "aa",
        shaped((8, 208, 512), BF),
        [vm(512, 128), vm(2, TILE, 512), vm(32, 512, kind=F32), sem],
        6.0,
    )
    dx, small = run(
        tail_kernel,
        (to_all(finished, rowgroup), att_d, att_e),
        "vvv",
        (shaped((4, 2, 128, 512), F32), shaped((256, 1280), BF)),
        [],
        3.0,
    )
    dp = lax.axis_size("dp")
    share = 256 // dp
    small = to_all(small.reshape(dp, share, 1280), "dp")
    small = jnp.sum(small.astype(F32), 0)

    outs_come = outs_come.reshape(2, 4, 128, 512).transpose(1, 0, 2, 3)

    def query_of(at):
        return small[:, at : at + 128].reshape(share, 2, 64).transpose(1, 0, 2)

    def output_of(at):
        return small[:, at + 128 : at + 256].T.reshape(2, 64, share)

    misc = small[:, 1152:1280].T

    def router_of(layer):
        return misc[ROUTER_LANES[layer] : ROUTER_LANES[layer] + 8].T

    return (
        outs_come.reshape(1, 4, 1, 256, 512),
        dx.reshape(1, 4, 1, 256, 512),
        misc[GAIN_ROW : GAIN_ROW + 6].reshape(2, 3, share),
        jnp.stack([router_of(0), router_of(1)]),
        jnp.stack([query_of(512), query_of(256)]),
        jnp.stack([small[:, 1024:1152], small[:, 768:896]]),
        jnp.stack([output_of(512), output_of(256)]),
        jnp.stack([ffn_e[:, :512], ffn_d[:, :512]]),
        jnp.stack([ffn_e[:, 512:].T, ffn_d[:, 512:].T]),
        router_of(2),
        query_of(0),
        small[:, 896:1024],
        output_of(0),
    )


def solution(mesh):
    placed = (
        P("section", None, "dp", "mp", None),
        P("section", None, "dp", None),
        P("section", None, "dp", "mp", None),
        P(None, "dp", "mp", None),
        P("section", None, None),
        P("section", None, None),
        P("section", "mp", None, None),
        P("section", None, None),
        P("section", "mp", None, None),
        P("section", None, "mp"),
        P("section", "mp", None),
        P(),
        P("mp", None, None),
        P(),
        P("mp", None, None),
        P(None, "dp", "mp", None),
    )
    return jax.shard_map(
        per_device,
        mesh=mesh,
        in_specs=placed,
        out_specs=(
            P("section", None, "dp", "mp", None),
            P("section", None, "dp", "mp", None),
            P(None, None, ("section", "dp")),
            P(None, ("section", "dp"), None),
            P(None, "mp", ("section", "dp"), None),
            P(None, ("section", "dp"), None),
            P(None, "mp", None, ("section", "dp")),
            P(None, ("section", "dp"), "mp"),
            P(None, "mp", ("section", "dp")),
            P(("section", "dp"), None),
            P("mp", ("section", "dp"), None),
            P(("section", "dp"), None),
            P("mp", None, ("section", "dp")),
        ),
        check_vma=False,
    )
```

```python
import functools

import jax
import jax.numpy as jnp
from jax import lax
from jax.experimental import pallas as pl
from jax.experimental.pallas import tpu as pltpu
from jax.sharding import PartitionSpec as P

EPS = 1e-05
MASK_VALUE = -1000000000.0
BF = jnp.bfloat16
F32 = jnp.float32
TILE = 256
EX_AT = 160
CODE_ROW = 3
LEN_ROW = 4
ROUTER_AT = 8
GAIN_ROW = 24
ROUTER_LANES = (0, 8, 16)
VMEM_LIMIT = 56 * 1024 * 1024


def nn(left, right):
    return lax.dot_general(left, right, (((1,), (0,)), ((), ())), preferred_element_type=F32)


def nt(left, right):
    return lax.dot_general(left, right, (((1,), (1,)), ((), ())), preferred_element_type=F32)


def tn(left, right):
    return lax.dot_general(left, right, (((0,), (0,)), ((), ())), preferred_element_type=F32)


def norm_of(values, gain_row):
    center = values - jnp.mean(values, 1, keepdims=True)
    scaled = lax.rsqrt(jnp.mean(center * center, 1, keepdims=True) + EPS)
    unit_rows = center * scaled
    return unit_rows * gain_row, unit_rows, scaled


def norm_back(upstream, unit_rows, scaled, gain_row):
    inner = upstream * gain_row
    result = scaled * (
        inner
        - jnp.mean(inner, 1, keepdims=True)
        - unit_rows * jnp.mean(inner * unit_rows, 1, keepdims=True)
    )
    return result, jnp.sum(upstream * unit_rows, 0, keepdims=True)


def eye_of(size):
    return lax.broadcasted_iota(jnp.int32, (size, size), 0) == lax.broadcasted_iota(
        jnp.int32, (size, size), 1
    )


def row_to_col(row):
    return jnp.sum(jnp.where(eye_of(128), row, 0.0), 1, keepdims=True)


def col_to_row(col):
    parts = []
    for at in range(0, col.shape[0], 128):
        part = jnp.where(eye_of(128), col[at : at + 128], 0.0)
        parts.append(jnp.sum(part, 0, keepdims=True))
    return jnp.concatenate(parts, 1)


def ends_of(extra):
    lengths = extra[LEN_ROW : LEN_ROW + 1, 0:8] * 32.0 + extra[LEN_ROW : LEN_ROW + 1, 128:136]
    ends = [lengths[:, 0:1]]
    for k in range(1, 8):
        ends.append(ends[-1] + lengths[:, k : k + 1])
    return ends


def segments(places, ends):
    total = jnp.where(places >= ends[0], 1.0, 0.0)
    for end in ends[1:]:
        total = total + jnp.where(places >= end, 1.0, 0.0)
    return total


def extra_of(recv_ref, layer, quarter):
    return recv_ref[4 * layer + quarter, EX_AT : EX_AT + 16, :]


def gain_of(recv_ref, layer, which):
    return extra_of(recv_ref, layer, 0).astype(F32)[which : which + 1, :]


def rows_of(recv_ref, layer, t):
    return recv_ref[pl.ds(4 * layer + 2 * t, 2), 0:128, :].reshape(TILE, 512).astype(F32)


def codes_of(recv_ref, layer, t, lane):
    cols = []
    for i in range(2):
        extra = extra_of(recv_ref, layer, 2 * t + i).astype(F32)
        cols.append(row_to_col(extra[CODE_ROW : CODE_ROW + 1, lane : lane + 128]))
    return jnp.concatenate(cols, 0)


def other_kv(recv_ref, layer, quarter):
    packed = recv_ref[4 * layer + quarter, 128:160, :]
    return jnp.concatenate([packed[:, 128 * c : 128 * c + 128] for c in range(4)], 0)


def routing(query_rows, router_block, code):
    second = jnp.floor(code * 0.125)
    first = code - 8.0 * second
    e0, e1 = first.astype(jnp.int32), second.astype(jnp.int32)
    logits = nt(query_rows, router_block)
    lanes = lax.broadcasted_iota(jnp.int32, logits.shape, 1)
    l0 = jnp.sum(jnp.where(lanes == e0 + ROUTER_AT, logits, 0.0), 1, keepdims=True)
    l1 = jnp.sum(jnp.where(lanes == e1 + ROUTER_AT, logits, 0.0), 1, keepdims=True)
    top = jnp.maximum(l0, l1)
    x0, x1 = jnp.exp(l0 - top), jnp.exp(l1 - top)
    total = x0 + x1
    owners = lax.broadcasted_iota(jnp.int32, (code.shape[0], 512), 1) >> 6
    return e0, e1, x0 / total, x1 / total, owners == e0, owners == e1


def fold(wide, mask):
    kept = jnp.where(mask, wide, 0.0)
    return kept[:, 0:128] + kept[:, 128:256] + kept[:, 256:384] + kept[:, 384:512]


def spread(a0, a1, m0, m1):
    parts = []
    for c in range(4):
        cut = slice(128 * c, 128 * c + 128)
        parts.append(jnp.where(m0[:, cut], a0, jnp.where(m1[:, cut], a1, 0.0)))
    return jnp.concatenate(parts, 1).astype(BF)


def rounded(value):
    return value.astype(BF).astype(F32)


def start_pick(cond, yes, no, dst, sem):
    @pl.when(cond)
    def _():
        pltpu.make_async_copy(yes, dst, sem).start()

    @pl.when(jnp.logical_not(cond))
    def _():
        pltpu.make_async_copy(no, dst, sem).start()


class Loads:
    def __init__(self, sems):
        self.sems, self.used = sems, 0

    def start(self, cond, yes, no, dst):
        sem = self.sems.at[self.used]
        self.used += 1
        start_pick(cond, yes, no, dst, sem)
        return functools.partial(lambda a, b, c: pltpu.make_async_copy(a, b, c).wait(), yes, dst, sem)

    def plain(self, src, dst):
        sem = self.sems.at[self.used]
        self.used += 1
        copy = pltpu.make_async_copy(src, dst, sem)
        copy.start()
        return copy.wait

    def rows(self, cond, yes, no, at, dst, m):
        cut = pl.ds(at, 128)
        return [
            self.start(cond, yes[b].at[cut], no[b].at[cut], dst.at[pl.ds(128 * (m ^ b), 128)])
            for b in range(4)
        ]

    def stacked(self, cond, yes, no, at, dst):
        cut = pl.ds(at, 128)
        return [
            self.start(cond, yes.at[i, cut], no.at[i, cut], dst.at[pl.ds(128 * i, 128)])
            for i in range(4)
        ]

    def pieces(self, cond, yes, no, dst, m):
        return [self.start(cond, yes[b], no[b], dst.at[m ^ b]) for b in range(4)]


def wait_all(waits):
    for wait in waits:
        wait()


def widen_kv(kv_ref, k2_ref, v2_ref):
    for j in range(4):
        kv = kv_ref[j].reshape(256, 128).astype(F32)
        turned = pltpu.roll(kv, 64, 1)
        low = lax.broadcasted_iota(jnp.int32, kv.shape, 1) < 64
        k2_ref[256 * j : 256 * j + 256, :] = jnp.where(low, kv, turned).astype(BF)
        v2_ref[256 * j : 256 * j + 256, :] = jnp.where(low, turned, kv).astype(BF)


def attend_tile(query_rows, route, w_qt, w_o, k2, v2, allowed):
    e0, e1, g0, g1, m0, m1 = route
    q_all = nt(query_rows, w_qt) * 0.125
    queries = jnp.concatenate([fold(q_all, m0), fold(q_all, m1)], 0).astype(BF)
    scores = nt(queries, k2)
    scores = jnp.concatenate(
        [
            jnp.where(allowed, scores[0:TILE], MASK_VALUE),
            jnp.where(allowed, scores[TILE:], MASK_VALUE),
        ],
        0,
    )
    top = jnp.max(scores, 1, keepdims=True)
    weights = jnp.exp(scores - top)
    total = jnp.sum(weights, 1, keepdims=True)
    mixed = nn(weights.astype(BF), v2) / total
    log_total = top + jnp.log(total)
    gated = spread(rounded(g0) * mixed[0:TILE], rounded(g1) * mixed[TILE:], m0, m1)
    return nn(gated, w_o), mixed, col_to_row(log_total)


def attend_back_tile(
    t, upstream, query_rows, route, mixed, log_row, w_qt, w_o, router_block, router_lane, k2, v2,
    allowed_t, grad_k, grad_v, gated_ref, dz_ref, dq_ref, dlog_ref,
):
    e0, e1, g0, g1, m0, m1 = route
    q_all = nt(query_rows, w_qt) * 0.125
    queries = jnp.concatenate([fold(q_all, m0), fold(q_all, m1)], 0).astype(BF)
    dz = upstream.astype(BF)
    dg_all = nt(dz, w_o)
    dgated0, dgated1 = fold(dg_all, m0), fold(dg_all, m1)
    r0, r1 = rounded(g0), rounded(g1)
    mixed0, mixed1 = mixed[0:TILE], mixed[TILE:]
    gated_ref[t] = spread(r0 * mixed0, r1 * mixed1, m0, m1)
    dz_ref[t] = dz
    dgate0 = rounded(jnp.sum(mixed0 * dgated0, 1, keepdims=True))
    dgate1 = rounded(jnp.sum(mixed1 * dgated1, 1, keepdims=True))
    do0, do1 = (r0 * dgated0).astype(BF), (r1 * dgated1).astype(BF)
    grad_mixed = jnp.concatenate([do0, do1], 0)
    inner_row = jnp.concatenate(
        [
            col_to_row(jnp.sum(do0.astype(F32) * mixed0, 1, keepdims=True)),
            col_to_row(jnp.sum(do1.astype(F32) * mixed1, 1, keepdims=True)),
        ],
        1,
    )
    scores = nt(k2, queries)
    scores = jnp.concatenate(
        [
            jnp.where(allowed_t, scores[:, 0:TILE], MASK_VALUE),
            jnp.where(allowed_t, scores[:, TILE:], MASK_VALUE),
        ],
        1,
    )
    probs = jnp.exp(scores - log_row)
    grad_probs = nt(v2, grad_mixed)
    grad_scores = (probs * (grad_probs - inner_row)).astype(BF)
    grad_v[...] += nn(probs.astype(BF), grad_mixed)
    grad_k[...] += nn(grad_scores, queries)
    grad_q = rounded(tn(grad_scores, k2) * 0.125)
    dq_all = spread(grad_q[0:TILE], grad_q[TILE:], m0, m1)
    dq_ref[t] = dq_all
    grad_rows = nn(dq_all, w_qt)
    mean_grad = g0 * dgate0 + g1 * dgate1
    dc0, dc1 = g0 * (dgate0 - mean_grad), g1 * (dgate1 - mean_grad)
    lanes = lax.broadcasted_iota(jnp.int32, (TILE, 16), 1)
    dlog = jnp.where(lanes == e0 + ROUTER_AT, dc0, 0.0) + jnp.where(
        lanes == e1 + ROUTER_AT, dc1, 0.0
    )
    wide = lax.broadcasted_iota(jnp.int32, (TILE, 128), 1)
    dlog_ref[t] = (
        jnp.where(wide == e0 + router_lane, dc0, 0.0)
        + jnp.where(wide == e1 + router_lane, dc1, 0.0)
    ).astype(BF)
    return grad_rows + nn(dlog.astype(BF), router_block)


def query_places(t, sec, dims, along):
    local = lax.broadcasted_iota(jnp.int32, dims, along)
    return (512 * t + 128 * sec + local + (local & ~127)).astype(F32)


def allowed_rows(t, sec, ends_q, ends_k, causal):
    query_at = query_places(t, sec, (TILE, 1), 0)
    key_at = lax.broadcasted_iota(jnp.int32, (1, 1024), 1).astype(F32)
    allowed = segments(query_at, ends_q) == segments(key_at, ends_k)
    if causal:
        allowed = allowed & (key_at <= query_at)
    return allowed


def key_segments_t(ends_k, segk_ref):
    for j in range(8):
        at = lax.broadcasted_iota(jnp.int32, (128, TILE), 0).astype(F32) + 128.0 * j
        segk_ref[128 * j : 128 * j + 128, :] = segments(at, ends_k)


def allowed_cols(t, sec, ends_q, segk_ref, causal):
    query_at = query_places(t, sec, (1, TILE), 1)
    allowed = segk_ref[...] == segments(query_at, ends_q)
    if causal:
        key_at = lax.broadcasted_iota(jnp.int32, (1024, TILE), 0).astype(F32)
        allowed = allowed & (key_at <= query_at)
    return allowed


def fold_kv(grad_k, grad_v, sec, own_ref, send_ref):
    for j in range(4):
        k = grad_k[256 * j : 256 * j + 256, :]
        v = grad_v[256 * j : 256 * j + 256, :]
        k = k + pltpu.roll(k, 64, 1)
        v = v + pltpu.roll(v, 64, 1)
        low = lax.broadcasted_iota(jnp.int32, k.shape, 1) < 64
        both = jnp.where(low, k, v)
        first, second = both[0:128], both[128:256]
        own_ref[j] = jnp.where(sec == 0, first, second)
        send_ref[j] = jnp.where(sec == 0, second, first).astype(send_ref.dtype)


def split_halves(value, sec, keep_ref, send_ref, m, lane):
    upper, lower = value[0:256], value[256:512]
    cut = slice(lane, lane + value.shape[1])
    keep_ref[m, :, cut] = jnp.where(sec == 0, upper, lower).astype(BF)
    send_ref[m, :, cut] = jnp.where(sec == 0, lower, upper).astype(BF)


def split_flat(value, sec, keep_ref, send_ref, lane):
    upper, lower = value[0:256], value[256:512]
    cut = slice(lane, lane + value.shape[1])
    keep_ref[:, cut] = jnp.where(sec == 0, upper, lower).astype(BF)
    send_ref[:, cut] = jnp.where(sec == 0, lower, upper).astype(BF)


def turned_rows(value):
    return value.astype(F32).T.astype(BF)


def flat(ref):
    return ref[...].reshape(512, ref.shape[-1])


def attention_weight_grads(first_t, gated_ref, dz_ref, dq_ref, sec, keep_ref, send_ref, lane):
    grad_q = nn(first_t, flat(dq_ref))
    grad_o = nn(turned_rows(flat(dz_ref)), flat(gated_ref))
    for b in range(4):
        cut = slice(128 * b, 128 * b + 128)
        split_halves(grad_q[:, cut], sec, keep_ref, send_ref, b, lane)
        split_halves(grad_o[:, cut], sec, keep_ref, send_ref, b, lane + 128)


def router_grads(dlog_ref, rows_ref):
    turned = flat(dlog_ref).astype(F32).T.astype(BF)
    return nn(turned, flat(rows_ref))[0:32]


def gelu_parts(pre):
    cdf = 0.5 * (1.0 + lax.erf(pre * 0.7071067811865476))
    slope = cdf + pre * (jnp.exp(-0.5 * pre * pre) * 0.3989422804014327)
    return pre * cdf, slope


def own_self_kv(recv_ref, layer, sec, w_kv, kv_ref):
    gain = gain_of(recv_ref, layer, 0)
    for t in range(2):
        first = norm_of(rows_of(recv_ref, layer, t), gain)[0].astype(BF)
        kv = nn(first, w_kv).astype(BF)
        for i in range(2):
            j = 2 * t + i
            kv_ref[j, sec] = kv[128 * i : 128 * i + 128]
            kv_ref[j, 1 - sec] = other_kv(recv_ref, layer, j)


def cross_kv(kvm_ref, kvo_ref, sec, kv_s):
    for j in range(4):
        kv_s[j, sec] = kvm_ref[j]
        kv_s[j, 1 - sec] = kvo_ref[j]


def pack_kernel(
    len_ref, x_ref, gain_ref, w_kv_ref, own_ref, cross_ref, router_ref, send_ref, extra_s
):
    gain = gain_ref[0:1, :].astype(F32)
    w_kv = w_kv_ref[...]
    extra_s[...] = jnp.zeros_like(extra_s)
    extra_s[0:3, :] = gain_ref[...].astype(F32)
    extra_s[ROUTER_AT : ROUTER_AT + 8, :] = router_ref[...].astype(F32)
    lanes = lax.broadcasted_iota(jnp.int32, (1, 512), 1)
    for i in range(4):
        first = norm_of(x_ref[i].astype(F32), gain)[0].astype(BF)
        kv = nn(first, w_kv).astype(BF)
        row = jnp.zeros((1, 512), jnp.int32)
        for k in range(8):
            length = len_ref[i, k]
            row = jnp.where(lanes == k, length >> 5, row)
            row = jnp.where(lanes == 128 + k, length & 31, row)
        extra_s[LEN_ROW : LEN_ROW + 1, :] = row.astype(F32)
        own, cross = own_ref[i], cross_ref[i]
        own_code = (own[0:1] + 8 * own[1:2]).astype(F32)
        cross_code = (cross[0:1] + 8 * cross[1:2]).astype(F32)
        for half in range(2):
            to = 4 * half + i
            here = slice(128 * half, 128 * half + 128)
            send_ref[to, 0:128, :] = x_ref[i, here, :]
            far = kv[128 * (1 - half) : 128 * (1 - half) + 128]
            send_ref[to, 128:160, :] = jnp.concatenate(
                [far[32 * c : 32 * c + 32] for c in range(4)], 1
            )
            extra_s[CODE_ROW : CODE_ROW + 1, 0:128] = own_code[:, here]
            extra_s[CODE_ROW : CODE_ROW + 1, 128:256] = cross_code[:, here]
            send_ref[to, EX_AT : EX_AT + 16, :] = extra_s[...].astype(BF)


def self_fwd_kernel(ids_ref, recv_ref, *refs):
    wa_own, wa_oth, kvw_own, kvw_oth = refs[:4], refs[4:8], refs[8], refs[9]
    h1_ref, g1_ref, mixed_e, mixed_d, log_e, log_d = refs[10:16]
    wq, wo, wkv, kv_s, k2, v2, sems = refs[16:]
    sec, m = ids_ref[0], ids_ref[1]
    loads = Loads(sems)
    kv_waits = [loads.start(sec == i, kvw_own, kvw_oth, wkv.at[i]) for i in range(2)]
    waits = []
    for layer in range(2):
        waits += loads.rows(sec == layer, wa_own, wa_oth, 0, wq.at[layer], m)
        waits += loads.rows(sec == layer, wa_own, wa_oth, 128, wo.at[layer], m)
    wait_all(kv_waits)
    for layer in range(2):
        own_self_kv(recv_ref, layer, sec, wkv[layer], kv_s)
        widen_kv(kv_s, k2.at[layer], v2.at[layer])
    wait_all(waits)
    ends = [ends_of(extra_of(recv_ref, layer, 0).astype(F32)) for layer in range(2)]

    def tile(t, carry):
        for layer, after_ref, mixed_ref, log_ref in (
            (0, h1_ref, mixed_e, log_e),
            (1, g1_ref, mixed_d, log_d),
        ):
            rows = rows_of(recv_ref, layer, t)
            first = norm_of(rows, gain_of(recv_ref, layer, 0))[0].astype(BF)
            route = routing(first, extra_of(recv_ref, layer, 0), codes_of(recv_ref, layer, t, 0))
            allowed = allowed_rows(t, sec, ends[layer], ends[layer], layer == 1)
            out, mixed, row_log = attend_tile(
                first, route, wq[layer], wo[layer], k2[layer], v2[layer], allowed
            )
            after_ref[t] = rows + out
            mixed_ref[t] = mixed
            log_ref[t] = row_log
        return carry

    lax.fori_loop(0, 2, tile, 0)


def enc_ffn_kernel(
    ids_ref, recv_ref, h1_ref, kvc_ref, *refs
):
    f_own, f_oth = refs[:4], refs[4:8]
    h2_ref, mem_ref, kvm_ref, w_in, w_out, third_s, sems = refs[8:]
    low, m = ids_ref[0] == 0, ids_ref[1]
    loads = Loads(sems)
    waits = loads.pieces(low, f_own, f_oth, w_in, m) + loads.pieces(low, f_oth, f_own, w_out, m)
    for t in range(2):
        h2_ref[t] = h1_ref[t]
        third_s[t] = norm_of(h1_ref[t], gain_of(recv_ref, 0, 2))[0].astype(BF)
    wait_all(waits)

    def chunk(c, carry):
        pre = nn(flat(third_s), w_in[c])
        hidden = (0.5 * pre * (1.0 + lax.erf(pre * 0.7071067811865476))).astype(BF)
        h2_ref[...] += nn(hidden, w_out[c]).reshape(2, TILE, 512)
        return carry

    lax.fori_loop(0, 4, chunk, 0)
    for t in range(2):
        memory = norm_of(h2_ref[t], gain_of(recv_ref, 0, 1))[0].astype(BF)
        mem_ref[t] = memory
        kv = nn(memory, kvc_ref[...]).astype(BF)
        kvm_ref[2 * t] = kv[0:128]
        kvm_ref[2 * t + 1] = kv[128:256]


def cross_fwd_kernel(
    ids_ref, recv_ref, g1_ref, kvm_ref, kvo_ref, rc_ref, cc_own, cc_oth, g2_ref, mixed_ref, log_ref,
    wq, wo, kv_s, k2, v2, sems,
):
    sec = ids_ref[0]
    loads = Loads(sems)
    waits = loads.stacked(sec == 0, cc_own, cc_oth, 128, wq)
    waits += loads.stacked(sec == 0, cc_oth, cc_own, 128, wo)
    cross_kv(kvm_ref, kvo_ref, sec, kv_s)
    widen_kv(kv_s, k2, v2)
    wait_all(waits)
    ends_k = ends_of(extra_of(recv_ref, 0, 0).astype(F32))
    ends_q = ends_of(extra_of(recv_ref, 1, 0).astype(F32))

    def tile(t, carry):
        before = g1_ref[t]
        second = norm_of(before, gain_of(recv_ref, 1, 1))[0].astype(BF)
        route = routing(second, rc_ref[...], codes_of(recv_ref, 1, t, 128))
        allowed = allowed_rows(t, sec, ends_q, ends_k, False)
        out, mixed, row_log = attend_tile(second, route, wq[...], wo[...], k2[...], v2[...], allowed)
        g2_ref[t] = before + out
        mixed_ref[t] = mixed
        log_ref[t] = row_log
        return carry

    lax.fori_loop(0, 2, tile, 0)


def ffn_both(c, third_s, third_t, dy_s, dy_t, w_in, w_out, dthird, sec, keep_ref, send_ref):
    pre = nn(flat(third_s), w_in[c])
    hidden, slope = gelu_parts(pre)
    hidden = hidden.astype(BF)
    dpre = (nt(flat(dy_s), w_out[c]) * slope).astype(BF)
    dthird[...] += nt(dpre, w_in[c])
    split_halves(nn(third_t[...], dpre), sec, keep_ref, send_ref, c, 0)
    split_halves(nn(dy_t[...], hidden), sec, keep_ref, send_ref, c, 512)
    return hidden


def dec_ffn_kernel(
    ids_ref, recv_ref, g2_ref, mem_ref, cc_own, *refs
):
    f_own, f_oth = refs[:4], refs[4:8]
    outs_ref, dg2_ref, gain_ref, keep_ref, send_ref = refs[8:13]
    w_in, w_out, cot_s, third_s, third_t, cot_t, acc, dthird, sems = refs[13:]
    sec, m = ids_ref[0], ids_ref[1]
    low = sec == 0
    loads = Loads(sems)
    cot_waits = [loads.plain(cc_own.at[i, pl.ds(0, 128)], cot_s.at[i]) for i in range(4)]
    waits = loads.pieces(low, f_own, f_oth, w_in, m) + loads.pieces(low, f_oth, f_own, w_out, m)
    for t in range(2):
        acc[t] = g2_ref[t]
        third_s[t] = norm_of(g2_ref[t], gain_of(recv_ref, 1, 2))[0].astype(BF)
        outs_ref[2 * t : 2 * t + 2] = mem_ref[t].reshape(2, 128, 512)
    third_t[...] = turned_rows(flat(third_s))
    wait_all(cot_waits)
    cot_t[...] = turned_rows(flat(cot_s))
    dthird[...] = jnp.zeros_like(dthird)
    wait_all(waits)

    def chunk(c, carry):
        hidden = ffn_both(
            c, third_s, third_t, cot_s, cot_t, w_in, w_out, dthird, sec, keep_ref, send_ref
        )
        acc[...] += nn(hidden, w_out[c]).reshape(2, TILE, 512)
        return carry

    lax.fori_loop(0, 4, chunk, 0)
    total = jnp.zeros((1, 512), F32)
    gain = gain_of(recv_ref, 1, 2)
    for t in range(2):
        outs_ref[4 + 2 * t : 6 + 2 * t] = acc[t].astype(BF).reshape(2, 128, 512)
        unused_out, unit, scaled = norm_of(g2_ref[t], gain)
        back, gain_grad = norm_back(dthird[TILE * t : TILE * t + TILE, :], unit, scaled, gain)
        dg2_ref[t] = cot_s[2 * t : 2 * t + 2].reshape(TILE, 512).astype(F32) + back
        total = total + gain_grad
    gain_ref[...] = total


def cross_back_kernel(
    ids_ref, recv_ref, g1_ref, dg2_ref, mixed_ref, log_ref, kvm_ref, kvo_ref, rc_ref, cc_own, cc_oth,
    dg1_ref, gain_ref, own_ref, send_ref, router_ref, keepw_ref, sendw_ref,
    wq, wo, kv_s, k2, v2, segk, grad_k, grad_v, second_s, gated_s, dz_s, dq_s, dlog_s, sems,
):
    sec = ids_ref[0]
    loads = Loads(sems)
    waits = loads.stacked(sec == 0, cc_own, cc_oth, 128, wq)
    waits += loads.stacked(sec == 0, cc_oth, cc_own, 128, wo)
    cross_kv(kvm_ref, kvo_ref, sec, kv_s)
    widen_kv(kv_s, k2, v2)
    ends_k = ends_of(extra_of(recv_ref, 0, 0).astype(F32))
    ends_q = ends_of(extra_of(recv_ref, 1, 0).astype(F32))
    key_segments_t(ends_k, segk)
    grad_k[...] = jnp.zeros_like(grad_k)
    grad_v[...] = jnp.zeros_like(grad_v)
    wait_all(waits)

    def tile(t, total):
        gain = gain_of(recv_ref, 1, 1)
        second, unit, scaled = norm_of(g1_ref[t], gain)
        second = second.astype(BF)
        second_s[t] = second
        route = routing(second, rc_ref[...], codes_of(recv_ref, 1, t, 128))
        allowed = allowed_cols(t, sec, ends_q, segk, False)
        grad_rows = attend_back_tile(
            t, dg2_ref[t], second, route, mixed_ref[t], log_ref[t], wq[...], wo[...], rc_ref[...],
            ROUTER_LANES[2], k2[...], v2[...], allowed, grad_k, grad_v, gated_s, dz_s, dq_s, dlog_s,
        )
        back, gain_grad = norm_back(grad_rows, unit, scaled, gain)
        dg1_ref[t] = dg2_ref[t] + back
        return total + gain_grad

    gain_ref[...] = lax.fori_loop(0, 2, tile, jnp.zeros((1, 512), F32))
    fold_kv(grad_k, grad_v, sec, own_ref, send_ref)
    router_ref[...] = router_grads(dlog_s, second_s)
    attention_weight_grads(
        turned_rows(flat(second_s)), gated_s, dz_s, dq_s, sec, keepw_ref, sendw_ref, 0
    )


def self_back_kernel(layer, ids_ref, recv_ref, up_ref, mixed_ref, log_ref, *refs):
    wa_own, wa_oth, kvw_own, kvw_oth = refs[:4], refs[4:8], refs[8], refs[9]
    refs = refs[10:]
    if layer == 1:
        before, refs = refs[:2], refs[2:]
    dfirst_ref, own_ref, send_ref, router_ref, keepw_ref, sendw_ref = refs[:6]
    wq, wo, wkv, kv_s, k2, v2, segk, grad_k, grad_v = refs[6:15]
    first_s, gated_s, dz_s, dq_s, dlog_s, sems = refs[15:]
    sec, m = ids_ref[0], ids_ref[1]
    mine = sec == layer
    loads = Loads(sems)
    kv_wait = loads.start(mine, kvw_own, kvw_oth, wkv)
    waits = loads.rows(mine, wa_own, wa_oth, 0, wq, m) + loads.rows(mine, wa_own, wa_oth, 128, wo, m)
    lane = 0
    if layer == 1:
        lane = 256
        for src, dst in zip(before, (keepw_ref, sendw_ref)):
            waits.append(loads.plain(src, dst.at[:, :, pl.ds(0, 256)]))
    ends = ends_of(extra_of(recv_ref, layer, 0).astype(F32))
    key_segments_t(ends, segk)
    grad_k[...] = jnp.zeros_like(grad_k)
    grad_v[...] = jnp.zeros_like(grad_v)
    kv_wait()
    own_self_kv(recv_ref, layer, sec, wkv[...], kv_s)
    widen_kv(kv_s, k2, v2)
    wait_all(waits)
    router_block = extra_of(recv_ref, layer, 0)

    def tile(t, carry):
        first = norm_of(rows_of(recv_ref, layer, t), gain_of(recv_ref, layer, 0))[0].astype(BF)
        first_s[t] = first
        route = routing(first, router_block, codes_of(recv_ref, layer, t, 0))
        allowed = allowed_cols(t, sec, ends, segk, layer == 1)
        dfirst_ref[t] = attend_back_tile(
            t, up_ref[t], first, route, mixed_ref[t], log_ref[t], wq[...], wo[...], router_block,
            ROUTER_LANES[layer], k2[...], v2[...], allowed, grad_k, grad_v, gated_s, dz_s, dq_s,
            dlog_s,
        )
        return carry

    lax.fori_loop(0, 2, tile, 0)
    fold_kv(grad_k, grad_v, sec, own_ref, send_ref)
    router_ref[...] = router_grads(dlog_s, first_s)
    attention_weight_grads(
        turned_rows(flat(first_s)), gated_s, dz_s, dq_s, sec, keepw_ref, sendw_ref, lane
    )


def enc_ffn_back_kernel(
    ids_ref, recv_ref, h1_ref, h2_ref, own_ref, come_ref, kvc_ref, *refs
):
    f_own, f_oth = refs[:4], refs[4:8]
    dh1_ref, gain_ref, gain2_ref, keep_ref, send_ref = refs[8:13]
    w_in, w_out, third_s, third_t, dy_s, dy_t, dthird, sems = refs[13:]
    sec, m = ids_ref[0], ids_ref[1]
    low = sec == 0
    loads = Loads(sems)
    waits = loads.pieces(low, f_own, f_oth, w_in, m) + loads.pieces(low, f_oth, f_own, w_out, m)
    total = jnp.zeros((1, 512), F32)
    gain = gain_of(recv_ref, 0, 1)
    for t in range(2):
        dkv = (own_ref[2 * t : 2 * t + 2] + come_ref[2 * t : 2 * t + 2].astype(F32)).astype(BF)
        dmem = rounded(nt(dkv.reshape(TILE, 128), kvc_ref[...]))
        unused_out, unit, scaled = norm_of(h2_ref[t], gain)
        back, gain_grad = norm_back(dmem, unit, scaled, gain)
        dh1_ref[t] = back
        dy_s[t] = back.astype(BF)
        third_s[t] = norm_of(h1_ref[t], gain_of(recv_ref, 0, 2))[0].astype(BF)
        total = total + gain_grad
    gain_ref[...] = total
    third_t[...] = turned_rows(flat(third_s))
    dy_t[...] = turned_rows(flat(dy_s))
    dthird[...] = jnp.zeros_like(dthird)
    wait_all(waits)

    def chunk(c, carry):
        ffn_both(c, third_s, third_t, dy_s, dy_t, w_in, w_out, dthird, sec, keep_ref, send_ref)
        return carry

    lax.fori_loop(0, 4, chunk, 0)
    total = jnp.zeros((1, 512), F32)
    gain = gain_of(recv_ref, 0, 2)
    for t in range(2):
        unused_out, unit, scaled = norm_of(h1_ref[t], gain)
        back, gain_grad = norm_back(dthird[TILE * t : TILE * t + TILE, :], unit, scaled, gain)
        dh1_ref[t] += back
        total = total + gain_grad
    gain2_ref[...] = total


def finish_rows(layer, recv_ref, up_ref, df_ref, own_ref, come_ref, wkv, first_s, out_ref, at):
    total = jnp.zeros((1, 512), F32)
    gain = gain_of(recv_ref, layer, 0)
    dkvs = []
    for t in range(2):
        first, unit, scaled = norm_of(rows_of(recv_ref, layer, t), gain)
        first_s[t] = first.astype(BF)
        dkv = (own_ref[2 * t : 2 * t + 2] + come_ref[2 * t : 2 * t + 2].astype(F32)).astype(BF)
        dkv = dkv.reshape(TILE, 128)
        dkvs.append(dkv)
        back, gain_grad = norm_back(df_ref[t] + nt(dkv, wkv), unit, scaled, gain)
        dx = (up_ref[t] + back).astype(BF)
        for i in range(2):
            out_ref[at + 2 * t + i, 0:128, :] = dx[128 * i : 128 * i + 128]
        total = total + gain_grad
    grad = nn(turned_rows(flat(first_s)), jnp.concatenate(dkvs, 0))
    return total, grad


def dec_finish_kernel(
    ids_ref, recv_ref, up_ref, df_ref, own_ref, come_ref, own_c, come_c, mem_ref, kvw_own, kvw_oth,
    dx_ref, gain_ref, keep_ref, send_ref, wkv, first_s, sems,
):
    sec = ids_ref[0]
    wait = Loads(sems).start(sec == 1, kvw_own, kvw_oth, wkv)
    dkv_c = (own_c[...] + come_c[...].astype(F32)).astype(BF).reshape(512, 128)
    split_flat(nn(turned_rows(flat(mem_ref)), dkv_c), sec, keep_ref, send_ref, 128)
    wait()
    gain_ref[...], grad = finish_rows(
        1, recv_ref, up_ref, df_ref, own_ref, come_ref, wkv[...], first_s, dx_ref, 0
    )
    split_flat(grad, sec, keep_ref, send_ref, 0)


def enc_finish_kernel(
    ids_ref, recv_ref, up_ref, df_ref, own_ref, come_ref, dx1_ref, r0, r1, rc,
    gain_e1, gain_e2, gain_d0, gain_d1, gain_d2, kvw_own, kvw_oth,
    out_ref, wkv, first_s, misc, sems,
):
    sec = ids_ref[0]
    wait = Loads(sems).start(sec == 0, kvw_own, kvw_oth, wkv)
    misc[...] = r0[...] + r1[...] + rc[...]
    out_ref[4:8, 0:128, :] = dx1_ref[...]
    wait()
    gain_e0, grad = finish_rows(
        0, recv_ref, up_ref, df_ref, own_ref, come_ref, wkv[...], first_s, out_ref, 0
    )
    rows = (gain_e0, gain_e1[...], gain_e2[...], gain_d0[...], gain_d1[...], gain_d2[...])
    for i, row in enumerate(rows):
        misc[GAIN_ROW + i : GAIN_ROW + i + 1, :] = row
    both = misc[...]
    for half in range(2):
        cut = slice(256 * half, 256 * half + 256)
        part = grad[cut].astype(BF)
        small = both[:, cut].astype(BF)
        block = jnp.concatenate(
            [
                jnp.concatenate([part[64 * c : 64 * c + 64] for c in range(4)], 1),
                jnp.concatenate([small[0:16], small[16:32]], 1),
            ],
            0,
        )
        for i in range(4):
            out_ref[4 * half + i, 128:208, :] = block


def add_kernel(keep_ref, come_ref, *outs):
    lane = 0
    for out_ref in outs:
        cut = slice(lane, lane + out_ref.shape[-1])
        left, right = keep_ref[:, :, cut].astype(F32), come_ref[:, :, cut].astype(F32)
        out_ref[...] = (left + right).astype(BF)
        lane += out_ref.shape[-1]


def add_pieces_kernel(flats, ids_ref, *refs):
    n = len(flats)
    keeps, comes, outs = refs[:n], refs[n : 2 * n], refs[2 * n :]
    m = ids_ref[1]
    for b in range(4):
        lane = 0
        for is_flat, keep, come in zip(flats, keeps, comes):
            left = keep[...] if is_flat else keep[m ^ b]
            right = come[...] if is_flat else come[m ^ b]
            width = keep.shape[-1]
            outs[b][:, lane : lane + width] = (left.astype(F32) + right.astype(F32)).astype(BF)
            lane += width


def sum_ffn_kernel(ids_ref, dec_a, dec_b, enc_ref, *outs):
    rows = outs[0].shape[0]
    d = ids_ref[2]
    for k in range(len(outs)):
        cut = pl.ds(pl.multiple_of((d ^ k) * rows, rows), rows)
        for ref, lane in ((enc_ref, 0), (dec_a, 1024), (dec_b, 1536)):
            total = ref[0, cut, :].astype(F32)
            for i in range(1, 4):
                total = total + ref[i, cut, :].astype(F32)
            outs[k][:, lane : lane + ref.shape[-1]] = total.astype(BF)


def tail_kernel(dx_ref, *refs):
    att_d, att_e, (dx_out, out_ref) = refs[:4], refs[4:8], refs[8:]
    for i in range(4):
        for half in range(2):
            dx_out[i, half] = dx_ref[4 * half + i, 0:128, :].astype(F32)
    for parts, lane in ((att_d, 0), (att_e, 512)):
        total = parts[0][...].astype(F32)
        for part in parts[1:]:
            total = total + part[...].astype(F32)
        out_ref[:, lane : lane + 512] = total.astype(BF)
    small = dx_ref[0, 128:208, :].astype(F32)
    for i in range(1, 8):
        small = small + dx_ref[i, 128:208, :].astype(F32)
    for c in range(4):
        out_ref[64 * c : 64 * c + 64, 1024:1152] = small[0:64, 128 * c : 128 * c + 128].astype(BF)
    misc = jnp.concatenate([small[64:80, 0:256], small[64:80, 256:512]], 0)
    misc = jnp.concatenate([misc, jnp.zeros((96, 256), F32)], 0)
    out_ref[:, 1152:1280] = misc.T.astype(BF)


def final_kernel(come_ref, *refs):
    ffn, outs = refs[:4], refs[4:]
    gains, router, query, keyval, output, inner, outer, router_c, query_c, keyval_c, output_c = outs
    small = come_ref[0].astype(F32)
    for i in range(1, 4):
        small = small + come_ref[i].astype(F32)
    wide = ffn[0][...].astype(F32)
    for part in ffn[1:]:
        wide = wide + part[...].astype(F32)
    for layer in range(2):
        inner[layer] = wide[:, 1024 * layer : 1024 * layer + 512]
        outer[layer] = wide[:, 1024 * layer + 512 : 1024 * layer + 1024]
    keyval[0], keyval[1] = small[:, 1024:1152], small[:, 768:896]
    keyval_c[...] = small[:, 896:1024]
    for at, put_q, put_o in (
        (0, query_c, output_c),
        (256, query.at[1], output.at[1]),
        (512, query.at[0], output.at[0]),
    ):
        turned = small[:, at + 128 : at + 256].T
        for e in range(2):
            put_q[e] = small[:, at + 64 * e : at + 64 * e + 64]
            put_o[e] = turned[64 * e : 64 * e + 64]
    misc = small[:, 1152:1280].T
    router[0], router[1], router_c[...] = misc[0:8], misc[8:16], misc[16:24]
    gains[0], gains[1] = misc[24:27], misc[27:30]


def shaped(dims, kind):
    return jax.ShapeDtypeStruct(dims, kind)


def cost_of(micros):
    return pl.CostEstimate(
        flops=int(micros * 1.1535e9), bytes_accessed=int(micros * 3.0e6), transcendentals=0
    )


def run(kernel, args, places, outs, scratch, micros, after=()):
    space = {
        "s": pl.BlockSpec(memory_space=pltpu.SMEM),
        "v": pl.BlockSpec(memory_space=pltpu.VMEM),
        "a": pl.BlockSpec(memory_space=pl.ANY),
    }
    count, extra = len(args), len(after)

    def body(*refs):
        kernel(*refs[:count], *refs[count + extra :])

    return pl.pallas_call(
        body,
        out_shape=outs,
        in_specs=[space[p] for p in places] + [space["a"]] * extra,
        out_specs=jax.tree.map(lambda _: space["v"], outs),
        scratch_shapes=scratch,
        compiler_params=pltpu.CompilerParams(vmem_limit_bytes=VMEM_LIMIT),
        cost_estimate=cost_of(micros),
    )(*args, *after)


def vm(*dims, kind=BF):
    return pltpu.VMEM(dims, kind)


def dma(count):
    return pltpu.SemaphoreType.DMA((count,))


def across(value, axes, size, by):
    return lax.ppermute(value, axes, [(i, i ^ by) for i in range(size)])


def swapped(value):
    return across(value, "section", 2, 1)


def gathered(value):
    return [value] + [across(value, "mp", 4, b) for b in range(1, 4)]


def to_all(value, axes):
    return lax.all_to_all(value, axes, split_axis=0, concat_axis=0, tiled=True)


def add_shares(keep, come, micros, after, parts=1):
    blocks, rows, width = keep.shape
    whole = pl.BlockSpec((1, rows, width), lambda i: (i, 0, 0))
    part = pl.BlockSpec((1, rows, width // parts), lambda i: (i, 0, 0))
    extra = len(after)
    return pl.pallas_call(
        lambda k, c, *rest: add_kernel(k, c, *rest[extra:]),
        out_shape=[shaped((blocks, rows, width // parts), BF)] * parts,
        grid=(blocks,),
        in_specs=[whole, whole] + [pl.BlockSpec(memory_space=pl.ANY)] * extra,
        out_specs=[part] * parts,
        cost_estimate=cost_of(micros),
    )(keep, come, *after)


def add_pieces(ids, keeps, comes, micros, after=()):
    flats = tuple(keep.ndim == 2 for keep in keeps)
    width = sum(keep.shape[-1] for keep in keeps)
    return run(
        functools.partial(add_pieces_kernel, flats),
        (ids, *keeps, *comes),
        "s" + "v" * (2 * len(keeps)),
        [shaped((256, width), BF)] * 4,
        [],
        micros,
        after=after,
    )


def mp_exchange(pieces):
    return [pieces[0]] + [across(pieces[b], "mp", 4, b) for b in range(1, 4)]


def dp_exchange(pieces):
    return [pieces[0]] + [across(pieces[k], "dp", 4, k) for k in range(1, 4)]


def gated(values, after):
    anywhere = pl.BlockSpec(memory_space=pl.ANY)
    count = len(values)
    return pl.pallas_call(
        lambda *refs: None,
        out_shape=[shaped(v.shape, v.dtype) for v in values],
        in_specs=[anywhere] * (count + len(after)),
        out_specs=[anywhere] * count,
        input_output_aliases={i: i for i in range(count)},
        cost_estimate=cost_of(0.2),
    )(*values, *after)


def per_device(
    inputs,
    lengths,
    routes_self,
    routes_cross,
    gains,
    router_self,
    query_self,
    keyval_self,
    output_self,
    ffn_in,
    ffn_out,
    router_cross,
    query_cross,
    keyval_cross,
    output_cross,
    cotangent,
):
    sec, m, d = lax.axis_index("section"), lax.axis_index("mp"), lax.axis_index("dp")
    low = sec == 0
    ids = jnp.stack([sec, m, d]).astype(jnp.int32)
    sem = dma(24)
    rowgroup = ("section", "mp")

    q_rows = query_self[0].transpose(0, 2, 1).reshape(128, 512)
    o_rows = output_self[0].reshape(128, 512)
    wa = jnp.concatenate([q_rows, o_rows], 0)
    wa_own = gathered(wa)
    w_in, w_out = ffn_in[0], ffn_out[0]
    half_come = swapped(jnp.where(low, w_out, w_in))
    enc_half = jnp.where(low, w_in, half_come)
    dec_half = jnp.where(low, half_come, w_out)
    kvw_own = keyval_self[0]
    kvw_oth = swapped(kvw_own)
    router_c = jnp.concatenate([jnp.zeros((8, 512), BF), router_cross.T], 0)

    packed = run(
        pack_kernel,
        (
            lengths[0, :, 0],
            inputs[0, :, 0],
            gains[0],
            keyval_self[0],
            routes_self[0, :, 0].transpose(0, 2, 1),
            routes_cross[:, 0].transpose(0, 2, 1),
            router_self[0].T,
        ),
        "svvvvvv",
        shaped((8, 176, 512), BF),
        [vm(16, 512, kind=F32)],
        3.4,
        after=(wa, enc_half, dec_half),
    )
    recv = to_all(packed, rowgroup)
    wa_oth = [swapped(piece) for piece in wa_own]
    (enc_half,) = gated([enc_half], [packed, *wa_own[1:]])
    enc_own = gathered(enc_half)
    c_rows = jnp.where(
        low, query_cross.transpose(0, 2, 1).reshape(128, 512), output_cross.reshape(128, 512)
    )
    cot_cut = lax.dynamic_index_in_dim(cotangent[:, 0].reshape(4, 2, 128, 512), sec, 1, False)
    cc_in = jnp.concatenate([cot_cut, jnp.broadcast_to(c_rows[None], (4, 128, 512))], 1)

    act = shaped((2, TILE, 512), F32)
    actb = shaped((2, TILE, 512), BF)
    mixed_s = shaped((2, 2 * TILE, 128), F32)
    log_s = shaped((2, 1, 2 * TILE), F32)
    kv_b = shaped((4, 128, 128), BF)
    kv_f = shaped((4, 128, 128), F32)
    row_s = shaped((1, 512), F32)
    ffn_g = shaped((4, 256, 1024), BF)
    router_s = shaped((32, 512), F32)
    wide = [vm(512, 512), vm(512, 512)]
    kv_scratch = [vm(4, 2, 128, 128), vm(1024, 128), vm(1024, 128)]
    back_scratch = [
        vm(1024, TILE, kind=F32), vm(1024, 128, kind=F32), vm(1024, 128, kind=F32),
        vm(2, TILE, 512), vm(2, TILE, 512), vm(2, TILE, 512), vm(2, TILE, 512), vm(2, TILE, 128),
    ]
    ffn_w = [vm(4, 512, 512), vm(4, 512, 512)]

    h1, g1, mixed_e, mixed_d, log_e, log_d = run(
        self_fwd_kernel,
        (ids, recv, *wa_own, *wa_oth, kvw_own, kvw_oth),
        "sv" + "a" * 10,
        (act, act, mixed_s, mixed_s, log_s, log_s),
        [vm(2, 512, 512), vm(2, 512, 512), vm(2, 512, 128), vm(4, 2, 128, 128)]
        + [vm(2, 1024, 128), vm(2, 1024, 128), sem],
        13.6,
    )
    enc_own[1:] = gated(enc_own[1:], [h1])
    enc_oth = [swapped(piece) for piece in enc_own]
    (dec_half,) = gated([dec_half], [enc_own[1]])
    dec_own = gathered(dec_half)
    (cc_in,) = gated([cc_in], [enc_own[1]])
    cc_own = to_all(cc_in, "mp")
    h2, memory, kvm = run(
        enc_ffn_kernel,
        (ids, recv, h1, keyval_cross, *enc_own, *enc_oth),
        "svvv" + "a" * 8,
        (act, actb, kv_b),
        ffn_w + [vm(2, TILE, 512), sem],
        4.0,
        after=(dec_half, cc_in),
    )
    kvm_oth = swapped(kvm)
    (cc_own,) = gated([cc_own], [h2])
    cc_oth = swapped(cc_own)
    g2, mixed_c, log_c = run(
        cross_fwd_kernel,
        (ids, recv, g1, kvm, kvm_oth, router_c, cc_own, cc_oth),
        "svvvvvaa",
        (act, mixed_s, log_s),
        wide + kv_scratch + [sem],
        2.0,
    )
    dec_own[1:] = gated(dec_own[1:], [g2])
    dec_oth = [swapped(piece) for piece in dec_own]
    outs, dg2, gain_d2, keep_d, send_d = run(
        dec_ffn_kernel,
        (ids, recv, g2, memory, cc_own, *dec_own, *dec_oth),
        "svvva" + "a" * 8,
        (shaped((8, 128, 512), BF), act, row_s, ffn_g, ffn_g),
        ffn_w
        + [vm(4, 128, 512), vm(2, TILE, 512), vm(512, 512), vm(512, 512)]
        + [vm(2, TILE, 512, kind=F32), vm(512, 512, kind=F32), sem],
        15.0,
    )
    come_d = swapped(send_d)
    outs_come = to_all(outs, rowgroup)
    att_g = shaped((4, 256, 256), BF)
    flat_g = shaped((256, 256), BF)
    dg1, gain_d1, own_c, sendkv_c, router_cg, keep_wc, send_wc = run(
        cross_back_kernel,
        (ids, recv, g1, dg2, mixed_c, log_c, kvm, kvm_oth, router_c, cc_own, cc_oth),
        "svvvvvvvvaa",
        (act, row_s, kv_f, kv_b, router_s, att_g, att_g),
        wide + kv_scratch + back_scratch + [sem],
        13.0,
    )
    comekv_c = swapped(sendkv_c)
    dec_a, dec_b = add_shares(keep_d, come_d, 4.0, (dg1, outs_come), 2)
    dh1, gain_e1, gain_e2, keep_e, send_e = run(
        enc_ffn_back_kernel,
        (ids, recv, h1, h2, own_c, comekv_c, keyval_cross, *enc_own, *enc_oth),
        "svvvvvv" + "a" * 8,
        (act, row_s, row_s, ffn_g, ffn_g),
        ffn_w
        + [vm(2, TILE, 512), vm(512, 512), vm(2, TILE, 512), vm(512, 512)]
        + [vm(512, 512, kind=F32), sem],
        13.4,
        after=(dec_a,),
    )
    dec_a = to_all(dec_a, "mp")
    (dec_b,) = gated([dec_b], [dec_a])
    dec_b = to_all(dec_b, "mp")
    come_e = swapped(send_e)
    self_scratch = wide + [vm(512, 128)] + kv_scratch + back_scratch + [sem]
    att_dg = shaped((4, 256, 512), BF)
    df1, own_1, sendkv_1, router_1g, keep_w1, send_w1 = run(
        functools.partial(self_back_kernel, 1),
        (
            ids, recv, dg1, mixed_d, log_d, *wa_own, *wa_oth, kvw_own, kvw_oth, keep_wc, send_wc,
        ),
        "svvvv" + "a" * 12,
        (act, kv_f, kv_b, router_s, att_dg, att_dg),
        self_scratch,
        12.2,
        after=(dh1, dec_a),
    )
    comekv_1 = swapped(sendkv_1)
    come_w1 = swapped(send_w1)
    (ffn_e,) = add_shares(keep_e, come_e, 4.0, (df1, dec_b))
    att_d = add_pieces(ids, [keep_w1], [come_w1], 3.6, (ffn_e,))
    df0, own_0, sendkv_0, router_0g, keep_w0, send_w0 = run(
        functools.partial(self_back_kernel, 0),
        (ids, recv, dh1, mixed_e, log_e, *wa_own, *wa_oth, kvw_own, kvw_oth),
        "svvvv" + "a" * 10,
        (act, kv_f, kv_b, router_s, att_g, att_g),
        self_scratch,
        11.8,
        after=(ffn_e, *att_d),
    )
    comekv_0 = swapped(sendkv_0)
    come_w0 = swapped(send_w0)
    ffn_e = to_all(ffn_e, "mp")
    att_d = mp_exchange(att_d)
    dx1, gain_d0, keep_s1, send_s1 = run(
        dec_finish_kernel,
        (ids, recv, dg1, df1, own_1, comekv_1, own_c, comekv_c, memory, kvw_own, kvw_oth),
        "svvvvvvvvaa",
        (shaped((4, 128, 512), BF), row_s, flat_g, flat_g),
        [vm(512, 128), vm(2, TILE, 512), sem],
        5.5,
        after=(*att_d[1:], df0),
    )
    come_s1 = swapped(send_s1)
    finished = run(
        enc_finish_kernel,
        (
            ids, recv, dh1, df0, own_0, comekv_0, dx1, router_0g, router_1g, router_cg,
            gain_e1, gain_e2, gain_d0, gain_d1, gain_d2, kvw_own, kvw_oth,
        ),
        "s" + "v" * 14 + "aa",
        shaped((8, 208, 512), BF),
        [vm(512, 128), vm(2, TILE, 512), vm(32, 512, kind=F32), sem],
        6.0,
    )
    att_e = add_pieces(
        ids, [keep_w0, keep_s1], [come_w0, come_s1], 3.6, (finished,)
    )
    att_e = mp_exchange(att_e)
    dp = lax.axis_size("dp")
    share = 256 // dp
    if dp == 4:
        ffn = dp_exchange(
            run(
                sum_ffn_kernel,
                (ids, dec_a, dec_b, ffn_e),
                "svvv",
                [shaped((64, 2048), BF)] * 4,
                [],
                4.0,
                after=(att_e[0],),
            )
        )
        after = ffn[1:]
    else:
        after = ()
    dx, small = run(
        tail_kernel,
        (to_all(finished, rowgroup), *att_d, *att_e),
        "v" * 9,
        (shaped((4, 2, 128, 512), F32), shaped((256, 1280), BF)),
        [],
        3.0,
        after=after,
    )
    small = to_all(small.reshape(dp, share, 1280), "dp")
    outs_come = outs_come.reshape(2, 4, 128, 512).transpose(1, 0, 2, 3)
    results = (outs_come.reshape(1, 4, 1, 256, 512), dx.reshape(1, 4, 1, 256, 512))
    if dp == 4:
        made = run(
            final_kernel,
            (small, *ffn),
            "v" * 5,
            (
                shaped((2, 3, 64), F32),
                shaped((2, 8, 64), F32),
                shaped((2, 2, 64, 64), F32),
                shaped((2, 64, 128), F32),
                shaped((2, 2, 64, 64), F32),
                shaped((2, 64, 512), F32),
                shaped((2, 64, 512), F32),
                shaped((8, 64), F32),
                shaped((2, 64, 64), F32),
                shaped((64, 128), F32),
                shaped((2, 64, 64), F32),
            ),
            [],
            3.0,
        )
        made = list(made)
        made[1] = made[1].transpose(0, 2, 1)
        made[6] = made[6].transpose(0, 2, 1)
        made[7] = made[7].T
        return (*results, *made)

    small = jnp.sum(small.astype(F32), 0)
    ffn_d = jnp.concatenate([dec_a, dec_b], 2)
    sums = [jnp.sum(part.astype(F32), 0).astype(BF) for part in (ffn_d, ffn_e)]
    ffn_d, ffn_e = [
        jnp.sum(to_all(part.reshape(dp, share, 1024), "dp").astype(F32), 0) for part in sums
    ]

    def query_of(at):
        return small[:, at : at + 128].reshape(share, 2, 64).transpose(1, 0, 2)

    def output_of(at):
        return small[:, at + 128 : at + 256].T.reshape(2, 64, share)

    misc = small[:, 1152:1280].T

    def router_of(layer):
        return misc[ROUTER_LANES[layer] : ROUTER_LANES[layer] + 8].T

    return (
        *results,
        misc[GAIN_ROW : GAIN_ROW + 6].reshape(2, 3, share),
        jnp.stack([router_of(0), router_of(1)]),
        jnp.stack([query_of(512), query_of(256)]),
        jnp.stack([small[:, 1024:1152], small[:, 768:896]]),
        jnp.stack([output_of(512), output_of(256)]),
        jnp.stack([ffn_e[:, :512], ffn_d[:, :512]]),
        jnp.stack([ffn_e[:, 512:].T, ffn_d[:, 512:].T]),
        router_of(2),
        query_of(0),
        small[:, 896:1024],
        output_of(0),
    )


def solution(mesh):
    placed = (
        P("section", None, "dp", "mp", None),
        P("section", None, "dp", None),
        P("section", None, "dp", "mp", None),
        P(None, "dp", "mp", None),
        P("section", None, None),
        P("section", None, None),
        P("section", "mp", None, None),
        P("section", None, None),
        P("section", "mp", None, None),
        P("section", None, "mp"),
        P("section", "mp", None),
        P(),
        P("mp", None, None),
        P(),
        P("mp", None, None),
        P(None, "dp", "mp", None),
    )
    return jax.shard_map(
        per_device,
        mesh=mesh,
        in_specs=placed,
        out_specs=(
            P("section", None, "dp", "mp", None),
            P("section", None, "dp", "mp", None),
            P(None, None, ("section", "dp")),
            P(None, ("section", "dp"), None),
            P(None, "mp", ("section", "dp"), None),
            P(None, ("section", "dp"), None),
            P(None, "mp", None, ("section", "dp")),
            P(None, ("section", "dp"), "mp"),
            P(None, "mp", ("section", "dp")),
            P(("section", "dp"), None),
            P("mp", ("section", "dp"), None),
            P(("section", "dp"), None),
            P("mp", None, ("section", "dp")),
        ),
        check_vma=False,
    )
```

```python
import functools

import jax
import jax.numpy as jnp
from jax import lax
from jax.experimental import pallas as pl
from jax.experimental.pallas import tpu as pltpu
from jax.sharding import PartitionSpec as P

EPS = 1e-05
MASK_VALUE = -1000000000.0
BF = jnp.bfloat16
F32 = jnp.float32
TILE = 256
EX_AT = 160
CODE_ROW = 3
LEN_ROW = 4
ROUTER_AT = 8
GAIN_ROW = 24
ROUTER_LANES = (0, 8, 16)
VMEM_LIMIT = 56 * 1024 * 1024
LARGE = 60000


def nn(left, right):
    return lax.dot_general(left, right, (((1,), (0,)), ((), ())), preferred_element_type=F32)


def nt(left, right):
    return lax.dot_general(left, right, (((1,), (1,)), ((), ())), preferred_element_type=F32)


def tn(left, right):
    return lax.dot_general(left, right, (((0,), (0,)), ((), ())), preferred_element_type=F32)


def norm_of(values, gain_row):
    center = values - jnp.mean(values, 1, keepdims=True)
    scaled = lax.rsqrt(jnp.mean(center * center, 1, keepdims=True) + EPS)
    unit_rows = center * scaled
    return unit_rows * gain_row, unit_rows, scaled


def norm_back(upstream, unit_rows, scaled, gain_row):
    inner = upstream * gain_row
    result = scaled * (
        inner
        - jnp.mean(inner, 1, keepdims=True)
        - unit_rows * jnp.mean(inner * unit_rows, 1, keepdims=True)
    )
    return result, jnp.sum(upstream * unit_rows, 0, keepdims=True)


def eye_of(size):
    return lax.broadcasted_iota(jnp.int32, (size, size), 0) == lax.broadcasted_iota(
        jnp.int32, (size, size), 1
    )


def row_to_col(row):
    return jnp.sum(jnp.where(eye_of(128), row, 0.0), 1, keepdims=True)


def col_to_row(col):
    parts = []
    for at in range(0, col.shape[0], 128):
        part = jnp.where(eye_of(128), col[at : at + 128], 0.0)
        parts.append(jnp.sum(part, 0, keepdims=True))
    return jnp.concatenate(parts, 1)


def ends_of(extra):
    lengths = extra[LEN_ROW : LEN_ROW + 1, 0:8] * 32.0 + extra[LEN_ROW : LEN_ROW + 1, 128:136]
    ends = [lengths[:, 0:1]]
    for k in range(1, 8):
        ends.append(ends[-1] + lengths[:, k : k + 1])
    return ends


def segments(places, ends):
    total = jnp.where(places >= ends[0], 1.0, 0.0)
    for end in ends[1:]:
        total = total + jnp.where(places >= end, 1.0, 0.0)
    return total


def extra_of(recv_ref, layer, quarter):
    return recv_ref[4 * layer + quarter, EX_AT : EX_AT + 16, :]


def gain_of(recv_ref, layer, which):
    return extra_of(recv_ref, layer, 0).astype(F32)[which : which + 1, :]


def rows_of(recv_ref, layer, t):
    return recv_ref[pl.ds(4 * layer + 2 * t, 2), 0:128, :].reshape(TILE, 512).astype(F32)


def codes_of(recv_ref, layer, t, lane):
    cols = []
    for i in range(2):
        extra = extra_of(recv_ref, layer, 2 * t + i).astype(F32)
        cols.append(row_to_col(extra[CODE_ROW : CODE_ROW + 1, lane : lane + 128]))
    return jnp.concatenate(cols, 0)


def other_kv(recv_ref, layer, quarter):
    packed = recv_ref[4 * layer + quarter, 128:160, :]
    return jnp.concatenate([packed[:, 128 * c : 128 * c + 128] for c in range(4)], 0)


def routing(query_rows, router_block, code):
    second = jnp.floor(code * 0.125)
    first = code - 8.0 * second
    e0, e1 = first.astype(jnp.int32), second.astype(jnp.int32)
    logits = nt(query_rows, router_block)
    lanes = lax.broadcasted_iota(jnp.int32, logits.shape, 1)
    l0 = jnp.sum(jnp.where(lanes == e0 + ROUTER_AT, logits, 0.0), 1, keepdims=True)
    l1 = jnp.sum(jnp.where(lanes == e1 + ROUTER_AT, logits, 0.0), 1, keepdims=True)
    top = jnp.maximum(l0, l1)
    x0, x1 = jnp.exp(l0 - top), jnp.exp(l1 - top)
    total = x0 + x1
    owners = lax.broadcasted_iota(jnp.int32, (code.shape[0], 512), 1) >> 6
    return e0, e1, x0 / total, x1 / total, owners == e0, owners == e1


def fold(wide, mask):
    kept = jnp.where(mask, wide, 0.0)
    return kept[:, 0:128] + kept[:, 128:256] + kept[:, 256:384] + kept[:, 384:512]


def spread(a0, a1, m0, m1):
    parts = []
    for c in range(4):
        cut = slice(128 * c, 128 * c + 128)
        parts.append(jnp.where(m0[:, cut], a0, jnp.where(m1[:, cut], a1, 0.0)))
    return jnp.concatenate(parts, 1).astype(BF)


def rounded(value):
    return value.astype(BF).astype(F32)


def start_pick(cond, yes, no, dst, sem):
    @pl.when(cond)
    def _():
        pltpu.make_async_copy(yes, dst, sem).start()

    @pl.when(jnp.logical_not(cond))
    def _():
        pltpu.make_async_copy(no, dst, sem).start()


class Loads:
    def __init__(self, sems):
        self.sems, self.used = sems, 0

    def start(self, cond, yes, no, dst):
        sem = self.sems.at[self.used]
        self.used += 1
        start_pick(cond, yes, no, dst, sem)
        return functools.partial(lambda a, b, c: pltpu.make_async_copy(a, b, c).wait(), yes, dst, sem)

    def plain(self, src, dst):
        sem = self.sems.at[self.used]
        self.used += 1
        copy = pltpu.make_async_copy(src, dst, sem)
        copy.start()
        return copy.wait

    def rows(self, cond, yes, no, at, dst, m):
        cut = pl.ds(at, 128)
        return [
            self.start(cond, yes[b].at[cut], no[b].at[cut], dst.at[pl.ds(128 * (m ^ b), 128)])
            for b in range(4)
        ]

    def pieces(self, cond, yes, no, dst, m):
        return [self.start(cond, yes[b], no[b], dst.at[m ^ b]) for b in range(4)]


def wait_all(waits):
    for wait in waits:
        wait()


def widen_kv(kv_ref, k2_ref, v2_ref):
    for j in range(4):
        kv = kv_ref[j].reshape(256, 128).astype(F32)
        turned = pltpu.roll(kv, 64, 1)
        low = lax.broadcasted_iota(jnp.int32, kv.shape, 1) < 64
        k2_ref[256 * j : 256 * j + 256, :] = jnp.where(low, kv, turned).astype(BF)
        v2_ref[256 * j : 256 * j + 256, :] = jnp.where(low, turned, kv).astype(BF)


def attend_tile(query_rows, route, w_qt, w_o, k2, v2, allowed):
    e0, e1, g0, g1, m0, m1 = route
    q_all = nt(query_rows, w_qt) * 0.125
    queries = jnp.concatenate([fold(q_all, m0), fold(q_all, m1)], 0).astype(BF)
    scores = nt(queries, k2)
    scores = jnp.concatenate(
        [
            jnp.where(allowed, scores[0:TILE], MASK_VALUE),
            jnp.where(allowed, scores[TILE:], MASK_VALUE),
        ],
        0,
    )
    top = jnp.max(scores, 1, keepdims=True)
    weights = jnp.exp(scores - top)
    total = jnp.sum(weights, 1, keepdims=True)
    mixed = nn(weights.astype(BF), v2) / total
    log_total = top + jnp.log(total)
    gated = spread(rounded(g0) * mixed[0:TILE], rounded(g1) * mixed[TILE:], m0, m1)
    return nn(gated, w_o), mixed, col_to_row(log_total)


def attend_back_tile(
    t, upstream, query_rows, route, mixed, log_row, w_qt, w_o, router_block, router_lane, k2, v2,
    allowed_t, grad_k, grad_v, gated_ref, dz_ref, dq_ref, dlog_ref,
):
    e0, e1, g0, g1, m0, m1 = route
    q_all = nt(query_rows, w_qt) * 0.125
    queries = jnp.concatenate([fold(q_all, m0), fold(q_all, m1)], 0).astype(BF)
    dz = upstream.astype(BF)
    dg_all = nt(dz, w_o)
    dgated0, dgated1 = fold(dg_all, m0), fold(dg_all, m1)
    r0, r1 = rounded(g0), rounded(g1)
    mixed0, mixed1 = mixed[0:TILE], mixed[TILE:]
    gated_ref[t] = spread(r0 * mixed0, r1 * mixed1, m0, m1)
    dz_ref[t] = dz
    dgate0 = rounded(jnp.sum(mixed0 * dgated0, 1, keepdims=True))
    dgate1 = rounded(jnp.sum(mixed1 * dgated1, 1, keepdims=True))
    do0, do1 = (r0 * dgated0).astype(BF), (r1 * dgated1).astype(BF)
    grad_mixed = jnp.concatenate([do0, do1], 0)
    inner_row = jnp.concatenate(
        [
            col_to_row(jnp.sum(do0.astype(F32) * mixed0, 1, keepdims=True)),
            col_to_row(jnp.sum(do1.astype(F32) * mixed1, 1, keepdims=True)),
        ],
        1,
    )
    scores = nt(k2, queries)
    scores = jnp.concatenate(
        [
            jnp.where(allowed_t, scores[:, 0:TILE], MASK_VALUE),
            jnp.where(allowed_t, scores[:, TILE:], MASK_VALUE),
        ],
        1,
    )
    probs = jnp.exp(scores - log_row)
    grad_probs = nt(v2, grad_mixed)
    grad_scores = (probs * (grad_probs - inner_row)).astype(BF)
    grad_v[...] += nn(probs.astype(BF), grad_mixed)
    grad_k[...] += nn(grad_scores, queries)
    grad_q = rounded(tn(grad_scores, k2) * 0.125)
    dq_all = spread(grad_q[0:TILE], grad_q[TILE:], m0, m1)
    dq_ref[t] = dq_all
    grad_rows = nn(dq_all, w_qt)
    mean_grad = g0 * dgate0 + g1 * dgate1
    dc0, dc1 = g0 * (dgate0 - mean_grad), g1 * (dgate1 - mean_grad)
    lanes = lax.broadcasted_iota(jnp.int32, (TILE, 16), 1)
    dlog = jnp.where(lanes == e0 + ROUTER_AT, dc0, 0.0) + jnp.where(
        lanes == e1 + ROUTER_AT, dc1, 0.0
    )
    wide = lax.broadcasted_iota(jnp.int32, (TILE, 128), 1)
    dlog_ref[t] = (
        jnp.where(wide == e0 + router_lane, dc0, 0.0)
        + jnp.where(wide == e1 + router_lane, dc1, 0.0)
    ).astype(BF)
    return grad_rows + nn(dlog.astype(BF), router_block)


def query_places(t, sec, dims, along):
    local = lax.broadcasted_iota(jnp.int32, dims, along)
    return (512 * t + 128 * sec + local + (local & ~127)).astype(F32)


def allowed_rows(t, sec, ends_q, ends_k, causal):
    query_at = query_places(t, sec, (TILE, 1), 0)
    key_at = lax.broadcasted_iota(jnp.int32, (1, 1024), 1).astype(F32)
    allowed = segments(query_at, ends_q) == segments(key_at, ends_k)
    if causal:
        allowed = allowed & (key_at <= query_at)
    return allowed


def key_segments_t(ends_k, segk_ref):
    for j in range(8):
        at = lax.broadcasted_iota(jnp.int32, (128, TILE), 0).astype(F32) + 128.0 * j
        segk_ref[128 * j : 128 * j + 128, :] = segments(at, ends_k)


def allowed_cols(t, sec, ends_q, segk_ref, causal):
    query_at = query_places(t, sec, (1, TILE), 1)
    allowed = segk_ref[...] == segments(query_at, ends_q)
    if causal:
        key_at = lax.broadcasted_iota(jnp.int32, (1024, TILE), 0).astype(F32)
        allowed = allowed & (key_at <= query_at)
    return allowed


def fold_kv(grad_k, grad_v, sec, own_ref, send_ref):
    for j in range(4):
        k = grad_k[256 * j : 256 * j + 256, :]
        v = grad_v[256 * j : 256 * j + 256, :]
        k = k + pltpu.roll(k, 64, 1)
        v = v + pltpu.roll(v, 64, 1)
        low = lax.broadcasted_iota(jnp.int32, k.shape, 1) < 64
        both = jnp.where(low, k, v)
        first, second = both[0:128], both[128:256]
        own_ref[j] = jnp.where(sec == 0, first, second)
        send_ref[j] = jnp.where(sec == 0, second, first).astype(send_ref.dtype)


def split_halves(value, sec, keep_ref, send_ref, m, lane):
    upper, lower = value[0:256], value[256:512]
    cut = slice(lane, lane + value.shape[1])
    keep_ref[m, :, cut] = jnp.where(sec == 0, upper, lower).astype(BF)
    send_ref[m, :, cut] = jnp.where(sec == 0, lower, upper).astype(BF)


def split_flat(value, sec, keep_ref, send_ref, lane):
    upper, lower = value[0:256], value[256:512]
    cut = slice(lane, lane + value.shape[1])
    keep_ref[:, cut] = jnp.where(sec == 0, upper, lower).astype(BF)
    send_ref[:, cut] = jnp.where(sec == 0, lower, upper).astype(BF)


def turned_rows(value):
    return value.astype(F32).T.astype(BF)


def flat(ref):
    return ref[...].reshape(512, ref.shape[-1])


def attention_weight_grads(first_t, gated_ref, dz_ref, dq_ref, sec, keep_ref, send_ref, lane):
    grad_q = nn(first_t, flat(dq_ref))
    grad_o = nn(turned_rows(flat(dz_ref)), flat(gated_ref))
    for b in range(4):
        cut = slice(128 * b, 128 * b + 128)
        split_halves(grad_q[:, cut], sec, keep_ref, send_ref, b, lane)
        split_halves(grad_o[:, cut], sec, keep_ref, send_ref, b, lane + 128)


def router_grads(dlog_ref, rows_ref):
    turned = flat(dlog_ref).astype(F32).T.astype(BF)
    return nn(turned, flat(rows_ref))[0:32]


def gelu_parts(pre):
    cdf = 0.5 * (1.0 + lax.erf(pre * 0.7071067811865476))
    slope = cdf + pre * (jnp.exp(-0.5 * pre * pre) * 0.3989422804014327)
    return pre * cdf, slope


def own_self_kv(recv_ref, layer, sec, w_kv, kv_ref):
    gain = gain_of(recv_ref, layer, 0)
    for t in range(2):
        first = norm_of(rows_of(recv_ref, layer, t), gain)[0].astype(BF)
        kv = nn(first, w_kv).astype(BF)
        for i in range(2):
            j = 2 * t + i
            kv_ref[j, sec] = kv[128 * i : 128 * i + 128]
            kv_ref[j, 1 - sec] = other_kv(recv_ref, layer, j)


def cross_kv(kvm_ref, kvo_ref, sec, kv_s):
    for j in range(4):
        kv_s[j, sec] = kvm_ref[j]
        kv_s[j, 1 - sec] = kvo_ref[j]


def pack_kernel(
    ready, len_ref, x_ref, gain_ref, w_kv_ref, own_ref, cross_ref, router_ref, send_ref, extra_s
):
    ready()
    gain = gain_ref[0:1, :].astype(F32)
    w_kv = w_kv_ref[...]
    extra_s[...] = jnp.zeros_like(extra_s)
    extra_s[0:3, :] = gain_ref[...].astype(F32)
    extra_s[ROUTER_AT : ROUTER_AT + 8, :] = router_ref[...].astype(F32)
    lanes = lax.broadcasted_iota(jnp.int32, (1, 512), 1)
    for i in range(4):
        first = norm_of(x_ref[i].astype(F32), gain)[0].astype(BF)
        kv = nn(first, w_kv).astype(BF)
        row = jnp.zeros((1, 512), jnp.int32)
        for k in range(8):
            length = len_ref[i, k]
            row = jnp.where(lanes == k, length >> 5, row)
            row = jnp.where(lanes == 128 + k, length & 31, row)
        extra_s[LEN_ROW : LEN_ROW + 1, :] = row.astype(F32)
        own, cross = own_ref[i], cross_ref[i]
        own_code = (own[0:1] + 8 * own[1:2]).astype(F32)
        cross_code = (cross[0:1] + 8 * cross[1:2]).astype(F32)
        for half in range(2):
            to = 4 * half + i
            here = slice(128 * half, 128 * half + 128)
            send_ref[to, 0:128, :] = x_ref[i, here, :]
            far = kv[128 * (1 - half) : 128 * (1 - half) + 128]
            send_ref[to, 128:160, :] = jnp.concatenate(
                [far[32 * c : 32 * c + 32] for c in range(4)], 1
            )
            extra_s[CODE_ROW : CODE_ROW + 1, 0:128] = own_code[:, here]
            extra_s[CODE_ROW : CODE_ROW + 1, 128:256] = cross_code[:, here]
            send_ref[to, EX_AT : EX_AT + 16, :] = extra_s[...].astype(BF)


def self_fwd_kernel(ready, ids_ref, recv_ref, *refs):
    wa_own, wa_oth, kvw_own, kvw_oth = refs[:4], refs[4:8], refs[8], refs[9]
    h1_ref, g1_ref, mixed_e, mixed_d, log_e, log_d = refs[10:16]
    wq, wo, wkv, kv_s, k2, v2, sems = refs[16:]
    sec, m = ids_ref[0], ids_ref[1]
    loads = Loads(sems)
    kv_waits = [loads.start(sec == i, kvw_own, kvw_oth, wkv.at[i]) for i in range(2)]
    waits = []
    for layer in range(2):
        waits += loads.rows(sec == layer, wa_own, wa_oth, 0, wq.at[layer], m)
        waits += loads.rows(sec == layer, wa_own, wa_oth, 128, wo.at[layer], m)
    ready()
    wait_all(kv_waits)
    for layer in range(2):
        own_self_kv(recv_ref, layer, sec, wkv[layer], kv_s)
        widen_kv(kv_s, k2.at[layer], v2.at[layer])
    wait_all(waits)
    ends = [ends_of(extra_of(recv_ref, layer, 0).astype(F32)) for layer in range(2)]

    def tile(t, carry):
        for layer, after_ref, mixed_ref, log_ref in (
            (0, h1_ref, mixed_e, log_e),
            (1, g1_ref, mixed_d, log_d),
        ):
            rows = rows_of(recv_ref, layer, t)
            first = norm_of(rows, gain_of(recv_ref, layer, 0))[0].astype(BF)
            route = routing(first, extra_of(recv_ref, layer, 0), codes_of(recv_ref, layer, t, 0))
            allowed = allowed_rows(t, sec, ends[layer], ends[layer], layer == 1)
            out, mixed, row_log = attend_tile(
                first, route, wq[layer], wo[layer], k2[layer], v2[layer], allowed
            )
            after_ref[t] = rows + out
            mixed_ref[t] = mixed
            log_ref[t] = row_log
        return carry

    lax.fori_loop(0, 2, tile, 0)


def enc_ffn_kernel(ready, ids_ref, recv_ref, h1_ref, kvc_ref, *refs):
    f_own, f_oth = refs[:4], refs[4:8]
    h2_ref, mem_ref, kvm_ref, w_in, w_out, third_s, sems = refs[8:]
    low, m = ids_ref[0] == 0, ids_ref[1]
    loads = Loads(sems)
    waits = loads.pieces(low, f_own, f_oth, w_in, m) + loads.pieces(low, f_oth, f_own, w_out, m)
    ready()
    for t in range(2):
        h2_ref[t] = h1_ref[t]
        third_s[t] = norm_of(h1_ref[t], gain_of(recv_ref, 0, 2))[0].astype(BF)
    wait_all(waits)

    def chunk(c, carry):
        pre = nn(flat(third_s), w_in[c])
        hidden = (0.5 * pre * (1.0 + lax.erf(pre * 0.7071067811865476))).astype(BF)
        h2_ref[...] += nn(hidden, w_out[c]).reshape(2, TILE, 512)
        return carry

    lax.fori_loop(0, 4, chunk, 0)
    for t in range(2):
        memory = norm_of(h2_ref[t], gain_of(recv_ref, 0, 1))[0].astype(BF)
        mem_ref[t] = memory
        kv = nn(memory, kvc_ref[...]).astype(BF)
        kvm_ref[2 * t] = kv[0:128]
        kvm_ref[2 * t + 1] = kv[128:256]


def cross_fwd_kernel(
    ready, ids_ref, recv_ref, g1_ref, kvm_ref, kvo_ref, rc_ref, *refs
):
    wa_own, wa_oth = refs[:4], refs[4:8]
    g2_ref, mixed_ref, log_ref, wq, wo, kv_s, k2, v2, sems = refs[8:]
    sec, m = ids_ref[0], ids_ref[1]
    loads = Loads(sems)
    waits = loads.rows(sec == 0, wa_own, wa_oth, 256, wq, m)
    waits += loads.rows(sec == 0, wa_oth, wa_own, 256, wo, m)
    ready()
    cross_kv(kvm_ref, kvo_ref, sec, kv_s)
    widen_kv(kv_s, k2, v2)
    wait_all(waits)
    ends_k = ends_of(extra_of(recv_ref, 0, 0).astype(F32))
    ends_q = ends_of(extra_of(recv_ref, 1, 0).astype(F32))

    def tile(t, carry):
        before = g1_ref[t]
        second = norm_of(before, gain_of(recv_ref, 1, 1))[0].astype(BF)
        route = routing(second, rc_ref[...], codes_of(recv_ref, 1, t, 128))
        allowed = allowed_rows(t, sec, ends_q, ends_k, False)
        out, mixed, row_log = attend_tile(second, route, wq[...], wo[...], k2[...], v2[...], allowed)
        g2_ref[t] = before + out
        mixed_ref[t] = mixed
        log_ref[t] = row_log
        return carry

    lax.fori_loop(0, 2, tile, 0)


def ffn_both(c, third_s, third_t, dy_s, dy_t, w_in, w_out, dthird, sec, keep_ref, send_ref):
    pre = nn(flat(third_s), w_in[c])
    hidden, slope = gelu_parts(pre)
    hidden = hidden.astype(BF)
    dpre = (nt(flat(dy_s), w_out[c]) * slope).astype(BF)
    dthird[...] += nt(dpre, w_in[c])
    split_halves(nn(third_t[...], dpre), sec, keep_ref, send_ref, c, 0)
    split_halves(nn(dy_t[...], hidden), sec, keep_ref, send_ref, c, 512)
    return hidden


def dec_ffn_kernel(ready, ids_ref, recv_ref, g2_ref, mem_ref, cot_in, *refs):
    f_own, f_oth = refs[:4], refs[4:8]
    outs_ref, dg2_ref, gain_ref, keep_ref, send_ref = refs[8:13]
    w_in, w_out, cot_s, third_s, third_t, cot_t, acc, dthird, sems = refs[13:]
    sec, m = ids_ref[0], ids_ref[1]
    low = sec == 0
    loads = Loads(sems)
    cot_waits = [loads.plain(cot_in.at[i], cot_s.at[i]) for i in range(4)]
    waits = loads.pieces(low, f_own, f_oth, w_in, m) + loads.pieces(low, f_oth, f_own, w_out, m)
    ready()
    for t in range(2):
        acc[t] = g2_ref[t]
        third_s[t] = norm_of(g2_ref[t], gain_of(recv_ref, 1, 2))[0].astype(BF)
        outs_ref[2 * t : 2 * t + 2] = mem_ref[t].reshape(2, 128, 512)
    third_t[...] = turned_rows(flat(third_s))
    wait_all(cot_waits)
    cot_t[...] = turned_rows(flat(cot_s))
    dthird[...] = jnp.zeros_like(dthird)
    wait_all(waits)

    def chunk(c, carry):
        hidden = ffn_both(
            c, third_s, third_t, cot_s, cot_t, w_in, w_out, dthird, sec, keep_ref, send_ref
        )
        acc[...] += nn(hidden, w_out[c]).reshape(2, TILE, 512)
        return carry

    lax.fori_loop(0, 4, chunk, 0)
    total = jnp.zeros((1, 512), F32)
    gain = gain_of(recv_ref, 1, 2)
    for t in range(2):
        outs_ref[4 + 2 * t : 6 + 2 * t] = acc[t].astype(BF).reshape(2, 128, 512)
        unused_out, unit, scaled = norm_of(g2_ref[t], gain)
        back, gain_grad = norm_back(dthird[TILE * t : TILE * t + TILE, :], unit, scaled, gain)
        dg2_ref[t] = cot_s[2 * t : 2 * t + 2].reshape(TILE, 512).astype(F32) + back
        total = total + gain_grad
    gain_ref[...] = total


def cross_back_kernel(
    ready, ids_ref, recv_ref, g1_ref, dg2_ref, mixed_ref, log_ref, kvm_ref, kvo_ref, rc_ref, *refs
):
    wa_own, wa_oth = refs[:4], refs[4:8]
    dg1_ref, gain_ref, own_ref, send_ref, router_ref, keepw_ref, sendw_ref = refs[8:15]
    wq, wo, kv_s, k2, v2, segk, grad_k, grad_v, second_s, gated_s, dz_s, dq_s, dlog_s, sems = refs[15:]
    sec, m = ids_ref[0], ids_ref[1]
    loads = Loads(sems)
    waits = loads.rows(sec == 0, wa_own, wa_oth, 256, wq, m)
    waits += loads.rows(sec == 0, wa_oth, wa_own, 256, wo, m)
    ready()
    cross_kv(kvm_ref, kvo_ref, sec, kv_s)
    widen_kv(kv_s, k2, v2)
    ends_k = ends_of(extra_of(recv_ref, 0, 0).astype(F32))
    ends_q = ends_of(extra_of(recv_ref, 1, 0).astype(F32))
    key_segments_t(ends_k, segk)
    grad_k[...] = jnp.zeros_like(grad_k)
    grad_v[...] = jnp.zeros_like(grad_v)
    wait_all(waits)

    def tile(t, total):
        gain = gain_of(recv_ref, 1, 1)
        second, unit, scaled = norm_of(g1_ref[t], gain)
        second = second.astype(BF)
        second_s[t] = second
        route = routing(second, rc_ref[...], codes_of(recv_ref, 1, t, 128))
        allowed = allowed_cols(t, sec, ends_q, segk, False)
        grad_rows = attend_back_tile(
            t, dg2_ref[t], second, route, mixed_ref[t], log_ref[t], wq[...], wo[...], rc_ref[...],
            ROUTER_LANES[2], k2[...], v2[...], allowed, grad_k, grad_v, gated_s, dz_s, dq_s, dlog_s,
        )
        back, gain_grad = norm_back(grad_rows, unit, scaled, gain)
        dg1_ref[t] = dg2_ref[t] + back
        return total + gain_grad

    gain_ref[...] = lax.fori_loop(0, 2, tile, jnp.zeros((1, 512), F32))
    fold_kv(grad_k, grad_v, sec, own_ref, send_ref)
    router_ref[...] = router_grads(dlog_s, second_s)
    attention_weight_grads(
        turned_rows(flat(second_s)), gated_s, dz_s, dq_s, sec, keepw_ref, sendw_ref, 0
    )


def self_back_kernel(layer, ready, ids_ref, recv_ref, up_ref, mixed_ref, log_ref, *refs):
    wa_own, wa_oth, kvw_own, kvw_oth = refs[:4], refs[4:8], refs[8], refs[9]
    refs = refs[10:]
    if layer == 1:
        before, refs = refs[:2], refs[2:]
    dfirst_ref, own_ref, send_ref, router_ref, keepw_ref, sendw_ref = refs[:6]
    wq, wo, wkv, kv_s, k2, v2, segk, grad_k, grad_v = refs[6:15]
    first_s, gated_s, dz_s, dq_s, dlog_s, sems = refs[15:]
    sec, m = ids_ref[0], ids_ref[1]
    mine = sec == layer
    loads = Loads(sems)
    kv_wait = loads.start(mine, kvw_own, kvw_oth, wkv)
    waits = loads.rows(mine, wa_own, wa_oth, 0, wq, m) + loads.rows(mine, wa_own, wa_oth, 128, wo, m)
    lane = 0
    if layer == 1:
        lane = 256
        for src, dst in zip(before, (keepw_ref, sendw_ref)):
            waits.append(loads.plain(src, dst.at[:, :, pl.ds(0, 256)]))
    ready()
    ends = ends_of(extra_of(recv_ref, layer, 0).astype(F32))
    key_segments_t(ends, segk)
    grad_k[...] = jnp.zeros_like(grad_k)
    grad_v[...] = jnp.zeros_like(grad_v)
    kv_wait()
    own_self_kv(recv_ref, layer, sec, wkv[...], kv_s)
    widen_kv(kv_s, k2, v2)
    wait_all(waits)
    router_block = extra_of(recv_ref, layer, 0)

    def tile(t, carry):
        first = norm_of(rows_of(recv_ref, layer, t), gain_of(recv_ref, layer, 0))[0].astype(BF)
        first_s[t] = first
        route = routing(first, router_block, codes_of(recv_ref, layer, t, 0))
        allowed = allowed_cols(t, sec, ends, segk, layer == 1)
        dfirst_ref[t] = attend_back_tile(
            t, up_ref[t], first, route, mixed_ref[t], log_ref[t], wq[...], wo[...], router_block,
            ROUTER_LANES[layer], k2[...], v2[...], allowed, grad_k, grad_v, gated_s, dz_s, dq_s,
            dlog_s,
        )
        return carry

    lax.fori_loop(0, 2, tile, 0)
    fold_kv(grad_k, grad_v, sec, own_ref, send_ref)
    router_ref[...] = router_grads(dlog_s, first_s)
    attention_weight_grads(
        turned_rows(flat(first_s)), gated_s, dz_s, dq_s, sec, keepw_ref, sendw_ref, lane
    )


def enc_ffn_back_kernel(
    ready, ids_ref, recv_ref, h1_ref, h2_ref, own_ref, come_ref, kvc_ref, *refs
):
    f_own, f_oth = refs[:4], refs[4:8]
    dh1_ref, gain_ref, gain2_ref, keep_ref, send_ref = refs[8:13]
    w_in, w_out, third_s, third_t, dy_s, dy_t, dthird, sems = refs[13:]
    sec, m = ids_ref[0], ids_ref[1]
    low = sec == 0
    loads = Loads(sems)
    waits = loads.pieces(low, f_own, f_oth, w_in, m) + loads.pieces(low, f_oth, f_own, w_out, m)
    ready()
    total = jnp.zeros((1, 512), F32)
    gain = gain_of(recv_ref, 0, 1)
    for t in range(2):
        dkv = (own_ref[2 * t : 2 * t + 2] + come_ref[2 * t : 2 * t + 2].astype(F32)).astype(BF)
        dmem = rounded(nt(dkv.reshape(TILE, 128), kvc_ref[...]))
        unused_out, unit, scaled = norm_of(h2_ref[t], gain)
        back, gain_grad = norm_back(dmem, unit, scaled, gain)
        dh1_ref[t] = back
        dy_s[t] = back.astype(BF)
        third_s[t] = norm_of(h1_ref[t], gain_of(recv_ref, 0, 2))[0].astype(BF)
        total = total + gain_grad
    gain_ref[...] = total
    third_t[...] = turned_rows(flat(third_s))
    dy_t[...] = turned_rows(flat(dy_s))
    dthird[...] = jnp.zeros_like(dthird)
    wait_all(waits)

    def chunk(c, carry):
        ffn_both(c, third_s, third_t, dy_s, dy_t, w_in, w_out, dthird, sec, keep_ref, send_ref)
        return carry

    lax.fori_loop(0, 4, chunk, 0)
    total = jnp.zeros((1, 512), F32)
    gain = gain_of(recv_ref, 0, 2)
    for t in range(2):
        unused_out, unit, scaled = norm_of(h1_ref[t], gain)
        back, gain_grad = norm_back(dthird[TILE * t : TILE * t + TILE, :], unit, scaled, gain)
        dh1_ref[t] += back
        total = total + gain_grad
    gain2_ref[...] = total


def finish_rows(layer, recv_ref, up_ref, df_ref, own_ref, come_ref, wkv, first_s, out_ref, at):
    total = jnp.zeros((1, 512), F32)
    gain = gain_of(recv_ref, layer, 0)
    dkvs = []
    for t in range(2):
        first, unit, scaled = norm_of(rows_of(recv_ref, layer, t), gain)
        first_s[t] = first.astype(BF)
        dkv = (own_ref[2 * t : 2 * t + 2] + come_ref[2 * t : 2 * t + 2].astype(F32)).astype(BF)
        dkv = dkv.reshape(TILE, 128)
        dkvs.append(dkv)
        back, gain_grad = norm_back(df_ref[t] + nt(dkv, wkv), unit, scaled, gain)
        dx = (up_ref[t] + back).astype(BF)
        for i in range(2):
            out_ref[at + 2 * t + i, 0:128, :] = dx[128 * i : 128 * i + 128]
        total = total + gain_grad
    grad = nn(turned_rows(flat(first_s)), jnp.concatenate(dkvs, 0))
    return total, grad


def dec_finish_kernel(
    ready, ids_ref, recv_ref, up_ref, df_ref, own_ref, come_ref, own_c, come_c, mem_ref, kvw_own, kvw_oth,
    dx_ref, gain_ref, keep_ref, send_ref, wkv, first_s, sems,
):
    sec = ids_ref[0]
    wait = Loads(sems).start(sec == 1, kvw_own, kvw_oth, wkv)
    ready()
    dkv_c = (own_c[...] + come_c[...].astype(F32)).astype(BF).reshape(512, 128)
    split_flat(nn(turned_rows(flat(mem_ref)), dkv_c), sec, keep_ref, send_ref, 128)
    wait()
    gain_ref[...], grad = finish_rows(
        1, recv_ref, up_ref, df_ref, own_ref, come_ref, wkv[...], first_s, dx_ref, 0
    )
    split_flat(grad, sec, keep_ref, send_ref, 0)


def enc_finish_kernel(
    ready, ids_ref, recv_ref, up_ref, df_ref, own_ref, come_ref, dx1_ref, r0, r1, rc,
    gain_e1, gain_e2, gain_d0, gain_d1, gain_d2, kvw_own, kvw_oth,
    out_ref, wkv, first_s, misc, sems,
):
    sec = ids_ref[0]
    wait = Loads(sems).start(sec == 0, kvw_own, kvw_oth, wkv)
    ready()
    misc[...] = r0[...] + r1[...] + rc[...]
    out_ref[4:8, 0:128, :] = dx1_ref[...]
    wait()
    gain_e0, grad = finish_rows(
        0, recv_ref, up_ref, df_ref, own_ref, come_ref, wkv[...], first_s, out_ref, 0
    )
    rows = (gain_e0, gain_e1[...], gain_e2[...], gain_d0[...], gain_d1[...], gain_d2[...])
    for i, row in enumerate(rows):
        misc[GAIN_ROW + i : GAIN_ROW + i + 1, :] = row
    both = misc[...]
    for half in range(2):
        cut = slice(256 * half, 256 * half + 256)
        part = grad[cut].astype(BF)
        small = both[:, cut].astype(BF)
        block = jnp.concatenate(
            [
                jnp.concatenate([part[64 * c : 64 * c + 64] for c in range(4)], 1),
                jnp.concatenate([small[0:16], small[16:32]], 1),
            ],
            0,
        )
        for i in range(4):
            out_ref[4 * half + i, 128:208, :] = block


def add_kernel(keep_ref, come_ref, *outs):
    lane = 0
    for out_ref in outs:
        cut = slice(lane, lane + out_ref.shape[-1])
        left, right = keep_ref[:, :, cut].astype(F32), come_ref[:, :, cut].astype(F32)
        out_ref[...] = (left + right).astype(BF)
        lane += out_ref.shape[-1]


def add_pieces_kernel(flats, ready, ids_ref, *refs):
    ready()
    n = len(flats)
    keeps, comes, outs = refs[:n], refs[n : 2 * n], refs[2 * n :]
    m = ids_ref[1]
    for b in range(4):
        lane = 0
        for is_flat, keep, come in zip(flats, keeps, comes):
            left = keep[...] if is_flat else keep[m ^ b]
            right = come[...] if is_flat else come[m ^ b]
            width = keep.shape[-1]
            outs[b][:, lane : lane + width] = (left.astype(F32) + right.astype(F32)).astype(BF)
            lane += width


def sum_middle_kernel(ready, ids_ref, dec_a, dec_b, enc_ref, *refs):
    att, outs = refs[:4], refs[4:]
    ready()
    rows = outs[0].shape[0]
    d = ids_ref[2]
    for k in range(len(outs)):
        cut = pl.ds(pl.multiple_of((d ^ k) * rows, rows), rows)
        for ref, lane in ((enc_ref, 0), (dec_a, 1024), (dec_b, 1536)):
            total = ref[0, cut, :].astype(F32)
            for i in range(1, 4):
                total = total + ref[i, cut, :].astype(F32)
            outs[k][:, lane : lane + ref.shape[-1]] = total.astype(BF)
        total = att[0][cut, :].astype(F32)
        for part in att[1:]:
            total = total + part[cut, :].astype(F32)
        outs[k][:, 2048:2560] = total.astype(BF)


def tail_kernel(ready, dx_ref, *refs):
    att_e, (dx_out, out_ref) = refs[:4], refs[4:]
    ready()
    for i in range(4):
        for half in range(2):
            dx_out[i, half] = dx_ref[4 * half + i, 0:128, :].astype(F32)
    total = att_e[0][...].astype(F32)
    for part in att_e[1:]:
        total = total + part[...].astype(F32)
    out_ref[:, 0:512] = total.astype(BF)
    small = dx_ref[0, 128:208, :].astype(F32)
    for i in range(1, 8):
        small = small + dx_ref[i, 128:208, :].astype(F32)
    for c in range(4):
        out_ref[64 * c : 64 * c + 64, 512:640] = small[0:64, 128 * c : 128 * c + 128].astype(BF)
    misc = jnp.concatenate([small[64:80, 0:256], small[64:80, 256:512]], 0)
    misc = jnp.concatenate([misc, jnp.zeros((96, 256), F32)], 0)
    out_ref[:, 640:768] = misc.T.astype(BF)


def final_kernel(ready, come_ref, *refs):
    middle, outs = refs[:4], refs[4:]
    ready()
    gains, router, query, keyval, output, inner, outer, router_c, query_c, keyval_c, output_c = outs
    small = come_ref[0].astype(F32)
    for i in range(1, 4):
        small = small + come_ref[i].astype(F32)
    wide = middle[0][...].astype(F32)
    for part in middle[1:]:
        wide = wide + part[...].astype(F32)
    for layer in range(2):
        inner[layer] = wide[:, 1024 * layer : 1024 * layer + 512]
        outer[layer] = wide[:, 1024 * layer + 512 : 1024 * layer + 1024]
    keyval[0], keyval[1] = small[:, 512:640], small[:, 256:384]
    keyval_c[...] = small[:, 384:512]
    for source, at, put_q, put_o in (
        (wide, 2048, query_c, output_c),
        (wide, 2304, query.at[1], output.at[1]),
        (small, 0, query.at[0], output.at[0]),
    ):
        turned = source[:, at + 128 : at + 256].T
        for e in range(2):
            put_q[e] = source[:, at + 64 * e : at + 64 * e + 64]
            put_o[e] = turned[64 * e : 64 * e + 64]
    misc = small[:, 640:768].T
    router[0], router[1], router_c[...] = misc[0:8], misc[8:16], misc[16:24]
    for i in range(3):
        gains[i, 0:1] = misc[24 + i : 25 + i]
        gains[i, 1:2] = misc[27 + i : 28 + i]


def shaped(dims, kind):
    return jax.ShapeDtypeStruct(dims, kind)


def cost_of(micros):
    return pl.CostEstimate(
        flops=int(micros * 1.1535e9), bytes_accessed=int(micros * 3.0e6), transcendentals=0
    )


def run(kernel, args, places, outs, scratch, micros, after=()):
    space = {
        "s": pl.BlockSpec(memory_space=pltpu.SMEM),
        "v": pl.BlockSpec(memory_space=pltpu.VMEM),
        "a": pl.BlockSpec(memory_space=pl.ANY),
    }
    large = [
        i for i, (p, a) in enumerate(zip(places, args)) if p == "v" and a.size * a.dtype.itemsize > LARGE
    ]
    places = ["a" if i in large else p for i, p in enumerate(places)]
    count, extra = len(args), len(after)
    copies = [pltpu.VMEM(args[i].shape, args[i].dtype) for i in large]

    def body(*refs):
        given, rest = list(refs[:count]), refs[count + extra :]
        if large:
            rest, held, sems = rest[: -len(large) - 1], rest[-len(large) - 1 : -1], rest[-1]
            moves = []
            for n, i in enumerate(large):
                moves.append(pltpu.make_async_copy(given[i], held[n], sems.at[n]))
                given[i] = held[n]
            for move in moves:
                move.start()
        else:
            moves = []

        def ready():
            for move in moves:
                move.wait()

        kernel(ready, *given, *rest)

    return pl.pallas_call(
        body,
        out_shape=outs,
        in_specs=[space[p] for p in places] + [space["a"]] * extra,
        out_specs=jax.tree.map(lambda _: space["v"], outs),
        scratch_shapes=scratch + copies + ([dma(len(large))] if large else []),
        compiler_params=pltpu.CompilerParams(vmem_limit_bytes=VMEM_LIMIT),
        cost_estimate=cost_of(micros),
    )(*args, *after)


def vm(*dims, kind=BF):
    return pltpu.VMEM(dims, kind)


def dma(count):
    return pltpu.SemaphoreType.DMA((count,))


def across(value, axes, size, by):
    return lax.ppermute(value, axes, [(i, i ^ by) for i in range(size)])


def swapped(value):
    return across(value, "section", 2, 1)


def gathered(value):
    return [value] + [across(value, "mp", 4, b) for b in range(1, 4)]


def to_all(value, axes):
    return lax.all_to_all(value, axes, split_axis=0, concat_axis=0, tiled=True)


def add_shares(keep, come, micros, after, parts=1):
    blocks, rows, width = keep.shape
    whole = pl.BlockSpec((1, rows, width), lambda i: (i, 0, 0))
    part = pl.BlockSpec((1, rows, width // parts), lambda i: (i, 0, 0))
    extra = len(after)
    return pl.pallas_call(
        lambda k, c, *rest: add_kernel(k, c, *rest[extra:]),
        out_shape=[shaped((blocks, rows, width // parts), BF)] * parts,
        grid=(blocks,),
        in_specs=[whole, whole] + [pl.BlockSpec(memory_space=pl.ANY)] * extra,
        out_specs=[part] * parts,
        cost_estimate=cost_of(micros),
    )(keep, come, *after)


def add_pieces(ids, keeps, comes, micros, after=()):
    flats = tuple(keep.ndim == 2 for keep in keeps)
    width = sum(keep.shape[-1] for keep in keeps)
    return run(
        functools.partial(add_pieces_kernel, flats),
        (ids, *keeps, *comes),
        "s" + "v" * (2 * len(keeps)),
        [shaped((256, width), BF)] * 4,
        [],
        micros,
        after=after,
    )


def mp_exchange(pieces):
    return [pieces[0]] + [across(pieces[b], "mp", 4, b) for b in range(1, 4)]


def dp_exchange(pieces):
    return [pieces[0]] + [across(pieces[k], "dp", 4, k) for k in range(1, 4)]


def gated(values, after):
    anywhere = pl.BlockSpec(memory_space=pl.ANY)
    count = len(values)
    return pl.pallas_call(
        lambda *refs: None,
        out_shape=[shaped(v.shape, v.dtype) for v in values],
        in_specs=[anywhere] * (count + len(after)),
        out_specs=[anywhere] * count,
        input_output_aliases={i: i for i in range(count)},
        cost_estimate=cost_of(0.2),
    )(*values, *after)


def per_device(
    inputs,
    lengths,
    routes_self,
    routes_cross,
    gains,
    router_self,
    query_self,
    keyval_self,
    output_self,
    ffn_in,
    ffn_out,
    router_cross,
    query_cross,
    keyval_cross,
    output_cross,
    cotangent,
):
    sec, m, d = lax.axis_index("section"), lax.axis_index("mp"), lax.axis_index("dp")
    low = sec == 0
    ids = jnp.stack([sec, m, d]).astype(jnp.int32)
    sem = dma(24)
    rowgroup = ("section", "mp")

    q_rows = query_self[0].transpose(0, 2, 1).reshape(128, 512)
    o_rows = output_self[0].reshape(128, 512)
    c_rows = jnp.where(
        low, query_cross.transpose(0, 2, 1).reshape(128, 512), output_cross.reshape(128, 512)
    )
    wa = jnp.concatenate([q_rows, o_rows, c_rows], 0)
    wa_own = gathered(wa)
    w_in, w_out = ffn_in[0], ffn_out[0]
    half_come = swapped(jnp.where(low, w_out, w_in))
    enc_half = jnp.where(low, w_in, half_come)
    dec_half = jnp.where(low, half_come, w_out)
    kvw_own = keyval_self[0]
    kvw_oth = swapped(kvw_own)
    router_c = jnp.concatenate([jnp.zeros((8, 512), BF), router_cross.T], 0)

    packed = run(
        pack_kernel,
        (
            lengths[0, :, 0],
            inputs[0, :, 0],
            gains[0],
            keyval_self[0],
            routes_self[0, :, 0].transpose(0, 2, 1),
            routes_cross[:, 0].transpose(0, 2, 1),
            router_self[0].T,
        ),
        "svvvvvv",
        shaped((8, 176, 512), BF),
        [vm(16, 512, kind=F32)],
        3.4,
        after=(wa, enc_half, dec_half),
    )
    recv = to_all(packed, rowgroup)
    wa_oth = [swapped(piece) for piece in wa_own]
    (enc_half,) = gated([enc_half], [packed, wa_own[1]])
    enc_own = gathered(enc_half)
    cot_in = lax.dynamic_index_in_dim(cotangent[:, 0].reshape(4, 2, 128, 512), sec, 1, False)

    act = shaped((2, TILE, 512), F32)
    actb = shaped((2, TILE, 512), BF)
    mixed_s = shaped((2, 2 * TILE, 128), F32)
    log_s = shaped((2, 1, 2 * TILE), F32)
    kv_b = shaped((4, 128, 128), BF)
    kv_f = shaped((4, 128, 128), F32)
    row_s = shaped((1, 512), F32)
    ffn_g = shaped((4, 256, 1024), BF)
    router_s = shaped((32, 512), F32)
    wide = [vm(512, 512), vm(512, 512)]
    kv_scratch = [vm(4, 2, 128, 128), vm(1024, 128), vm(1024, 128)]
    back_scratch = [
        vm(1024, TILE, kind=F32), vm(1024, 128, kind=F32), vm(1024, 128, kind=F32),
        vm(2, TILE, 512), vm(2, TILE, 512), vm(2, TILE, 512), vm(2, TILE, 512), vm(2, TILE, 128),
    ]
    ffn_w = [vm(4, 512, 512), vm(4, 512, 512)]

    h1, g1, mixed_e, mixed_d, log_e, log_d = run(
        self_fwd_kernel,
        (ids, recv, *wa_own, *wa_oth, kvw_own, kvw_oth),
        "sv" + "a" * 10,
        (act, act, mixed_s, mixed_s, log_s, log_s),
        [vm(2, 512, 512), vm(2, 512, 512), vm(2, 512, 128), vm(4, 2, 128, 128)]
        + [vm(2, 1024, 128), vm(2, 1024, 128), sem],
        13.6,
    )
    enc_own[1:] = gated(enc_own[1:], [h1])
    enc_oth = [swapped(piece) for piece in enc_own]
    (dec_half,) = gated([dec_half], [enc_own[1]])
    dec_own = gathered(dec_half)
    (cot_in,) = gated([cot_in], [enc_own[1]])
    cot = to_all(cot_in, "mp")
    h2, memory, kvm = run(
        enc_ffn_kernel,
        (ids, recv, h1, keyval_cross, *enc_own, *enc_oth),
        "svvv" + "a" * 8,
        (act, actb, kv_b),
        ffn_w + [vm(2, TILE, 512), sem],
        4.0,
        after=(dec_half, cot_in),
    )
    kvm_oth = swapped(kvm)
    g2, mixed_c, log_c = run(
        cross_fwd_kernel,
        (ids, recv, g1, kvm, kvm_oth, router_c, *wa_own, *wa_oth),
        "svvvvv" + "a" * 8,
        (act, mixed_s, log_s),
        wide + kv_scratch + [sem],
        0.3,
        after=(cot,),
    )
    dec_own[1:] = gated(dec_own[1:], [g2])
    dec_oth = [swapped(piece) for piece in dec_own]
    outs, dg2, gain_d2, keep_d, send_d = run(
        dec_ffn_kernel,
        (ids, recv, g2, memory, cot, *dec_own, *dec_oth),
        "svvva" + "a" * 8,
        (shaped((8, 128, 512), BF), act, row_s, ffn_g, ffn_g),
        ffn_w
        + [vm(4, 128, 512), vm(2, TILE, 512), vm(512, 512), vm(512, 512)]
        + [vm(2, TILE, 512, kind=F32), vm(512, 512, kind=F32), sem],
        15.0,
    )
    come_d = swapped(send_d)
    outs_come = to_all(outs, rowgroup)
    att_g = shaped((4, 256, 256), BF)
    flat_g = shaped((256, 256), BF)
    dg1, gain_d1, own_c, sendkv_c, router_cg, keep_wc, send_wc = run(
        cross_back_kernel,
        (ids, recv, g1, dg2, mixed_c, log_c, kvm, kvm_oth, router_c, *wa_own, *wa_oth),
        "svvvvvvvv" + "a" * 8,
        (act, row_s, kv_f, kv_b, router_s, att_g, att_g),
        wide + kv_scratch + back_scratch + [sem],
        13.0,
    )
    comekv_c = swapped(sendkv_c)
    dec_a, dec_b = add_shares(keep_d, come_d, 4.0, (dg1, outs_come), 2)
    dh1, gain_e1, gain_e2, keep_e, send_e = run(
        enc_ffn_back_kernel,
        (ids, recv, h1, h2, own_c, comekv_c, keyval_cross, *enc_own, *enc_oth),
        "svvvvvv" + "a" * 8,
        (act, row_s, row_s, ffn_g, ffn_g),
        ffn_w
        + [vm(2, TILE, 512), vm(512, 512), vm(2, TILE, 512), vm(512, 512)]
        + [vm(512, 512, kind=F32), sem],
        13.4,
        after=(dec_a,),
    )
    dec_a = to_all(dec_a, "mp")
    (dec_b,) = gated([dec_b], [dec_a])
    dec_b = to_all(dec_b, "mp")
    come_e = swapped(send_e)
    self_scratch = wide + [vm(512, 128)] + kv_scratch + back_scratch + [sem]
    att_dg = shaped((4, 256, 512), BF)
    df1, own_1, sendkv_1, router_1g, keep_w1, send_w1 = run(
        functools.partial(self_back_kernel, 1),
        (
            ids, recv, dg1, mixed_d, log_d, *wa_own, *wa_oth, kvw_own, kvw_oth, keep_wc, send_wc,
        ),
        "svvvv" + "a" * 12,
        (act, kv_f, kv_b, router_s, att_dg, att_dg),
        self_scratch,
        12.2,
        after=(dh1, dec_a),
    )
    comekv_1 = swapped(sendkv_1)
    come_w1 = swapped(send_w1)
    (ffn_e,) = add_shares(keep_e, come_e, 4.0, (df1, dec_b))
    att_d = add_pieces(ids, [keep_w1], [come_w1], 3.6, (ffn_e,))
    df0, own_0, sendkv_0, router_0g, keep_w0, send_w0 = run(
        functools.partial(self_back_kernel, 0),
        (ids, recv, dh1, mixed_e, log_e, *wa_own, *wa_oth, kvw_own, kvw_oth),
        "svvvv" + "a" * 10,
        (act, kv_f, kv_b, router_s, att_g, att_g),
        self_scratch,
        11.8,
        after=(ffn_e, *att_d),
    )
    comekv_0 = swapped(sendkv_0)
    come_w0 = swapped(send_w0)
    ffn_e = to_all(ffn_e, "mp")
    att_d = mp_exchange(att_d)
    dx1, gain_d0, keep_s1, send_s1 = run(
        dec_finish_kernel,
        (ids, recv, dg1, df1, own_1, comekv_1, own_c, comekv_c, memory, kvw_own, kvw_oth),
        "svvvvvvvvaa",
        (shaped((4, 128, 512), BF), row_s, flat_g, flat_g),
        [vm(512, 128), vm(2, TILE, 512), sem],
        0.3,
        after=(df0,),
    )
    come_s1 = swapped(send_s1)
    finished = run(
        enc_finish_kernel,
        (
            ids, recv, dh1, df0, own_0, comekv_0, dx1, router_0g, router_1g, router_cg,
            gain_e1, gain_e2, gain_d0, gain_d1, gain_d2, kvw_own, kvw_oth,
        ),
        "s" + "v" * 14 + "aa",
        shaped((8, 208, 512), BF),
        [vm(512, 128), vm(2, TILE, 512), vm(32, 512, kind=F32), sem],
        0.3,
        after=att_d[1:],
    )
    att_e = add_pieces(
        ids, [keep_w0, keep_s1], [come_w0, come_s1], 3.6, (finished,)
    )
    att_e = mp_exchange(att_e)
    dp = lax.axis_size("dp")
    share = 256 // dp
    if dp == 4:
        ffn = dp_exchange(
            run(
                sum_middle_kernel,
                (ids, dec_a, dec_b, ffn_e, *att_d),
                "s" + "v" * 7,
                [shaped((64, 2560), BF)] * 4,
                [],
                4.0,
                after=(att_e[0],),
            )
        )
        after = ffn[1:]
    else:
        after = ()
    dx, small = run(
        tail_kernel,
        (to_all(finished, rowgroup), *att_e),
        "v" * 5,
        (shaped((4, 2, 128, 512), F32), shaped((256, 768), BF)),
        [],
        3.0,
        after=after,
    )
    small = to_all(small.reshape(dp, share, 768), "dp")
    outs_come = outs_come.reshape(2, 4, 128, 512).transpose(1, 0, 2, 3)
    results = (outs_come.reshape(1, 4, 1, 256, 512), dx.reshape(1, 4, 1, 256, 512))
    if dp == 4:
        made = run(
            final_kernel,
            (small, *ffn),
            "v" * 5,
            (
                shaped((3, 2, 64), F32),
                shaped((2, 8, 64), F32),
                shaped((2, 2, 64, 64), F32),
                shaped((2, 64, 128), F32),
                shaped((2, 2, 64, 64), F32),
                shaped((2, 64, 512), F32),
                shaped((2, 64, 512), F32),
                shaped((8, 64), F32),
                shaped((2, 64, 64), F32),
                shaped((64, 128), F32),
                shaped((2, 64, 64), F32),
            ),
            [],
            3.0,
        )
        made = list(made)
        made[0] = made[0].transpose(1, 0, 2)
        made[1] = made[1].transpose(0, 2, 1)
        made[6] = made[6].transpose(0, 2, 1)
        made[7] = made[7].T
        return (*results, *made)

    small = jnp.sum(small.astype(F32), 0)
    middle = jnp.concatenate(
        [jnp.sum(part.astype(F32), 0) for part in (ffn_e, dec_a, dec_b)]
        + [sum(part.astype(F32) for part in att_d)],
        1,
    )
    middle = to_all(middle.astype(BF).reshape(dp, share, 2560), "dp")
    middle = jnp.sum(middle.astype(F32), 0)

    def query_of(value, at):
        return value[:, at : at + 128].reshape(share, 2, 64).transpose(1, 0, 2)

    def output_of(value, at):
        return value[:, at + 128 : at + 256].T.reshape(2, 64, share)

    misc = small[:, 640:768].T

    def router_of(layer):
        return misc[ROUTER_LANES[layer] : ROUTER_LANES[layer] + 8].T

    return (
        *results,
        misc[GAIN_ROW : GAIN_ROW + 6].reshape(2, 3, share),
        jnp.stack([router_of(0), router_of(1)]),
        jnp.stack([query_of(small, 0), query_of(middle, 2304)]),
        jnp.stack([small[:, 512:640], small[:, 256:384]]),
        jnp.stack([output_of(small, 0), output_of(middle, 2304)]),
        jnp.stack([middle[:, :512], middle[:, 1024:1536]]),
        jnp.stack([middle[:, 512:1024].T, middle[:, 1536:2048].T]),
        router_of(2),
        query_of(middle, 2048),
        small[:, 384:512],
        output_of(middle, 2048),
    )


def solution(mesh):
    placed = (
        P("section", None, "dp", "mp", None),
        P("section", None, "dp", None),
        P("section", None, "dp", "mp", None),
        P(None, "dp", "mp", None),
        P("section", None, None),
        P("section", None, None),
        P("section", "mp", None, None),
        P("section", None, None),
        P("section", "mp", None, None),
        P("section", None, "mp"),
        P("section", "mp", None),
        P(),
        P("mp", None, None),
        P(),
        P("mp", None, None),
        P(None, "dp", "mp", None),
    )
    return jax.shard_map(
        per_device,
        mesh=mesh,
        in_specs=placed,
        out_specs=(
            P("section", None, "dp", "mp", None),
            P("section", None, "dp", "mp", None),
            P(None, None, ("section", "dp")),
            P(None, ("section", "dp"), None),
            P(None, "mp", ("section", "dp"), None),
            P(None, ("section", "dp"), None),
            P(None, "mp", None, ("section", "dp")),
            P(None, ("section", "dp"), "mp"),
            P(None, "mp", ("section", "dp")),
            P(("section", "dp"), None),
            P("mp", ("section", "dp"), None),
            P(("section", "dp"), None),
            P("mp", None, ("section", "dp")),
        ),
        check_vma=False,
    )
```

```python
import functools

import jax
import jax.numpy as jnp
from jax import lax
from jax.experimental import pallas as pl
from jax.experimental.pallas import tpu as pltpu
from jax.sharding import PartitionSpec as P

EPS = 1e-05
MASK_VALUE = -1000000000.0
BF = jnp.bfloat16
F32 = jnp.float32
TILE = 256
EX_AT = 160
CODE_ROW = 3
LEN_ROW = 4
ROUTER_AT = 8
GAIN_ROW = 24
ROUTER_LANES = (0, 8, 16)
VMEM_LIMIT = 56 * 1024 * 1024
LARGE = 1 << 40


def nn(left, right):
    return lax.dot_general(left, right, (((1,), (0,)), ((), ())), preferred_element_type=F32)


def nt(left, right):
    return lax.dot_general(left, right, (((1,), (1,)), ((), ())), preferred_element_type=F32)


def tn(left, right):
    return lax.dot_general(left, right, (((0,), (0,)), ((), ())), preferred_element_type=F32)


def norm_of(values, gain_row):
    center = values - jnp.mean(values, 1, keepdims=True)
    scaled = lax.rsqrt(jnp.mean(center * center, 1, keepdims=True) + EPS)
    unit_rows = center * scaled
    return unit_rows * gain_row, unit_rows, scaled


def norm_back(upstream, unit_rows, scaled, gain_row):
    inner = upstream * gain_row
    result = scaled * (
        inner
        - jnp.mean(inner, 1, keepdims=True)
        - unit_rows * jnp.mean(inner * unit_rows, 1, keepdims=True)
    )
    return result, jnp.sum(upstream * unit_rows, 0, keepdims=True)


def eye_of(size):
    return lax.broadcasted_iota(jnp.int32, (size, size), 0) == lax.broadcasted_iota(
        jnp.int32, (size, size), 1
    )


def row_to_col(row):
    return jnp.sum(jnp.where(eye_of(128), row, 0.0), 1, keepdims=True)


def col_to_row(col):
    parts = []
    for at in range(0, col.shape[0], 128):
        part = jnp.where(eye_of(128), col[at : at + 128], 0.0)
        parts.append(jnp.sum(part, 0, keepdims=True))
    return jnp.concatenate(parts, 1)


def ends_of(extra):
    lengths = extra[LEN_ROW : LEN_ROW + 1, 0:8] * 32.0 + extra[LEN_ROW : LEN_ROW + 1, 128:136]
    ends = [lengths[:, 0:1]]
    for k in range(1, 8):
        ends.append(ends[-1] + lengths[:, k : k + 1])
    return ends


def segments(places, ends):
    total = jnp.where(places >= ends[0], 1.0, 0.0)
    for end in ends[1:]:
        total = total + jnp.where(places >= end, 1.0, 0.0)
    return total


def extra_of(recv_ref, layer, quarter):
    return recv_ref[4 * layer + quarter, EX_AT : EX_AT + 16, :]


def gain_of(recv_ref, layer, which):
    return extra_of(recv_ref, layer, 0).astype(F32)[which : which + 1, :]


def rows_of(recv_ref, layer, t):
    return recv_ref[pl.ds(4 * layer + 2 * t, 2), 0:128, :].reshape(TILE, 512).astype(F32)


def codes_of(recv_ref, layer, t, lane):
    cols = []
    for i in range(2):
        extra = extra_of(recv_ref, layer, 2 * t + i).astype(F32)
        cols.append(row_to_col(extra[CODE_ROW : CODE_ROW + 1, lane : lane + 128]))
    return jnp.concatenate(cols, 0)


def other_kv(recv_ref, layer, quarter):
    packed = recv_ref[4 * layer + quarter, 128:160, :]
    return jnp.concatenate([packed[:, 128 * c : 128 * c + 128] for c in range(4)], 0)


def routing(query_rows, router_block, code):
    second = jnp.floor(code * 0.125)
    first = code - 8.0 * second
    e0, e1 = first.astype(jnp.int32), second.astype(jnp.int32)
    logits = nt(query_rows, router_block)
    lanes = lax.broadcasted_iota(jnp.int32, logits.shape, 1)
    l0 = jnp.sum(jnp.where(lanes == e0 + ROUTER_AT, logits, 0.0), 1, keepdims=True)
    l1 = jnp.sum(jnp.where(lanes == e1 + ROUTER_AT, logits, 0.0), 1, keepdims=True)
    top = jnp.maximum(l0, l1)
    x0, x1 = jnp.exp(l0 - top), jnp.exp(l1 - top)
    total = x0 + x1
    owners = lax.broadcasted_iota(jnp.int32, (code.shape[0], 512), 1) >> 6
    return e0, e1, x0 / total, x1 / total, owners == e0, owners == e1


def fold(wide, mask):
    kept = jnp.where(mask, wide, 0.0)
    return kept[:, 0:128] + kept[:, 128:256] + kept[:, 256:384] + kept[:, 384:512]


def spread(a0, a1, m0, m1):
    parts = []
    for c in range(4):
        cut = slice(128 * c, 128 * c + 128)
        parts.append(jnp.where(m0[:, cut], a0, jnp.where(m1[:, cut], a1, 0.0)))
    return jnp.concatenate(parts, 1).astype(BF)


def rounded(value):
    return value.astype(BF).astype(F32)


def start_pick(cond, yes, no, dst, sem):
    @pl.when(cond)
    def _():
        pltpu.make_async_copy(yes, dst, sem).start()

    @pl.when(jnp.logical_not(cond))
    def _():
        pltpu.make_async_copy(no, dst, sem).start()


class Loads:
    def __init__(self, sems):
        self.sems, self.used = sems, 0

    def start(self, cond, yes, no, dst):
        sem = self.sems.at[self.used]
        self.used += 1
        start_pick(cond, yes, no, dst, sem)
        return functools.partial(lambda a, b, c: pltpu.make_async_copy(a, b, c).wait(), yes, dst, sem)

    def plain(self, src, dst):
        sem = self.sems.at[self.used]
        self.used += 1
        copy = pltpu.make_async_copy(src, dst, sem)
        copy.start()
        return copy.wait

    def rows(self, cond, yes, no, at, dst, m):
        cut = pl.ds(at, 128)
        return [
            self.start(cond, yes[b].at[cut], no[b].at[cut], dst.at[pl.ds(128 * (m ^ b), 128)])
            for b in range(4)
        ]

    def pieces(self, cond, yes, no, dst, m):
        return [self.start(cond, yes[b], no[b], dst.at[m ^ b]) for b in range(4)]


def wait_all(waits):
    for wait in waits:
        wait()


def widen_kv(kv_ref, k2_ref, v2_ref):
    for j in range(4):
        kv = kv_ref[j].reshape(256, 128).astype(F32)
        turned = pltpu.roll(kv, 64, 1)
        low = lax.broadcasted_iota(jnp.int32, kv.shape, 1) < 64
        k2_ref[256 * j : 256 * j + 256, :] = jnp.where(low, kv, turned).astype(BF)
        v2_ref[256 * j : 256 * j + 256, :] = jnp.where(low, turned, kv).astype(BF)


def attend_tile(query_rows, route, w_qt, w_o, k2, v2, allowed):
    e0, e1, g0, g1, m0, m1 = route
    q_all = nt(query_rows, w_qt) * 0.125
    queries = jnp.concatenate([fold(q_all, m0), fold(q_all, m1)], 0).astype(BF)
    scores = nt(queries, k2)
    scores = jnp.concatenate(
        [
            jnp.where(allowed, scores[0:TILE], MASK_VALUE),
            jnp.where(allowed, scores[TILE:], MASK_VALUE),
        ],
        0,
    )
    top = jnp.max(scores, 1, keepdims=True)
    weights = jnp.exp(scores - top)
    total = jnp.sum(weights, 1, keepdims=True)
    mixed = nn(weights.astype(BF), v2) / total
    log_total = top + jnp.log(total)
    gated = spread(rounded(g0) * mixed[0:TILE], rounded(g1) * mixed[TILE:], m0, m1)
    return nn(gated, w_o), mixed, col_to_row(log_total)


def attend_back_tile(
    t, upstream, query_rows, route, mixed, log_row, w_qt, w_o, router_block, router_lane, k2, v2,
    allowed_t, grad_k, grad_v, gated_ref, dz_ref, dq_ref, dlog_ref,
):
    e0, e1, g0, g1, m0, m1 = route
    q_all = nt(query_rows, w_qt) * 0.125
    queries = jnp.concatenate([fold(q_all, m0), fold(q_all, m1)], 0).astype(BF)
    dz = upstream.astype(BF)
    dg_all = nt(dz, w_o)
    dgated0, dgated1 = fold(dg_all, m0), fold(dg_all, m1)
    r0, r1 = rounded(g0), rounded(g1)
    mixed0, mixed1 = mixed[0:TILE], mixed[TILE:]
    gated_ref[t] = spread(r0 * mixed0, r1 * mixed1, m0, m1)
    dz_ref[t] = dz
    dgate0 = rounded(jnp.sum(mixed0 * dgated0, 1, keepdims=True))
    dgate1 = rounded(jnp.sum(mixed1 * dgated1, 1, keepdims=True))
    do0, do1 = (r0 * dgated0).astype(BF), (r1 * dgated1).astype(BF)
    grad_mixed = jnp.concatenate([do0, do1], 0)
    inner_row = jnp.concatenate(
        [
            col_to_row(jnp.sum(do0.astype(F32) * mixed0, 1, keepdims=True)),
            col_to_row(jnp.sum(do1.astype(F32) * mixed1, 1, keepdims=True)),
        ],
        1,
    )
    scores = nt(k2, queries)
    scores = jnp.concatenate(
        [
            jnp.where(allowed_t, scores[:, 0:TILE], MASK_VALUE),
            jnp.where(allowed_t, scores[:, TILE:], MASK_VALUE),
        ],
        1,
    )
    probs = jnp.exp(scores - log_row)
    grad_probs = nt(v2, grad_mixed)
    grad_scores = (probs * (grad_probs - inner_row)).astype(BF)
    grad_v[...] += nn(probs.astype(BF), grad_mixed)
    grad_k[...] += nn(grad_scores, queries)
    grad_q = rounded(tn(grad_scores, k2) * 0.125)
    dq_all = spread(grad_q[0:TILE], grad_q[TILE:], m0, m1)
    dq_ref[t] = dq_all
    grad_rows = nn(dq_all, w_qt)
    mean_grad = g0 * dgate0 + g1 * dgate1
    dc0, dc1 = g0 * (dgate0 - mean_grad), g1 * (dgate1 - mean_grad)
    lanes = lax.broadcasted_iota(jnp.int32, (TILE, 16), 1)
    dlog = jnp.where(lanes == e0 + ROUTER_AT, dc0, 0.0) + jnp.where(
        lanes == e1 + ROUTER_AT, dc1, 0.0
    )
    wide = lax.broadcasted_iota(jnp.int32, (TILE, 128), 1)
    dlog_ref[t] = (
        jnp.where(wide == e0 + router_lane, dc0, 0.0)
        + jnp.where(wide == e1 + router_lane, dc1, 0.0)
    ).astype(BF)
    return grad_rows + nn(dlog.astype(BF), router_block)


def query_places(t, sec, dims, along):
    local = lax.broadcasted_iota(jnp.int32, dims, along)
    return (512 * t + 128 * sec + local + (local & ~127)).astype(F32)


def allowed_rows(t, sec, ends_q, ends_k, causal):
    query_at = query_places(t, sec, (TILE, 1), 0)
    key_at = lax.broadcasted_iota(jnp.int32, (1, 1024), 1).astype(F32)
    allowed = segments(query_at, ends_q) == segments(key_at, ends_k)
    if causal:
        allowed = allowed & (key_at <= query_at)
    return allowed


def key_segments_t(ends_k, segk_ref):
    for j in range(8):
        at = lax.broadcasted_iota(jnp.int32, (128, TILE), 0).astype(F32) + 128.0 * j
        segk_ref[128 * j : 128 * j + 128, :] = segments(at, ends_k)


def allowed_cols(t, sec, ends_q, segk_ref, causal):
    query_at = query_places(t, sec, (1, TILE), 1)
    allowed = segk_ref[...] == segments(query_at, ends_q)
    if causal:
        key_at = lax.broadcasted_iota(jnp.int32, (1024, TILE), 0).astype(F32)
        allowed = allowed & (key_at <= query_at)
    return allowed


def fold_kv(grad_k, grad_v, sec, own_ref, send_ref):
    for j in range(4):
        k = grad_k[256 * j : 256 * j + 256, :]
        v = grad_v[256 * j : 256 * j + 256, :]
        k = k + pltpu.roll(k, 64, 1)
        v = v + pltpu.roll(v, 64, 1)
        low = lax.broadcasted_iota(jnp.int32, k.shape, 1) < 64
        both = jnp.where(low, k, v)
        first, second = both[0:128], both[128:256]
        own_ref[j] = jnp.where(sec == 0, first, second)
        send_ref[j] = jnp.where(sec == 0, second, first).astype(send_ref.dtype)


def split_halves(value, sec, keep_ref, send_ref, m, lane):
    upper, lower = value[0:256], value[256:512]
    cut = slice(lane, lane + value.shape[1])
    keep_ref[m, :, cut] = jnp.where(sec == 0, upper, lower).astype(BF)
    send_ref[m, :, cut] = jnp.where(sec == 0, lower, upper).astype(BF)


def split_flat(value, sec, keep_ref, send_ref, lane):
    upper, lower = value[0:256], value[256:512]
    cut = slice(lane, lane + value.shape[1])
    keep_ref[:, cut] = jnp.where(sec == 0, upper, lower).astype(BF)
    send_ref[:, cut] = jnp.where(sec == 0, lower, upper).astype(BF)


def turned_rows(value):
    return value.astype(F32).T.astype(BF)


def flat(ref):
    return ref[...].reshape(512, ref.shape[-1])


def attention_weight_grads(first_t, gated_ref, dz_ref, dq_ref, sec, keep_ref, send_ref, lane):
    grad_q = nn(first_t, flat(dq_ref))
    grad_o = nn(turned_rows(flat(dz_ref)), flat(gated_ref))
    for b in range(4):
        cut = slice(128 * b, 128 * b + 128)
        split_halves(grad_q[:, cut], sec, keep_ref, send_ref, b, lane)
        split_halves(grad_o[:, cut], sec, keep_ref, send_ref, b, lane + 128)


def router_grads(dlog_ref, rows_ref):
    turned = flat(dlog_ref).astype(F32).T.astype(BF)
    return nn(turned, flat(rows_ref))[0:32]


def gelu_parts(pre):
    cdf = 0.5 * (1.0 + lax.erf(pre * 0.7071067811865476))
    slope = cdf + pre * (jnp.exp(-0.5 * pre * pre) * 0.3989422804014327)
    return pre * cdf, slope


def own_self_kv(recv_ref, layer, sec, w_kv, kv_ref):
    gain = gain_of(recv_ref, layer, 0)
    for t in range(2):
        first = norm_of(rows_of(recv_ref, layer, t), gain)[0].astype(BF)
        kv = nn(first, w_kv).astype(BF)
        for i in range(2):
            j = 2 * t + i
            kv_ref[j, sec] = kv[128 * i : 128 * i + 128]
            kv_ref[j, 1 - sec] = other_kv(recv_ref, layer, j)


def cross_kv(kvm_ref, kvo_ref, sec, kv_s):
    for j in range(4):
        kv_s[j, sec] = kvm_ref[j]
        kv_s[j, 1 - sec] = kvo_ref[j]


def pack_kernel(
    ready, len_ref, x_ref, gain_ref, w_kv_ref, own_ref, cross_ref, router_ref, send_ref, extra_s
):
    ready()
    gain = gain_ref[0:1, :].astype(F32)
    w_kv = w_kv_ref[...]
    extra_s[...] = jnp.zeros_like(extra_s)
    extra_s[0:3, :] = gain_ref[...].astype(F32)
    extra_s[ROUTER_AT : ROUTER_AT + 8, :] = router_ref[...].astype(F32)
    lanes = lax.broadcasted_iota(jnp.int32, (1, 512), 1)
    for i in range(4):
        first = norm_of(x_ref[i].astype(F32), gain)[0].astype(BF)
        kv = nn(first, w_kv).astype(BF)
        row = jnp.zeros((1, 512), jnp.int32)
        for k in range(8):
            length = len_ref[i, k]
            row = jnp.where(lanes == k, length >> 5, row)
            row = jnp.where(lanes == 128 + k, length & 31, row)
        extra_s[LEN_ROW : LEN_ROW + 1, :] = row.astype(F32)
        own, cross = own_ref[i], cross_ref[i]
        own_code = (own[0:1] + 8 * own[1:2]).astype(F32)
        cross_code = (cross[0:1] + 8 * cross[1:2]).astype(F32)
        for half in range(2):
            to = 4 * half + i
            here = slice(128 * half, 128 * half + 128)
            send_ref[to, 0:128, :] = x_ref[i, here, :]
            far = kv[128 * (1 - half) : 128 * (1 - half) + 128]
            send_ref[to, 128:160, :] = jnp.concatenate(
                [far[32 * c : 32 * c + 32] for c in range(4)], 1
            )
            extra_s[CODE_ROW : CODE_ROW + 1, 0:128] = own_code[:, here]
            extra_s[CODE_ROW : CODE_ROW + 1, 128:256] = cross_code[:, here]
            send_ref[to, EX_AT : EX_AT + 16, :] = extra_s[...].astype(BF)


def self_fwd_kernel(ready, ids_ref, recv_ref, *refs):
    wa_own, wa_oth, kvw_own, kvw_oth = refs[:4], refs[4:8], refs[8], refs[9]
    h1_ref, g1_ref, mixed_e, mixed_d, log_e, log_d = refs[10:16]
    wq, wo, wkv, kv_s, k2, v2, sems = refs[16:]
    sec, m = ids_ref[0], ids_ref[1]
    loads = Loads(sems)
    kv_waits = [loads.start(sec == i, kvw_own, kvw_oth, wkv.at[i]) for i in range(2)]
    waits = []
    for layer in range(2):
        waits += loads.rows(sec == layer, wa_own, wa_oth, 0, wq.at[layer], m)
        waits += loads.rows(sec == layer, wa_own, wa_oth, 128, wo.at[layer], m)
    ready()
    wait_all(kv_waits)
    for layer in range(2):
        own_self_kv(recv_ref, layer, sec, wkv[layer], kv_s)
        widen_kv(kv_s, k2.at[layer], v2.at[layer])
    wait_all(waits)
    ends = [ends_of(extra_of(recv_ref, layer, 0).astype(F32)) for layer in range(2)]

    def tile(t, carry):
        for layer, after_ref, mixed_ref, log_ref in (
            (0, h1_ref, mixed_e, log_e),
            (1, g1_ref, mixed_d, log_d),
        ):
            rows = rows_of(recv_ref, layer, t)
            first = norm_of(rows, gain_of(recv_ref, layer, 0))[0].astype(BF)
            route = routing(first, extra_of(recv_ref, layer, 0), codes_of(recv_ref, layer, t, 0))
            allowed = allowed_rows(t, sec, ends[layer], ends[layer], layer == 1)
            out, mixed, row_log = attend_tile(
                first, route, wq[layer], wo[layer], k2[layer], v2[layer], allowed
            )
            after_ref[t] = rows + out
            mixed_ref[t] = mixed
            log_ref[t] = row_log
        return carry

    lax.fori_loop(0, 2, tile, 0)


def enc_ffn_kernel(ready, ids_ref, recv_ref, h1_ref, kvc_ref, *refs):
    f_own, f_oth = refs[:4], refs[4:8]
    h2_ref, mem_ref, kvm_ref, w_in, w_out, third_s, sems = refs[8:]
    low, m = ids_ref[0] == 0, ids_ref[1]
    loads = Loads(sems)
    waits = loads.pieces(low, f_own, f_oth, w_in, m) + loads.pieces(low, f_oth, f_own, w_out, m)
    ready()
    for t in range(2):
        h2_ref[t] = h1_ref[t]
        third_s[t] = norm_of(h1_ref[t], gain_of(recv_ref, 0, 2))[0].astype(BF)
    wait_all(waits)

    def chunk(c, carry):
        pre = nn(flat(third_s), w_in[c])
        hidden = (0.5 * pre * (1.0 + lax.erf(pre * 0.7071067811865476))).astype(BF)
        h2_ref[...] += nn(hidden, w_out[c]).reshape(2, TILE, 512)
        return carry

    lax.fori_loop(0, 4, chunk, 0)
    for t in range(2):
        memory = norm_of(h2_ref[t], gain_of(recv_ref, 0, 1))[0].astype(BF)
        mem_ref[t] = memory
        kv = nn(memory, kvc_ref[...]).astype(BF)
        kvm_ref[2 * t] = kv[0:128]
        kvm_ref[2 * t + 1] = kv[128:256]


def cross_fwd_kernel(
    ready, ids_ref, recv_ref, g1_ref, kvm_ref, kvo_ref, rc_ref, *refs
):
    wa_own, wa_oth = refs[:4], refs[4:8]
    g2_ref, mixed_ref, log_ref, wq, wo, kv_s, k2, v2, sems = refs[8:]
    sec, m = ids_ref[0], ids_ref[1]
    loads = Loads(sems)
    waits = loads.rows(sec == 0, wa_own, wa_oth, 256, wq, m)
    waits += loads.rows(sec == 0, wa_oth, wa_own, 256, wo, m)
    ready()
    cross_kv(kvm_ref, kvo_ref, sec, kv_s)
    widen_kv(kv_s, k2, v2)
    wait_all(waits)
    ends_k = ends_of(extra_of(recv_ref, 0, 0).astype(F32))
    ends_q = ends_of(extra_of(recv_ref, 1, 0).astype(F32))

    def tile(t, carry):
        before = g1_ref[t]
        second = norm_of(before, gain_of(recv_ref, 1, 1))[0].astype(BF)
        route = routing(second, rc_ref[...], codes_of(recv_ref, 1, t, 128))
        allowed = allowed_rows(t, sec, ends_q, ends_k, False)
        out, mixed, row_log = attend_tile(second, route, wq[...], wo[...], k2[...], v2[...], allowed)
        g2_ref[t] = before + out
        mixed_ref[t] = mixed
        log_ref[t] = row_log
        return carry

    lax.fori_loop(0, 2, tile, 0)


def ffn_both(c, third_s, third_t, dy_s, dy_t, w_in, w_out, dthird, sec, keep_ref, send_ref):
    pre = nn(flat(third_s), w_in[c])
    hidden, slope = gelu_parts(pre)
    hidden = hidden.astype(BF)
    dpre = (nt(flat(dy_s), w_out[c]) * slope).astype(BF)
    dthird[...] += nt(dpre, w_in[c])
    split_halves(nn(third_t[...], dpre), sec, keep_ref, send_ref, c, 0)
    split_halves(nn(dy_t[...], hidden), sec, keep_ref, send_ref, c, 512)
    return hidden


def dec_ffn_kernel(ready, ids_ref, recv_ref, g2_ref, mem_ref, cot_in, *refs):
    f_own, f_oth = refs[:4], refs[4:8]
    outs_ref, dg2_ref, gain_ref, keep_ref, send_ref = refs[8:13]
    w_in, w_out, cot_s, third_s, third_t, cot_t, acc, dthird, sems = refs[13:]
    sec, m = ids_ref[0], ids_ref[1]
    low = sec == 0
    loads = Loads(sems)
    cot_waits = [loads.plain(cot_in.at[i], cot_s.at[i]) for i in range(4)]
    waits = loads.pieces(low, f_own, f_oth, w_in, m) + loads.pieces(low, f_oth, f_own, w_out, m)
    ready()
    for t in range(2):
        acc[t] = g2_ref[t]
        third_s[t] = norm_of(g2_ref[t], gain_of(recv_ref, 1, 2))[0].astype(BF)
        outs_ref[2 * t : 2 * t + 2] = mem_ref[t].reshape(2, 128, 512)
    third_t[...] = turned_rows(flat(third_s))
    wait_all(cot_waits)
    cot_t[...] = turned_rows(flat(cot_s))
    dthird[...] = jnp.zeros_like(dthird)
    wait_all(waits)

    def chunk(c, carry):
        hidden = ffn_both(
            c, third_s, third_t, cot_s, cot_t, w_in, w_out, dthird, sec, keep_ref, send_ref
        )
        acc[...] += nn(hidden, w_out[c]).reshape(2, TILE, 512)
        return carry

    lax.fori_loop(0, 4, chunk, 0)
    total = jnp.zeros((1, 512), F32)
    gain = gain_of(recv_ref, 1, 2)
    for t in range(2):
        outs_ref[4 + 2 * t : 6 + 2 * t] = acc[t].astype(BF).reshape(2, 128, 512)
        unused_out, unit, scaled = norm_of(g2_ref[t], gain)
        back, gain_grad = norm_back(dthird[TILE * t : TILE * t + TILE, :], unit, scaled, gain)
        dg2_ref[t] = cot_s[2 * t : 2 * t + 2].reshape(TILE, 512).astype(F32) + back
        total = total + gain_grad
    gain_ref[...] = total


def cross_back_kernel(
    ready, ids_ref, recv_ref, g1_ref, dg2_ref, mixed_ref, log_ref, kvm_ref, kvo_ref, rc_ref, *refs
):
    wa_own, wa_oth = refs[:4], refs[4:8]
    dg1_ref, gain_ref, own_ref, send_ref, router_ref, keepw_ref, sendw_ref = refs[8:15]
    wq, wo, kv_s, k2, v2, segk, grad_k, grad_v, second_s, gated_s, dz_s, dq_s, dlog_s, sems = refs[15:]
    sec, m = ids_ref[0], ids_ref[1]
    loads = Loads(sems)
    waits = loads.rows(sec == 0, wa_own, wa_oth, 256, wq, m)
    waits += loads.rows(sec == 0, wa_oth, wa_own, 256, wo, m)
    ready()
    cross_kv(kvm_ref, kvo_ref, sec, kv_s)
    widen_kv(kv_s, k2, v2)
    ends_k = ends_of(extra_of(recv_ref, 0, 0).astype(F32))
    ends_q = ends_of(extra_of(recv_ref, 1, 0).astype(F32))
    key_segments_t(ends_k, segk)
    grad_k[...] = jnp.zeros_like(grad_k)
    grad_v[...] = jnp.zeros_like(grad_v)
    wait_all(waits)

    def tile(t, total):
        gain = gain_of(recv_ref, 1, 1)
        second, unit, scaled = norm_of(g1_ref[t], gain)
        second = second.astype(BF)
        second_s[t] = second
        route = routing(second, rc_ref[...], codes_of(recv_ref, 1, t, 128))
        allowed = allowed_cols(t, sec, ends_q, segk, False)
        grad_rows = attend_back_tile(
            t, dg2_ref[t], second, route, mixed_ref[t], log_ref[t], wq[...], wo[...], rc_ref[...],
            ROUTER_LANES[2], k2[...], v2[...], allowed, grad_k, grad_v, gated_s, dz_s, dq_s, dlog_s,
        )
        back, gain_grad = norm_back(grad_rows, unit, scaled, gain)
        dg1_ref[t] = dg2_ref[t] + back
        return total + gain_grad

    gain_ref[...] = lax.fori_loop(0, 2, tile, jnp.zeros((1, 512), F32))
    fold_kv(grad_k, grad_v, sec, own_ref, send_ref)
    router_ref[...] = router_grads(dlog_s, second_s)
    attention_weight_grads(
        turned_rows(flat(second_s)), gated_s, dz_s, dq_s, sec, keepw_ref, sendw_ref, 0
    )


def self_back_kernel(layer, ready, ids_ref, recv_ref, up_ref, mixed_ref, log_ref, *refs):
    wa_own, wa_oth, kvw_own, kvw_oth = refs[:4], refs[4:8], refs[8], refs[9]
    refs = refs[10:]
    if layer == 1:
        before, refs = refs[:2], refs[2:]
    dfirst_ref, own_ref, send_ref, router_ref, keepw_ref, sendw_ref = refs[:6]
    wq, wo, wkv, kv_s, k2, v2, segk, grad_k, grad_v = refs[6:15]
    first_s, gated_s, dz_s, dq_s, dlog_s, sems = refs[15:]
    sec, m = ids_ref[0], ids_ref[1]
    mine = sec == layer
    loads = Loads(sems)
    kv_wait = loads.start(mine, kvw_own, kvw_oth, wkv)
    waits = loads.rows(mine, wa_own, wa_oth, 0, wq, m) + loads.rows(mine, wa_own, wa_oth, 128, wo, m)
    lane = 0
    if layer == 1:
        lane = 256
        for src, dst in zip(before, (keepw_ref, sendw_ref)):
            waits.append(loads.plain(src, dst.at[:, :, pl.ds(0, 256)]))
    ready()
    ends = ends_of(extra_of(recv_ref, layer, 0).astype(F32))
    key_segments_t(ends, segk)
    grad_k[...] = jnp.zeros_like(grad_k)
    grad_v[...] = jnp.zeros_like(grad_v)
    kv_wait()
    own_self_kv(recv_ref, layer, sec, wkv[...], kv_s)
    widen_kv(kv_s, k2, v2)
    wait_all(waits)
    router_block = extra_of(recv_ref, layer, 0)

    def tile(t, carry):
        first = norm_of(rows_of(recv_ref, layer, t), gain_of(recv_ref, layer, 0))[0].astype(BF)
        first_s[t] = first
        route = routing(first, router_block, codes_of(recv_ref, layer, t, 0))
        allowed = allowed_cols(t, sec, ends, segk, layer == 1)
        dfirst_ref[t] = attend_back_tile(
            t, up_ref[t], first, route, mixed_ref[t], log_ref[t], wq[...], wo[...], router_block,
            ROUTER_LANES[layer], k2[...], v2[...], allowed, grad_k, grad_v, gated_s, dz_s, dq_s,
            dlog_s,
        )
        return carry

    lax.fori_loop(0, 2, tile, 0)
    fold_kv(grad_k, grad_v, sec, own_ref, send_ref)
    router_ref[...] = router_grads(dlog_s, first_s)
    attention_weight_grads(
        turned_rows(flat(first_s)), gated_s, dz_s, dq_s, sec, keepw_ref, sendw_ref, lane
    )


def enc_ffn_back_kernel(
    ready, ids_ref, recv_ref, h1_ref, h2_ref, own_ref, come_ref, kvc_ref, *refs
):
    f_own, f_oth = refs[:4], refs[4:8]
    dh1_ref, gain_ref, gain2_ref, keep_ref, send_ref = refs[8:13]
    w_in, w_out, third_s, third_t, dy_s, dy_t, dthird, sems = refs[13:]
    sec, m = ids_ref[0], ids_ref[1]
    low = sec == 0
    loads = Loads(sems)
    waits = loads.pieces(low, f_own, f_oth, w_in, m) + loads.pieces(low, f_oth, f_own, w_out, m)
    ready()
    total = jnp.zeros((1, 512), F32)
    gain = gain_of(recv_ref, 0, 1)
    for t in range(2):
        dkv = (own_ref[2 * t : 2 * t + 2] + come_ref[2 * t : 2 * t + 2].astype(F32)).astype(BF)
        dmem = rounded(nt(dkv.reshape(TILE, 128), kvc_ref[...]))
        unused_out, unit, scaled = norm_of(h2_ref[t], gain)
        back, gain_grad = norm_back(dmem, unit, scaled, gain)
        dh1_ref[t] = back
        dy_s[t] = back.astype(BF)
        third_s[t] = norm_of(h1_ref[t], gain_of(recv_ref, 0, 2))[0].astype(BF)
        total = total + gain_grad
    gain_ref[...] = total
    third_t[...] = turned_rows(flat(third_s))
    dy_t[...] = turned_rows(flat(dy_s))
    dthird[...] = jnp.zeros_like(dthird)
    wait_all(waits)

    def chunk(c, carry):
        ffn_both(c, third_s, third_t, dy_s, dy_t, w_in, w_out, dthird, sec, keep_ref, send_ref)
        return carry

    lax.fori_loop(0, 4, chunk, 0)
    total = jnp.zeros((1, 512), F32)
    gain = gain_of(recv_ref, 0, 2)
    for t in range(2):
        unused_out, unit, scaled = norm_of(h1_ref[t], gain)
        back, gain_grad = norm_back(dthird[TILE * t : TILE * t + TILE, :], unit, scaled, gain)
        dh1_ref[t] += back
        total = total + gain_grad
    gain2_ref[...] = total


def finish_rows(layer, recv_ref, up_ref, df_ref, own_ref, come_ref, wkv, first_s, out_ref, at):
    total = jnp.zeros((1, 512), F32)
    gain = gain_of(recv_ref, layer, 0)
    dkvs = []
    for t in range(2):
        first, unit, scaled = norm_of(rows_of(recv_ref, layer, t), gain)
        first_s[t] = first.astype(BF)
        dkv = (own_ref[2 * t : 2 * t + 2] + come_ref[2 * t : 2 * t + 2].astype(F32)).astype(BF)
        dkv = dkv.reshape(TILE, 128)
        dkvs.append(dkv)
        back, gain_grad = norm_back(df_ref[t] + nt(dkv, wkv), unit, scaled, gain)
        dx = (up_ref[t] + back).astype(BF)
        for i in range(2):
            out_ref[at + 2 * t + i, 0:128, :] = dx[128 * i : 128 * i + 128]
        total = total + gain_grad
    grad = nn(turned_rows(flat(first_s)), jnp.concatenate(dkvs, 0))
    return total, grad


def dec_finish_kernel(
    ready, ids_ref, recv_ref, up_ref, df_ref, own_ref, come_ref, own_c, come_c, mem_ref, kvw_own, kvw_oth,
    dx_ref, gain_ref, keep_ref, send_ref, wkv, first_s, sems,
):
    sec = ids_ref[0]
    wait = Loads(sems).start(sec == 1, kvw_own, kvw_oth, wkv)
    ready()
    dkv_c = (own_c[...] + come_c[...].astype(F32)).astype(BF).reshape(512, 128)
    split_flat(nn(turned_rows(flat(mem_ref)), dkv_c), sec, keep_ref, send_ref, 128)
    wait()
    gain_ref[...], grad = finish_rows(
        1, recv_ref, up_ref, df_ref, own_ref, come_ref, wkv[...], first_s, dx_ref, 0
    )
    split_flat(grad, sec, keep_ref, send_ref, 0)


def enc_finish_kernel(
    ready, ids_ref, recv_ref, up_ref, df_ref, own_ref, come_ref, dx1_ref, r0, r1, rc,
    gain_e1, gain_e2, gain_d0, gain_d1, gain_d2, kvw_own, kvw_oth,
    out_ref, wkv, first_s, misc, sems,
):
    sec = ids_ref[0]
    wait = Loads(sems).start(sec == 0, kvw_own, kvw_oth, wkv)
    ready()
    misc[...] = r0[...] + r1[...] + rc[...]
    out_ref[4:8, 0:128, :] = dx1_ref[...]
    wait()
    gain_e0, grad = finish_rows(
        0, recv_ref, up_ref, df_ref, own_ref, come_ref, wkv[...], first_s, out_ref, 0
    )
    rows = (gain_e0, gain_e1[...], gain_e2[...], gain_d0[...], gain_d1[...], gain_d2[...])
    for i, row in enumerate(rows):
        misc[GAIN_ROW + i : GAIN_ROW + i + 1, :] = row
    both = misc[...]
    for half in range(2):
        cut = slice(256 * half, 256 * half + 256)
        part = grad[cut].astype(BF)
        small = both[:, cut].astype(BF)
        block = jnp.concatenate(
            [
                jnp.concatenate([part[64 * c : 64 * c + 64] for c in range(4)], 1),
                jnp.concatenate([small[0:16], small[16:32]], 1),
            ],
            0,
        )
        for i in range(4):
            out_ref[4 * half + i, 128:208, :] = block


def add_kernel(keep_ref, come_ref, *outs):
    lane = 0
    for out_ref in outs:
        cut = slice(lane, lane + out_ref.shape[-1])
        out_ref[...] = keep_ref[:, :, cut] + come_ref[:, :, cut]
        lane += out_ref.shape[-1]


def add_pieces_kernel(flats, ready, ids_ref, *refs):
    ready()
    n = len(flats)
    keeps, comes, outs = refs[:n], refs[n : 2 * n], refs[2 * n :]
    m = ids_ref[1]
    for b in range(4):
        lane = 0
        for is_flat, keep, come in zip(flats, keeps, comes):
            left = keep[...] if is_flat else keep[m ^ b]
            right = come[...] if is_flat else come[m ^ b]
            width = keep.shape[-1]
            outs[b][:, lane : lane + width] = left + right
            lane += width


def sum_middle_kernel(ready, ids_ref, dec_a, dec_b, enc_ref, *refs):
    att, outs = refs[:4], refs[4:]
    ready()
    rows = outs[0].shape[0]
    d = ids_ref[2]
    for k in range(len(outs)):
        cut = pl.ds(pl.multiple_of((d ^ k) * rows, rows), rows)
        for ref, lane in ((enc_ref, 0), (dec_a, 1024), (dec_b, 1536)):
            total = ref[0, cut, :].astype(F32)
            for i in range(1, 4):
                total = total + ref[i, cut, :].astype(F32)
            outs[k][:, lane : lane + ref.shape[-1]] = total.astype(BF)
        total = att[0][cut, :].astype(F32)
        for part in att[1:]:
            total = total + part[cut, :].astype(F32)
        outs[k][:, 2048:2560] = total.astype(BF)


def tail_kernel(ready, dx_ref, *refs):
    att_e, (dx_out, out_ref) = refs[:4], refs[4:]
    ready()
    for i in range(4):
        for half in range(2):
            dx_out[i, half] = dx_ref[4 * half + i, 0:128, :].astype(F32)
    total = att_e[0][...].astype(F32)
    for part in att_e[1:]:
        total = total + part[...].astype(F32)
    out_ref[:, 0:512] = total.astype(BF)
    small = dx_ref[0, 128:208, :].astype(F32)
    for i in range(1, 8):
        small = small + dx_ref[i, 128:208, :].astype(F32)
    for c in range(4):
        out_ref[64 * c : 64 * c + 64, 512:640] = small[0:64, 128 * c : 128 * c + 128].astype(BF)
    misc = jnp.concatenate([small[64:80, 0:256], small[64:80, 256:512]], 0)
    misc = jnp.concatenate([misc, jnp.zeros((96, 256), F32)], 0)
    out_ref[:, 640:768] = misc.T.astype(BF)


def final_kernel(ready, come_ref, *refs):
    middle, outs = refs[:4], refs[4:]
    ready()
    gains, router, query, keyval, output, inner, outer, router_c, query_c, keyval_c, output_c = outs
    small = come_ref[0].astype(F32)
    for i in range(1, 4):
        small = small + come_ref[i].astype(F32)
    wide = middle[0][...].astype(F32)
    for part in middle[1:]:
        wide = wide + part[...].astype(F32)
    for layer in range(2):
        inner[layer] = wide[:, 1024 * layer : 1024 * layer + 512]
        outer[layer] = wide[:, 1024 * layer + 512 : 1024 * layer + 1024]
    keyval[0], keyval[1] = small[:, 512:640], small[:, 256:384]
    keyval_c[...] = small[:, 384:512]
    for source, at, put_q, put_o in (
        (wide, 2048, query_c, output_c),
        (wide, 2304, query.at[1], output.at[1]),
        (small, 0, query.at[0], output.at[0]),
    ):
        turned = source[:, at + 128 : at + 256].T
        for e in range(2):
            put_q[e] = source[:, at + 64 * e : at + 64 * e + 64]
            put_o[e] = turned[64 * e : 64 * e + 64]
    misc = small[:, 640:768].T
    router[0], router[1], router_c[...] = misc[0:8], misc[8:16], misc[16:24]
    for i in range(3):
        gains[i, 0:1] = misc[24 + i : 25 + i]
        gains[i, 1:2] = misc[27 + i : 28 + i]


def shaped(dims, kind):
    return jax.ShapeDtypeStruct(dims, kind)


def cost_of(micros):
    return pl.CostEstimate(
        flops=int(micros * 1.1535e9), bytes_accessed=int(micros * 3.0e6), transcendentals=0
    )


def run(kernel, args, places, outs, scratch, micros, after=()):
    space = {
        "s": pl.BlockSpec(memory_space=pltpu.SMEM),
        "v": pl.BlockSpec(memory_space=pltpu.VMEM),
        "a": pl.BlockSpec(memory_space=pl.ANY),
    }
    large = [
        i for i, (p, a) in enumerate(zip(places, args)) if p == "v" and a.size * a.dtype.itemsize > LARGE
    ]
    places = ["a" if i in large else p for i, p in enumerate(places)]
    count, extra = len(args), len(after)
    copies = [pltpu.VMEM(args[i].shape, args[i].dtype) for i in large]

    def body(*refs):
        given, rest = list(refs[:count]), refs[count + extra :]
        if large:
            rest, held, sems = rest[: -len(large) - 1], rest[-len(large) - 1 : -1], rest[-1]
            moves = []
            for n, i in enumerate(large):
                moves.append(pltpu.make_async_copy(given[i], held[n], sems.at[n]))
                given[i] = held[n]
            for move in moves:
                move.start()
        else:
            moves = []

        def ready():
            for move in moves:
                move.wait()

        kernel(ready, *given, *rest)

    return pl.pallas_call(
        body,
        out_shape=outs,
        in_specs=[space[p] for p in places] + [space["a"]] * extra,
        out_specs=jax.tree.map(lambda _: space["v"], outs),
        scratch_shapes=scratch + copies + ([dma(len(large))] if large else []),
        compiler_params=pltpu.CompilerParams(vmem_limit_bytes=VMEM_LIMIT),
        cost_estimate=cost_of(micros),
    )(*args, *after)


def vm(*dims, kind=BF):
    return pltpu.VMEM(dims, kind)


def dma(count):
    return pltpu.SemaphoreType.DMA((count,))


def across(value, axes, size, by):
    return lax.ppermute(value, axes, [(i, i ^ by) for i in range(size)])


def swapped(value):
    return across(value, "section", 2, 1)


def gathered(value):
    return [value] + [across(value, "mp", 4, b) for b in range(1, 4)]


def to_all(value, axes):
    return lax.all_to_all(value, axes, split_axis=0, concat_axis=0, tiled=True)


def add_shares(keep, come, micros, after, parts=1):
    blocks, rows, width = keep.shape
    whole = pl.BlockSpec((1, rows, width), lambda i: (i, 0, 0))
    part = pl.BlockSpec((1, rows, width // parts), lambda i: (i, 0, 0))
    extra = len(after)
    return pl.pallas_call(
        lambda k, c, *rest: add_kernel(k, c, *rest[extra:]),
        out_shape=[shaped((blocks, rows, width // parts), BF)] * parts,
        grid=(blocks,),
        in_specs=[whole, whole] + [pl.BlockSpec(memory_space=pl.ANY)] * extra,
        out_specs=[part] * parts,
        cost_estimate=cost_of(micros),
    )(keep, come, *after)


def add_pieces(ids, keeps, comes, micros, after=()):
    flats = tuple(keep.ndim == 2 for keep in keeps)
    width = sum(keep.shape[-1] for keep in keeps)
    return run(
        functools.partial(add_pieces_kernel, flats),
        (ids, *keeps, *comes),
        "s" + "v" * (2 * len(keeps)),
        [shaped((256, width), BF)] * 4,
        [],
        micros,
        after=after,
    )


def mp_exchange(pieces):
    return [pieces[0]] + [across(pieces[b], "mp", 4, b) for b in range(1, 4)]


def dp_exchange(pieces):
    return [pieces[0]] + [across(pieces[k], "dp", 4, k) for k in range(1, 4)]


def gated(values, after):
    anywhere = pl.BlockSpec(memory_space=pl.ANY)
    count = len(values)
    return pl.pallas_call(
        lambda *refs: None,
        out_shape=[shaped(v.shape, v.dtype) for v in values],
        in_specs=[anywhere] * (count + len(after)),
        out_specs=[anywhere] * count,
        input_output_aliases={i: i for i in range(count)},
        cost_estimate=cost_of(0.2),
    )(*values, *after)


def per_device(
    inputs,
    lengths,
    routes_self,
    routes_cross,
    gains,
    router_self,
    query_self,
    keyval_self,
    output_self,
    ffn_in,
    ffn_out,
    router_cross,
    query_cross,
    keyval_cross,
    output_cross,
    cotangent,
):
    sec, m, d = lax.axis_index("section"), lax.axis_index("mp"), lax.axis_index("dp")
    low = sec == 0
    ids = jnp.stack([sec, m, d]).astype(jnp.int32)
    sem = dma(24)
    rowgroup = ("section", "mp")

    q_rows = query_self[0].transpose(0, 2, 1).reshape(128, 512)
    o_rows = output_self[0].reshape(128, 512)
    c_rows = jnp.where(
        low, query_cross.transpose(0, 2, 1).reshape(128, 512), output_cross.reshape(128, 512)
    )
    wa = jnp.concatenate([q_rows, o_rows, c_rows], 0)
    wa_own = gathered(wa)
    w_in, w_out = ffn_in[0], ffn_out[0]
    half_come = swapped(jnp.where(low, w_out, w_in))
    enc_half = jnp.where(low, w_in, half_come)
    dec_half = jnp.where(low, half_come, w_out)
    kvw_own = keyval_self[0]
    kvw_oth = swapped(kvw_own)
    router_c = jnp.concatenate([jnp.zeros((8, 512), BF), router_cross.T], 0)

    packed = run(
        pack_kernel,
        (
            lengths[0, :, 0],
            inputs[0, :, 0],
            gains[0],
            keyval_self[0],
            routes_self[0, :, 0].transpose(0, 2, 1),
            routes_cross[:, 0].transpose(0, 2, 1),
            router_self[0].T,
        ),
        "svvvvvv",
        shaped((8, 176, 512), BF),
        [vm(16, 512, kind=F32)],
        3.4,
        after=(wa, enc_half, dec_half),
    )
    (packed,) = gated([packed], wa_own[1:])
    recv = to_all(packed, rowgroup)
    wa_oth = [swapped(piece) for piece in wa_own]
    (enc_half,) = gated([enc_half], [packed])
    enc_own = gathered(enc_half)
    cot_in = lax.dynamic_index_in_dim(cotangent[:, 0].reshape(4, 2, 128, 512), sec, 1, False)

    act = shaped((2, TILE, 512), F32)
    actb = shaped((2, TILE, 512), BF)
    mixed_s = shaped((2, 2 * TILE, 128), F32)
    log_s = shaped((2, 1, 2 * TILE), F32)
    kv_b = shaped((4, 128, 128), BF)
    kv_f = shaped((4, 128, 128), F32)
    row_s = shaped((1, 512), F32)
    ffn_g = shaped((4, 256, 1024), BF)
    router_s = shaped((32, 512), F32)
    wide = [vm(512, 512), vm(512, 512)]
    kv_scratch = [vm(4, 2, 128, 128), vm(1024, 128), vm(1024, 128)]
    back_scratch = [
        vm(1024, TILE, kind=F32), vm(1024, 128, kind=F32), vm(1024, 128, kind=F32),
        vm(2, TILE, 512), vm(2, TILE, 512), vm(2, TILE, 512), vm(2, TILE, 512), vm(2, TILE, 128),
    ]
    ffn_w = [vm(4, 512, 512), vm(4, 512, 512)]

    h1, g1, mixed_e, mixed_d, log_e, log_d = run(
        self_fwd_kernel,
        (ids, recv, *wa_own, *wa_oth, kvw_own, kvw_oth),
        "sv" + "a" * 10,
        (act, act, mixed_s, mixed_s, log_s, log_s),
        [vm(2, 512, 512), vm(2, 512, 512), vm(2, 512, 128), vm(4, 2, 128, 128)]
        + [vm(2, 1024, 128), vm(2, 1024, 128), sem],
        0.3,
    )
    enc_own[1:] = gated(enc_own[1:], [h1])
    enc_oth = [swapped(piece) for piece in enc_own]
    (dec_half,) = gated([dec_half], [enc_own[1]])
    dec_own = gathered(dec_half)
    (cot_in,) = gated([cot_in], [enc_own[1]])
    cot = to_all(cot_in, "mp")
    h2, memory, kvm = run(
        enc_ffn_kernel,
        (ids, recv, h1, keyval_cross, *enc_own, *enc_oth),
        "svvv" + "a" * 8,
        (act, actb, kv_b),
        ffn_w + [vm(2, TILE, 512), sem],
        4.0,
        after=(dec_half, cot_in),
    )
    kvm_oth = swapped(kvm)
    g2, mixed_c, log_c = run(
        cross_fwd_kernel,
        (ids, recv, g1, kvm, kvm_oth, router_c, *wa_own, *wa_oth),
        "svvvvv" + "a" * 8,
        (act, mixed_s, log_s),
        wide + kv_scratch + [sem],
        0.3,
        after=(cot,),
    )
    dec_own[1:] = gated(dec_own[1:], [g2])
    dec_oth = [swapped(piece) for piece in dec_own]
    outs, dg2, gain_d2, keep_d, send_d = run(
        dec_ffn_kernel,
        (ids, recv, g2, memory, cot, *dec_own, *dec_oth),
        "svvva" + "a" * 8,
        (shaped((8, 128, 512), BF), act, row_s, ffn_g, ffn_g),
        ffn_w
        + [vm(4, 128, 512), vm(2, TILE, 512), vm(512, 512), vm(512, 512)]
        + [vm(2, TILE, 512, kind=F32), vm(512, 512, kind=F32), sem],
        15.0,
    )
    come_d = swapped(send_d)
    outs_come = to_all(outs, rowgroup)
    att_g = shaped((4, 256, 256), BF)
    flat_g = shaped((256, 256), BF)
    dg1, gain_d1, own_c, sendkv_c, router_cg, keep_wc, send_wc = run(
        cross_back_kernel,
        (ids, recv, g1, dg2, mixed_c, log_c, kvm, kvm_oth, router_c, *wa_own, *wa_oth),
        "svvvvvvvv" + "a" * 8,
        (act, row_s, kv_f, kv_b, router_s, att_g, att_g),
        wide + kv_scratch + back_scratch + [sem],
        13.0,
    )
    comekv_c = swapped(sendkv_c)
    dec_a, dec_b = add_shares(keep_d, come_d, 4.0, (dg1, outs_come), 2)
    dh1, gain_e1, gain_e2, keep_e, send_e = run(
        enc_ffn_back_kernel,
        (ids, recv, h1, h2, own_c, comekv_c, keyval_cross, *enc_own, *enc_oth),
        "svvvvvv" + "a" * 8,
        (act, row_s, row_s, ffn_g, ffn_g),
        ffn_w
        + [vm(2, TILE, 512), vm(512, 512), vm(2, TILE, 512), vm(512, 512)]
        + [vm(512, 512, kind=F32), sem],
        13.4,
        after=(dec_a,),
    )
    dec_a = to_all(dec_a, "mp")
    (dec_b,) = gated([dec_b], [dec_a])
    dec_b = to_all(dec_b, "mp")
    come_e = swapped(send_e)
    self_scratch = wide + [vm(512, 128)] + kv_scratch + back_scratch + [sem]
    att_dg = shaped((4, 256, 512), BF)
    df1, own_1, sendkv_1, router_1g, keep_w1, send_w1 = run(
        functools.partial(self_back_kernel, 1),
        (
            ids, recv, dg1, mixed_d, log_d, *wa_own, *wa_oth, kvw_own, kvw_oth, keep_wc, send_wc,
        ),
        "svvvv" + "a" * 12,
        (act, kv_f, kv_b, router_s, att_dg, att_dg),
        self_scratch,
        12.2,
        after=(dh1, dec_a),
    )
    comekv_1 = swapped(sendkv_1)
    come_w1 = swapped(send_w1)
    (ffn_e,) = add_shares(keep_e, come_e, 4.0, (df1, dec_b))
    att_d = add_pieces(ids, [keep_w1], [come_w1], 3.6, (ffn_e,))
    df0, own_0, sendkv_0, router_0g, keep_w0, send_w0 = run(
        functools.partial(self_back_kernel, 0),
        (ids, recv, dh1, mixed_e, log_e, *wa_own, *wa_oth, kvw_own, kvw_oth),
        "svvvv" + "a" * 10,
        (act, kv_f, kv_b, router_s, att_g, att_g),
        self_scratch,
        11.8,
        after=(ffn_e, *att_d),
    )
    comekv_0 = swapped(sendkv_0)
    come_w0 = swapped(send_w0)
    ffn_e = to_all(ffn_e, "mp")
    att_d = mp_exchange(att_d)
    dx1, gain_d0, keep_s1, send_s1 = run(
        dec_finish_kernel,
        (ids, recv, dg1, df1, own_1, comekv_1, own_c, comekv_c, memory, kvw_own, kvw_oth),
        "svvvvvvvvaa",
        (shaped((4, 128, 512), BF), row_s, flat_g, flat_g),
        [vm(512, 128), vm(2, TILE, 512), sem],
        0.3,
        after=(df0,),
    )
    come_s1 = swapped(send_s1)
    finished = run(
        enc_finish_kernel,
        (
            ids, recv, dh1, df0, own_0, comekv_0, dx1, router_0g, router_1g, router_cg,
            gain_e1, gain_e2, gain_d0, gain_d1, gain_d2, kvw_own, kvw_oth,
        ),
        "s" + "v" * 14 + "aa",
        shaped((8, 208, 512), BF),
        [vm(512, 128), vm(2, TILE, 512), vm(32, 512, kind=F32), sem],
        0.3,
        after=att_d[1:],
    )
    att_e = add_pieces(
        ids, [keep_w0, keep_s1], [come_w0, come_s1], 3.6, (finished,)
    )
    att_e = mp_exchange(att_e)
    dp = lax.axis_size("dp")
    share = 256 // dp
    if dp == 4:
        ffn = dp_exchange(
            run(
                sum_middle_kernel,
                (ids, dec_a, dec_b, ffn_e, *att_d),
                "s" + "v" * 7,
                [shaped((64, 2560), BF)] * 4,
                [],
                4.0,
                after=(att_e[0],),
            )
        )
        after = ffn[1:]
    else:
        after = ()
    dx, small = run(
        tail_kernel,
        (to_all(finished, rowgroup), *att_e),
        "v" * 5,
        (shaped((4, 2, 128, 512), F32), shaped((256, 768), BF)),
        [],
        3.0,
        after=after,
    )
    small = to_all(small.reshape(dp, share, 768), "dp")
    outs_come = outs_come.reshape(2, 4, 128, 512).transpose(1, 0, 2, 3)
    results = (outs_come.reshape(1, 4, 1, 256, 512), dx.reshape(1, 4, 1, 256, 512))
    if dp == 4:
        made = run(
            final_kernel,
            (small, *ffn),
            "v" * 5,
            (
                shaped((3, 2, 64), F32),
                shaped((2, 8, 64), F32),
                shaped((2, 2, 64, 64), F32),
                shaped((2, 64, 128), F32),
                shaped((2, 2, 64, 64), F32),
                shaped((2, 64, 512), F32),
                shaped((2, 64, 512), F32),
                shaped((8, 64), F32),
                shaped((2, 64, 64), F32),
                shaped((64, 128), F32),
                shaped((2, 64, 64), F32),
            ),
            [],
            3.0,
        )
        made = list(made)
        made[0] = made[0].transpose(1, 0, 2)
        made[1] = made[1].transpose(0, 2, 1)
        made[6] = made[6].transpose(0, 2, 1)
        made[7] = made[7].T
        return (*results, *made)

    small = jnp.sum(small.astype(F32), 0)
    middle = jnp.concatenate(
        [jnp.sum(part.astype(F32), 0) for part in (ffn_e, dec_a, dec_b)]
        + [sum(part.astype(F32) for part in att_d)],
        1,
    )
    middle = to_all(middle.astype(BF).reshape(dp, share, 2560), "dp")
    middle = jnp.sum(middle.astype(F32), 0)

    def query_of(value, at):
        return value[:, at : at + 128].reshape(share, 2, 64).transpose(1, 0, 2)

    def output_of(value, at):
        return value[:, at + 128 : at + 256].T.reshape(2, 64, share)

    misc = small[:, 640:768].T

    def router_of(layer):
        return misc[ROUTER_LANES[layer] : ROUTER_LANES[layer] + 8].T

    return (
        *results,
        misc[GAIN_ROW : GAIN_ROW + 6].reshape(2, 3, share),
        jnp.stack([router_of(0), router_of(1)]),
        jnp.stack([query_of(small, 0), query_of(middle, 2304)]),
        jnp.stack([small[:, 512:640], small[:, 256:384]]),
        jnp.stack([output_of(small, 0), output_of(middle, 2304)]),
        jnp.stack([middle[:, :512], middle[:, 1024:1536]]),
        jnp.stack([middle[:, 512:1024].T, middle[:, 1536:2048].T]),
        router_of(2),
        query_of(middle, 2048),
        small[:, 384:512],
        output_of(middle, 2048),
    )


def solution(mesh):
    placed = (
        P("section", None, "dp", "mp", None),
        P("section", None, "dp", None),
        P("section", None, "dp", "mp", None),
        P(None, "dp", "mp", None),
        P("section", None, None),
        P("section", None, None),
        P("section", "mp", None, None),
        P("section", None, None),
        P("section", "mp", None, None),
        P("section", None, "mp"),
        P("section", "mp", None),
        P(),
        P("mp", None, None),
        P(),
        P("mp", None, None),
        P(None, "dp", "mp", None),
    )
    return jax.shard_map(
        per_device,
        mesh=mesh,
        in_specs=placed,
        out_specs=(
            P("section", None, "dp", "mp", None),
            P("section", None, "dp", "mp", None),
            P(None, None, ("section", "dp")),
            P(None, ("section", "dp"), None),
            P(None, "mp", ("section", "dp"), None),
            P(None, ("section", "dp"), None),
            P(None, "mp", None, ("section", "dp")),
            P(None, ("section", "dp"), "mp"),
            P(None, "mp", ("section", "dp")),
            P(("section", "dp"), None),
            P("mp", ("section", "dp"), None),
            P(("section", "dp"), None),
            P("mp", None, ("section", "dp")),
        ),
        check_vma=False,
    )
```

```python
import functools

import jax
import jax.numpy as jnp
from jax import lax
from jax.experimental import pallas as pl
from jax.experimental.pallas import tpu as pltpu
from jax.sharding import PartitionSpec as P

EPS = 1e-05
MASK_VALUE = -1000000000.0
BF = jnp.bfloat16
F32 = jnp.float32
TILE = 256
EX_AT = 160
CODE_ROW = 3
LEN_ROW = 4
ROUTER_AT = 8
GAIN_ROW = 24
ROUTER_LANES = (0, 8, 16)
VMEM_LIMIT = 32 * 1024 * 1024
LARGE = 1 << 40


def nn(left, right):
    return lax.dot_general(left, right, (((1,), (0,)), ((), ())), preferred_element_type=F32)


def nt(left, right):
    return lax.dot_general(left, right, (((1,), (1,)), ((), ())), preferred_element_type=F32)


def tn(left, right):
    return lax.dot_general(left, right, (((0,), (0,)), ((), ())), preferred_element_type=F32)


def norm_of(values, gain_row):
    center = values - jnp.mean(values, 1, keepdims=True)
    scaled = lax.rsqrt(jnp.mean(center * center, 1, keepdims=True) + EPS)
    unit_rows = center * scaled
    return unit_rows * gain_row, unit_rows, scaled


def norm_back(upstream, unit_rows, scaled, gain_row):
    inner = upstream * gain_row
    result = scaled * (
        inner
        - jnp.mean(inner, 1, keepdims=True)
        - unit_rows * jnp.mean(inner * unit_rows, 1, keepdims=True)
    )
    return result, jnp.sum(upstream * unit_rows, 0, keepdims=True)


def eye_of(size):
    return lax.broadcasted_iota(jnp.int32, (size, size), 0) == lax.broadcasted_iota(
        jnp.int32, (size, size), 1
    )


def row_to_col(row):
    return jnp.sum(jnp.where(eye_of(128), row, 0.0), 1, keepdims=True)


def col_to_row(col):
    parts = []
    for at in range(0, col.shape[0], 128):
        part = jnp.where(eye_of(128), col[at : at + 128], 0.0)
        parts.append(jnp.sum(part, 0, keepdims=True))
    return jnp.concatenate(parts, 1)


def ends_of(extra):
    lengths = extra[LEN_ROW : LEN_ROW + 1, 0:8] * 32.0 + extra[LEN_ROW : LEN_ROW + 1, 128:136]
    ends = [lengths[:, 0:1]]
    for k in range(1, 8):
        ends.append(ends[-1] + lengths[:, k : k + 1])
    return ends


def segments(places, ends):
    total = jnp.where(places >= ends[0], 1.0, 0.0)
    for end in ends[1:]:
        total = total + jnp.where(places >= end, 1.0, 0.0)
    return total


def extra_of(recv_ref, layer, quarter):
    return recv_ref[4 * layer + quarter, EX_AT : EX_AT + 16, :]


def gain_of(recv_ref, layer, which):
    return extra_of(recv_ref, layer, 0).astype(F32)[which : which + 1, :]


def rows_of(recv_ref, layer, t):
    return recv_ref[pl.ds(4 * layer + 2 * t, 2), 0:128, :].reshape(TILE, 512).astype(F32)


def codes_of(recv_ref, layer, t, lane):
    cols = []
    for i in range(2):
        extra = extra_of(recv_ref, layer, 2 * t + i).astype(F32)
        cols.append(row_to_col(extra[CODE_ROW : CODE_ROW + 1, lane : lane + 128]))
    return jnp.concatenate(cols, 0)


def other_kv(recv_ref, layer, quarter):
    packed = recv_ref[4 * layer + quarter, 128:160, :]
    return jnp.concatenate([packed[:, 128 * c : 128 * c + 128] for c in range(4)], 0)


def routing(query_rows, router_block, code):
    second = jnp.floor(code * 0.125)
    first = code - 8.0 * second
    e0, e1 = first.astype(jnp.int32), second.astype(jnp.int32)
    logits = nt(query_rows, router_block)
    lanes = lax.broadcasted_iota(jnp.int32, logits.shape, 1)
    l0 = jnp.sum(jnp.where(lanes == e0 + ROUTER_AT, logits, 0.0), 1, keepdims=True)
    l1 = jnp.sum(jnp.where(lanes == e1 + ROUTER_AT, logits, 0.0), 1, keepdims=True)
    top = jnp.maximum(l0, l1)
    x0, x1 = jnp.exp(l0 - top), jnp.exp(l1 - top)
    total = x0 + x1
    owners = lax.broadcasted_iota(jnp.int32, (code.shape[0], 512), 1) >> 6
    return e0, e1, x0 / total, x1 / total, owners == e0, owners == e1


def fold(wide, mask):
    kept = jnp.where(mask, wide, 0.0)
    return kept[:, 0:128] + kept[:, 128:256] + kept[:, 256:384] + kept[:, 384:512]


def spread(a0, a1, m0, m1):
    parts = []
    for c in range(4):
        cut = slice(128 * c, 128 * c + 128)
        parts.append(jnp.where(m0[:, cut], a0, jnp.where(m1[:, cut], a1, 0.0)))
    return jnp.concatenate(parts, 1).astype(BF)


def rounded(value):
    return value.astype(BF).astype(F32)


def start_pick(cond, yes, no, dst, sem):
    @pl.when(cond)
    def _():
        pltpu.make_async_copy(yes, dst, sem).start()

    @pl.when(jnp.logical_not(cond))
    def _():
        pltpu.make_async_copy(no, dst, sem).start()


class Loads:
    def __init__(self, sems):
        self.sems, self.used = sems, 0

    def start(self, cond, yes, no, dst):
        sem = self.sems.at[self.used]
        self.used += 1
        start_pick(cond, yes, no, dst, sem)
        return functools.partial(lambda a, b, c: pltpu.make_async_copy(a, b, c).wait(), yes, dst, sem)

    def plain(self, src, dst):
        sem = self.sems.at[self.used]
        self.used += 1
        copy = pltpu.make_async_copy(src, dst, sem)
        copy.start()
        return copy.wait

    def rows(self, cond, yes, no, at, dst, m):
        cut = pl.ds(at, 128)
        return [
            self.start(cond, yes[b].at[cut], no[b].at[cut], dst.at[pl.ds(128 * (m ^ b), 128)])
            for b in range(4)
        ]

    def pieces(self, cond, yes, no, dst, m):
        return [self.start(cond, yes[b], no[b], dst.at[m ^ b]) for b in range(4)]


def wait_all(waits):
    for wait in waits:
        wait()


def widen_kv(kv_ref, k2_ref, v2_ref):
    for j in range(4):
        kv = kv_ref[j].reshape(256, 128).astype(F32)
        turned = pltpu.roll(kv, 64, 1)
        low = lax.broadcasted_iota(jnp.int32, kv.shape, 1) < 64
        k2_ref[256 * j : 256 * j + 256, :] = jnp.where(low, kv, turned).astype(BF)
        v2_ref[256 * j : 256 * j + 256, :] = jnp.where(low, turned, kv).astype(BF)


def attend_tile(query_rows, route, w_qt, w_o, k2, v2, allowed):
    e0, e1, g0, g1, m0, m1 = route
    q_all = nt(query_rows, w_qt) * 0.125
    queries = jnp.concatenate([fold(q_all, m0), fold(q_all, m1)], 0).astype(BF)
    scores = nt(queries, k2)
    scores = jnp.concatenate(
        [
            jnp.where(allowed, scores[0:TILE], MASK_VALUE),
            jnp.where(allowed, scores[TILE:], MASK_VALUE),
        ],
        0,
    )
    top = jnp.max(scores, 1, keepdims=True)
    weights = jnp.exp(scores - top)
    total = jnp.sum(weights, 1, keepdims=True)
    mixed = nn(weights.astype(BF), v2) / total
    log_total = top + jnp.log(total)
    gated = spread(rounded(g0) * mixed[0:TILE], rounded(g1) * mixed[TILE:], m0, m1)
    return nn(gated, w_o), mixed, col_to_row(log_total)


def attend_back_tile(
    t, upstream, query_rows, route, mixed, log_row, w_qt, w_o, router_block, router_lane, k2, v2,
    allowed_t, grad_k, grad_v, gated_ref, dz_ref, dq_ref, dlog_ref,
):
    e0, e1, g0, g1, m0, m1 = route
    q_all = nt(query_rows, w_qt) * 0.125
    queries = jnp.concatenate([fold(q_all, m0), fold(q_all, m1)], 0).astype(BF)
    dz = upstream.astype(BF)
    dg_all = nt(dz, w_o)
    dgated0, dgated1 = fold(dg_all, m0), fold(dg_all, m1)
    r0, r1 = rounded(g0), rounded(g1)
    mixed0, mixed1 = mixed[0:TILE], mixed[TILE:]
    gated_ref[t] = spread(r0 * mixed0, r1 * mixed1, m0, m1)
    dz_ref[t] = dz
    dgate0 = rounded(jnp.sum(mixed0 * dgated0, 1, keepdims=True))
    dgate1 = rounded(jnp.sum(mixed1 * dgated1, 1, keepdims=True))
    do0, do1 = (r0 * dgated0).astype(BF), (r1 * dgated1).astype(BF)
    grad_mixed = jnp.concatenate([do0, do1], 0)
    inner_row = jnp.concatenate(
        [
            col_to_row(jnp.sum(do0.astype(F32) * mixed0, 1, keepdims=True)),
            col_to_row(jnp.sum(do1.astype(F32) * mixed1, 1, keepdims=True)),
        ],
        1,
    )
    scores = nt(k2, queries)
    scores = jnp.concatenate(
        [
            jnp.where(allowed_t, scores[:, 0:TILE], MASK_VALUE),
            jnp.where(allowed_t, scores[:, TILE:], MASK_VALUE),
        ],
        1,
    )
    probs = jnp.exp(scores - log_row)
    grad_probs = nt(v2, grad_mixed)
    grad_scores = (probs * (grad_probs - inner_row)).astype(BF)
    grad_v[...] += nn(probs.astype(BF), grad_mixed)
    grad_k[...] += nn(grad_scores, queries)
    grad_q = rounded(tn(grad_scores, k2) * 0.125)
    dq_all = spread(grad_q[0:TILE], grad_q[TILE:], m0, m1)
    dq_ref[t] = dq_all
    grad_rows = nn(dq_all, w_qt)
    mean_grad = g0 * dgate0 + g1 * dgate1
    dc0, dc1 = g0 * (dgate0 - mean_grad), g1 * (dgate1 - mean_grad)
    lanes = lax.broadcasted_iota(jnp.int32, (TILE, 16), 1)
    dlog = jnp.where(lanes == e0 + ROUTER_AT, dc0, 0.0) + jnp.where(
        lanes == e1 + ROUTER_AT, dc1, 0.0
    )
    wide = lax.broadcasted_iota(jnp.int32, (TILE, 128), 1)
    dlog_ref[t] = (
        jnp.where(wide == e0 + router_lane, dc0, 0.0)
        + jnp.where(wide == e1 + router_lane, dc1, 0.0)
    ).astype(BF)
    return grad_rows + nn(dlog.astype(BF), router_block)


def query_places(t, sec, dims, along):
    local = lax.broadcasted_iota(jnp.int32, dims, along)
    return (512 * t + 128 * sec + local + (local & ~127)).astype(F32)


def allowed_rows(t, sec, ends_q, ends_k, causal):
    query_at = query_places(t, sec, (TILE, 1), 0)
    key_at = lax.broadcasted_iota(jnp.int32, (1, 1024), 1).astype(F32)
    allowed = segments(query_at, ends_q) == segments(key_at, ends_k)
    if causal:
        allowed = allowed & (key_at <= query_at)
    return allowed


def key_segments_t(ends_k, segk_ref):
    for j in range(8):
        at = lax.broadcasted_iota(jnp.int32, (128, TILE), 0).astype(F32) + 128.0 * j
        segk_ref[128 * j : 128 * j + 128, :] = segments(at, ends_k)


def allowed_cols(t, sec, ends_q, segk_ref, causal):
    query_at = query_places(t, sec, (1, TILE), 1)
    allowed = segk_ref[...] == segments(query_at, ends_q)
    if causal:
        key_at = lax.broadcasted_iota(jnp.int32, (1024, TILE), 0).astype(F32)
        allowed = allowed & (key_at <= query_at)
    return allowed


def fold_kv(grad_k, grad_v, sec, own_ref, send_ref):
    for j in range(4):
        k = grad_k[256 * j : 256 * j + 256, :]
        v = grad_v[256 * j : 256 * j + 256, :]
        k = k + pltpu.roll(k, 64, 1)
        v = v + pltpu.roll(v, 64, 1)
        low = lax.broadcasted_iota(jnp.int32, k.shape, 1) < 64
        both = jnp.where(low, k, v)
        first, second = both[0:128], both[128:256]
        own_ref[j] = jnp.where(sec == 0, first, second)
        send_ref[j] = jnp.where(sec == 0, second, first).astype(send_ref.dtype)


def split_halves(value, sec, keep_ref, send_ref, m, lane):
    upper, lower = value[0:256], value[256:512]
    cut = slice(lane, lane + value.shape[1])
    keep_ref[m, :, cut] = jnp.where(sec == 0, upper, lower).astype(BF)
    send_ref[m, :, cut] = jnp.where(sec == 0, lower, upper).astype(BF)


def split_flat(value, sec, keep_ref, send_ref, lane):
    upper, lower = value[0:256], value[256:512]
    cut = slice(lane, lane + value.shape[1])
    keep_ref[:, cut] = jnp.where(sec == 0, upper, lower).astype(BF)
    send_ref[:, cut] = jnp.where(sec == 0, lower, upper).astype(BF)


def turned_rows(value):
    return value.astype(F32).T.astype(BF)


def flat(ref):
    return ref[...].reshape(512, ref.shape[-1])


def attention_weight_grads(first_t, gated_ref, dz_ref, dq_ref, sec, keep_ref, send_ref, lane):
    grad_q = nn(first_t, flat(dq_ref))
    grad_o = nn(turned_rows(flat(dz_ref)), flat(gated_ref))
    for b in range(4):
        cut = slice(128 * b, 128 * b + 128)
        split_halves(grad_q[:, cut], sec, keep_ref, send_ref, b, lane)
        split_halves(grad_o[:, cut], sec, keep_ref, send_ref, b, lane + 128)


def router_grads(dlog_ref, rows_ref):
    turned = flat(dlog_ref).astype(F32).T.astype(BF)
    return nn(turned, flat(rows_ref))[0:32]


def gelu_parts(pre):
    cdf = 0.5 * (1.0 + lax.erf(pre * 0.7071067811865476))
    slope = cdf + pre * (jnp.exp(-0.5 * pre * pre) * 0.3989422804014327)
    return pre * cdf, slope


def own_self_kv(recv_ref, layer, sec, w_kv, kv_ref):
    gain = gain_of(recv_ref, layer, 0)
    for t in range(2):
        first = norm_of(rows_of(recv_ref, layer, t), gain)[0].astype(BF)
        kv = nn(first, w_kv).astype(BF)
        for i in range(2):
            j = 2 * t + i
            kv_ref[j, sec] = kv[128 * i : 128 * i + 128]
            kv_ref[j, 1 - sec] = other_kv(recv_ref, layer, j)


def cross_kv(kvm_ref, kvo_ref, sec, kv_s):
    for j in range(4):
        kv_s[j, sec] = kvm_ref[j]
        kv_s[j, 1 - sec] = kvo_ref[j]


def pack_kernel(
    ready, len_ref, x_ref, gain_ref, w_kv_ref, own_ref, cross_ref, router_ref, send_ref, extra_s
):
    ready()
    gain = gain_ref[0:1, :].astype(F32)
    w_kv = w_kv_ref[...]
    extra_s[...] = jnp.zeros_like(extra_s)
    extra_s[0:3, :] = gain_ref[...].astype(F32)
    extra_s[ROUTER_AT : ROUTER_AT + 8, :] = router_ref[...].astype(F32)
    lanes = lax.broadcasted_iota(jnp.int32, (1, 512), 1)
    for i in range(4):
        first = norm_of(x_ref[i].astype(F32), gain)[0].astype(BF)
        kv = nn(first, w_kv).astype(BF)
        row = jnp.zeros((1, 512), jnp.int32)
        for k in range(8):
            length = len_ref[i, k]
            row = jnp.where(lanes == k, length >> 5, row)
            row = jnp.where(lanes == 128 + k, length & 31, row)
        extra_s[LEN_ROW : LEN_ROW + 1, :] = row.astype(F32)
        own, cross = own_ref[i], cross_ref[i]
        own_code = (own[0:1] + 8 * own[1:2]).astype(F32)
        cross_code = (cross[0:1] + 8 * cross[1:2]).astype(F32)
        for half in range(2):
            to = 4 * half + i
            here = slice(128 * half, 128 * half + 128)
            send_ref[to, 0:128, :] = x_ref[i, here, :]
            far = kv[128 * (1 - half) : 128 * (1 - half) + 128]
            send_ref[to, 128:160, :] = jnp.concatenate(
                [far[32 * c : 32 * c + 32] for c in range(4)], 1
            )
            extra_s[CODE_ROW : CODE_ROW + 1, 0:128] = own_code[:, here]
            extra_s[CODE_ROW : CODE_ROW + 1, 128:256] = cross_code[:, here]
            send_ref[to, EX_AT : EX_AT + 16, :] = extra_s[...].astype(BF)


def self_fwd_kernel(ready, ids_ref, recv_ref, *refs):
    wa_own, wa_oth, kvw_own, kvw_oth = refs[:4], refs[4:8], refs[8], refs[9]
    h1_ref, g1_ref, mixed_e, mixed_d, log_e, log_d = refs[10:16]
    wq, wo, wkv, kv_s, k2, v2, sems = refs[16:]
    sec, m = ids_ref[0], ids_ref[1]
    loads = Loads(sems)
    kv_waits = [loads.start(sec == i, kvw_own, kvw_oth, wkv.at[i]) for i in range(2)]
    waits = []
    for layer in range(2):
        waits += loads.rows(sec == layer, wa_own, wa_oth, 0, wq.at[layer], m)
        waits += loads.rows(sec == layer, wa_own, wa_oth, 128, wo.at[layer], m)
    ready()
    wait_all(kv_waits)
    for layer in range(2):
        own_self_kv(recv_ref, layer, sec, wkv[layer], kv_s)
        widen_kv(kv_s, k2.at[layer], v2.at[layer])
    wait_all(waits)
    ends = [ends_of(extra_of(recv_ref, layer, 0).astype(F32)) for layer in range(2)]

    def tile(t, carry):
        for layer, after_ref, mixed_ref, log_ref in (
            (0, h1_ref, mixed_e, log_e),
            (1, g1_ref, mixed_d, log_d),
        ):
            rows = rows_of(recv_ref, layer, t)
            first = norm_of(rows, gain_of(recv_ref, layer, 0))[0].astype(BF)
            route = routing(first, extra_of(recv_ref, layer, 0), codes_of(recv_ref, layer, t, 0))
            allowed = allowed_rows(t, sec, ends[layer], ends[layer], layer == 1)
            out, mixed, row_log = attend_tile(
                first, route, wq[layer], wo[layer], k2[layer], v2[layer], allowed
            )
            after_ref[t] = rows + out
            mixed_ref[t] = mixed
            log_ref[t] = row_log
        return carry

    lax.fori_loop(0, 2, tile, 0)


def enc_ffn_kernel(ready, ids_ref, recv_ref, h1_ref, kvc_ref, *refs):
    f_own, f_oth = refs[:4], refs[4:8]
    h2_ref, mem_ref, kvm_ref, w_in, w_out, third_s, sems = refs[8:]
    low, m = ids_ref[0] == 0, ids_ref[1]
    loads = Loads(sems)
    waits = loads.pieces(low, f_own, f_oth, w_in, m) + loads.pieces(low, f_oth, f_own, w_out, m)
    ready()
    for t in range(2):
        h2_ref[t] = h1_ref[t]
        third_s[t] = norm_of(h1_ref[t], gain_of(recv_ref, 0, 2))[0].astype(BF)
    wait_all(waits)

    def chunk(c, carry):
        pre = nn(flat(third_s), w_in[c])
        hidden = (0.5 * pre * (1.0 + lax.erf(pre * 0.7071067811865476))).astype(BF)
        h2_ref[...] += nn(hidden, w_out[c]).reshape(2, TILE, 512)
        return carry

    lax.fori_loop(0, 4, chunk, 0)
    for t in range(2):
        memory = norm_of(h2_ref[t], gain_of(recv_ref, 0, 1))[0].astype(BF)
        mem_ref[t] = memory
        kv = nn(memory, kvc_ref[...]).astype(BF)
        kvm_ref[2 * t] = kv[0:128]
        kvm_ref[2 * t + 1] = kv[128:256]


def cross_fwd_kernel(
    ready, ids_ref, recv_ref, g1_ref, kvm_ref, kvo_ref, rc_ref, *refs
):
    wa_own, wa_oth = refs[:4], refs[4:8]
    g2_ref, mixed_ref, log_ref, wq, wo, kv_s, k2, v2, sems = refs[8:]
    sec, m = ids_ref[0], ids_ref[1]
    loads = Loads(sems)
    waits = loads.rows(sec == 0, wa_own, wa_oth, 256, wq, m)
    waits += loads.rows(sec == 0, wa_oth, wa_own, 256, wo, m)
    ready()
    cross_kv(kvm_ref, kvo_ref, sec, kv_s)
    widen_kv(kv_s, k2, v2)
    wait_all(waits)
    ends_k = ends_of(extra_of(recv_ref, 0, 0).astype(F32))
    ends_q = ends_of(extra_of(recv_ref, 1, 0).astype(F32))

    def tile(t, carry):
        before = g1_ref[t]
        second = norm_of(before, gain_of(recv_ref, 1, 1))[0].astype(BF)
        route = routing(second, rc_ref[...], codes_of(recv_ref, 1, t, 128))
        allowed = allowed_rows(t, sec, ends_q, ends_k, False)
        out, mixed, row_log = attend_tile(second, route, wq[...], wo[...], k2[...], v2[...], allowed)
        g2_ref[t] = before + out
        mixed_ref[t] = mixed
        log_ref[t] = row_log
        return carry

    lax.fori_loop(0, 2, tile, 0)


def ffn_both(c, third_s, third_t, dy_s, dy_t, w_in, w_out, dthird, sec, keep_ref, send_ref):
    pre = nn(flat(third_s), w_in[c])
    hidden, slope = gelu_parts(pre)
    hidden = hidden.astype(BF)
    dpre = (nt(flat(dy_s), w_out[c]) * slope).astype(BF)
    dthird[...] += nt(dpre, w_in[c])
    split_halves(nn(third_t[...], dpre), sec, keep_ref, send_ref, c, 0)
    split_halves(nn(dy_t[...], hidden), sec, keep_ref, send_ref, c, 512)
    return hidden


def dec_ffn_kernel(ready, ids_ref, recv_ref, g2_ref, mem_ref, cot_in, *refs):
    f_own, f_oth = refs[:4], refs[4:8]
    outs_ref, dg2_ref, gain_ref, keep_ref, send_ref = refs[8:13]
    w_in, w_out, cot_s, third_s, third_t, cot_t, acc, dthird, sems = refs[13:]
    sec, m = ids_ref[0], ids_ref[1]
    low = sec == 0
    loads = Loads(sems)
    cot_waits = [loads.plain(cot_in.at[i], cot_s.at[i]) for i in range(4)]
    waits = loads.pieces(low, f_own, f_oth, w_in, m) + loads.pieces(low, f_oth, f_own, w_out, m)
    ready()
    for t in range(2):
        acc[t] = g2_ref[t]
        third_s[t] = norm_of(g2_ref[t], gain_of(recv_ref, 1, 2))[0].astype(BF)
        outs_ref[2 * t : 2 * t + 2] = mem_ref[t].reshape(2, 128, 512)
    third_t[...] = turned_rows(flat(third_s))
    wait_all(cot_waits)
    cot_t[...] = turned_rows(flat(cot_s))
    dthird[...] = jnp.zeros_like(dthird)
    wait_all(waits)

    def chunk(c, carry):
        hidden = ffn_both(
            c, third_s, third_t, cot_s, cot_t, w_in, w_out, dthird, sec, keep_ref, send_ref
        )
        acc[...] += nn(hidden, w_out[c]).reshape(2, TILE, 512)
        return carry

    lax.fori_loop(0, 4, chunk, 0)
    total = jnp.zeros((1, 512), F32)
    gain = gain_of(recv_ref, 1, 2)
    for t in range(2):
        outs_ref[4 + 2 * t : 6 + 2 * t] = acc[t].astype(BF).reshape(2, 128, 512)
        unused_out, unit, scaled = norm_of(g2_ref[t], gain)
        back, gain_grad = norm_back(dthird[TILE * t : TILE * t + TILE, :], unit, scaled, gain)
        dg2_ref[t] = cot_s[2 * t : 2 * t + 2].reshape(TILE, 512).astype(F32) + back
        total = total + gain_grad
    gain_ref[...] = total


def cross_back_kernel(
    ready, ids_ref, recv_ref, g1_ref, dg2_ref, mixed_ref, log_ref, kvm_ref, kvo_ref, rc_ref, *refs
):
    wa_own, wa_oth = refs[:4], refs[4:8]
    dg1_ref, gain_ref, own_ref, send_ref, router_ref, keepw_ref, sendw_ref = refs[8:15]
    wq, wo, kv_s, k2, v2, segk, grad_k, grad_v, second_s, gated_s, dz_s, dq_s, dlog_s, sems = refs[15:]
    sec, m = ids_ref[0], ids_ref[1]
    loads = Loads(sems)
    waits = loads.rows(sec == 0, wa_own, wa_oth, 256, wq, m)
    waits += loads.rows(sec == 0, wa_oth, wa_own, 256, wo, m)
    ready()
    cross_kv(kvm_ref, kvo_ref, sec, kv_s)
    widen_kv(kv_s, k2, v2)
    ends_k = ends_of(extra_of(recv_ref, 0, 0).astype(F32))
    ends_q = ends_of(extra_of(recv_ref, 1, 0).astype(F32))
    key_segments_t(ends_k, segk)
    grad_k[...] = jnp.zeros_like(grad_k)
    grad_v[...] = jnp.zeros_like(grad_v)
    wait_all(waits)

    def tile(t, total):
        gain = gain_of(recv_ref, 1, 1)
        second, unit, scaled = norm_of(g1_ref[t], gain)
        second = second.astype(BF)
        second_s[t] = second
        route = routing(second, rc_ref[...], codes_of(recv_ref, 1, t, 128))
        allowed = allowed_cols(t, sec, ends_q, segk, False)
        grad_rows = attend_back_tile(
            t, dg2_ref[t], second, route, mixed_ref[t], log_ref[t], wq[...], wo[...], rc_ref[...],
            ROUTER_LANES[2], k2[...], v2[...], allowed, grad_k, grad_v, gated_s, dz_s, dq_s, dlog_s,
        )
        back, gain_grad = norm_back(grad_rows, unit, scaled, gain)
        dg1_ref[t] = dg2_ref[t] + back
        return total + gain_grad

    gain_ref[...] = lax.fori_loop(0, 2, tile, jnp.zeros((1, 512), F32))
    fold_kv(grad_k, grad_v, sec, own_ref, send_ref)
    router_ref[...] = router_grads(dlog_s, second_s)
    attention_weight_grads(
        turned_rows(flat(second_s)), gated_s, dz_s, dq_s, sec, keepw_ref, sendw_ref, 0
    )


def self_back_kernel(layer, ready, ids_ref, recv_ref, up_ref, mixed_ref, log_ref, *refs):
    wa_own, wa_oth, kvw_own, kvw_oth = refs[:4], refs[4:8], refs[8], refs[9]
    refs = refs[10:]
    if layer == 1:
        before, refs = refs[:2], refs[2:]
    dfirst_ref, own_ref, send_ref, router_ref, keepw_ref, sendw_ref = refs[:6]
    wq, wo, wkv, kv_s, k2, v2, segk, grad_k, grad_v = refs[6:15]
    first_s, gated_s, dz_s, dq_s, dlog_s, sems = refs[15:]
    sec, m = ids_ref[0], ids_ref[1]
    mine = sec == layer
    loads = Loads(sems)
    kv_wait = loads.start(mine, kvw_own, kvw_oth, wkv)
    waits = loads.rows(mine, wa_own, wa_oth, 0, wq, m) + loads.rows(mine, wa_own, wa_oth, 128, wo, m)
    lane = 0
    if layer == 1:
        lane = 256
        for src, dst in zip(before, (keepw_ref, sendw_ref)):
            waits.append(loads.plain(src, dst.at[:, :, pl.ds(0, 256)]))
    ready()
    ends = ends_of(extra_of(recv_ref, layer, 0).astype(F32))
    key_segments_t(ends, segk)
    grad_k[...] = jnp.zeros_like(grad_k)
    grad_v[...] = jnp.zeros_like(grad_v)
    kv_wait()
    own_self_kv(recv_ref, layer, sec, wkv[...], kv_s)
    widen_kv(kv_s, k2, v2)
    wait_all(waits)
    router_block = extra_of(recv_ref, layer, 0)

    def tile(t, carry):
        first = norm_of(rows_of(recv_ref, layer, t), gain_of(recv_ref, layer, 0))[0].astype(BF)
        first_s[t] = first
        route = routing(first, router_block, codes_of(recv_ref, layer, t, 0))
        allowed = allowed_cols(t, sec, ends, segk, layer == 1)
        dfirst_ref[t] = attend_back_tile(
            t, up_ref[t], first, route, mixed_ref[t], log_ref[t], wq[...], wo[...], router_block,
            ROUTER_LANES[layer], k2[...], v2[...], allowed, grad_k, grad_v, gated_s, dz_s, dq_s,
            dlog_s,
        )
        return carry

    lax.fori_loop(0, 2, tile, 0)
    fold_kv(grad_k, grad_v, sec, own_ref, send_ref)
    router_ref[...] = router_grads(dlog_s, first_s)
    attention_weight_grads(
        turned_rows(flat(first_s)), gated_s, dz_s, dq_s, sec, keepw_ref, sendw_ref, lane
    )


def enc_ffn_back_kernel(
    ready, ids_ref, recv_ref, h1_ref, h2_ref, own_ref, come_ref, kvc_ref, *refs
):
    f_own, f_oth = refs[:4], refs[4:8]
    dh1_ref, gain_ref, gain2_ref, keep_ref, send_ref = refs[8:13]
    w_in, w_out, third_s, third_t, dy_s, dy_t, dthird, sems = refs[13:]
    sec, m = ids_ref[0], ids_ref[1]
    low = sec == 0
    loads = Loads(sems)
    waits = loads.pieces(low, f_own, f_oth, w_in, m) + loads.pieces(low, f_oth, f_own, w_out, m)
    ready()
    total = jnp.zeros((1, 512), F32)
    gain = gain_of(recv_ref, 0, 1)
    for t in range(2):
        dkv = (own_ref[2 * t : 2 * t + 2] + come_ref[2 * t : 2 * t + 2].astype(F32)).astype(BF)
        dmem = rounded(nt(dkv.reshape(TILE, 128), kvc_ref[...]))
        unused_out, unit, scaled = norm_of(h2_ref[t], gain)
        back, gain_grad = norm_back(dmem, unit, scaled, gain)
        dh1_ref[t] = back
        dy_s[t] = back.astype(BF)
        third_s[t] = norm_of(h1_ref[t], gain_of(recv_ref, 0, 2))[0].astype(BF)
        total = total + gain_grad
    gain_ref[...] = total
    third_t[...] = turned_rows(flat(third_s))
    dy_t[...] = turned_rows(flat(dy_s))
    dthird[...] = jnp.zeros_like(dthird)
    wait_all(waits)

    def chunk(c, carry):
        ffn_both(c, third_s, third_t, dy_s, dy_t, w_in, w_out, dthird, sec, keep_ref, send_ref)
        return carry

    lax.fori_loop(0, 4, chunk, 0)
    total = jnp.zeros((1, 512), F32)
    gain = gain_of(recv_ref, 0, 2)
    for t in range(2):
        unused_out, unit, scaled = norm_of(h1_ref[t], gain)
        back, gain_grad = norm_back(dthird[TILE * t : TILE * t + TILE, :], unit, scaled, gain)
        dh1_ref[t] += back
        total = total + gain_grad
    gain2_ref[...] = total


def finish_rows(layer, recv_ref, up_ref, df_ref, own_ref, come_ref, wkv, first_s, out_ref, at):
    total = jnp.zeros((1, 512), F32)
    gain = gain_of(recv_ref, layer, 0)
    dkvs = []
    for t in range(2):
        first, unit, scaled = norm_of(rows_of(recv_ref, layer, t), gain)
        first_s[t] = first.astype(BF)
        dkv = (own_ref[2 * t : 2 * t + 2] + come_ref[2 * t : 2 * t + 2].astype(F32)).astype(BF)
        dkv = dkv.reshape(TILE, 128)
        dkvs.append(dkv)
        back, gain_grad = norm_back(df_ref[t] + nt(dkv, wkv), unit, scaled, gain)
        dx = (up_ref[t] + back).astype(BF)
        for i in range(2):
            out_ref[at + 2 * t + i, 0:128, :] = dx[128 * i : 128 * i + 128]
        total = total + gain_grad
    grad = nn(turned_rows(flat(first_s)), jnp.concatenate(dkvs, 0))
    return total, grad


def dec_finish_kernel(
    ready, ids_ref, recv_ref, up_ref, df_ref, own_ref, come_ref, own_c, come_c, mem_ref, kvw_own, kvw_oth,
    dx_ref, gain_ref, keep_ref, send_ref, wkv, first_s, sems,
):
    sec = ids_ref[0]
    wait = Loads(sems).start(sec == 1, kvw_own, kvw_oth, wkv)
    ready()
    dkv_c = (own_c[...] + come_c[...].astype(F32)).astype(BF).reshape(512, 128)
    split_flat(nn(turned_rows(flat(mem_ref)), dkv_c), sec, keep_ref, send_ref, 128)
    wait()
    gain_ref[...], grad = finish_rows(
        1, recv_ref, up_ref, df_ref, own_ref, come_ref, wkv[...], first_s, dx_ref, 0
    )
    split_flat(grad, sec, keep_ref, send_ref, 0)


def enc_finish_kernel(
    ready, ids_ref, recv_ref, up_ref, df_ref, own_ref, come_ref, dx1_ref, r0, r1, rc,
    gain_e1, gain_e2, gain_d0, gain_d1, gain_d2, kvw_own, kvw_oth,
    out_ref, wkv, first_s, misc, sems,
):
    sec = ids_ref[0]
    wait = Loads(sems).start(sec == 0, kvw_own, kvw_oth, wkv)
    ready()
    misc[...] = r0[...] + r1[...] + rc[...]
    out_ref[4:8, 0:128, :] = dx1_ref[...]
    wait()
    gain_e0, grad = finish_rows(
        0, recv_ref, up_ref, df_ref, own_ref, come_ref, wkv[...], first_s, out_ref, 0
    )
    rows = (gain_e0, gain_e1[...], gain_e2[...], gain_d0[...], gain_d1[...], gain_d2[...])
    for i, row in enumerate(rows):
        misc[GAIN_ROW + i : GAIN_ROW + i + 1, :] = row
    both = misc[...]
    for half in range(2):
        cut = slice(256 * half, 256 * half + 256)
        part = grad[cut].astype(BF)
        small = both[:, cut].astype(BF)
        block = jnp.concatenate(
            [
                jnp.concatenate([part[64 * c : 64 * c + 64] for c in range(4)], 1),
                jnp.concatenate([small[0:16], small[16:32]], 1),
            ],
            0,
        )
        for i in range(4):
            out_ref[4 * half + i, 128:208, :] = block


def add_kernel(keep_ref, come_ref, *outs):
    lane = 0
    for out_ref in outs:
        cut = slice(lane, lane + out_ref.shape[-1])
        out_ref[...] = keep_ref[:, :, cut] + come_ref[:, :, cut]
        lane += out_ref.shape[-1]


def add_pieces_kernel(flats, ready, ids_ref, *refs):
    ready()
    n = len(flats)
    keeps, comes, outs = refs[:n], refs[n : 2 * n], refs[2 * n :]
    m = ids_ref[1]
    for b in range(4):
        lane = 0
        for is_flat, keep, come in zip(flats, keeps, comes):
            left = keep[...] if is_flat else keep[m ^ b]
            right = come[...] if is_flat else come[m ^ b]
            width = keep.shape[-1]
            outs[b][:, lane : lane + width] = left + right
            lane += width


def sum_middle_kernel(ready, ids_ref, dec_a, dec_b, enc_ref, *refs):
    att, outs = refs[:4], refs[4:]
    ready()
    rows = outs[0].shape[0]
    d = ids_ref[2]
    for k in range(len(outs)):
        cut = pl.ds(pl.multiple_of((d ^ k) * rows, rows), rows)
        for ref, lane in ((enc_ref, 0), (dec_a, 1024), (dec_b, 1536)):
            total = ref[0, cut, :].astype(F32)
            for i in range(1, 4):
                total = total + ref[i, cut, :].astype(F32)
            outs[k][:, lane : lane + ref.shape[-1]] = total.astype(BF)
        total = att[0][cut, :].astype(F32)
        for part in att[1:]:
            total = total + part[cut, :].astype(F32)
        outs[k][:, 2048:2560] = total.astype(BF)


def tail_kernel(ready, dx_ref, *refs):
    att_e, shared, (dx_out, out_ref) = refs[:4], refs[4:8], refs[8:]
    ready()
    for i in range(4):
        for half in range(2):
            dx_out[i, half] = dx_ref[4 * half + i, 0:128, :].astype(F32)
    for parts, lane in ((att_e, 0), (shared, 256)):
        total = parts[0][...].astype(F32)
        for part in parts[1:]:
            total = total + part[...].astype(F32)
        out_ref[:, lane : lane + 256] = total.astype(BF)
    small = dx_ref[0, 128:208, :].astype(F32)
    for i in range(1, 8):
        small = small + dx_ref[i, 128:208, :].astype(F32)
    for c in range(4):
        out_ref[64 * c : 64 * c + 64, 512:640] = small[0:64, 128 * c : 128 * c + 128].astype(BF)
    misc = jnp.concatenate([small[64:80, 0:256], small[64:80, 256:512]], 0)
    misc = jnp.concatenate([misc, jnp.zeros((96, 256), F32)], 0)
    out_ref[:, 640:768] = misc.T.astype(BF)


def final_kernel(ready, come_ref, *refs):
    middle, outs = refs[:4], refs[4:]
    ready()
    gains, router, query, keyval, output, inner, outer, router_c, query_c, keyval_c, output_c = outs
    small = come_ref[0].astype(F32)
    for i in range(1, 4):
        small = small + come_ref[i].astype(F32)
    wide = middle[0][...].astype(F32)
    for part in middle[1:]:
        wide = wide + part[...].astype(F32)
    for layer in range(2):
        inner[layer] = wide[:, 1024 * layer : 1024 * layer + 512]
        outer[layer] = wide[:, 1024 * layer + 512 : 1024 * layer + 1024]
    keyval[0], keyval[1] = small[:, 512:640], small[:, 256:384]
    keyval_c[...] = small[:, 384:512]
    for source, at, put_q, put_o in (
        (wide, 2048, query_c, output_c),
        (wide, 2304, query.at[1], output.at[1]),
        (small, 0, query.at[0], output.at[0]),
    ):
        turned = source[:, at + 128 : at + 256].T
        for e in range(2):
            put_q[e] = source[:, at + 64 * e : at + 64 * e + 64]
            put_o[e] = turned[64 * e : 64 * e + 64]
    misc = small[:, 640:768].T
    router[0], router[1], router_c[...] = misc[0:8], misc[8:16], misc[16:24]
    for i in range(3):
        gains[i, 0:1] = misc[24 + i : 25 + i]
        gains[i, 1:2] = misc[27 + i : 28 + i]


def shaped(dims, kind):
    return jax.ShapeDtypeStruct(dims, kind)


def cost_of(micros):
    return pl.CostEstimate(
        flops=int(micros * 1.1535e9), bytes_accessed=int(micros * 3.0e6), transcendentals=0
    )


def run(kernel, args, places, outs, scratch, micros, after=()):
    space = {
        "s": pl.BlockSpec(memory_space=pltpu.SMEM),
        "v": pl.BlockSpec(memory_space=pltpu.VMEM),
        "a": pl.BlockSpec(memory_space=pl.ANY),
    }
    large = [
        i for i, (p, a) in enumerate(zip(places, args)) if p == "v" and a.size * a.dtype.itemsize > LARGE
    ]
    places = ["a" if i in large else p for i, p in enumerate(places)]
    count, extra = len(args), len(after)
    copies = [pltpu.VMEM(args[i].shape, args[i].dtype) for i in large]

    def body(*refs):
        given, rest = list(refs[:count]), refs[count + extra :]
        if large:
            rest, held, sems = rest[: -len(large) - 1], rest[-len(large) - 1 : -1], rest[-1]
            moves = []
            for n, i in enumerate(large):
                moves.append(pltpu.make_async_copy(given[i], held[n], sems.at[n]))
                given[i] = held[n]
            for move in moves:
                move.start()
        else:
            moves = []

        def ready():
            for move in moves:
                move.wait()

        kernel(ready, *given, *rest)

    return pl.pallas_call(
        body,
        out_shape=outs,
        in_specs=[space[p] for p in places] + [space["a"]] * extra,
        out_specs=jax.tree.map(lambda _: space["v"], outs),
        scratch_shapes=scratch + copies + ([dma(len(large))] if large else []),
        compiler_params=pltpu.CompilerParams(vmem_limit_bytes=VMEM_LIMIT),
        cost_estimate=cost_of(micros),
    )(*args, *after)


def vm(*dims, kind=BF):
    return pltpu.VMEM(dims, kind)


def dma(count):
    return pltpu.SemaphoreType.DMA((count,))


def across(value, axes, size, by):
    return lax.ppermute(value, axes, [(i, i ^ by) for i in range(size)])


def swapped(value):
    return across(value, "section", 2, 1)


def gathered(value):
    return [value] + [across(value, "mp", 4, b) for b in range(1, 4)]


def to_all(value, axes):
    return lax.all_to_all(value, axes, split_axis=0, concat_axis=0, tiled=True)


def add_shares(keep, come, micros, after, parts=1):
    blocks, rows, width = keep.shape
    whole = pl.BlockSpec((1, rows, width), lambda i: (i, 0, 0))
    part = pl.BlockSpec((1, rows, width // parts), lambda i: (i, 0, 0))
    extra = len(after)
    return pl.pallas_call(
        lambda k, c, *rest: add_kernel(k, c, *rest[extra:]),
        out_shape=[shaped((blocks, rows, width // parts), BF)] * parts,
        grid=(blocks,),
        in_specs=[whole, whole] + [pl.BlockSpec(memory_space=pl.ANY)] * extra,
        out_specs=[part] * parts,
        cost_estimate=cost_of(micros),
    )(keep, come, *after)


def add_pieces(ids, keeps, comes, micros, after=()):
    flats = tuple(keep.ndim == 2 for keep in keeps)
    width = sum(keep.shape[-1] for keep in keeps)
    return run(
        functools.partial(add_pieces_kernel, flats),
        (ids, *keeps, *comes),
        "s" + "v" * (2 * len(keeps)),
        [shaped((256, width), BF)] * 4,
        [],
        micros,
        after=after,
    )


def mp_exchange(pieces):
    return [pieces[0]] + [across(pieces[b], "mp", 4, b) for b in range(1, 4)]


def dp_exchange(pieces):
    return [pieces[0]] + [across(pieces[k], "dp", 4, k) for k in range(1, 4)]


def gated(values, after):
    anywhere = pl.BlockSpec(memory_space=pl.ANY)
    count = len(values)
    return pl.pallas_call(
        lambda *refs: None,
        out_shape=[shaped(v.shape, v.dtype) for v in values],
        in_specs=[anywhere] * (count + len(after)),
        out_specs=[anywhere] * count,
        input_output_aliases={i: i for i in range(count)},
        cost_estimate=cost_of(0.2),
    )(*values, *after)


def per_device(
    inputs,
    lengths,
    routes_self,
    routes_cross,
    gains,
    router_self,
    query_self,
    keyval_self,
    output_self,
    ffn_in,
    ffn_out,
    router_cross,
    query_cross,
    keyval_cross,
    output_cross,
    cotangent,
):
    sec, m, d = lax.axis_index("section"), lax.axis_index("mp"), lax.axis_index("dp")
    low = sec == 0
    ids = jnp.stack([sec, m, d]).astype(jnp.int32)
    sem = dma(24)
    rowgroup = ("section", "mp")

    q_rows = query_self[0].transpose(0, 2, 1).reshape(128, 512)
    o_rows = output_self[0].reshape(128, 512)
    c_rows = jnp.where(
        low, query_cross.transpose(0, 2, 1).reshape(128, 512), output_cross.reshape(128, 512)
    )
    wa = jnp.concatenate([q_rows, o_rows, c_rows], 0)
    wa_own = gathered(wa)
    w_in, w_out = ffn_in[0], ffn_out[0]
    half_come = swapped(jnp.where(low, w_out, w_in))
    enc_half = jnp.where(low, w_in, half_come)
    dec_half = jnp.where(low, half_come, w_out)
    kvw_own = keyval_self[0]
    kvw_oth = swapped(kvw_own)
    router_c = jnp.concatenate([jnp.zeros((8, 512), BF), router_cross.T], 0)

    packed = run(
        pack_kernel,
        (
            lengths[0, :, 0],
            inputs[0, :, 0],
            gains[0],
            keyval_self[0],
            routes_self[0, :, 0].transpose(0, 2, 1),
            routes_cross[:, 0].transpose(0, 2, 1),
            router_self[0].T,
        ),
        "svvvvvv",
        shaped((8, 176, 512), BF),
        [vm(16, 512, kind=F32)],
        3.4,
        after=(wa, enc_half, dec_half),
    )
    (packed,) = gated([packed], wa_own[1:])
    recv = to_all(packed, rowgroup)
    wa_oth = [swapped(piece) for piece in wa_own]
    (enc_half,) = gated([enc_half], [packed])
    enc_own = gathered(enc_half)
    cot_in = lax.dynamic_index_in_dim(cotangent[:, 0].reshape(4, 2, 128, 512), sec, 1, False)

    act = shaped((2, TILE, 512), F32)
    actb = shaped((2, TILE, 512), BF)
    mixed_s = shaped((2, 2 * TILE, 128), F32)
    log_s = shaped((2, 1, 2 * TILE), F32)
    kv_b = shaped((4, 128, 128), BF)
    kv_f = shaped((4, 128, 128), F32)
    row_s = shaped((1, 512), F32)
    ffn_g = shaped((4, 256, 1024), BF)
    router_s = shaped((32, 512), F32)
    wide = [vm(512, 512), vm(512, 512)]
    kv_scratch = [vm(4, 2, 128, 128), vm(1024, 128), vm(1024, 128)]
    back_scratch = [
        vm(1024, TILE, kind=F32), vm(1024, 128, kind=F32), vm(1024, 128, kind=F32),
        vm(2, TILE, 512), vm(2, TILE, 512), vm(2, TILE, 512), vm(2, TILE, 512), vm(2, TILE, 128),
    ]
    ffn_w = [vm(4, 512, 512), vm(4, 512, 512)]

    h1, g1, mixed_e, mixed_d, log_e, log_d = run(
        self_fwd_kernel,
        (ids, recv, *wa_own, *wa_oth, kvw_own, kvw_oth),
        "sv" + "a" * 10,
        (act, act, mixed_s, mixed_s, log_s, log_s),
        [vm(2, 512, 512), vm(2, 512, 512), vm(2, 512, 128), vm(4, 2, 128, 128)]
        + [vm(2, 1024, 128), vm(2, 1024, 128), sem],
        0.3,
    )
    enc_own[1:] = gated(enc_own[1:], [h1])
    enc_oth = [swapped(piece) for piece in enc_own]
    (dec_half,) = gated([dec_half], [enc_own[1]])
    dec_own = gathered(dec_half)
    (cot_in,) = gated([cot_in], [enc_own[1]])
    cot = to_all(cot_in, "mp")
    h2, memory, kvm = run(
        enc_ffn_kernel,
        (ids, recv, h1, keyval_cross, *enc_own, *enc_oth),
        "svvv" + "a" * 8,
        (act, actb, kv_b),
        ffn_w + [vm(2, TILE, 512), sem],
        4.0,
        after=(dec_half, cot_in),
    )
    kvm_oth = swapped(kvm)
    g2, mixed_c, log_c = run(
        cross_fwd_kernel,
        (ids, recv, g1, kvm, kvm_oth, router_c, *wa_own, *wa_oth),
        "svvvvv" + "a" * 8,
        (act, mixed_s, log_s),
        wide + kv_scratch + [sem],
        0.3,
        after=(cot,),
    )
    dec_own[1:] = gated(dec_own[1:], [g2])
    dec_oth = [swapped(piece) for piece in dec_own]
    outs, dg2, gain_d2, keep_d, send_d = run(
        dec_ffn_kernel,
        (ids, recv, g2, memory, cot, *dec_own, *dec_oth),
        "svvva" + "a" * 8,
        (shaped((8, 128, 512), BF), act, row_s, ffn_g, ffn_g),
        ffn_w
        + [vm(4, 128, 512), vm(2, TILE, 512), vm(512, 512), vm(512, 512)]
        + [vm(2, TILE, 512, kind=F32), vm(512, 512, kind=F32), sem],
        15.0,
    )
    come_d = swapped(send_d)
    outs_come = to_all(outs, rowgroup)
    att_g = shaped((4, 256, 256), BF)
    flat_g = shaped((256, 256), BF)
    dg1, gain_d1, own_c, sendkv_c, router_cg, keep_wc, send_wc = run(
        cross_back_kernel,
        (ids, recv, g1, dg2, mixed_c, log_c, kvm, kvm_oth, router_c, *wa_own, *wa_oth),
        "svvvvvvvv" + "a" * 8,
        (act, row_s, kv_f, kv_b, router_s, att_g, att_g),
        wide + kv_scratch + back_scratch + [sem],
        13.0,
    )
    comekv_c = swapped(sendkv_c)
    dec_a, dec_b = add_shares(keep_d, come_d, 4.0, (dg1, outs_come), 2)
    dh1, gain_e1, gain_e2, keep_e, send_e = run(
        enc_ffn_back_kernel,
        (ids, recv, h1, h2, own_c, comekv_c, keyval_cross, *enc_own, *enc_oth),
        "svvvvvv" + "a" * 8,
        (act, row_s, row_s, ffn_g, ffn_g),
        ffn_w
        + [vm(2, TILE, 512), vm(512, 512), vm(2, TILE, 512), vm(512, 512)]
        + [vm(512, 512, kind=F32), sem],
        13.4,
        after=(dec_a,),
    )
    dec_a = to_all(dec_a, "mp")
    (dec_b,) = gated([dec_b], [dec_a])
    dec_b = to_all(dec_b, "mp")
    come_e = swapped(send_e)
    self_scratch = wide + [vm(512, 128)] + kv_scratch + back_scratch + [sem]
    att_dg = shaped((4, 256, 512), BF)
    df1, own_1, sendkv_1, router_1g, keep_w1, send_w1 = run(
        functools.partial(self_back_kernel, 1),
        (
            ids, recv, dg1, mixed_d, log_d, *wa_own, *wa_oth, kvw_own, kvw_oth, keep_wc, send_wc,
        ),
        "svvvv" + "a" * 12,
        (act, kv_f, kv_b, router_s, att_dg, att_dg),
        self_scratch,
        12.2,
        after=(dh1, dec_a),
    )
    comekv_1 = swapped(sendkv_1)
    come_w1 = swapped(send_w1)
    (ffn_e,) = add_shares(keep_e, come_e, 4.0, (df1, dec_b))
    att_d = add_pieces(ids, [keep_w1], [come_w1], 3.6, (ffn_e,))
    df0, own_0, sendkv_0, router_0g, keep_w0, send_w0 = run(
        functools.partial(self_back_kernel, 0),
        (ids, recv, dh1, mixed_e, log_e, *wa_own, *wa_oth, kvw_own, kvw_oth),
        "svvvv" + "a" * 10,
        (act, kv_f, kv_b, router_s, att_g, att_g),
        self_scratch,
        11.8,
        after=(ffn_e, *att_d),
    )
    comekv_0 = swapped(sendkv_0)
    come_w0 = swapped(send_w0)
    ffn_e = to_all(ffn_e, "mp")
    att_d = mp_exchange(att_d)
    dx1, gain_d0, keep_s1, send_s1 = run(
        dec_finish_kernel,
        (ids, recv, dg1, df1, own_1, comekv_1, own_c, comekv_c, memory, kvw_own, kvw_oth),
        "svvvvvvvvaa",
        (shaped((4, 128, 512), BF), row_s, flat_g, flat_g),
        [vm(512, 128), vm(2, TILE, 512), sem],
        0.3,
        after=(df0,),
    )
    come_s1 = swapped(send_s1)
    finished = run(
        enc_finish_kernel,
        (
            ids, recv, dh1, df0, own_0, comekv_0, dx1, router_0g, router_1g, router_cg,
            gain_e1, gain_e2, gain_d0, gain_d1, gain_d2, kvw_own, kvw_oth,
        ),
        "s" + "v" * 14 + "aa",
        shaped((8, 208, 512), BF),
        [vm(512, 128), vm(2, TILE, 512), vm(32, 512, kind=F32), sem],
        0.3,
        after=att_d[1:3],
    )
    att_e = add_pieces(
        ids, [keep_w0], [come_w0], 3.6, (finished, *att_d[1:])
    )
    shared = mp_exchange([keep_s1 + come_s1] * 4)
    att_e = mp_exchange(att_e)
    dp = lax.axis_size("dp")
    share = 256 // dp
    if dp == 4:
        ffn = dp_exchange(
            run(
                sum_middle_kernel,
                (ids, dec_a, dec_b, ffn_e, *att_d),
                "s" + "v" * 7,
                [shaped((64, 2560), BF)] * 4,
                [],
                4.0,
                after=(att_e[0],),
            )
        )
        after = ffn[1:]
    else:
        after = ()
    dx, small = run(
        tail_kernel,
        (to_all(finished, rowgroup), *att_e, *shared),
        "v" * 9,
        (shaped((4, 2, 128, 512), F32), shaped((256, 768), BF)),
        [],
        3.0,
        after=after,
    )
    small = to_all(small.reshape(dp, share, 768), "dp")
    outs_come = outs_come.reshape(2, 4, 128, 512).transpose(1, 0, 2, 3)
    results = (outs_come.reshape(1, 4, 1, 256, 512), dx.reshape(1, 4, 1, 256, 512))
    if dp == 4:
        made = run(
            final_kernel,
            (small, *ffn),
            "v" * 5,
            (
                shaped((3, 2, 64), F32),
                shaped((2, 8, 64), F32),
                shaped((2, 2, 64, 64), F32),
                shaped((2, 64, 128), F32),
                shaped((2, 2, 64, 64), F32),
                shaped((2, 64, 512), F32),
                shaped((2, 64, 512), F32),
                shaped((8, 64), F32),
                shaped((2, 64, 64), F32),
                shaped((64, 128), F32),
                shaped((2, 64, 64), F32),
            ),
            [],
            3.0,
        )
        made = list(made)
        made[0] = made[0].transpose(1, 0, 2)
        made[1] = made[1].transpose(0, 2, 1)
        made[6] = made[6].transpose(0, 2, 1)
        made[7] = made[7].T
        return (*results, *made)

    small = jnp.sum(small.astype(F32), 0)
    middle = jnp.concatenate(
        [jnp.sum(part.astype(F32), 0) for part in (ffn_e, dec_a, dec_b)]
        + [sum(part.astype(F32) for part in att_d)],
        1,
    )
    middle = to_all(middle.astype(BF).reshape(dp, share, 2560), "dp")
    middle = jnp.sum(middle.astype(F32), 0)

    def query_of(value, at):
        return value[:, at : at + 128].reshape(share, 2, 64).transpose(1, 0, 2)

    def output_of(value, at):
        return value[:, at + 128 : at + 256].T.reshape(2, 64, share)

    misc = small[:, 640:768].T

    def router_of(layer):
        return misc[ROUTER_LANES[layer] : ROUTER_LANES[layer] + 8].T

    return (
        *results,
        misc[GAIN_ROW : GAIN_ROW + 6].reshape(2, 3, share),
        jnp.stack([router_of(0), router_of(1)]),
        jnp.stack([query_of(small, 0), query_of(middle, 2304)]),
        jnp.stack([small[:, 512:640], small[:, 256:384]]),
        jnp.stack([output_of(small, 0), output_of(middle, 2304)]),
        jnp.stack([middle[:, :512], middle[:, 1024:1536]]),
        jnp.stack([middle[:, 512:1024].T, middle[:, 1536:2048].T]),
        router_of(2),
        query_of(middle, 2048),
        small[:, 384:512],
        output_of(middle, 2048),
    )


def solution(mesh):
    placed = (
        P("section", None, "dp", "mp", None),
        P("section", None, "dp", None),
        P("section", None, "dp", "mp", None),
        P(None, "dp", "mp", None),
        P("section", None, None),
        P("section", None, None),
        P("section", "mp", None, None),
        P("section", None, None),
        P("section", "mp", None, None),
        P("section", None, "mp"),
        P("section", "mp", None),
        P(),
        P("mp", None, None),
        P(),
        P("mp", None, None),
        P(None, "dp", "mp", None),
    )
    return jax.shard_map(
        per_device,
        mesh=mesh,
        in_specs=placed,
        out_specs=(
            P("section", None, "dp", "mp", None),
            P("section", None, "dp", "mp", None),
            P(None, None, ("section", "dp")),
            P(None, ("section", "dp"), None),
            P(None, "mp", ("section", "dp"), None),
            P(None, ("section", "dp"), None),
            P(None, "mp", None, ("section", "dp")),
            P(None, ("section", "dp"), "mp"),
            P(None, "mp", ("section", "dp")),
            P(("section", "dp"), None),
            P("mp", ("section", "dp"), None),
            P(("section", "dp"), None),
            P("mp", None, ("section", "dp")),
        ),
        check_vma=False,
    )
```

```python
import functools

import jax
import jax.numpy as jnp
from jax import lax
from jax.experimental import pallas as pl
from jax.experimental.pallas import tpu as pltpu
from jax.sharding import PartitionSpec as P

EPS = 1e-05
MASK_VALUE = -1000000000.0
BF = jnp.bfloat16
F32 = jnp.float32
TILE = 256
EX_AT = 160
CODE_ROW = 3
LEN_ROW = 4
ROUTER_AT = 8
GAIN_ROW = 24
ROUTER_LANES = (0, 8, 16)
VMEM_LIMIT = 63 * 1024 * 1024
LARGE = 1 << 40


def nn(left, right):
    return lax.dot_general(left, right, (((1,), (0,)), ((), ())), preferred_element_type=F32)


def nt(left, right):
    return lax.dot_general(left, right, (((1,), (1,)), ((), ())), preferred_element_type=F32)


def tn(left, right):
    return lax.dot_general(left, right, (((0,), (0,)), ((), ())), preferred_element_type=F32)


def norm_of(values, gain_row):
    center = values - jnp.mean(values, 1, keepdims=True)
    scaled = lax.rsqrt(jnp.mean(center * center, 1, keepdims=True) + EPS)
    unit_rows = center * scaled
    return unit_rows * gain_row, unit_rows, scaled


def norm_back(upstream, unit_rows, scaled, gain_row):
    inner = upstream * gain_row
    result = scaled * (
        inner
        - jnp.mean(inner, 1, keepdims=True)
        - unit_rows * jnp.mean(inner * unit_rows, 1, keepdims=True)
    )
    return result, jnp.sum(upstream * unit_rows, 0, keepdims=True)


def eye_of(size):
    return lax.broadcasted_iota(jnp.int32, (size, size), 0) == lax.broadcasted_iota(
        jnp.int32, (size, size), 1
    )


def row_to_col(row):
    return jnp.sum(jnp.where(eye_of(128), row, 0.0), 1, keepdims=True)


def col_to_row(col):
    parts = []
    for at in range(0, col.shape[0], 128):
        part = jnp.where(eye_of(128), col[at : at + 128], 0.0)
        parts.append(jnp.sum(part, 0, keepdims=True))
    return jnp.concatenate(parts, 1)


def ends_of(extra):
    lengths = extra[LEN_ROW : LEN_ROW + 1, 0:8] * 32.0 + extra[LEN_ROW : LEN_ROW + 1, 128:136]
    ends = [lengths[:, 0:1]]
    for k in range(1, 8):
        ends.append(ends[-1] + lengths[:, k : k + 1])
    return ends


def segments(places, ends):
    total = jnp.where(places >= ends[0], 1.0, 0.0)
    for end in ends[1:]:
        total = total + jnp.where(places >= end, 1.0, 0.0)
    return total


def extra_of(recv_ref, layer, quarter):
    at = EX_AT if recv_ref.shape[1] > 16 else 0
    return recv_ref[4 * layer + quarter, at : at + 16, :]


def gain_of(recv_ref, layer, which):
    return extra_of(recv_ref, layer, 0).astype(F32)[which : which + 1, :]


def rows_of(recv_ref, layer, t):
    return recv_ref[pl.ds(4 * layer + 2 * t, 2), 0:128, :].reshape(TILE, 512).astype(F32)


def codes_of(recv_ref, layer, t, lane):
    cols = []
    for i in range(2):
        extra = extra_of(recv_ref, layer, 2 * t + i).astype(F32)
        cols.append(row_to_col(extra[CODE_ROW : CODE_ROW + 1, lane : lane + 128]))
    return jnp.concatenate(cols, 0)


def other_kv(recv_ref, layer, quarter):
    packed = recv_ref[4 * layer + quarter, 128:160, :]
    return jnp.concatenate([packed[:, 128 * c : 128 * c + 128] for c in range(4)], 0)


def routing(query_rows, router_block, code):
    second = jnp.floor(code * 0.125)
    first = code - 8.0 * second
    e0, e1 = first.astype(jnp.int32), second.astype(jnp.int32)
    logits = nt(query_rows, router_block)
    lanes = lax.broadcasted_iota(jnp.int32, logits.shape, 1)
    l0 = jnp.sum(jnp.where(lanes == e0 + ROUTER_AT, logits, 0.0), 1, keepdims=True)
    l1 = jnp.sum(jnp.where(lanes == e1 + ROUTER_AT, logits, 0.0), 1, keepdims=True)
    top = jnp.maximum(l0, l1)
    x0, x1 = jnp.exp(l0 - top), jnp.exp(l1 - top)
    total = x0 + x1
    owners = lax.broadcasted_iota(jnp.int32, (code.shape[0], 512), 1) >> 6
    return e0, e1, x0 / total, x1 / total, owners == e0, owners == e1


def fold(wide, mask):
    kept = jnp.where(mask, wide, 0.0)
    return kept[:, 0:128] + kept[:, 128:256] + kept[:, 256:384] + kept[:, 384:512]


def spread(a0, a1, m0, m1):
    parts = []
    for c in range(4):
        cut = slice(128 * c, 128 * c + 128)
        parts.append(jnp.where(m0[:, cut], a0, jnp.where(m1[:, cut], a1, 0.0)))
    return jnp.concatenate(parts, 1).astype(BF)


def rounded(value):
    return value.astype(BF).astype(F32)


def start_pick(cond, yes, no, dst, sem):
    @pl.when(cond)
    def _():
        pltpu.make_async_copy(yes, dst, sem).start()

    @pl.when(jnp.logical_not(cond))
    def _():
        pltpu.make_async_copy(no, dst, sem).start()


class Loads:
    def __init__(self, sems):
        self.sems, self.used = sems, 0

    def start(self, cond, yes, no, dst):
        sem = self.sems.at[self.used]
        self.used += 1
        start_pick(cond, yes, no, dst, sem)
        return functools.partial(lambda a, b, c: pltpu.make_async_copy(a, b, c).wait(), yes, dst, sem)

    def plain(self, src, dst):
        sem = self.sems.at[self.used]
        self.used += 1
        copy = pltpu.make_async_copy(src, dst, sem)
        copy.start()
        return copy.wait

    def rows(self, cond, yes, no, at, dst, m):
        cut = pl.ds(at, 128)
        return [
            self.start(cond, yes[b].at[cut], no[b].at[cut], dst.at[pl.ds(128 * (m ^ b), 128)])
            for b in range(4)
        ]

    def pieces(self, cond, yes, no, dst, m):
        return [self.start(cond, yes[b], no[b], dst.at[m ^ b]) for b in range(4)]


def wait_all(waits):
    for wait in waits:
        wait()


def widen_kv(kv_ref, k2_ref, v2_ref):
    for j in range(4):
        kv = kv_ref[j].reshape(256, 128).astype(F32)
        turned = pltpu.roll(kv, 64, 1)
        low = lax.broadcasted_iota(jnp.int32, kv.shape, 1) < 64
        k2_ref[256 * j : 256 * j + 256, :] = jnp.where(low, kv, turned).astype(BF)
        v2_ref[256 * j : 256 * j + 256, :] = jnp.where(low, turned, kv).astype(BF)


def attend_tile(query_rows, route, w_qt, w_o, k2, v2, allowed):
    e0, e1, g0, g1, m0, m1 = route
    q_all = nt(query_rows, w_qt) * 0.125
    queries = jnp.concatenate([fold(q_all, m0), fold(q_all, m1)], 0).astype(BF)
    scores = nt(queries, k2)
    scores = jnp.concatenate(
        [
            jnp.where(allowed, scores[0:TILE], MASK_VALUE),
            jnp.where(allowed, scores[TILE:], MASK_VALUE),
        ],
        0,
    )
    top = jnp.max(scores, 1, keepdims=True)
    weights = jnp.exp(scores - top)
    total = jnp.sum(weights, 1, keepdims=True)
    mixed = nn(weights.astype(BF), v2) / total
    log_total = top + jnp.log(total)
    gated = spread(rounded(g0) * mixed[0:TILE], rounded(g1) * mixed[TILE:], m0, m1)
    return nn(gated, w_o), mixed, col_to_row(log_total)


def attend_back_tile(
    t, upstream, query_rows, route, mixed, log_row, w_qt, w_o, router_block, router_lane, k2, v2,
    allowed_t, grad_k, grad_v, gated_ref, dz_ref, dq_ref, dlog_ref,
):
    e0, e1, g0, g1, m0, m1 = route
    q_all = nt(query_rows, w_qt) * 0.125
    queries = jnp.concatenate([fold(q_all, m0), fold(q_all, m1)], 0).astype(BF)
    dz = upstream.astype(BF)
    dg_all = nt(dz, w_o)
    dgated0, dgated1 = fold(dg_all, m0), fold(dg_all, m1)
    r0, r1 = rounded(g0), rounded(g1)
    mixed0, mixed1 = mixed[0:TILE], mixed[TILE:]
    gated_ref[t] = spread(r0 * mixed0, r1 * mixed1, m0, m1)
    dz_ref[t] = dz
    dgate0 = rounded(jnp.sum(mixed0 * dgated0, 1, keepdims=True))
    dgate1 = rounded(jnp.sum(mixed1 * dgated1, 1, keepdims=True))
    do0, do1 = (r0 * dgated0).astype(BF), (r1 * dgated1).astype(BF)
    grad_mixed = jnp.concatenate([do0, do1], 0)
    inner_row = jnp.concatenate(
        [
            col_to_row(jnp.sum(do0.astype(F32) * mixed0, 1, keepdims=True)),
            col_to_row(jnp.sum(do1.astype(F32) * mixed1, 1, keepdims=True)),
        ],
        1,
    )
    scores = nt(k2, queries)
    scores = jnp.concatenate(
        [
            jnp.where(allowed_t, scores[:, 0:TILE], MASK_VALUE),
            jnp.where(allowed_t, scores[:, TILE:], MASK_VALUE),
        ],
        1,
    )
    probs = jnp.exp(scores - log_row)
    grad_probs = nt(v2, grad_mixed)
    grad_scores = (probs * (grad_probs - inner_row)).astype(BF)
    grad_v[...] += nn(probs.astype(BF), grad_mixed)
    grad_k[...] += nn(grad_scores, queries)
    grad_q = rounded(tn(grad_scores, k2) * 0.125)
    dq_all = spread(grad_q[0:TILE], grad_q[TILE:], m0, m1)
    dq_ref[t] = dq_all
    grad_rows = nn(dq_all, w_qt)
    mean_grad = g0 * dgate0 + g1 * dgate1
    dc0, dc1 = g0 * (dgate0 - mean_grad), g1 * (dgate1 - mean_grad)
    lanes = lax.broadcasted_iota(jnp.int32, (TILE, 16), 1)
    dlog = jnp.where(lanes == e0 + ROUTER_AT, dc0, 0.0) + jnp.where(
        lanes == e1 + ROUTER_AT, dc1, 0.0
    )
    wide = lax.broadcasted_iota(jnp.int32, (TILE, 128), 1)
    dlog_ref[t] = (
        jnp.where(wide == e0 + router_lane, dc0, 0.0)
        + jnp.where(wide == e1 + router_lane, dc1, 0.0)
    ).astype(BF)
    return grad_rows + nn(dlog.astype(BF), router_block)


def query_places(t, sec, dims, along):
    local = lax.broadcasted_iota(jnp.int32, dims, along)
    return (512 * t + 128 * sec + local + (local & ~127)).astype(F32)


def allowed_rows(t, sec, ends_q, ends_k, causal):
    query_at = query_places(t, sec, (TILE, 1), 0)
    key_at = lax.broadcasted_iota(jnp.int32, (1, 1024), 1).astype(F32)
    allowed = segments(query_at, ends_q) == segments(key_at, ends_k)
    if causal:
        allowed = allowed & (key_at <= query_at)
    return allowed


def key_segments_t(ends_k, segk_ref):
    for j in range(8):
        at = lax.broadcasted_iota(jnp.int32, (128, TILE), 0).astype(F32) + 128.0 * j
        segk_ref[128 * j : 128 * j + 128, :] = segments(at, ends_k)


def allowed_cols(t, sec, ends_q, segk_ref, causal):
    query_at = query_places(t, sec, (1, TILE), 1)
    allowed = segk_ref[...] == segments(query_at, ends_q)
    if causal:
        key_at = lax.broadcasted_iota(jnp.int32, (1024, TILE), 0).astype(F32)
        allowed = allowed & (key_at <= query_at)
    return allowed


def fold_kv(grad_k, grad_v, sec, own_ref, send_ref):
    for j in range(4):
        k = grad_k[256 * j : 256 * j + 256, :]
        v = grad_v[256 * j : 256 * j + 256, :]
        k = k + pltpu.roll(k, 64, 1)
        v = v + pltpu.roll(v, 64, 1)
        low = lax.broadcasted_iota(jnp.int32, k.shape, 1) < 64
        both = jnp.where(low, k, v)
        first, second = both[0:128], both[128:256]
        own_ref[j] = jnp.where(sec == 0, first, second)
        send_ref[j] = jnp.where(sec == 0, second, first).astype(send_ref.dtype)


def split_halves(value, sec, keep_ref, send_ref, m, lane):
    upper, lower = value[0:256], value[256:512]
    cut = slice(lane, lane + value.shape[1])
    keep_ref[m, :, cut] = jnp.where(sec == 0, upper, lower).astype(BF)
    send_ref[m, :, cut] = jnp.where(sec == 0, lower, upper).astype(BF)


def split_flat(value, sec, keep_ref, send_ref, lane):
    upper, lower = value[0:256], value[256:512]
    cut = slice(lane, lane + value.shape[1])
    keep_ref[:, cut] = jnp.where(sec == 0, upper, lower).astype(BF)
    send_ref[:, cut] = jnp.where(sec == 0, lower, upper).astype(BF)


def turned_rows(value):
    return value.astype(F32).T.astype(BF)


def flat(ref):
    return ref[...].reshape(512, ref.shape[-1])


def attention_weight_grads(first_t, gated_ref, dz_ref, dq_ref, sec, keep_ref, send_ref, lane):
    grad_q = nn(first_t, flat(dq_ref))
    grad_o = nn(turned_rows(flat(dz_ref)), flat(gated_ref))
    for b in range(4):
        cut = slice(128 * b, 128 * b + 128)
        split_halves(grad_q[:, cut], sec, keep_ref, send_ref, b, lane)
        split_halves(grad_o[:, cut], sec, keep_ref, send_ref, b, lane + 128)


def router_grads(dlog_ref, rows_ref):
    turned = flat(dlog_ref).astype(F32).T.astype(BF)
    return nn(turned, flat(rows_ref))[0:32]


def gelu_parts(pre):
    cdf = 0.5 * (1.0 + lax.erf(pre * 0.7071067811865476))
    slope = cdf + pre * (jnp.exp(-0.5 * pre * pre) * 0.3989422804014327)
    return pre * cdf, slope


def own_self_kv(recv_ref, layer, sec, w_kv, kv_ref):
    gain = gain_of(recv_ref, layer, 0)
    for t in range(2):
        first = norm_of(rows_of(recv_ref, layer, t), gain)[0].astype(BF)
        kv = nn(first, w_kv).astype(BF)
        for i in range(2):
            j = 2 * t + i
            kv_ref[j, sec] = kv[128 * i : 128 * i + 128]
            kv_ref[j, 1 - sec] = other_kv(recv_ref, layer, j)


def cross_kv(kvm_ref, kvo_ref, sec, kv_s):
    for j in range(4):
        kv_s[j, sec] = kvm_ref[j]
        kv_s[j, 1 - sec] = kvo_ref[j]


def pack_kernel(
    ready, len_ref, x_ref, gain_ref, w_kv_ref, own_ref, cross_ref, router_ref, send_ref, extra_s
):
    ready()
    gain = gain_ref[0:1, :].astype(F32)
    w_kv = w_kv_ref[...]
    extra_s[...] = jnp.zeros_like(extra_s)
    extra_s[0:3, :] = gain_ref[...].astype(F32)
    extra_s[ROUTER_AT : ROUTER_AT + 8, :] = router_ref[...].astype(F32)
    lanes = lax.broadcasted_iota(jnp.int32, (1, 512), 1)
    for i in range(4):
        first = norm_of(x_ref[i].astype(F32), gain)[0].astype(BF)
        kv = nn(first, w_kv).astype(BF)
        row = jnp.zeros((1, 512), jnp.int32)
        for k in range(8):
            length = len_ref[i, k]
            row = jnp.where(lanes == k, length >> 5, row)
            row = jnp.where(lanes == 128 + k, length & 31, row)
        extra_s[LEN_ROW : LEN_ROW + 1, :] = row.astype(F32)
        own, cross = own_ref[i], cross_ref[i]
        own_code = (own[0:1] + 8 * own[1:2]).astype(F32)
        cross_code = (cross[0:1] + 8 * cross[1:2]).astype(F32)
        for half in range(2):
            to = 4 * half + i
            here = slice(128 * half, 128 * half + 128)
            send_ref[to, 0:128, :] = x_ref[i, here, :]
            far = kv[128 * (1 - half) : 128 * (1 - half) + 128]
            send_ref[to, 128:160, :] = jnp.concatenate(
                [far[32 * c : 32 * c + 32] for c in range(4)], 1
            )
            extra_s[CODE_ROW : CODE_ROW + 1, 0:128] = own_code[:, here]
            extra_s[CODE_ROW : CODE_ROW + 1, 128:256] = cross_code[:, here]
            send_ref[to, EX_AT : EX_AT + 16, :] = extra_s[...].astype(BF)


def self_fwd_kernel(ready, ids_ref, recv_ref, *refs):
    wa_own, wa_oth, kvw_own, kvw_oth = refs[:4], refs[4:8], refs[8], refs[9]
    h1_ref, g1_ref, mixed_e, mixed_d, log_e, log_d, meta_ref = refs[10:17]
    wq, wo, wkv, kv_s, k2, v2, sems = refs[17:]
    sec, m = ids_ref[0], ids_ref[1]
    loads = Loads(sems)
    kv_waits = [loads.start(sec == i, kvw_own, kvw_oth, wkv.at[i]) for i in range(2)]
    waits = []
    for layer in range(2):
        waits += loads.rows(sec == layer, wa_own, wa_oth, 0, wq.at[layer], m)
        waits += loads.rows(sec == layer, wa_own, wa_oth, 128, wo.at[layer], m)
    ready()
    meta_ref[...] = recv_ref[:, EX_AT : EX_AT + 16, :]
    wait_all(kv_waits)
    for layer in range(2):
        own_self_kv(recv_ref, layer, sec, wkv[layer], kv_s)
        widen_kv(kv_s, k2.at[layer], v2.at[layer])
    wait_all(waits)
    ends = [ends_of(extra_of(recv_ref, layer, 0).astype(F32)) for layer in range(2)]

    def tile(t, carry):
        for layer, after_ref, mixed_ref, log_ref in (
            (0, h1_ref, mixed_e, log_e),
            (1, g1_ref, mixed_d, log_d),
        ):
            rows = rows_of(recv_ref, layer, t)
            first = norm_of(rows, gain_of(recv_ref, layer, 0))[0].astype(BF)
            route = routing(first, extra_of(recv_ref, layer, 0), codes_of(recv_ref, layer, t, 0))
            allowed = allowed_rows(t, sec, ends[layer], ends[layer], layer == 1)
            out, mixed, row_log = attend_tile(
                first, route, wq[layer], wo[layer], k2[layer], v2[layer], allowed
            )
            after_ref[t] = rows + out
            mixed_ref[t] = mixed
            log_ref[t] = row_log
        return carry

    lax.fori_loop(0, 2, tile, 0)


def enc_ffn_kernel(ready, ids_ref, recv_ref, h1_ref, kvc_ref, *refs):
    f_own, f_oth = refs[:4], refs[4:8]
    h2_ref, mem_ref, kvm_ref, w_in, w_out, third_s, sems = refs[8:]
    low, m = ids_ref[0] == 0, ids_ref[1]
    loads = Loads(sems)
    waits = loads.pieces(low, f_own, f_oth, w_in, m) + loads.pieces(low, f_oth, f_own, w_out, m)
    ready()
    for t in range(2):
        h2_ref[t] = h1_ref[t]
        third_s[t] = norm_of(h1_ref[t], gain_of(recv_ref, 0, 2))[0].astype(BF)
    wait_all(waits)

    def chunk(c, carry):
        pre = nn(flat(third_s), w_in[c])
        hidden = (0.5 * pre * (1.0 + lax.erf(pre * 0.7071067811865476))).astype(BF)
        h2_ref[...] += nn(hidden, w_out[c]).reshape(2, TILE, 512)
        return carry

    lax.fori_loop(0, 4, chunk, 0)
    for t in range(2):
        memory = norm_of(h2_ref[t], gain_of(recv_ref, 0, 1))[0].astype(BF)
        mem_ref[t] = memory
        kv = nn(memory, kvc_ref[...]).astype(BF)
        kvm_ref[2 * t] = kv[0:128]
        kvm_ref[2 * t + 1] = kv[128:256]


def cross_fwd_kernel(
    ready, ids_ref, recv_ref, g1_ref, kvm_ref, kvo_ref, rc_ref, *refs
):
    wa_own, wa_oth = refs[:4], refs[4:8]
    g2_ref, mixed_ref, log_ref, wq, wo, kv_s, k2, v2, sems = refs[8:]
    sec, m = ids_ref[0], ids_ref[1]
    loads = Loads(sems)
    waits = loads.rows(sec == 0, wa_own, wa_oth, 256, wq, m)
    waits += loads.rows(sec == 0, wa_oth, wa_own, 256, wo, m)
    ready()
    cross_kv(kvm_ref, kvo_ref, sec, kv_s)
    widen_kv(kv_s, k2, v2)
    wait_all(waits)
    ends_k = ends_of(extra_of(recv_ref, 0, 0).astype(F32))
    ends_q = ends_of(extra_of(recv_ref, 1, 0).astype(F32))

    def tile(t, carry):
        before = g1_ref[t]
        second = norm_of(before, gain_of(recv_ref, 1, 1))[0].astype(BF)
        route = routing(second, rc_ref[...], codes_of(recv_ref, 1, t, 128))
        allowed = allowed_rows(t, sec, ends_q, ends_k, False)
        out, mixed, row_log = attend_tile(second, route, wq[...], wo[...], k2[...], v2[...], allowed)
        g2_ref[t] = before + out
        mixed_ref[t] = mixed
        log_ref[t] = row_log
        return carry

    lax.fori_loop(0, 2, tile, 0)


def ffn_both(c, third_s, third_t, dy_s, dy_t, w_in, w_out, dthird, sec, keep_ref, send_ref):
    pre = nn(flat(third_s), w_in[c])
    hidden, slope = gelu_parts(pre)
    hidden = hidden.astype(BF)
    dpre = (nt(flat(dy_s), w_out[c]) * slope).astype(BF)
    dthird[...] += nt(dpre, w_in[c])
    split_halves(nn(third_t[...], dpre), sec, keep_ref, send_ref, c, 0)
    split_halves(nn(dy_t[...], hidden), sec, keep_ref, send_ref, c, 512)
    return hidden


def dec_ffn_kernel(ready, ids_ref, recv_ref, g2_ref, mem_ref, cot_in, *refs):
    f_own, f_oth = refs[:4], refs[4:8]
    outs_ref, dg2_ref, gain_ref, keep_ref, send_ref = refs[8:13]
    w_in, w_out, cot_s, third_s, third_t, cot_t, acc, dthird, sems = refs[13:]
    sec, m = ids_ref[0], ids_ref[1]
    low = sec == 0
    loads = Loads(sems)
    cot_waits = [loads.plain(cot_in.at[i], cot_s.at[i]) for i in range(4)]
    waits = loads.pieces(low, f_own, f_oth, w_in, m) + loads.pieces(low, f_oth, f_own, w_out, m)
    ready()
    for t in range(2):
        acc[t] = g2_ref[t]
        third_s[t] = norm_of(g2_ref[t], gain_of(recv_ref, 1, 2))[0].astype(BF)
        outs_ref[2 * t : 2 * t + 2] = mem_ref[t].reshape(2, 128, 512)
    third_t[...] = turned_rows(flat(third_s))
    wait_all(cot_waits)
    cot_t[...] = turned_rows(flat(cot_s))
    dthird[...] = jnp.zeros_like(dthird)
    wait_all(waits)

    def chunk(c, carry):
        hidden = ffn_both(
            c, third_s, third_t, cot_s, cot_t, w_in, w_out, dthird, sec, keep_ref, send_ref
        )
        acc[...] += nn(hidden, w_out[c]).reshape(2, TILE, 512)
        return carry

    lax.fori_loop(0, 4, chunk, 0)
    total = jnp.zeros((1, 512), F32)
    gain = gain_of(recv_ref, 1, 2)
    for t in range(2):
        outs_ref[4 + 2 * t : 6 + 2 * t] = acc[t].astype(BF).reshape(2, 128, 512)
        unused_out, unit, scaled = norm_of(g2_ref[t], gain)
        back, gain_grad = norm_back(dthird[TILE * t : TILE * t + TILE, :], unit, scaled, gain)
        dg2_ref[t] = cot_s[2 * t : 2 * t + 2].reshape(TILE, 512).astype(F32) + back
        total = total + gain_grad
    gain_ref[...] = total


def cross_back_kernel(
    ready, ids_ref, recv_ref, g1_ref, dg2_ref, mixed_ref, log_ref, kvm_ref, kvo_ref, rc_ref, *refs
):
    wa_own, wa_oth = refs[:4], refs[4:8]
    dg1_ref, gain_ref, own_ref, send_ref, router_ref, keepw_ref, sendw_ref = refs[8:15]
    wq, wo, kv_s, k2, v2, segk, grad_k, grad_v, second_s, gated_s, dz_s, dq_s, dlog_s, sems = refs[15:]
    sec, m = ids_ref[0], ids_ref[1]
    loads = Loads(sems)
    waits = loads.rows(sec == 0, wa_own, wa_oth, 256, wq, m)
    waits += loads.rows(sec == 0, wa_oth, wa_own, 256, wo, m)
    ready()
    cross_kv(kvm_ref, kvo_ref, sec, kv_s)
    widen_kv(kv_s, k2, v2)
    ends_k = ends_of(extra_of(recv_ref, 0, 0).astype(F32))
    ends_q = ends_of(extra_of(recv_ref, 1, 0).astype(F32))
    key_segments_t(ends_k, segk)
    grad_k[...] = jnp.zeros_like(grad_k)
    grad_v[...] = jnp.zeros_like(grad_v)
    wait_all(waits)

    def tile(t, total):
        gain = gain_of(recv_ref, 1, 1)
        second, unit, scaled = norm_of(g1_ref[t], gain)
        second = second.astype(BF)
        second_s[t] = second
        route = routing(second, rc_ref[...], codes_of(recv_ref, 1, t, 128))
        allowed = allowed_cols(t, sec, ends_q, segk, False)
        grad_rows = attend_back_tile(
            t, dg2_ref[t], second, route, mixed_ref[t], log_ref[t], wq[...], wo[...], rc_ref[...],
            ROUTER_LANES[2], k2[...], v2[...], allowed, grad_k, grad_v, gated_s, dz_s, dq_s, dlog_s,
        )
        back, gain_grad = norm_back(grad_rows, unit, scaled, gain)
        dg1_ref[t] = dg2_ref[t] + back
        return total + gain_grad

    gain_ref[...] = lax.fori_loop(0, 2, tile, jnp.zeros((1, 512), F32))
    fold_kv(grad_k, grad_v, sec, own_ref, send_ref)
    router_ref[...] = router_grads(dlog_s, second_s)
    attention_weight_grads(
        turned_rows(flat(second_s)), gated_s, dz_s, dq_s, sec, keepw_ref, sendw_ref, 0
    )


def self_back_kernel(layer, ready, ids_ref, recv_ref, up_ref, mixed_ref, log_ref, *refs):
    wa_own, wa_oth, kvw_own, kvw_oth = refs[:4], refs[4:8], refs[8], refs[9]
    refs = refs[10:]
    if layer == 1:
        before, refs = refs[:2], refs[2:]
    dfirst_ref, own_ref, send_ref, router_ref, keepw_ref, sendw_ref = refs[:6]
    wq, wo, wkv, kv_s, k2, v2, segk, grad_k, grad_v = refs[6:15]
    first_s, gated_s, dz_s, dq_s, dlog_s, sems = refs[15:]
    sec, m = ids_ref[0], ids_ref[1]
    mine = sec == layer
    loads = Loads(sems)
    kv_wait = loads.start(mine, kvw_own, kvw_oth, wkv)
    waits = loads.rows(mine, wa_own, wa_oth, 0, wq, m) + loads.rows(mine, wa_own, wa_oth, 128, wo, m)
    lane = 0
    if layer == 1:
        lane = 256
        for src, dst in zip(before, (keepw_ref, sendw_ref)):
            waits.append(loads.plain(src, dst.at[:, :, pl.ds(0, 256)]))
    ready()
    ends = ends_of(extra_of(recv_ref, layer, 0).astype(F32))
    key_segments_t(ends, segk)
    grad_k[...] = jnp.zeros_like(grad_k)
    grad_v[...] = jnp.zeros_like(grad_v)
    kv_wait()
    own_self_kv(recv_ref, layer, sec, wkv[...], kv_s)
    widen_kv(kv_s, k2, v2)
    wait_all(waits)
    router_block = extra_of(recv_ref, layer, 0)

    def tile(t, carry):
        first = norm_of(rows_of(recv_ref, layer, t), gain_of(recv_ref, layer, 0))[0].astype(BF)
        first_s[t] = first
        route = routing(first, router_block, codes_of(recv_ref, layer, t, 0))
        allowed = allowed_cols(t, sec, ends, segk, layer == 1)
        dfirst_ref[t] = attend_back_tile(
            t, up_ref[t], first, route, mixed_ref[t], log_ref[t], wq[...], wo[...], router_block,
            ROUTER_LANES[layer], k2[...], v2[...], allowed, grad_k, grad_v, gated_s, dz_s, dq_s,
            dlog_s,
        )
        return carry

    lax.fori_loop(0, 2, tile, 0)
    fold_kv(grad_k, grad_v, sec, own_ref, send_ref)
    router_ref[...] = router_grads(dlog_s, first_s)
    attention_weight_grads(
        turned_rows(flat(first_s)), gated_s, dz_s, dq_s, sec, keepw_ref, sendw_ref, lane
    )


def enc_ffn_back_kernel(
    ready, ids_ref, recv_ref, h1_ref, h2_ref, own_ref, come_ref, kvc_ref, *refs
):
    f_own, f_oth = refs[:4], refs[4:8]
    dh1_ref, gain_ref, gain2_ref, keep_ref, send_ref = refs[8:13]
    w_in, w_out, third_s, third_t, dy_s, dy_t, dthird, sems = refs[13:]
    sec, m = ids_ref[0], ids_ref[1]
    low = sec == 0
    loads = Loads(sems)
    waits = loads.pieces(low, f_own, f_oth, w_in, m) + loads.pieces(low, f_oth, f_own, w_out, m)
    ready()
    total = jnp.zeros((1, 512), F32)
    gain = gain_of(recv_ref, 0, 1)
    for t in range(2):
        dkv = (own_ref[2 * t : 2 * t + 2] + come_ref[2 * t : 2 * t + 2].astype(F32)).astype(BF)
        dmem = rounded(nt(dkv.reshape(TILE, 128), kvc_ref[...]))
        unused_out, unit, scaled = norm_of(h2_ref[t], gain)
        back, gain_grad = norm_back(dmem, unit, scaled, gain)
        dh1_ref[t] = back
        dy_s[t] = back.astype(BF)
        third_s[t] = norm_of(h1_ref[t], gain_of(recv_ref, 0, 2))[0].astype(BF)
        total = total + gain_grad
    gain_ref[...] = total
    third_t[...] = turned_rows(flat(third_s))
    dy_t[...] = turned_rows(flat(dy_s))
    dthird[...] = jnp.zeros_like(dthird)
    wait_all(waits)

    def chunk(c, carry):
        ffn_both(c, third_s, third_t, dy_s, dy_t, w_in, w_out, dthird, sec, keep_ref, send_ref)
        return carry

    lax.fori_loop(0, 4, chunk, 0)
    total = jnp.zeros((1, 512), F32)
    gain = gain_of(recv_ref, 0, 2)
    for t in range(2):
        unused_out, unit, scaled = norm_of(h1_ref[t], gain)
        back, gain_grad = norm_back(dthird[TILE * t : TILE * t + TILE, :], unit, scaled, gain)
        dh1_ref[t] += back
        total = total + gain_grad
    gain2_ref[...] = total


def finish_rows(layer, recv_ref, up_ref, df_ref, own_ref, come_ref, wkv, first_s, out_ref, at):
    total = jnp.zeros((1, 512), F32)
    gain = gain_of(recv_ref, layer, 0)
    dkvs = []
    for t in range(2):
        first, unit, scaled = norm_of(rows_of(recv_ref, layer, t), gain)
        first_s[t] = first.astype(BF)
        dkv = (own_ref[2 * t : 2 * t + 2] + come_ref[2 * t : 2 * t + 2].astype(F32)).astype(BF)
        dkv = dkv.reshape(TILE, 128)
        dkvs.append(dkv)
        back, gain_grad = norm_back(df_ref[t] + nt(dkv, wkv), unit, scaled, gain)
        dx = (up_ref[t] + back).astype(BF)
        for i in range(2):
            out_ref[at + 2 * t + i, 0:128, :] = dx[128 * i : 128 * i + 128]
        total = total + gain_grad
    grad = nn(turned_rows(flat(first_s)), jnp.concatenate(dkvs, 0))
    return total, grad


def dec_finish_kernel(
    ready, ids_ref, recv_ref, up_ref, df_ref, own_ref, come_ref, own_c, come_c, mem_ref, kvw_own, kvw_oth,
    dx_ref, gain_ref, keep_ref, send_ref, wkv, first_s, sems,
):
    sec = ids_ref[0]
    wait = Loads(sems).start(sec == 1, kvw_own, kvw_oth, wkv)
    ready()
    dkv_c = (own_c[...] + come_c[...].astype(F32)).astype(BF).reshape(512, 128)
    split_flat(nn(turned_rows(flat(mem_ref)), dkv_c), sec, keep_ref, send_ref, 128)
    wait()
    gain_ref[...], grad = finish_rows(
        1, recv_ref, up_ref, df_ref, own_ref, come_ref, wkv[...], first_s, dx_ref, 0
    )
    split_flat(grad, sec, keep_ref, send_ref, 0)


def enc_finish_kernel(
    ready, ids_ref, recv_ref, up_ref, df_ref, own_ref, come_ref, dx1_ref, r0, r1, rc,
    gain_e1, gain_e2, gain_d0, gain_d1, gain_d2, kvw_own, kvw_oth,
    out_ref, wkv, first_s, misc, sems,
):
    sec = ids_ref[0]
    wait = Loads(sems).start(sec == 0, kvw_own, kvw_oth, wkv)
    ready()
    misc[...] = r0[...] + r1[...] + rc[...]
    out_ref[4:8, 0:128, :] = dx1_ref[...]
    wait()
    gain_e0, grad = finish_rows(
        0, recv_ref, up_ref, df_ref, own_ref, come_ref, wkv[...], first_s, out_ref, 0
    )
    rows = (gain_e0, gain_e1[...], gain_e2[...], gain_d0[...], gain_d1[...], gain_d2[...])
    for i, row in enumerate(rows):
        misc[GAIN_ROW + i : GAIN_ROW + i + 1, :] = row
    both = misc[...]
    for half in range(2):
        cut = slice(256 * half, 256 * half + 256)
        part = grad[cut].astype(BF)
        small = both[:, cut].astype(BF)
        block = jnp.concatenate(
            [
                jnp.concatenate([part[64 * c : 64 * c + 64] for c in range(4)], 1),
                jnp.concatenate([small[0:16], small[16:32]], 1),
            ],
            0,
        )
        for i in range(4):
            out_ref[4 * half + i, 128:208, :] = block


def add_kernel(keep_ref, come_ref, *outs):
    lane = 0
    for out_ref in outs:
        cut = slice(lane, lane + out_ref.shape[-1])
        out_ref[...] = keep_ref[:, :, cut] + come_ref[:, :, cut]
        lane += out_ref.shape[-1]


def add_pieces_kernel(flats, ready, ids_ref, *refs):
    ready()
    n = len(flats)
    keeps, comes, outs = refs[:n], refs[n : 2 * n], refs[2 * n :]
    m = ids_ref[1]
    for b in range(4):
        lane = 0
        for is_flat, keep, come in zip(flats, keeps, comes):
            left = keep[...] if is_flat else keep[m ^ b]
            right = come[...] if is_flat else come[m ^ b]
            width = keep.shape[-1]
            outs[b][:, lane : lane + width] = left + right
            lane += width


def sum_middle_kernel(ready, ids_ref, dec_a, dec_b, enc_ref, *refs):
    att, outs = refs[:4], refs[4:]
    ready()
    rows = outs[0].shape[0]
    d = ids_ref[2]
    for k in range(len(outs)):
        cut = pl.ds(pl.multiple_of((d ^ k) * rows, rows), rows)
        for ref, lane in ((enc_ref, 0), (dec_a, 1024), (dec_b, 1536)):
            total = ref[0, cut, :].astype(F32)
            for i in range(1, 4):
                total = total + ref[i, cut, :].astype(F32)
            outs[k][:, lane : lane + ref.shape[-1]] = total.astype(BF)
        total = att[0][cut, :].astype(F32)
        for part in att[1:]:
            total = total + part[cut, :].astype(F32)
        outs[k][:, 2048:2560] = total.astype(BF)


def place_kernel(ready, dx_ref, dx_out):
    ready()
    for i in range(4):
        for half in range(2):
            dx_out[i, half] = dx_ref[4 * half + i, 0:128, :].astype(F32)


def tail_kernel(ready, dx_ref, *refs):
    att_e, (out_ref,) = refs[:4], refs[4:]
    ready()
    total = att_e[0][...].astype(F32)
    for part in att_e[1:]:
        total = total + part[...].astype(F32)
    out_ref[:, 0:512] = total.astype(BF)
    small = dx_ref[0, 128:208, :].astype(F32)
    for i in range(1, 8):
        small = small + dx_ref[i, 128:208, :].astype(F32)
    for c in range(4):
        out_ref[64 * c : 64 * c + 64, 512:640] = small[0:64, 128 * c : 128 * c + 128].astype(BF)
    misc = jnp.concatenate([small[64:80, 0:256], small[64:80, 256:512]], 0)
    misc = jnp.concatenate([misc, jnp.zeros((96, 256), F32)], 0)
    out_ref[:, 640:768] = misc.T.astype(BF)


def final_kernel(ready, come_ref, *refs):
    middle, outs = refs[:4], refs[4:]
    ready()
    gains, router, query, keyval, output, inner, outer, router_c, query_c, keyval_c, output_c = outs
    small = come_ref[0].astype(F32)
    for i in range(1, 4):
        small = small + come_ref[i].astype(F32)
    wide = middle[0][...].astype(F32)
    for part in middle[1:]:
        wide = wide + part[...].astype(F32)
    for layer in range(2):
        inner[layer] = wide[:, 1024 * layer : 1024 * layer + 512]
        outer[layer] = wide[:, 1024 * layer + 512 : 1024 * layer + 1024]
    keyval[0], keyval[1] = small[:, 512:640], small[:, 256:384]
    keyval_c[...] = small[:, 384:512]
    for source, at, put_q, put_o in (
        (wide, 2048, query_c, output_c),
        (wide, 2304, query.at[1], output.at[1]),
        (small, 0, query.at[0], output.at[0]),
    ):
        turned = source[:, at + 128 : at + 256].T
        for e in range(2):
            put_q[e] = source[:, at + 64 * e : at + 64 * e + 64]
            put_o[e] = turned[64 * e : 64 * e + 64]
    misc = small[:, 640:768].T
    router[0], router[1], router_c[...] = misc[0:8], misc[8:16], misc[16:24]
    for i in range(3):
        gains[i, 0:1] = misc[24 + i : 25 + i]
        gains[i, 1:2] = misc[27 + i : 28 + i]


def shaped(dims, kind):
    return jax.ShapeDtypeStruct(dims, kind)


def cost_of(micros):
    return pl.CostEstimate(
        flops=int(micros * 1.1535e9), bytes_accessed=int(micros * 3.0e6), transcendentals=0
    )


def run(kernel, args, places, outs, scratch, micros, after=()):
    space = {
        "s": pl.BlockSpec(memory_space=pltpu.SMEM),
        "v": pl.BlockSpec(memory_space=pltpu.VMEM),
        "a": pl.BlockSpec(memory_space=pl.ANY),
    }
    large = [
        i for i, (p, a) in enumerate(zip(places, args)) if p == "v" and a.size * a.dtype.itemsize > LARGE
    ]
    places = ["a" if i in large else p for i, p in enumerate(places)]
    count, extra = len(args), len(after)
    copies = [pltpu.VMEM(args[i].shape, args[i].dtype) for i in large]

    def body(*refs):
        given, rest = list(refs[:count]), refs[count + extra :]
        if large:
            rest, held, sems = rest[: -len(large) - 1], rest[-len(large) - 1 : -1], rest[-1]
            moves = []
            for n, i in enumerate(large):
                moves.append(pltpu.make_async_copy(given[i], held[n], sems.at[n]))
                given[i] = held[n]
            for move in moves:
                move.start()
        else:
            moves = []

        def ready():
            for move in moves:
                move.wait()

        kernel(ready, *given, *rest)

    return pl.pallas_call(
        body,
        out_shape=outs,
        in_specs=[space[p] for p in places] + [space["a"]] * extra,
        out_specs=jax.tree.map(lambda _: space["v"], outs),
        scratch_shapes=scratch + copies + ([dma(len(large))] if large else []),
        compiler_params=pltpu.CompilerParams(vmem_limit_bytes=VMEM_LIMIT),
        cost_estimate=cost_of(micros),
    )(*args, *after)


def vm(*dims, kind=BF):
    return pltpu.VMEM(dims, kind)


def dma(count):
    return pltpu.SemaphoreType.DMA((count,))


def across(value, axes, size, by):
    return lax.ppermute(value, axes, [(i, i ^ by) for i in range(size)])


def swapped(value):
    return across(value, "section", 2, 1)


def gathered(value):
    return [value] + [across(value, "mp", 4, b) for b in range(1, 4)]


def to_all(value, axes):
    return lax.all_to_all(value, axes, split_axis=0, concat_axis=0, tiled=True)


def add_shares(keep, come, micros, after, parts=1):
    blocks, rows, width = keep.shape
    whole = pl.BlockSpec((1, rows, width), lambda i: (i, 0, 0))
    part = pl.BlockSpec((1, rows, width // parts), lambda i: (i, 0, 0))
    extra = len(after)
    return pl.pallas_call(
        lambda k, c, *rest: add_kernel(k, c, *rest[extra:]),
        out_shape=[shaped((blocks, rows, width // parts), BF)] * parts,
        grid=(blocks,),
        in_specs=[whole, whole] + [pl.BlockSpec(memory_space=pl.ANY)] * extra,
        out_specs=[part] * parts,
        cost_estimate=cost_of(micros),
    )(keep, come, *after)


def add_pieces(ids, keeps, comes, micros, after=()):
    flats = tuple(keep.ndim == 2 for keep in keeps)
    width = sum(keep.shape[-1] for keep in keeps)
    return run(
        functools.partial(add_pieces_kernel, flats),
        (ids, *keeps, *comes),
        "s" + "v" * (2 * len(keeps)),
        [shaped((256, width), BF)] * 4,
        [],
        micros,
        after=after,
    )


def mp_exchange(pieces):
    return [pieces[0]] + [across(pieces[b], "mp", 4, b) for b in range(1, 4)]


def dp_exchange(pieces):
    return [pieces[0]] + [across(pieces[k], "dp", 4, k) for k in range(1, 4)]


def gated(values, after):
    anywhere = pl.BlockSpec(memory_space=pl.ANY)
    count = len(values)
    return pl.pallas_call(
        lambda *refs: None,
        out_shape=[shaped(v.shape, v.dtype) for v in values],
        in_specs=[anywhere] * (count + len(after)),
        out_specs=[anywhere] * count,
        input_output_aliases={i: i for i in range(count)},
        cost_estimate=cost_of(0.2),
    )(*values, *after)


def per_device(
    inputs,
    lengths,
    routes_self,
    routes_cross,
    gains,
    router_self,
    query_self,
    keyval_self,
    output_self,
    ffn_in,
    ffn_out,
    router_cross,
    query_cross,
    keyval_cross,
    output_cross,
    cotangent,
):
    sec, m, d = lax.axis_index("section"), lax.axis_index("mp"), lax.axis_index("dp")
    low = sec == 0
    ids = jnp.stack([sec, m, d]).astype(jnp.int32)
    sem = dma(24)
    rowgroup = ("section", "mp")

    q_rows = query_self[0].transpose(0, 2, 1).reshape(128, 512)
    o_rows = output_self[0].reshape(128, 512)
    c_rows = jnp.where(
        low, query_cross.transpose(0, 2, 1).reshape(128, 512), output_cross.reshape(128, 512)
    )
    wa = jnp.concatenate([q_rows, o_rows, c_rows], 0)
    wa_own = gathered(wa)
    w_in, w_out = ffn_in[0], ffn_out[0]
    half_come = swapped(jnp.where(low, w_out, w_in))
    enc_half = jnp.where(low, w_in, half_come)
    dec_half = jnp.where(low, half_come, w_out)
    kvw_own = keyval_self[0]
    kvw_oth = swapped(kvw_own)
    router_c = jnp.concatenate([jnp.zeros((8, 512), BF), router_cross.T], 0)

    packed = run(
        pack_kernel,
        (
            lengths[0, :, 0],
            inputs[0, :, 0],
            gains[0],
            keyval_self[0],
            routes_self[0, :, 0].transpose(0, 2, 1),
            routes_cross[:, 0].transpose(0, 2, 1),
            router_self[0].T,
        ),
        "svvvvvv",
        shaped((8, 176, 512), BF),
        [vm(16, 512, kind=F32)],
        3.4,
        after=(wa, enc_half, dec_half),
    )
    (packed,) = gated([packed], wa_own[1:])
    recv = to_all(packed, rowgroup)
    wa_oth = [swapped(piece) for piece in wa_own]
    (enc_half,) = gated([enc_half], [packed])
    enc_own = gathered(enc_half)
    cot_in = lax.dynamic_index_in_dim(cotangent[:, 0].reshape(4, 2, 128, 512), sec, 1, False)

    act = shaped((2, TILE, 512), F32)
    actb = shaped((2, TILE, 512), BF)
    mixed_s = shaped((2, 2 * TILE, 128), F32)
    log_s = shaped((2, 1, 2 * TILE), F32)
    kv_b = shaped((4, 128, 128), BF)
    kv_f = shaped((4, 128, 128), F32)
    row_s = shaped((1, 512), F32)
    ffn_g = shaped((4, 256, 1024), BF)
    router_s = shaped((32, 512), F32)
    wide = [vm(512, 512), vm(512, 512)]
    kv_scratch = [vm(4, 2, 128, 128), vm(1024, 128), vm(1024, 128)]
    back_scratch = [
        vm(1024, TILE, kind=F32), vm(1024, 128, kind=F32), vm(1024, 128, kind=F32),
        vm(2, TILE, 512), vm(2, TILE, 512), vm(2, TILE, 512), vm(2, TILE, 512), vm(2, TILE, 128),
    ]
    ffn_w = [vm(4, 512, 512), vm(4, 512, 512)]

    h1, g1, mixed_e, mixed_d, log_e, log_d, meta = run(
        self_fwd_kernel,
        (ids, recv, *wa_own, *wa_oth, kvw_own, kvw_oth),
        "sv" + "a" * 10,
        (act, act, mixed_s, mixed_s, log_s, log_s, shaped((8, 16, 512), BF)),
        [vm(2, 512, 512), vm(2, 512, 512), vm(2, 512, 128), vm(4, 2, 128, 128)]
        + [vm(2, 1024, 128), vm(2, 1024, 128), sem],
        0.3,
    )
    enc_own[1:] = gated(enc_own[1:], [h1])
    enc_oth = [swapped(piece) for piece in enc_own]
    (dec_half,) = gated([dec_half], [enc_own[1]])
    dec_own = gathered(dec_half)
    (cot_in,) = gated([cot_in], [enc_own[1]])
    cot = to_all(cot_in, "mp")
    h2, memory, kvm = run(
        enc_ffn_kernel,
        (ids, meta, h1, keyval_cross, *enc_own, *enc_oth),
        "svvv" + "a" * 8,
        (act, actb, kv_b),
        ffn_w + [vm(2, TILE, 512), sem],
        4.0,
        after=(dec_half, cot_in),
    )
    kvm_oth = swapped(kvm)
    g2, mixed_c, log_c = run(
        cross_fwd_kernel,
        (ids, meta, g1, kvm, kvm_oth, router_c, *wa_own, *wa_oth),
        "svvvvv" + "a" * 8,
        (act, mixed_s, log_s),
        wide + kv_scratch + [sem],
        0.3,
        after=(cot,),
    )
    dec_own[1:] = gated(dec_own[1:], [g2])
    dec_oth = [swapped(piece) for piece in dec_own]
    outs, dg2, gain_d2, keep_d, send_d = run(
        dec_ffn_kernel,
        (ids, meta, g2, memory, cot, *dec_own, *dec_oth),
        "svvva" + "a" * 8,
        (shaped((8, 128, 512), BF), act, row_s, ffn_g, ffn_g),
        ffn_w
        + [vm(4, 128, 512), vm(2, TILE, 512), vm(512, 512), vm(512, 512)]
        + [vm(2, TILE, 512, kind=F32), vm(512, 512, kind=F32), sem],
        15.0,
    )
    come_d = swapped(send_d)
    outs_come = to_all(outs, rowgroup)
    att_g = shaped((4, 256, 256), BF)
    flat_g = shaped((256, 256), BF)
    dg1, gain_d1, own_c, sendkv_c, router_cg, keep_wc, send_wc = run(
        cross_back_kernel,
        (ids, meta, g1, dg2, mixed_c, log_c, kvm, kvm_oth, router_c, *wa_own, *wa_oth),
        "svvvvvvvv" + "a" * 8,
        (act, row_s, kv_f, kv_b, router_s, att_g, att_g),
        wide + kv_scratch + back_scratch + [sem],
        13.0,
    )
    comekv_c = swapped(sendkv_c)
    dec_a, dec_b = add_shares(keep_d, come_d, 4.0, (dg1, outs_come), 2)
    dh1, gain_e1, gain_e2, keep_e, send_e = run(
        enc_ffn_back_kernel,
        (ids, meta, h1, h2, own_c, comekv_c, keyval_cross, *enc_own, *enc_oth),
        "svvvvvv" + "a" * 8,
        (act, row_s, row_s, ffn_g, ffn_g),
        ffn_w
        + [vm(2, TILE, 512), vm(512, 512), vm(2, TILE, 512), vm(512, 512)]
        + [vm(512, 512, kind=F32), sem],
        13.4,
        after=(dec_a,),
    )
    dec_a = to_all(dec_a, "mp")
    (dec_b,) = gated([dec_b], [dec_a])
    dec_b = to_all(dec_b, "mp")
    come_e = swapped(send_e)
    self_scratch = wide + [vm(512, 128)] + kv_scratch + back_scratch + [sem]
    att_dg = shaped((4, 256, 512), BF)
    df1, own_1, sendkv_1, router_1g, keep_w1, send_w1 = run(
        functools.partial(self_back_kernel, 1),
        (
            ids, recv, dg1, mixed_d, log_d, *wa_own, *wa_oth, kvw_own, kvw_oth, keep_wc, send_wc,
        ),
        "svvvv" + "a" * 12,
        (act, kv_f, kv_b, router_s, att_dg, att_dg),
        self_scratch,
        12.2,
        after=(dh1, dec_a),
    )
    comekv_1 = swapped(sendkv_1)
    come_w1 = swapped(send_w1)
    (ffn_e,) = add_shares(keep_e, come_e, 4.0, (df1, dec_b))
    att_d = add_pieces(ids, [keep_w1], [come_w1], 3.6, (ffn_e,))
    df0, own_0, sendkv_0, router_0g, keep_w0, send_w0 = run(
        functools.partial(self_back_kernel, 0),
        (ids, recv, dh1, mixed_e, log_e, *wa_own, *wa_oth, kvw_own, kvw_oth),
        "svvvv" + "a" * 10,
        (act, kv_f, kv_b, router_s, att_g, att_g),
        self_scratch,
        11.8,
        after=(ffn_e, *att_d),
    )
    comekv_0 = swapped(sendkv_0)
    come_w0 = swapped(send_w0)
    ffn_e = to_all(ffn_e, "mp")
    att_d = mp_exchange(att_d)
    dx1, gain_d0, keep_s1, send_s1 = run(
        dec_finish_kernel,
        (ids, recv, dg1, df1, own_1, comekv_1, own_c, comekv_c, memory, kvw_own, kvw_oth),
        "svvvvvvvvaa",
        (shaped((4, 128, 512), BF), row_s, flat_g, flat_g),
        [vm(512, 128), vm(2, TILE, 512), sem],
        0.3,
        after=(df0,),
    )
    come_s1 = swapped(send_s1)
    finished = run(
        enc_finish_kernel,
        (
            ids, recv, dh1, df0, own_0, comekv_0, dx1, router_0g, router_1g, router_cg,
            gain_e1, gain_e2, gain_d0, gain_d1, gain_d2, kvw_own, kvw_oth,
        ),
        "s" + "v" * 14 + "aa",
        shaped((8, 208, 512), BF),
        [vm(512, 128), vm(2, TILE, 512), vm(32, 512, kind=F32), sem],
        0.3,
        after=att_d[1:],
    )
    att_e = add_pieces(
        ids, [keep_w0, keep_s1], [come_w0, come_s1], 3.6, (finished,)
    )
    att_e = mp_exchange(att_e)
    dp = lax.axis_size("dp")
    share = 256 // dp
    if dp == 4:
        ffn = dp_exchange(
            run(
                sum_middle_kernel,
                (ids, dec_a, dec_b, ffn_e, *att_d),
                "s" + "v" * 7,
                [shaped((64, 2560), BF)] * 4,
                [],
                4.0,
                after=(att_e[0],),
            )
        )
        after = ffn[1:]
    else:
        after = ()
    finished = to_all(finished, rowgroup)
    small = run(
        tail_kernel,
        (finished, *att_e),
        "v" * 5,
        shaped((256, 768), BF),
        [],
        3.0,
        after=after,
    )
    dx = run(
        place_kernel,
        (finished,),
        "v",
        shaped((4, 2, 128, 512), F32),
        [],
        3.0,
        after=(small,),
    )
    small = to_all(small.reshape(dp, share, 768), "dp")
    outs_come = outs_come.reshape(2, 4, 128, 512).transpose(1, 0, 2, 3)
    results = (outs_come.reshape(1, 4, 1, 256, 512), dx.reshape(1, 4, 1, 256, 512))
    if dp == 4:
        made = run(
            final_kernel,
            (small, *ffn),
            "v" * 5,
            (
                shaped((3, 2, 64), F32),
                shaped((2, 8, 64), F32),
                shaped((2, 2, 64, 64), F32),
                shaped((2, 64, 128), F32),
                shaped((2, 2, 64, 64), F32),
                shaped((2, 64, 512), F32),
                shaped((2, 64, 512), F32),
                shaped((8, 64), F32),
                shaped((2, 64, 64), F32),
                shaped((64, 128), F32),
                shaped((2, 64, 64), F32),
            ),
            [],
            3.0,
        )
        made = list(made)
        made[0] = made[0].transpose(1, 0, 2)
        made[1] = made[1].transpose(0, 2, 1)
        made[6] = made[6].transpose(0, 2, 1)
        made[7] = made[7].T
        return (*results, *made)

    small = jnp.sum(small.astype(F32), 0)
    middle = jnp.concatenate(
        [jnp.sum(part.astype(F32), 0) for part in (ffn_e, dec_a, dec_b)]
        + [sum(part.astype(F32) for part in att_d)],
        1,
    )
    middle = to_all(middle.astype(BF).reshape(dp, share, 2560), "dp")
    middle = jnp.sum(middle.astype(F32), 0)

    def query_of(value, at):
        return value[:, at : at + 128].reshape(share, 2, 64).transpose(1, 0, 2)

    def output_of(value, at):
        return value[:, at + 128 : at + 256].T.reshape(2, 64, share)

    misc = small[:, 640:768].T

    def router_of(layer):
        return misc[ROUTER_LANES[layer] : ROUTER_LANES[layer] + 8].T

    return (
        *results,
        misc[GAIN_ROW : GAIN_ROW + 6].reshape(2, 3, share),
        jnp.stack([router_of(0), router_of(1)]),
        jnp.stack([query_of(small, 0), query_of(middle, 2304)]),
        jnp.stack([small[:, 512:640], small[:, 256:384]]),
        jnp.stack([output_of(small, 0), output_of(middle, 2304)]),
        jnp.stack([middle[:, :512], middle[:, 1024:1536]]),
        jnp.stack([middle[:, 512:1024].T, middle[:, 1536:2048].T]),
        router_of(2),
        query_of(middle, 2048),
        small[:, 384:512],
        output_of(middle, 2048),
    )


def solution(mesh):
    placed = (
        P("section", None, "dp", "mp", None),
        P("section", None, "dp", None),
        P("section", None, "dp", "mp", None),
        P(None, "dp", "mp", None),
        P("section", None, None),
        P("section", None, None),
        P("section", "mp", None, None),
        P("section", None, None),
        P("section", "mp", None, None),
        P("section", None, "mp"),
        P("section", "mp", None),
        P(),
        P("mp", None, None),
        P(),
        P("mp", None, None),
        P(None, "dp", "mp", None),
    )
    return jax.shard_map(
        per_device,
        mesh=mesh,
        in_specs=placed,
        out_specs=(
            P("section", None, "dp", "mp", None),
            P("section", None, "dp", "mp", None),
            P(None, None, ("section", "dp")),
            P(None, ("section", "dp"), None),
            P(None, "mp", ("section", "dp"), None),
            P(None, ("section", "dp"), None),
            P(None, "mp", None, ("section", "dp")),
            P(None, ("section", "dp"), "mp"),
            P(None, "mp", ("section", "dp")),
            P(("section", "dp"), None),
            P("mp", ("section", "dp"), None),
            P(("section", "dp"), None),
            P("mp", None, ("section", "dp")),
        ),
        check_vma=False,
    )
```

```python
import functools

import jax
import jax.numpy as jnp
from jax import lax
from jax.experimental import pallas as pl
from jax.experimental.pallas import tpu as pltpu
from jax.sharding import PartitionSpec as P

EPS = 1e-05
MASK_VALUE = -1000000000.0
BF = jnp.bfloat16
F32 = jnp.float32
TILE = 256
EX_AT = 160
CODE_ROW = 3
LEN_ROW = 4
ROUTER_AT = 8
GAIN_ROW = 24
ROUTER_LANES = (0, 8, 16)
VMEM_LIMIT = 63 * 1024 * 1024
BLOCK = 32
LARGE = 1 << 40


def nn(left, right):
    return lax.dot_general(left, right, (((1,), (0,)), ((), ())), preferred_element_type=F32)


def nt(left, right):
    return lax.dot_general(left, right, (((1,), (1,)), ((), ())), preferred_element_type=F32)


def tn(left, right):
    return lax.dot_general(left, right, (((0,), (0,)), ((), ())), preferred_element_type=F32)


def norm_of(values, gain_row):
    center = values - jnp.mean(values, 1, keepdims=True)
    scaled = lax.rsqrt(jnp.mean(center * center, 1, keepdims=True) + EPS)
    unit_rows = center * scaled
    return unit_rows * gain_row, unit_rows, scaled


def norm_back(upstream, unit_rows, scaled, gain_row):
    inner = upstream * gain_row
    result = scaled * (
        inner
        - jnp.mean(inner, 1, keepdims=True)
        - unit_rows * jnp.mean(inner * unit_rows, 1, keepdims=True)
    )
    return result, jnp.sum(upstream * unit_rows, 0, keepdims=True)


def eye_of(size):
    return lax.broadcasted_iota(jnp.int32, (size, size), 0) == lax.broadcasted_iota(
        jnp.int32, (size, size), 1
    )


def row_to_col(row):
    return jnp.sum(jnp.where(eye_of(128), row, 0.0), 1, keepdims=True)


def col_to_row(col):
    parts = []
    for at in range(0, col.shape[0], 128):
        part = jnp.where(eye_of(128), col[at : at + 128], 0.0)
        parts.append(jnp.sum(part, 0, keepdims=True))
    return jnp.concatenate(parts, 1)


def ends_of(extra):
    lengths = extra[LEN_ROW : LEN_ROW + 1, 0:8] * 32.0 + extra[LEN_ROW : LEN_ROW + 1, 128:136]
    ends = [lengths[:, 0:1]]
    for k in range(1, 8):
        ends.append(ends[-1] + lengths[:, k : k + 1])
    return ends


def segments(places, ends):
    total = jnp.where(places >= ends[0], 1.0, 0.0)
    for end in ends[1:]:
        total = total + jnp.where(places >= end, 1.0, 0.0)
    return total


def extra_of(recv_ref, layer, quarter):
    at = EX_AT if recv_ref.shape[1] > 16 else 0
    return recv_ref[4 * layer + quarter, at : at + 16, :]


def gain_of(recv_ref, layer, which):
    return extra_of(recv_ref, layer, 0).astype(F32)[which : which + 1, :]


def rows_of(recv_ref, layer, t):
    return recv_ref[pl.ds(4 * layer + 2 * t, 2), 0:128, :].reshape(TILE, 512).astype(F32)


def codes_of(recv_ref, layer, t, lane):
    cols = []
    for i in range(2):
        extra = extra_of(recv_ref, layer, 2 * t + i).astype(F32)
        cols.append(row_to_col(extra[CODE_ROW : CODE_ROW + 1, lane : lane + 128]))
    return jnp.concatenate(cols, 0)


def other_kv(recv_ref, layer, quarter):
    packed = recv_ref[4 * layer + quarter, 128:160, :]
    return jnp.concatenate([packed[:, 128 * c : 128 * c + 128] for c in range(4)], 0)


def routing(query_rows, router_block, code):
    second = jnp.floor(code * 0.125)
    first = code - 8.0 * second
    e0, e1 = first.astype(jnp.int32), second.astype(jnp.int32)
    logits = nt(query_rows, router_block)
    lanes = lax.broadcasted_iota(jnp.int32, logits.shape, 1)
    l0 = jnp.sum(jnp.where(lanes == e0 + ROUTER_AT, logits, 0.0), 1, keepdims=True)
    l1 = jnp.sum(jnp.where(lanes == e1 + ROUTER_AT, logits, 0.0), 1, keepdims=True)
    top = jnp.maximum(l0, l1)
    x0, x1 = jnp.exp(l0 - top), jnp.exp(l1 - top)
    total = x0 + x1
    owners = lax.broadcasted_iota(jnp.int32, (code.shape[0], 512), 1) >> 6
    return e0, e1, x0 / total, x1 / total, owners == e0, owners == e1


def fold(wide, mask):
    kept = jnp.where(mask, wide, 0.0)
    return kept[:, 0:128] + kept[:, 128:256] + kept[:, 256:384] + kept[:, 384:512]


def spread(a0, a1, m0, m1):
    parts = []
    for c in range(4):
        cut = slice(128 * c, 128 * c + 128)
        parts.append(jnp.where(m0[:, cut], a0, jnp.where(m1[:, cut], a1, 0.0)))
    return jnp.concatenate(parts, 1).astype(BF)


def rounded(value):
    return value.astype(BF).astype(F32)


def start_pick(cond, yes, no, dst, sem):
    @pl.when(cond)
    def _():
        pltpu.make_async_copy(yes, dst, sem).start()

    @pl.when(jnp.logical_not(cond))
    def _():
        pltpu.make_async_copy(no, dst, sem).start()


class Loads:
    def __init__(self, sems):
        self.sems, self.used = sems, 0

    def start(self, cond, yes, no, dst):
        sem = self.sems.at[self.used]
        self.used += 1
        start_pick(cond, yes, no, dst, sem)
        return functools.partial(lambda a, b, c: pltpu.make_async_copy(a, b, c).wait(), yes, dst, sem)

    def plain(self, src, dst):
        sem = self.sems.at[self.used]
        self.used += 1
        copy = pltpu.make_async_copy(src, dst, sem)
        copy.start()
        return copy.wait

    def rows(self, cond, yes, no, at, dst, m):
        cut = pl.ds(at, 128)
        return [
            self.start(cond, yes[b].at[cut], no[b].at[cut], dst.at[pl.ds(128 * (m ^ b), 128)])
            for b in range(4)
        ]

    def pieces(self, cond, yes, no, dst, m):
        return [self.start(cond, yes[b], no[b], dst.at[m ^ b]) for b in range(4)]


def wait_all(waits):
    for wait in waits:
        wait()


def widen_kv(kv_ref, k2_ref, v2_ref):
    for j in range(4):
        kv = kv_ref[j].reshape(256, 128).astype(F32)
        turned = pltpu.roll(kv, 64, 1)
        low = lax.broadcasted_iota(jnp.int32, kv.shape, 1) < 64
        k2_ref[256 * j : 256 * j + 256, :] = jnp.where(low, kv, turned).astype(BF)
        v2_ref[256 * j : 256 * j + 256, :] = jnp.where(low, turned, kv).astype(BF)


def attend_tile(query_rows, route, w_qt, w_o, k2, v2, allowed):
    e0, e1, g0, g1, m0, m1 = route
    q_all = nt(query_rows, w_qt) * 0.125
    queries = jnp.concatenate([fold(q_all, m0), fold(q_all, m1)], 0).astype(BF)
    scores = nt(queries, k2)
    scores = jnp.concatenate(
        [
            jnp.where(allowed, scores[0:TILE], MASK_VALUE),
            jnp.where(allowed, scores[TILE:], MASK_VALUE),
        ],
        0,
    )
    top = jnp.max(scores, 1, keepdims=True)
    weights = jnp.exp(scores - top)
    total = jnp.sum(weights, 1, keepdims=True)
    mixed = nn(weights.astype(BF), v2) / total
    log_total = top + jnp.log(total)
    gated = spread(rounded(g0) * mixed[0:TILE], rounded(g1) * mixed[TILE:], m0, m1)
    return nn(gated, w_o), mixed, col_to_row(log_total)


def attend_back_tile(
    t, upstream, query_rows, route, mixed, log_row, w_qt, w_o, router_block, router_lane, k2, v2,
    allowed_t, work, grad_k, grad_v, gated_ref, dz_ref, dq_ref, dlog_ref,
):
    e0, e1, g0, g1, m0, m1 = route
    q_all = nt(query_rows, w_qt) * 0.125
    queries = jnp.concatenate([fold(q_all, m0), fold(q_all, m1)], 0).astype(BF)
    dz = upstream.astype(BF)
    dg_all = nt(dz, w_o)
    dgated0, dgated1 = fold(dg_all, m0), fold(dg_all, m1)
    r0, r1 = rounded(g0), rounded(g1)
    mixed0, mixed1 = mixed[0:TILE], mixed[TILE:]
    gated_ref[t] = spread(r0 * mixed0, r1 * mixed1, m0, m1)
    dz_ref[t] = dz
    dgate0 = rounded(jnp.sum(mixed0 * dgated0, 1, keepdims=True))
    dgate1 = rounded(jnp.sum(mixed1 * dgated1, 1, keepdims=True))
    do0, do1 = (r0 * dgated0).astype(BF), (r1 * dgated1).astype(BF)
    grad_mixed = jnp.concatenate([do0, do1], 0)
    inner_row = jnp.concatenate(
        [
            col_to_row(jnp.sum(do0.astype(F32) * mixed0, 1, keepdims=True)),
            col_to_row(jnp.sum(do1.astype(F32) * mixed1, 1, keepdims=True)),
        ],
        1,
    )
    s_s, dp_s, p_s, ds_s = work
    s_s[...] = nt(k2, queries)
    dp_s[...] = nt(v2, grad_mixed)

    def block(i, carry):
        at = pl.multiple_of(BLOCK * i, BLOCK)
        cut = pl.ds(at, BLOCK)
        allowed = allowed_t(at)
        scores = s_s[cut, :]
        scores = jnp.concatenate(
            [
                jnp.where(allowed, scores[:, 0:TILE], MASK_VALUE),
                jnp.where(allowed, scores[:, TILE:], MASK_VALUE),
            ],
            1,
        )
        probs = jnp.exp(scores - log_row)
        p_s[cut, :] = probs.astype(BF)
        ds_s[cut, :] = (probs * (dp_s[cut, :] - inner_row)).astype(BF)
        return carry

    lax.fori_loop(0, 1024 // BLOCK, block, 0)
    grad_scores = ds_s[...]
    grad_v[...] += nn(p_s[...], grad_mixed)
    grad_k[...] += nn(grad_scores, queries)
    grad_q = rounded(tn(grad_scores, k2) * 0.125)
    dq_all = spread(grad_q[0:TILE], grad_q[TILE:], m0, m1)
    dq_ref[t] = dq_all
    grad_rows = nn(dq_all, w_qt)
    mean_grad = g0 * dgate0 + g1 * dgate1
    dc0, dc1 = g0 * (dgate0 - mean_grad), g1 * (dgate1 - mean_grad)
    lanes = lax.broadcasted_iota(jnp.int32, (TILE, 16), 1)
    dlog = jnp.where(lanes == e0 + ROUTER_AT, dc0, 0.0) + jnp.where(
        lanes == e1 + ROUTER_AT, dc1, 0.0
    )
    wide = lax.broadcasted_iota(jnp.int32, (TILE, 128), 1)
    dlog_ref[t] = (
        jnp.where(wide == e0 + router_lane, dc0, 0.0)
        + jnp.where(wide == e1 + router_lane, dc1, 0.0)
    ).astype(BF)
    return grad_rows + nn(dlog.astype(BF), router_block)


def query_places(t, sec, dims, along):
    local = lax.broadcasted_iota(jnp.int32, dims, along)
    return (512 * t + 128 * sec + local + (local & ~127)).astype(F32)


def allowed_rows(t, sec, ends_q, ends_k, causal):
    query_at = query_places(t, sec, (TILE, 1), 0)
    key_at = lax.broadcasted_iota(jnp.int32, (1, 1024), 1).astype(F32)
    allowed = segments(query_at, ends_q) == segments(key_at, ends_k)
    if causal:
        allowed = allowed & (key_at <= query_at)
    return allowed


def key_segments_t(ends_k, segk_ref):
    for j in range(8):
        at = lax.broadcasted_iota(jnp.int32, (128, TILE), 0).astype(F32) + 128.0 * j
        segk_ref[128 * j : 128 * j + 128, :] = segments(at, ends_k)


def allowed_cols(t, sec, ends_q, segk_ref, causal):
    query_at = query_places(t, sec, (1, TILE), 1)
    query_segments = segments(query_at, ends_q)

    def block(at):
        allowed = segk_ref[pl.ds(at, BLOCK), :] == query_segments
        if causal:
            key_at = (at + lax.broadcasted_iota(jnp.int32, (BLOCK, TILE), 0)).astype(F32)
            allowed = allowed & (key_at <= query_at)
        return allowed

    return block


def fold_kv(grad_k, grad_v, sec, own_ref, send_ref):
    for j in range(4):
        k = grad_k[256 * j : 256 * j + 256, :]
        v = grad_v[256 * j : 256 * j + 256, :]
        k = k + pltpu.roll(k, 64, 1)
        v = v + pltpu.roll(v, 64, 1)
        low = lax.broadcasted_iota(jnp.int32, k.shape, 1) < 64
        both = jnp.where(low, k, v)
        first, second = both[0:128], both[128:256]
        own_ref[j] = jnp.where(sec == 0, first, second)
        send_ref[j] = jnp.where(sec == 0, second, first).astype(send_ref.dtype)


def split_halves(value, sec, keep_ref, send_ref, m, lane):
    upper, lower = value[0:256], value[256:512]
    cut = slice(lane, lane + value.shape[1])
    keep_ref[m, :, cut] = jnp.where(sec == 0, upper, lower).astype(BF)
    send_ref[m, :, cut] = jnp.where(sec == 0, lower, upper).astype(BF)


def split_flat(value, sec, keep_ref, send_ref, lane):
    upper, lower = value[0:256], value[256:512]
    cut = slice(lane, lane + value.shape[1])
    keep_ref[:, cut] = jnp.where(sec == 0, upper, lower).astype(BF)
    send_ref[:, cut] = jnp.where(sec == 0, lower, upper).astype(BF)


def turned_rows(value):
    return value.astype(F32).T.astype(BF)


def flat(ref):
    return ref[...].reshape(512, ref.shape[-1])


def attention_weight_grads(first_t, gated_ref, dz_ref, dq_ref, sec, keep_ref, send_ref, lane):
    grad_q = nn(first_t, flat(dq_ref))
    grad_o = nn(turned_rows(flat(dz_ref)), flat(gated_ref))
    for b in range(4):
        cut = slice(128 * b, 128 * b + 128)
        split_halves(grad_q[:, cut], sec, keep_ref, send_ref, b, lane)
        split_halves(grad_o[:, cut], sec, keep_ref, send_ref, b, lane + 128)


def router_grads(dlog_ref, rows_ref):
    turned = flat(dlog_ref).astype(F32).T.astype(BF)
    return nn(turned, flat(rows_ref))[0:32]


def gelu_parts(pre):
    cdf = 0.5 * (1.0 + lax.erf(pre * 0.7071067811865476))
    slope = cdf + pre * (jnp.exp(-0.5 * pre * pre) * 0.3989422804014327)
    return pre * cdf, slope


def own_self_kv(recv_ref, layer, sec, w_kv, kv_ref):
    gain = gain_of(recv_ref, layer, 0)
    for t in range(2):
        first = norm_of(rows_of(recv_ref, layer, t), gain)[0].astype(BF)
        kv = nn(first, w_kv).astype(BF)
        for i in range(2):
            j = 2 * t + i
            kv_ref[j, sec] = kv[128 * i : 128 * i + 128]
            kv_ref[j, 1 - sec] = other_kv(recv_ref, layer, j)


def cross_kv(kvm_ref, kvo_ref, sec, kv_s):
    for j in range(4):
        kv_s[j, sec] = kvm_ref[j]
        kv_s[j, 1 - sec] = kvo_ref[j]


def pack_kernel(
    ready, len_ref, x_ref, gain_ref, w_kv_ref, own_ref, cross_ref, router_ref, send_ref, extra_s
):
    ready()
    gain = gain_ref[0:1, :].astype(F32)
    w_kv = w_kv_ref[...]
    extra_s[...] = jnp.zeros_like(extra_s)
    extra_s[0:3, :] = gain_ref[...].astype(F32)
    extra_s[ROUTER_AT : ROUTER_AT + 8, :] = router_ref[...].astype(F32)
    lanes = lax.broadcasted_iota(jnp.int32, (1, 512), 1)
    for i in range(4):
        first = norm_of(x_ref[i].astype(F32), gain)[0].astype(BF)
        kv = nn(first, w_kv).astype(BF)
        row = jnp.zeros((1, 512), jnp.int32)
        for k in range(8):
            length = len_ref[i, k]
            row = jnp.where(lanes == k, length >> 5, row)
            row = jnp.where(lanes == 128 + k, length & 31, row)
        extra_s[LEN_ROW : LEN_ROW + 1, :] = row.astype(F32)
        own, cross = own_ref[i], cross_ref[i]
        own_code = (own[0:1] + 8 * own[1:2]).astype(F32)
        cross_code = (cross[0:1] + 8 * cross[1:2]).astype(F32)
        for half in range(2):
            to = 4 * half + i
            here = slice(128 * half, 128 * half + 128)
            send_ref[to, 0:128, :] = x_ref[i, here, :]
            far = kv[128 * (1 - half) : 128 * (1 - half) + 128]
            send_ref[to, 128:160, :] = jnp.concatenate(
                [far[32 * c : 32 * c + 32] for c in range(4)], 1
            )
            extra_s[CODE_ROW : CODE_ROW + 1, 0:128] = own_code[:, here]
            extra_s[CODE_ROW : CODE_ROW + 1, 128:256] = cross_code[:, here]
            send_ref[to, EX_AT : EX_AT + 16, :] = extra_s[...].astype(BF)


def self_fwd_kernel(ready, ids_ref, recv_ref, *refs):
    wa_own, wa_oth, kvw_own, kvw_oth = refs[:4], refs[4:8], refs[8], refs[9]
    h1_ref, g1_ref, mixed_e, mixed_d, log_e, log_d, meta_ref = refs[10:17]
    wq, wo, wkv, kv_s, k2, v2, sems = refs[17:]
    sec, m = ids_ref[0], ids_ref[1]
    loads = Loads(sems)
    kv_waits = [loads.start(sec == i, kvw_own, kvw_oth, wkv.at[i]) for i in range(2)]
    waits = []
    for layer in range(2):
        waits += loads.rows(sec == layer, wa_own, wa_oth, 0, wq.at[layer], m)
        waits += loads.rows(sec == layer, wa_own, wa_oth, 128, wo.at[layer], m)
    ready()
    meta_ref[...] = recv_ref[:, EX_AT : EX_AT + 16, :]
    wait_all(kv_waits)
    for layer in range(2):
        own_self_kv(recv_ref, layer, sec, wkv[layer], kv_s)
        widen_kv(kv_s, k2.at[layer], v2.at[layer])
    wait_all(waits)
    ends = [ends_of(extra_of(recv_ref, layer, 0).astype(F32)) for layer in range(2)]

    def tile(t, carry):
        for layer, after_ref, mixed_ref, log_ref in (
            (0, h1_ref, mixed_e, log_e),
            (1, g1_ref, mixed_d, log_d),
        ):
            rows = rows_of(recv_ref, layer, t)
            first = norm_of(rows, gain_of(recv_ref, layer, 0))[0].astype(BF)
            route = routing(first, extra_of(recv_ref, layer, 0), codes_of(recv_ref, layer, t, 0))
            allowed = allowed_rows(t, sec, ends[layer], ends[layer], layer == 1)
            out, mixed, row_log = attend_tile(
                first, route, wq[layer], wo[layer], k2[layer], v2[layer], allowed
            )
            after_ref[t] = rows + out
            mixed_ref[t] = mixed
            log_ref[t] = row_log
        return carry

    lax.fori_loop(0, 2, tile, 0)


def enc_ffn_kernel(ready, ids_ref, recv_ref, h1_ref, kvc_ref, *refs):
    f_own, f_oth = refs[:4], refs[4:8]
    h2_ref, mem_ref, kvm_ref, w_in, w_out, third_s, sems = refs[8:]
    low, m = ids_ref[0] == 0, ids_ref[1]
    loads = Loads(sems)
    waits = loads.pieces(low, f_own, f_oth, w_in, m) + loads.pieces(low, f_oth, f_own, w_out, m)
    ready()
    for t in range(2):
        h2_ref[t] = h1_ref[t]
        third_s[t] = norm_of(h1_ref[t], gain_of(recv_ref, 0, 2))[0].astype(BF)
    wait_all(waits)

    def chunk(c, carry):
        pre = nn(flat(third_s), w_in[c])
        hidden = (0.5 * pre * (1.0 + lax.erf(pre * 0.7071067811865476))).astype(BF)
        h2_ref[...] += nn(hidden, w_out[c]).reshape(2, TILE, 512)
        return carry

    lax.fori_loop(0, 4, chunk, 0)
    for t in range(2):
        memory = norm_of(h2_ref[t], gain_of(recv_ref, 0, 1))[0].astype(BF)
        mem_ref[t] = memory
        kv = nn(memory, kvc_ref[...]).astype(BF)
        kvm_ref[2 * t] = kv[0:128]
        kvm_ref[2 * t + 1] = kv[128:256]


def cross_fwd_kernel(
    ready, ids_ref, recv_ref, g1_ref, kvm_ref, kvo_ref, rc_ref, *refs
):
    wa_own, wa_oth = refs[:4], refs[4:8]
    g2_ref, mixed_ref, log_ref, wq, wo, kv_s, k2, v2, sems = refs[8:]
    sec, m = ids_ref[0], ids_ref[1]
    loads = Loads(sems)
    waits = loads.rows(sec == 0, wa_own, wa_oth, 256, wq, m)
    waits += loads.rows(sec == 0, wa_oth, wa_own, 256, wo, m)
    ready()
    cross_kv(kvm_ref, kvo_ref, sec, kv_s)
    widen_kv(kv_s, k2, v2)
    wait_all(waits)
    ends_k = ends_of(extra_of(recv_ref, 0, 0).astype(F32))
    ends_q = ends_of(extra_of(recv_ref, 1, 0).astype(F32))

    def tile(t, carry):
        before = g1_ref[t]
        second = norm_of(before, gain_of(recv_ref, 1, 1))[0].astype(BF)
        route = routing(second, rc_ref[...], codes_of(recv_ref, 1, t, 128))
        allowed = allowed_rows(t, sec, ends_q, ends_k, False)
        out, mixed, row_log = attend_tile(second, route, wq[...], wo[...], k2[...], v2[...], allowed)
        g2_ref[t] = before + out
        mixed_ref[t] = mixed
        log_ref[t] = row_log
        return carry

    lax.fori_loop(0, 2, tile, 0)


def ffn_both(
    c, third_s, third_t, dy_s, dy_t, w_in, w_out, dthird, sec, keep_ref, send_ref, work
):
    pre_s, dh_s, hid_s, dpre_s = work
    pre_s[...] = nn(flat(third_s), w_in[c])
    dh_s[...] = nt(flat(dy_s), w_out[c])

    def block(i, carry):
        cut = pl.ds(pl.multiple_of(BLOCK * i, BLOCK), BLOCK)
        hidden, slope = gelu_parts(pre_s[cut, :])
        hid_s[cut, :] = hidden.astype(BF)
        dpre_s[cut, :] = (dh_s[cut, :] * slope).astype(BF)
        return carry

    lax.fori_loop(0, 512 // BLOCK, block, 0)
    hidden, dpre = hid_s[...], dpre_s[...]
    dthird[...] += nt(dpre, w_in[c])
    split_halves(nn(third_t[...], dpre), sec, keep_ref, send_ref, c, 0)
    split_halves(nn(dy_t[...], hidden), sec, keep_ref, send_ref, c, 512)
    return hidden


def dec_ffn_kernel(ready, ids_ref, recv_ref, g2_ref, mem_ref, cot_in, *refs):
    f_own, f_oth = refs[:4], refs[4:8]
    outs_ref, dg2_ref, gain_ref, keep_ref, send_ref = refs[8:13]
    w_in, w_out, cot_s, third_s, third_t, cot_t, acc, dthird, *work, sems = refs[13:]
    sec, m = ids_ref[0], ids_ref[1]
    low = sec == 0
    loads = Loads(sems)
    cot_waits = [loads.plain(cot_in.at[i], cot_s.at[i]) for i in range(4)]
    waits = loads.pieces(low, f_own, f_oth, w_in, m) + loads.pieces(low, f_oth, f_own, w_out, m)
    ready()
    for t in range(2):
        acc[t] = g2_ref[t]
        third_s[t] = norm_of(g2_ref[t], gain_of(recv_ref, 1, 2))[0].astype(BF)
        outs_ref[2 * t : 2 * t + 2] = mem_ref[t].reshape(2, 128, 512)
    third_t[...] = turned_rows(flat(third_s))
    wait_all(cot_waits)
    cot_t[...] = turned_rows(flat(cot_s))
    dthird[...] = jnp.zeros_like(dthird)
    wait_all(waits)

    def chunk(c, carry):
        hidden = ffn_both(
            c, third_s, third_t, cot_s, cot_t, w_in, w_out, dthird, sec, keep_ref, send_ref, work
        )
        acc[...] += nn(hidden, w_out[c]).reshape(2, TILE, 512)
        return carry

    lax.fori_loop(0, 4, chunk, 0)
    total = jnp.zeros((1, 512), F32)
    gain = gain_of(recv_ref, 1, 2)
    for t in range(2):
        outs_ref[4 + 2 * t : 6 + 2 * t] = acc[t].astype(BF).reshape(2, 128, 512)
        unused_out, unit, scaled = norm_of(g2_ref[t], gain)
        back, gain_grad = norm_back(dthird[TILE * t : TILE * t + TILE, :], unit, scaled, gain)
        dg2_ref[t] = cot_s[2 * t : 2 * t + 2].reshape(TILE, 512).astype(F32) + back
        total = total + gain_grad
    gain_ref[...] = total


def cross_back_kernel(
    ready, ids_ref, recv_ref, g1_ref, dg2_ref, mixed_ref, log_ref, kvm_ref, kvo_ref, rc_ref, *refs
):
    wa_own, wa_oth = refs[:4], refs[4:8]
    dg1_ref, gain_ref, own_ref, send_ref, router_ref, keepw_ref, sendw_ref = refs[8:15]
    wq, wo, kv_s, k2, v2, segk, grad_k, grad_v, second_s, gated_s, dz_s, dq_s, dlog_s = refs[15:28]
    work, sems = refs[28:32], refs[32]
    sec, m = ids_ref[0], ids_ref[1]
    loads = Loads(sems)
    waits = loads.rows(sec == 0, wa_own, wa_oth, 256, wq, m)
    waits += loads.rows(sec == 0, wa_oth, wa_own, 256, wo, m)
    ready()
    cross_kv(kvm_ref, kvo_ref, sec, kv_s)
    widen_kv(kv_s, k2, v2)
    ends_k = ends_of(extra_of(recv_ref, 0, 0).astype(F32))
    ends_q = ends_of(extra_of(recv_ref, 1, 0).astype(F32))
    key_segments_t(ends_k, segk)
    grad_k[...] = jnp.zeros_like(grad_k)
    grad_v[...] = jnp.zeros_like(grad_v)
    wait_all(waits)

    def tile(t, total):
        gain = gain_of(recv_ref, 1, 1)
        second, unit, scaled = norm_of(g1_ref[t], gain)
        second = second.astype(BF)
        second_s[t] = second
        route = routing(second, rc_ref[...], codes_of(recv_ref, 1, t, 128))
        allowed = allowed_cols(t, sec, ends_q, segk, False)
        grad_rows = attend_back_tile(
            t, dg2_ref[t], second, route, mixed_ref[t], log_ref[t], wq[...], wo[...], rc_ref[...],
            ROUTER_LANES[2], k2[...], v2[...], allowed, work, grad_k, grad_v, gated_s, dz_s, dq_s, dlog_s,
        )
        back, gain_grad = norm_back(grad_rows, unit, scaled, gain)
        dg1_ref[t] = dg2_ref[t] + back
        return total + gain_grad

    gain_ref[...] = lax.fori_loop(0, 2, tile, jnp.zeros((1, 512), F32))
    fold_kv(grad_k, grad_v, sec, own_ref, send_ref)
    router_ref[...] = router_grads(dlog_s, second_s)
    attention_weight_grads(
        turned_rows(flat(second_s)), gated_s, dz_s, dq_s, sec, keepw_ref, sendw_ref, 0
    )


def self_back_kernel(layer, ready, ids_ref, recv_ref, up_ref, mixed_ref, log_ref, *refs):
    wa_own, wa_oth, kvw_own, kvw_oth = refs[:4], refs[4:8], refs[8], refs[9]
    refs = refs[10:]
    if layer == 1:
        before, refs = refs[:2], refs[2:]
    dfirst_ref, own_ref, send_ref, router_ref, keepw_ref, sendw_ref = refs[:6]
    wq, wo, wkv, kv_s, k2, v2, segk, grad_k, grad_v = refs[6:15]
    first_s, gated_s, dz_s, dq_s, dlog_s = refs[15:20]
    work, sems = refs[20:24], refs[24]
    sec, m = ids_ref[0], ids_ref[1]
    mine = sec == layer
    loads = Loads(sems)
    kv_wait = loads.start(mine, kvw_own, kvw_oth, wkv)
    waits = loads.rows(mine, wa_own, wa_oth, 0, wq, m) + loads.rows(mine, wa_own, wa_oth, 128, wo, m)
    lane = 0
    if layer == 1:
        lane = 256
        for src, dst in zip(before, (keepw_ref, sendw_ref)):
            waits.append(loads.plain(src, dst.at[:, :, pl.ds(0, 256)]))
    ready()
    ends = ends_of(extra_of(recv_ref, layer, 0).astype(F32))
    key_segments_t(ends, segk)
    grad_k[...] = jnp.zeros_like(grad_k)
    grad_v[...] = jnp.zeros_like(grad_v)
    kv_wait()
    own_self_kv(recv_ref, layer, sec, wkv[...], kv_s)
    widen_kv(kv_s, k2, v2)
    wait_all(waits)
    router_block = extra_of(recv_ref, layer, 0)

    def tile(t, carry):
        first = norm_of(rows_of(recv_ref, layer, t), gain_of(recv_ref, layer, 0))[0].astype(BF)
        first_s[t] = first
        route = routing(first, router_block, codes_of(recv_ref, layer, t, 0))
        allowed = allowed_cols(t, sec, ends, segk, layer == 1)
        dfirst_ref[t] = attend_back_tile(
            t, up_ref[t], first, route, mixed_ref[t], log_ref[t], wq[...], wo[...], router_block,
            ROUTER_LANES[layer], k2[...], v2[...], allowed, work, grad_k, grad_v, gated_s, dz_s, dq_s,
            dlog_s,
        )
        return carry

    lax.fori_loop(0, 2, tile, 0)
    fold_kv(grad_k, grad_v, sec, own_ref, send_ref)
    router_ref[...] = router_grads(dlog_s, first_s)
    attention_weight_grads(
        turned_rows(flat(first_s)), gated_s, dz_s, dq_s, sec, keepw_ref, sendw_ref, lane
    )


def enc_ffn_back_kernel(
    ready, ids_ref, recv_ref, h1_ref, h2_ref, own_ref, come_ref, kvc_ref, *refs
):
    f_own, f_oth = refs[:4], refs[4:8]
    dh1_ref, gain_ref, gain2_ref, keep_ref, send_ref = refs[8:13]
    w_in, w_out, third_s, third_t, dy_s, dy_t, dthird, *work, sems = refs[13:]
    sec, m = ids_ref[0], ids_ref[1]
    low = sec == 0
    loads = Loads(sems)
    waits = loads.pieces(low, f_own, f_oth, w_in, m) + loads.pieces(low, f_oth, f_own, w_out, m)
    ready()
    total = jnp.zeros((1, 512), F32)
    gain = gain_of(recv_ref, 0, 1)
    for t in range(2):
        dkv = (own_ref[2 * t : 2 * t + 2] + come_ref[2 * t : 2 * t + 2].astype(F32)).astype(BF)
        dmem = rounded(nt(dkv.reshape(TILE, 128), kvc_ref[...]))
        unused_out, unit, scaled = norm_of(h2_ref[t], gain)
        back, gain_grad = norm_back(dmem, unit, scaled, gain)
        dh1_ref[t] = back
        dy_s[t] = back.astype(BF)
        third_s[t] = norm_of(h1_ref[t], gain_of(recv_ref, 0, 2))[0].astype(BF)
        total = total + gain_grad
    gain_ref[...] = total
    third_t[...] = turned_rows(flat(third_s))
    dy_t[...] = turned_rows(flat(dy_s))
    dthird[...] = jnp.zeros_like(dthird)
    wait_all(waits)

    def chunk(c, carry):
        ffn_both(
            c, third_s, third_t, dy_s, dy_t, w_in, w_out, dthird, sec, keep_ref, send_ref, work
        )
        return carry

    lax.fori_loop(0, 4, chunk, 0)
    total = jnp.zeros((1, 512), F32)
    gain = gain_of(recv_ref, 0, 2)
    for t in range(2):
        unused_out, unit, scaled = norm_of(h1_ref[t], gain)
        back, gain_grad = norm_back(dthird[TILE * t : TILE * t + TILE, :], unit, scaled, gain)
        dh1_ref[t] += back
        total = total + gain_grad
    gain2_ref[...] = total


def finish_rows(layer, recv_ref, up_ref, df_ref, own_ref, come_ref, wkv, first_s, out_ref, at):
    total = jnp.zeros((1, 512), F32)
    gain = gain_of(recv_ref, layer, 0)
    dkvs = []
    for t in range(2):
        first, unit, scaled = norm_of(rows_of(recv_ref, layer, t), gain)
        first_s[t] = first.astype(BF)
        dkv = (own_ref[2 * t : 2 * t + 2] + come_ref[2 * t : 2 * t + 2].astype(F32)).astype(BF)
        dkv = dkv.reshape(TILE, 128)
        dkvs.append(dkv)
        back, gain_grad = norm_back(df_ref[t] + nt(dkv, wkv), unit, scaled, gain)
        dx = (up_ref[t] + back).astype(BF)
        for i in range(2):
            out_ref[at + 2 * t + i, 0:128, :] = dx[128 * i : 128 * i + 128]
        total = total + gain_grad
    grad = nn(turned_rows(flat(first_s)), jnp.concatenate(dkvs, 0))
    return total, grad


def dec_finish_kernel(
    ready, ids_ref, recv_ref, up_ref, df_ref, own_ref, come_ref, own_c, come_c, mem_ref, kvw_own, kvw_oth,
    dx_ref, gain_ref, keep_ref, send_ref, wkv, first_s, sems,
):
    sec = ids_ref[0]
    wait = Loads(sems).start(sec == 1, kvw_own, kvw_oth, wkv)
    ready()
    dkv_c = (own_c[...] + come_c[...].astype(F32)).astype(BF).reshape(512, 128)
    split_flat(nn(turned_rows(flat(mem_ref)), dkv_c), sec, keep_ref, send_ref, 128)
    wait()
    gain_ref[...], grad = finish_rows(
        1, recv_ref, up_ref, df_ref, own_ref, come_ref, wkv[...], first_s, dx_ref, 0
    )
    split_flat(grad, sec, keep_ref, send_ref, 0)


def enc_finish_kernel(
    ready, ids_ref, recv_ref, up_ref, df_ref, own_ref, come_ref, dx1_ref, r0, r1, rc,
    gain_e1, gain_e2, gain_d0, gain_d1, gain_d2, kvw_own, kvw_oth,
    out_ref, wkv, first_s, misc, sems,
):
    sec = ids_ref[0]
    wait = Loads(sems).start(sec == 0, kvw_own, kvw_oth, wkv)
    ready()
    misc[...] = r0[...] + r1[...] + rc[...]
    out_ref[4:8, 0:128, :] = dx1_ref[...]
    wait()
    gain_e0, grad = finish_rows(
        0, recv_ref, up_ref, df_ref, own_ref, come_ref, wkv[...], first_s, out_ref, 0
    )
    rows = (gain_e0, gain_e1[...], gain_e2[...], gain_d0[...], gain_d1[...], gain_d2[...])
    for i, row in enumerate(rows):
        misc[GAIN_ROW + i : GAIN_ROW + i + 1, :] = row
    both = misc[...]
    for half in range(2):
        cut = slice(256 * half, 256 * half + 256)
        part = grad[cut].astype(BF)
        small = both[:, cut].astype(BF)
        block = jnp.concatenate(
            [
                jnp.concatenate([part[64 * c : 64 * c + 64] for c in range(4)], 1),
                jnp.concatenate([small[0:16], small[16:32]], 1),
            ],
            0,
        )
        for i in range(4):
            out_ref[4 * half + i, 128:208, :] = block


def add_kernel(keep_ref, come_ref, *outs):
    lane = 0
    for out_ref in outs:
        cut = slice(lane, lane + out_ref.shape[-1])
        out_ref[...] = keep_ref[:, :, cut] + come_ref[:, :, cut]
        lane += out_ref.shape[-1]


def add_pieces_kernel(flats, ready, ids_ref, *refs):
    ready()
    n = len(flats)
    keeps, comes, outs = refs[:n], refs[n : 2 * n], refs[2 * n :]
    m = ids_ref[1]
    for b in range(4):
        lane = 0
        for is_flat, keep, come in zip(flats, keeps, comes):
            left = keep[...] if is_flat else keep[m ^ b]
            right = come[...] if is_flat else come[m ^ b]
            width = keep.shape[-1]
            outs[b][:, lane : lane + width] = left + right
            lane += width


def sum_middle_kernel(ready, ids_ref, dec_a, dec_b, enc_ref, *refs):
    att, outs = refs[:4], refs[4:]
    ready()
    rows = outs[0].shape[0]
    d = ids_ref[2]
    for k in range(len(outs)):
        cut = pl.ds(pl.multiple_of((d ^ k) * rows, rows), rows)
        for ref, lane in ((enc_ref, 0), (dec_a, 1024), (dec_b, 1536)):
            total = ref[0, cut, :].astype(F32)
            for i in range(1, 4):
                total = total + ref[i, cut, :].astype(F32)
            outs[k][:, lane : lane + ref.shape[-1]] = total.astype(BF)
        total = att[0][cut, :].astype(F32)
        for part in att[1:]:
            total = total + part[cut, :].astype(F32)
        outs[k][:, 2048:2560] = total.astype(BF)


def place_kernel(ready, dx_ref, dx_out):
    ready()
    for i in range(4):
        for half in range(2):
            dx_out[i, half] = dx_ref[4 * half + i, 0:128, :].astype(F32)


def tail_kernel(ready, dx_ref, *refs):
    att_e, (out_ref,) = refs[:4], refs[4:]
    ready()
    total = att_e[0][...].astype(F32)
    for part in att_e[1:]:
        total = total + part[...].astype(F32)
    out_ref[:, 0:512] = total.astype(BF)
    small = dx_ref[0, 128:208, :].astype(F32)
    for i in range(1, 8):
        small = small + dx_ref[i, 128:208, :].astype(F32)
    for c in range(4):
        out_ref[64 * c : 64 * c + 64, 512:640] = small[0:64, 128 * c : 128 * c + 128].astype(BF)
    misc = jnp.concatenate([small[64:80, 0:256], small[64:80, 256:512]], 0)
    misc = jnp.concatenate([misc, jnp.zeros((96, 256), F32)], 0)
    out_ref[:, 640:768] = misc.T.astype(BF)


def final_kernel(ready, come_ref, *refs):
    middle, outs = refs[:4], refs[4:]
    ready()
    gains, router, query, keyval, output, inner, outer, router_c, query_c, keyval_c, output_c = outs
    small = come_ref[0].astype(F32)
    for i in range(1, 4):
        small = small + come_ref[i].astype(F32)
    wide = middle[0][...].astype(F32)
    for part in middle[1:]:
        wide = wide + part[...].astype(F32)
    for layer in range(2):
        inner[layer] = wide[:, 1024 * layer : 1024 * layer + 512]
        outer[layer] = wide[:, 1024 * layer + 512 : 1024 * layer + 1024]
    keyval[0], keyval[1] = small[:, 512:640], small[:, 256:384]
    keyval_c[...] = small[:, 384:512]
    for source, at, put_q, put_o in (
        (wide, 2048, query_c, output_c),
        (wide, 2304, query.at[1], output.at[1]),
        (small, 0, query.at[0], output.at[0]),
    ):
        turned = source[:, at + 128 : at + 256].T
        for e in range(2):
            put_q[e] = source[:, at + 64 * e : at + 64 * e + 64]
            put_o[e] = turned[64 * e : 64 * e + 64]
    misc = small[:, 640:768].T
    router[0], router[1], router_c[...] = misc[0:8], misc[8:16], misc[16:24]
    for i in range(3):
        gains[i, 0:1] = misc[24 + i : 25 + i]
        gains[i, 1:2] = misc[27 + i : 28 + i]


def shaped(dims, kind):
    return jax.ShapeDtypeStruct(dims, kind)


def cost_of(micros):
    return pl.CostEstimate(
        flops=int(micros * 1.1535e9), bytes_accessed=int(micros * 3.0e6), transcendentals=0
    )


def run(kernel, args, places, outs, scratch, micros, after=()):
    space = {
        "s": pl.BlockSpec(memory_space=pltpu.SMEM),
        "v": pl.BlockSpec(memory_space=pltpu.VMEM),
        "a": pl.BlockSpec(memory_space=pl.ANY),
    }
    large = [
        i for i, (p, a) in enumerate(zip(places, args)) if p == "v" and a.size * a.dtype.itemsize > LARGE
    ]
    places = ["a" if i in large else p for i, p in enumerate(places)]
    count, extra = len(args), len(after)
    copies = [pltpu.VMEM(args[i].shape, args[i].dtype) for i in large]

    def body(*refs):
        given, rest = list(refs[:count]), refs[count + extra :]
        if large:
            rest, held, sems = rest[: -len(large) - 1], rest[-len(large) - 1 : -1], rest[-1]
            moves = []
            for n, i in enumerate(large):
                moves.append(pltpu.make_async_copy(given[i], held[n], sems.at[n]))
                given[i] = held[n]
            for move in moves:
                move.start()
        else:
            moves = []

        def ready():
            for move in moves:
                move.wait()

        kernel(ready, *given, *rest)

    return pl.pallas_call(
        body,
        out_shape=outs,
        in_specs=[space[p] for p in places] + [space["a"]] * extra,
        out_specs=jax.tree.map(lambda _: space["v"], outs),
        scratch_shapes=scratch + copies + ([dma(len(large))] if large else []),
        compiler_params=pltpu.CompilerParams(vmem_limit_bytes=VMEM_LIMIT),
        cost_estimate=cost_of(micros),
    )(*args, *after)


def vm(*dims, kind=BF):
    return pltpu.VMEM(dims, kind)


def dma(count):
    return pltpu.SemaphoreType.DMA((count,))


def across(value, axes, size, by):
    return lax.ppermute(value, axes, [(i, i ^ by) for i in range(size)])


def swapped(value):
    return across(value, "section", 2, 1)


def gathered(value):
    return [value] + [across(value, "mp", 4, b) for b in range(1, 4)]


def to_all(value, axes):
    return lax.all_to_all(value, axes, split_axis=0, concat_axis=0, tiled=True)


def add_shares(keep, come, micros, after, parts=1):
    blocks, rows, width = keep.shape
    whole = pl.BlockSpec((1, rows, width), lambda i: (i, 0, 0))
    part = pl.BlockSpec((1, rows, width // parts), lambda i: (i, 0, 0))
    extra = len(after)
    return pl.pallas_call(
        lambda k, c, *rest: add_kernel(k, c, *rest[extra:]),
        out_shape=[shaped((blocks, rows, width // parts), BF)] * parts,
        grid=(blocks,),
        in_specs=[whole, whole] + [pl.BlockSpec(memory_space=pl.ANY)] * extra,
        out_specs=[part] * parts,
        cost_estimate=cost_of(micros),
    )(keep, come, *after)


def add_pieces(ids, keeps, comes, micros, after=()):
    flats = tuple(keep.ndim == 2 for keep in keeps)
    width = sum(keep.shape[-1] for keep in keeps)
    return run(
        functools.partial(add_pieces_kernel, flats),
        (ids, *keeps, *comes),
        "s" + "v" * (2 * len(keeps)),
        [shaped((256, width), BF)] * 4,
        [],
        micros,
        after=after,
    )


def mp_exchange(pieces):
    return [pieces[0]] + [across(pieces[b], "mp", 4, b) for b in range(1, 4)]


def dp_exchange(pieces):
    return [pieces[0]] + [across(pieces[k], "dp", 4, k) for k in range(1, 4)]


def gated(values, after):
    anywhere = pl.BlockSpec(memory_space=pl.ANY)
    count = len(values)
    return pl.pallas_call(
        lambda *refs: None,
        out_shape=[shaped(v.shape, v.dtype) for v in values],
        in_specs=[anywhere] * (count + len(after)),
        out_specs=[anywhere] * count,
        input_output_aliases={i: i for i in range(count)},
        cost_estimate=cost_of(0.2),
    )(*values, *after)


def per_device(
    inputs,
    lengths,
    routes_self,
    routes_cross,
    gains,
    router_self,
    query_self,
    keyval_self,
    output_self,
    ffn_in,
    ffn_out,
    router_cross,
    query_cross,
    keyval_cross,
    output_cross,
    cotangent,
):
    sec, m, d = lax.axis_index("section"), lax.axis_index("mp"), lax.axis_index("dp")
    low = sec == 0
    ids = jnp.stack([sec, m, d]).astype(jnp.int32)
    sem = dma(24)
    rowgroup = ("section", "mp")

    q_rows = query_self[0].transpose(0, 2, 1).reshape(128, 512)
    o_rows = output_self[0].reshape(128, 512)
    c_rows = jnp.where(
        low, query_cross.transpose(0, 2, 1).reshape(128, 512), output_cross.reshape(128, 512)
    )
    wa = jnp.concatenate([q_rows, o_rows, c_rows], 0)
    wa_own = gathered(wa)
    w_in, w_out = ffn_in[0], ffn_out[0]
    half_come = swapped(jnp.where(low, w_out, w_in))
    enc_half = jnp.where(low, w_in, half_come)
    dec_half = jnp.where(low, half_come, w_out)
    kvw_own = keyval_self[0]
    kvw_oth = swapped(kvw_own)
    router_c = jnp.concatenate([jnp.zeros((8, 512), BF), router_cross.T], 0)

    packed = run(
        pack_kernel,
        (
            lengths[0, :, 0],
            inputs[0, :, 0],
            gains[0],
            keyval_self[0],
            routes_self[0, :, 0].transpose(0, 2, 1),
            routes_cross[:, 0].transpose(0, 2, 1),
            router_self[0].T,
        ),
        "svvvvvv",
        shaped((8, 176, 512), BF),
        [vm(16, 512, kind=F32)],
        3.4,
        after=(wa, enc_half, dec_half),
    )
    (packed,) = gated([packed], wa_own[1:])
    recv = to_all(packed, rowgroup)
    wa_oth = [swapped(piece) for piece in wa_own]
    (enc_half,) = gated([enc_half], [packed])
    enc_own = gathered(enc_half)
    cot_in = lax.dynamic_index_in_dim(cotangent[:, 0].reshape(4, 2, 128, 512), sec, 1, False)

    act = shaped((2, TILE, 512), F32)
    actb = shaped((2, TILE, 512), BF)
    mixed_s = shaped((2, 2 * TILE, 128), F32)
    log_s = shaped((2, 1, 2 * TILE), F32)
    kv_b = shaped((4, 128, 128), BF)
    kv_f = shaped((4, 128, 128), F32)
    row_s = shaped((1, 512), F32)
    ffn_g = shaped((4, 256, 1024), BF)
    router_s = shaped((32, 512), F32)
    wide = [vm(512, 512), vm(512, 512)]
    kv_scratch = [vm(4, 2, 128, 128), vm(1024, 128), vm(1024, 128)]
    back_scratch = [
        vm(1024, TILE, kind=F32), vm(1024, 128, kind=F32), vm(1024, 128, kind=F32),
        vm(2, TILE, 512), vm(2, TILE, 512), vm(2, TILE, 512), vm(2, TILE, 512), vm(2, TILE, 128),
        vm(1024, 2 * TILE, kind=F32), vm(1024, 2 * TILE, kind=F32),
        vm(1024, 2 * TILE), vm(1024, 2 * TILE),
    ]
    ffn_w = [vm(4, 512, 512), vm(4, 512, 512)]
    ffn_work = [vm(512, 512, kind=F32), vm(512, 512, kind=F32), vm(512, 512), vm(512, 512)]

    h1, g1, mixed_e, mixed_d, log_e, log_d, meta = run(
        self_fwd_kernel,
        (ids, recv, *wa_own, *wa_oth, kvw_own, kvw_oth),
        "sv" + "a" * 10,
        (act, act, mixed_s, mixed_s, log_s, log_s, shaped((8, 16, 512), BF)),
        [vm(2, 512, 512), vm(2, 512, 512), vm(2, 512, 128), vm(4, 2, 128, 128)]
        + [vm(2, 1024, 128), vm(2, 1024, 128), sem],
        0.3,
    )
    enc_own[1:] = gated(enc_own[1:], [h1])
    enc_oth = [swapped(piece) for piece in enc_own]
    (dec_half,) = gated([dec_half], [enc_own[1]])
    dec_own = gathered(dec_half)
    (cot_in,) = gated([cot_in], [enc_own[1]])
    cot = to_all(cot_in, "mp")
    h2, memory, kvm = run(
        enc_ffn_kernel,
        (ids, meta, h1, keyval_cross, *enc_own, *enc_oth),
        "svvv" + "a" * 8,
        (act, actb, kv_b),
        ffn_w + [vm(2, TILE, 512), sem],
        4.0,
        after=(dec_half, cot_in),
    )
    kvm_oth = swapped(kvm)
    g2, mixed_c, log_c = run(
        cross_fwd_kernel,
        (ids, meta, g1, kvm, kvm_oth, router_c, *wa_own, *wa_oth),
        "svvvvv" + "a" * 8,
        (act, mixed_s, log_s),
        wide + kv_scratch + [sem],
        0.3,
        after=(cot,),
    )
    dec_own[1:] = gated(dec_own[1:], [g2])
    dec_oth = [swapped(piece) for piece in dec_own]
    outs, dg2, gain_d2, keep_d, send_d = run(
        dec_ffn_kernel,
        (ids, meta, g2, memory, cot, *dec_own, *dec_oth),
        "svvva" + "a" * 8,
        (shaped((8, 128, 512), BF), act, row_s, ffn_g, ffn_g),
        ffn_w
        + [vm(4, 128, 512), vm(2, TILE, 512), vm(512, 512), vm(512, 512)]
        + [vm(2, TILE, 512, kind=F32), vm(512, 512, kind=F32), *ffn_work, sem],
        15.0,
    )
    come_d = swapped(send_d)
    outs_come = to_all(outs, rowgroup)
    att_g = shaped((4, 256, 256), BF)
    flat_g = shaped((256, 256), BF)
    dg1, gain_d1, own_c, sendkv_c, router_cg, keep_wc, send_wc = run(
        cross_back_kernel,
        (ids, meta, g1, dg2, mixed_c, log_c, kvm, kvm_oth, router_c, *wa_own, *wa_oth),
        "svvvvvvvv" + "a" * 8,
        (act, row_s, kv_f, kv_b, router_s, att_g, att_g),
        wide + kv_scratch + back_scratch + [sem],
        13.0,
    )
    comekv_c = swapped(sendkv_c)
    dec_a, dec_b = add_shares(keep_d, come_d, 4.0, (dg1, outs_come), 2)
    dh1, gain_e1, gain_e2, keep_e, send_e = run(
        enc_ffn_back_kernel,
        (ids, meta, h1, h2, own_c, comekv_c, keyval_cross, *enc_own, *enc_oth),
        "svvvvvv" + "a" * 8,
        (act, row_s, row_s, ffn_g, ffn_g),
        ffn_w
        + [vm(2, TILE, 512), vm(512, 512), vm(2, TILE, 512), vm(512, 512)]
        + [vm(512, 512, kind=F32), *ffn_work, sem],
        13.4,
        after=(dec_a,),
    )
    dec_a = to_all(dec_a, "mp")
    (dec_b,) = gated([dec_b], [dec_a])
    dec_b = to_all(dec_b, "mp")
    come_e = swapped(send_e)
    self_scratch = wide + [vm(512, 128)] + kv_scratch + back_scratch + [sem]
    att_dg = shaped((4, 256, 512), BF)
    df1, own_1, sendkv_1, router_1g, keep_w1, send_w1 = run(
        functools.partial(self_back_kernel, 1),
        (
            ids, recv, dg1, mixed_d, log_d, *wa_own, *wa_oth, kvw_own, kvw_oth, keep_wc, send_wc,
        ),
        "svvvv" + "a" * 12,
        (act, kv_f, kv_b, router_s, att_dg, att_dg),
        self_scratch,
        12.2,
        after=(dh1, dec_a),
    )
    comekv_1 = swapped(sendkv_1)
    come_w1 = swapped(send_w1)
    (ffn_e,) = add_shares(keep_e, come_e, 4.0, (df1, dec_b))
    att_d = add_pieces(ids, [keep_w1], [come_w1], 3.6, (ffn_e,))
    df0, own_0, sendkv_0, router_0g, keep_w0, send_w0 = run(
        functools.partial(self_back_kernel, 0),
        (ids, recv, dh1, mixed_e, log_e, *wa_own, *wa_oth, kvw_own, kvw_oth),
        "svvvv" + "a" * 10,
        (act, kv_f, kv_b, router_s, att_g, att_g),
        self_scratch,
        11.8,
        after=(ffn_e, *att_d),
    )
    comekv_0 = swapped(sendkv_0)
    come_w0 = swapped(send_w0)
    ffn_e = to_all(ffn_e, "mp")
    att_d = mp_exchange(att_d)
    dx1, gain_d0, keep_s1, send_s1 = run(
        dec_finish_kernel,
        (ids, recv, dg1, df1, own_1, comekv_1, own_c, comekv_c, memory, kvw_own, kvw_oth),
        "svvvvvvvvaa",
        (shaped((4, 128, 512), BF), row_s, flat_g, flat_g),
        [vm(512, 128), vm(2, TILE, 512), sem],
        0.3,
        after=(df0,),
    )
    come_s1 = swapped(send_s1)
    finished = run(
        enc_finish_kernel,
        (
            ids, recv, dh1, df0, own_0, comekv_0, dx1, router_0g, router_1g, router_cg,
            gain_e1, gain_e2, gain_d0, gain_d1, gain_d2, kvw_own, kvw_oth,
        ),
        "s" + "v" * 14 + "aa",
        shaped((8, 208, 512), BF),
        [vm(512, 128), vm(2, TILE, 512), vm(32, 512, kind=F32), sem],
        0.3,
        after=att_d[1:],
    )
    att_e = add_pieces(
        ids, [keep_w0, keep_s1], [come_w0, come_s1], 3.6, (finished,)
    )
    att_e = mp_exchange(att_e)
    dp = lax.axis_size("dp")
    share = 256 // dp
    if dp == 4:
        ffn = dp_exchange(
            run(
                sum_middle_kernel,
                (ids, dec_a, dec_b, ffn_e, *att_d),
                "s" + "v" * 7,
                [shaped((64, 2560), BF)] * 4,
                [],
                4.0,
                after=(att_e[0],),
            )
        )
        after = ffn[1:]
    else:
        after = ()
    finished = to_all(finished, rowgroup)
    small = run(
        tail_kernel,
        (finished, *att_e),
        "v" * 5,
        shaped((256, 768), BF),
        [],
        3.0,
        after=after,
    )
    dx = run(
        place_kernel,
        (finished,),
        "v",
        shaped((4, 2, 128, 512), F32),
        [],
        3.0,
        after=(small,),
    )
    small = to_all(small.reshape(dp, share, 768), "dp")
    outs_come = outs_come.reshape(2, 4, 128, 512).transpose(1, 0, 2, 3)
    results = (outs_come.reshape(1, 4, 1, 256, 512), dx.reshape(1, 4, 1, 256, 512))
    if dp == 4:
        made = run(
            final_kernel,
            (small, *ffn),
            "v" * 5,
            (
                shaped((3, 2, 64), F32),
                shaped((2, 8, 64), F32),
                shaped((2, 2, 64, 64), F32),
                shaped((2, 64, 128), F32),
                shaped((2, 2, 64, 64), F32),
                shaped((2, 64, 512), F32),
                shaped((2, 64, 512), F32),
                shaped((8, 64), F32),
                shaped((2, 64, 64), F32),
                shaped((64, 128), F32),
                shaped((2, 64, 64), F32),
            ),
            [],
            3.0,
        )
        made = list(made)
        made[0] = made[0].transpose(1, 0, 2)
        made[1] = made[1].transpose(0, 2, 1)
        made[6] = made[6].transpose(0, 2, 1)
        made[7] = made[7].T
        return (*results, *made)

    small = jnp.sum(small.astype(F32), 0)
    middle = jnp.concatenate(
        [jnp.sum(part.astype(F32), 0) for part in (ffn_e, dec_a, dec_b)]
        + [sum(part.astype(F32) for part in att_d)],
        1,
    )
    middle = to_all(middle.astype(BF).reshape(dp, share, 2560), "dp")
    middle = jnp.sum(middle.astype(F32), 0)

    def query_of(value, at):
        return value[:, at : at + 128].reshape(share, 2, 64).transpose(1, 0, 2)

    def output_of(value, at):
        return value[:, at + 128 : at + 256].T.reshape(2, 64, share)

    misc = small[:, 640:768].T

    def router_of(layer):
        return misc[ROUTER_LANES[layer] : ROUTER_LANES[layer] + 8].T

    return (
        *results,
        misc[GAIN_ROW : GAIN_ROW + 6].reshape(2, 3, share),
        jnp.stack([router_of(0), router_of(1)]),
        jnp.stack([query_of(small, 0), query_of(middle, 2304)]),
        jnp.stack([small[:, 512:640], small[:, 256:384]]),
        jnp.stack([output_of(small, 0), output_of(middle, 2304)]),
        jnp.stack([middle[:, :512], middle[:, 1024:1536]]),
        jnp.stack([middle[:, 512:1024].T, middle[:, 1536:2048].T]),
        router_of(2),
        query_of(middle, 2048),
        small[:, 384:512],
        output_of(middle, 2048),
    )


def solution(mesh):
    placed = (
        P("section", None, "dp", "mp", None),
        P("section", None, "dp", None),
        P("section", None, "dp", "mp", None),
        P(None, "dp", "mp", None),
        P("section", None, None),
        P("section", None, None),
        P("section", "mp", None, None),
        P("section", None, None),
        P("section", "mp", None, None),
        P("section", None, "mp"),
        P("section", "mp", None),
        P(),
        P("mp", None, None),
        P(),
        P("mp", None, None),
        P(None, "dp", "mp", None),
    )
    return jax.shard_map(
        per_device,
        mesh=mesh,
        in_specs=placed,
        out_specs=(
            P("section", None, "dp", "mp", None),
            P("section", None, "dp", "mp", None),
            P(None, None, ("section", "dp")),
            P(None, ("section", "dp"), None),
            P(None, "mp", ("section", "dp"), None),
            P(None, ("section", "dp"), None),
            P(None, "mp", None, ("section", "dp")),
            P(None, ("section", "dp"), "mp"),
            P(None, "mp", ("section", "dp")),
            P(("section", "dp"), None),
            P("mp", ("section", "dp"), None),
            P(("section", "dp"), None),
            P("mp", None, ("section", "dp")),
        ),
        check_vma=False,
    )
```

```python
import functools

import jax
import jax.numpy as jnp
from jax import lax
from jax.experimental import pallas as pl
from jax.experimental.pallas import tpu as pltpu
from jax.sharding import PartitionSpec as P

EPS = 1e-05
MASK_VALUE = -1000000000.0
BF = jnp.bfloat16
F32 = jnp.float32
TILE = 256
EX_AT = 160
CODE_ROW = 3
LEN_ROW = 4
ROUTER_AT = 8
GAIN_ROW = 24
ROUTER_LANES = (0, 8, 16)
VMEM_LIMIT = 63 * 1024 * 1024
LARGE = 1 << 40


def nn(left, right):
    return lax.dot_general(left, right, (((1,), (0,)), ((), ())), preferred_element_type=F32)


def nt(left, right):
    return lax.dot_general(left, right, (((1,), (1,)), ((), ())), preferred_element_type=F32)


def tn(left, right):
    return lax.dot_general(left, right, (((0,), (0,)), ((), ())), preferred_element_type=F32)


def norm_of(values, gain_row):
    center = values - jnp.mean(values, 1, keepdims=True)
    scaled = lax.rsqrt(jnp.mean(center * center, 1, keepdims=True) + EPS)
    unit_rows = center * scaled
    return unit_rows * gain_row, unit_rows, scaled


def norm_back(upstream, unit_rows, scaled, gain_row):
    inner = upstream * gain_row
    result = scaled * (
        inner
        - jnp.mean(inner, 1, keepdims=True)
        - unit_rows * jnp.mean(inner * unit_rows, 1, keepdims=True)
    )
    return result, jnp.sum(upstream * unit_rows, 0, keepdims=True)


def eye_of(size):
    return lax.broadcasted_iota(jnp.int32, (size, size), 0) == lax.broadcasted_iota(
        jnp.int32, (size, size), 1
    )


def row_to_col(row):
    return jnp.sum(jnp.where(eye_of(128), row, 0.0), 1, keepdims=True)


def col_to_row(col):
    parts = []
    for at in range(0, col.shape[0], 128):
        part = jnp.where(eye_of(128), col[at : at + 128], 0.0)
        parts.append(jnp.sum(part, 0, keepdims=True))
    return jnp.concatenate(parts, 1)


def ends_of(extra):
    lengths = extra[LEN_ROW : LEN_ROW + 1, 0:8] * 32.0 + extra[LEN_ROW : LEN_ROW + 1, 128:136]
    ends = [lengths[:, 0:1]]
    for k in range(1, 8):
        ends.append(ends[-1] + lengths[:, k : k + 1])
    return ends


def segments(places, ends):
    total = jnp.where(places >= ends[0], 1.0, 0.0)
    for end in ends[1:]:
        total = total + jnp.where(places >= end, 1.0, 0.0)
    return total


def extra_of(recv_ref, layer, quarter):
    at = EX_AT if recv_ref.shape[1] > 16 else 0
    return recv_ref[4 * layer + quarter, at : at + 16, :]


def gain_of(recv_ref, layer, which):
    return extra_of(recv_ref, layer, 0).astype(F32)[which : which + 1, :]


def rows_of(recv_ref, layer, t):
    return recv_ref[pl.ds(4 * layer + 2 * t, 2), 0:128, :].reshape(TILE, 512).astype(F32)


def codes_of(recv_ref, layer, t, lane):
    cols = []
    for i in range(2):
        extra = extra_of(recv_ref, layer, 2 * t + i).astype(F32)
        cols.append(row_to_col(extra[CODE_ROW : CODE_ROW + 1, lane : lane + 128]))
    return jnp.concatenate(cols, 0)


def other_kv(recv_ref, layer, quarter):
    packed = recv_ref[4 * layer + quarter, 128:160, :]
    return jnp.concatenate([packed[:, 128 * c : 128 * c + 128] for c in range(4)], 0)


def routing(query_rows, router_block, code):
    second = jnp.floor(code * 0.125)
    first = code - 8.0 * second
    e0, e1 = first.astype(jnp.int32), second.astype(jnp.int32)
    logits = nt(query_rows, router_block)
    lanes = lax.broadcasted_iota(jnp.int32, logits.shape, 1)
    l0 = jnp.sum(jnp.where(lanes == e0 + ROUTER_AT, logits, 0.0), 1, keepdims=True)
    l1 = jnp.sum(jnp.where(lanes == e1 + ROUTER_AT, logits, 0.0), 1, keepdims=True)
    top = jnp.maximum(l0, l1)
    x0, x1 = jnp.exp(l0 - top), jnp.exp(l1 - top)
    total = x0 + x1
    owners = lax.broadcasted_iota(jnp.int32, (code.shape[0], 512), 1) >> 6
    return e0, e1, x0 / total, x1 / total, owners == e0, owners == e1


def fold(wide, mask):
    kept = jnp.where(mask, wide, 0.0)
    return kept[:, 0:128] + kept[:, 128:256] + kept[:, 256:384] + kept[:, 384:512]


def spread(a0, a1, m0, m1):
    parts = []
    for c in range(4):
        cut = slice(128 * c, 128 * c + 128)
        parts.append(jnp.where(m0[:, cut], a0, jnp.where(m1[:, cut], a1, 0.0)))
    return jnp.concatenate(parts, 1).astype(BF)


def rounded(value):
    return value.astype(BF).astype(F32)


def start_pick(cond, yes, no, dst, sem):
    @pl.when(cond)
    def _():
        pltpu.make_async_copy(yes, dst, sem).start()

    @pl.when(jnp.logical_not(cond))
    def _():
        pltpu.make_async_copy(no, dst, sem).start()


class Loads:
    def __init__(self, sems):
        self.sems, self.used = sems, 0

    def start(self, cond, yes, no, dst):
        sem = self.sems.at[self.used]
        self.used += 1
        start_pick(cond, yes, no, dst, sem)
        return functools.partial(lambda a, b, c: pltpu.make_async_copy(a, b, c).wait(), yes, dst, sem)

    def plain(self, src, dst):
        sem = self.sems.at[self.used]
        self.used += 1
        copy = pltpu.make_async_copy(src, dst, sem)
        copy.start()
        return copy.wait

    def rows(self, cond, yes, no, at, dst, m):
        cut = pl.ds(at, 128)
        return [
            self.start(cond, yes[b].at[cut], no[b].at[cut], dst.at[pl.ds(128 * (m ^ b), 128)])
            for b in range(4)
        ]

    def pieces(self, cond, yes, no, dst, m):
        waits = []
        for b, (one, other) in enumerate(zip(yes, no)):
            to = dst.at[m ^ b] if b < 3 else dst.at[m ^ 3, pl.ds(256 * (b - 3), 256)]
            if len(yes) == 4:
                to = dst.at[m ^ b]
            waits.append(self.start(cond, one, other, to))
        return waits


def wait_all(waits):
    for wait in waits:
        wait()


def widen_kv(kv_ref, k2_ref, v2_ref):
    for j in range(4):
        kv = kv_ref[j].reshape(256, 128).astype(F32)
        turned = pltpu.roll(kv, 64, 1)
        low = lax.broadcasted_iota(jnp.int32, kv.shape, 1) < 64
        k2_ref[256 * j : 256 * j + 256, :] = jnp.where(low, kv, turned).astype(BF)
        v2_ref[256 * j : 256 * j + 256, :] = jnp.where(low, turned, kv).astype(BF)


def attend_tile(query_rows, route, w_qt, w_o, k2, v2, allowed):
    e0, e1, g0, g1, m0, m1 = route
    q_all = nt(query_rows, w_qt) * 0.125
    queries = jnp.concatenate([fold(q_all, m0), fold(q_all, m1)], 0).astype(BF)
    scores = nt(queries, k2)
    scores = jnp.concatenate(
        [
            jnp.where(allowed, scores[0:TILE], MASK_VALUE),
            jnp.where(allowed, scores[TILE:], MASK_VALUE),
        ],
        0,
    )
    top = jnp.max(scores, 1, keepdims=True)
    weights = jnp.exp(scores - top)
    total = jnp.sum(weights, 1, keepdims=True)
    mixed = nn(weights.astype(BF), v2) / total
    log_total = top + jnp.log(total)
    gated = spread(rounded(g0) * mixed[0:TILE], rounded(g1) * mixed[TILE:], m0, m1)
    return nn(gated, w_o), mixed, col_to_row(log_total)


def attend_back_tile(
    t, upstream, query_rows, route, mixed, log_row, w_qt, w_o, router_block, router_lane, k2, v2,
    allowed_t, grad_k, grad_v, gated_ref, dz_ref, dq_ref, dlog_ref,
):
    e0, e1, g0, g1, m0, m1 = route
    q_all = nt(query_rows, w_qt) * 0.125
    queries = jnp.concatenate([fold(q_all, m0), fold(q_all, m1)], 0).astype(BF)
    dz = upstream.astype(BF)
    dg_all = nt(dz, w_o)
    dgated0, dgated1 = fold(dg_all, m0), fold(dg_all, m1)
    r0, r1 = rounded(g0), rounded(g1)
    mixed0, mixed1 = mixed[0:TILE], mixed[TILE:]
    gated_ref[t] = spread(r0 * mixed0, r1 * mixed1, m0, m1)
    dz_ref[t] = dz
    dgate0 = rounded(jnp.sum(mixed0 * dgated0, 1, keepdims=True))
    dgate1 = rounded(jnp.sum(mixed1 * dgated1, 1, keepdims=True))
    do0, do1 = (r0 * dgated0).astype(BF), (r1 * dgated1).astype(BF)
    grad_mixed = jnp.concatenate([do0, do1], 0)
    inner_row = jnp.concatenate(
        [
            col_to_row(jnp.sum(do0.astype(F32) * mixed0, 1, keepdims=True)),
            col_to_row(jnp.sum(do1.astype(F32) * mixed1, 1, keepdims=True)),
        ],
        1,
    )
    scores = nt(k2, queries)
    scores = jnp.concatenate(
        [
            jnp.where(allowed_t, scores[:, 0:TILE], MASK_VALUE),
            jnp.where(allowed_t, scores[:, TILE:], MASK_VALUE),
        ],
        1,
    )
    probs = jnp.exp(scores - log_row)
    grad_probs = nt(v2, grad_mixed)
    grad_scores = (probs * (grad_probs - inner_row)).astype(BF)
    grad_v[...] += nn(probs.astype(BF), grad_mixed)
    grad_k[...] += nn(grad_scores, queries)
    grad_q = rounded(tn(grad_scores, k2) * 0.125)
    dq_all = spread(grad_q[0:TILE], grad_q[TILE:], m0, m1)
    dq_ref[t] = dq_all
    grad_rows = nn(dq_all, w_qt)
    mean_grad = g0 * dgate0 + g1 * dgate1
    dc0, dc1 = g0 * (dgate0 - mean_grad), g1 * (dgate1 - mean_grad)
    lanes = lax.broadcasted_iota(jnp.int32, (TILE, 16), 1)
    dlog = jnp.where(lanes == e0 + ROUTER_AT, dc0, 0.0) + jnp.where(
        lanes == e1 + ROUTER_AT, dc1, 0.0
    )
    wide = lax.broadcasted_iota(jnp.int32, (TILE, 128), 1)
    dlog_ref[t] = (
        jnp.where(wide == e0 + router_lane, dc0, 0.0)
        + jnp.where(wide == e1 + router_lane, dc1, 0.0)
    ).astype(BF)
    return grad_rows + nn(dlog.astype(BF), router_block)


def query_places(t, sec, dims, along):
    local = lax.broadcasted_iota(jnp.int32, dims, along)
    return (512 * t + 128 * sec + local + (local & ~127)).astype(F32)


def allowed_rows(t, sec, ends_q, ends_k, causal):
    query_at = query_places(t, sec, (TILE, 1), 0)
    key_at = lax.broadcasted_iota(jnp.int32, (1, 1024), 1).astype(F32)
    allowed = segments(query_at, ends_q) == segments(key_at, ends_k)
    if causal:
        allowed = allowed & (key_at <= query_at)
    return allowed


def key_segments_t(ends_k, segk_ref):
    for j in range(8):
        at = lax.broadcasted_iota(jnp.int32, (128, TILE), 0).astype(F32) + 128.0 * j
        segk_ref[128 * j : 128 * j + 128, :] = segments(at, ends_k)


def allowed_cols(t, sec, ends_q, segk_ref, causal):
    query_at = query_places(t, sec, (1, TILE), 1)
    allowed = segk_ref[...] == segments(query_at, ends_q)
    if causal:
        key_at = lax.broadcasted_iota(jnp.int32, (1024, TILE), 0).astype(F32)
        allowed = allowed & (key_at <= query_at)
    return allowed


def fold_kv(grad_k, grad_v, sec, own_ref, send_ref):
    for j in range(4):
        k = grad_k[256 * j : 256 * j + 256, :]
        v = grad_v[256 * j : 256 * j + 256, :]
        k = k + pltpu.roll(k, 64, 1)
        v = v + pltpu.roll(v, 64, 1)
        low = lax.broadcasted_iota(jnp.int32, k.shape, 1) < 64
        both = jnp.where(low, k, v)
        first, second = both[0:128], both[128:256]
        own_ref[j] = jnp.where(sec == 0, first, second)
        send_ref[j] = jnp.where(sec == 0, second, first).astype(send_ref.dtype)


def split_halves(value, sec, keep_ref, send_ref, m, lane):
    upper, lower = value[0:256], value[256:512]
    cut = slice(lane, lane + value.shape[1])
    keep_ref[m, :, cut] = jnp.where(sec == 0, upper, lower).astype(BF)
    send_ref[m, :, cut] = jnp.where(sec == 0, lower, upper).astype(BF)


def split_flat(value, sec, keep_ref, send_ref, lane):
    upper, lower = value[0:256], value[256:512]
    cut = slice(lane, lane + value.shape[1])
    keep_ref[:, cut] = jnp.where(sec == 0, upper, lower).astype(BF)
    send_ref[:, cut] = jnp.where(sec == 0, lower, upper).astype(BF)


def turned_rows(value):
    return value.astype(F32).T.astype(BF)


def flat(ref):
    return ref[...].reshape(512, ref.shape[-1])


def attention_weight_grads(first_t, gated_ref, dz_ref, dq_ref, sec, keep_ref, send_ref, lane):
    grad_q = nn(first_t, flat(dq_ref))
    grad_o = nn(turned_rows(flat(dz_ref)), flat(gated_ref))
    for b in range(4):
        cut = slice(128 * b, 128 * b + 128)
        split_halves(grad_q[:, cut], sec, keep_ref, send_ref, b, lane)
        split_halves(grad_o[:, cut], sec, keep_ref, send_ref, b, lane + 128)


def router_grads(dlog_ref, rows_ref):
    turned = flat(dlog_ref).astype(F32).T.astype(BF)
    return nn(turned, flat(rows_ref))[0:32]


def gelu_parts(pre):
    cdf = 0.5 * (1.0 + lax.erf(pre * 0.7071067811865476))
    slope = cdf + pre * (jnp.exp(-0.5 * pre * pre) * 0.3989422804014327)
    return pre * cdf, slope


def own_self_kv(recv_ref, layer, sec, w_kv, kv_ref):
    gain = gain_of(recv_ref, layer, 0)
    for t in range(2):
        first = norm_of(rows_of(recv_ref, layer, t), gain)[0].astype(BF)
        kv = nn(first, w_kv).astype(BF)
        for i in range(2):
            j = 2 * t + i
            kv_ref[j, sec] = kv[128 * i : 128 * i + 128]
            kv_ref[j, 1 - sec] = other_kv(recv_ref, layer, j)


def cross_kv(kvm_ref, kvo_ref, sec, kv_s):
    for j in range(4):
        kv_s[j, sec] = kvm_ref[j]
        kv_s[j, 1 - sec] = kvo_ref[j]


def pack_kernel(
    ready, len_ref, x_ref, gain_ref, w_kv_ref, own_ref, cross_ref, router_ref, send_ref, extra_s
):
    ready()
    gain = gain_ref[0:1, :].astype(F32)
    w_kv = w_kv_ref[...]
    extra_s[...] = jnp.zeros_like(extra_s)
    extra_s[0:3, :] = gain_ref[...].astype(F32)
    extra_s[ROUTER_AT : ROUTER_AT + 8, :] = router_ref[...].astype(F32)
    lanes = lax.broadcasted_iota(jnp.int32, (1, 512), 1)
    for i in range(4):
        first = norm_of(x_ref[i].astype(F32), gain)[0].astype(BF)
        kv = nn(first, w_kv).astype(BF)
        row = jnp.zeros((1, 512), jnp.int32)
        for k in range(8):
            length = len_ref[i, k]
            row = jnp.where(lanes == k, length >> 5, row)
            row = jnp.where(lanes == 128 + k, length & 31, row)
        extra_s[LEN_ROW : LEN_ROW + 1, :] = row.astype(F32)
        own, cross = own_ref[i], cross_ref[i]
        own_code = (own[0:1] + 8 * own[1:2]).astype(F32)
        cross_code = (cross[0:1] + 8 * cross[1:2]).astype(F32)
        for half in range(2):
            to = 4 * half + i
            here = slice(128 * half, 128 * half + 128)
            send_ref[to, 0:128, :] = x_ref[i, here, :]
            far = kv[128 * (1 - half) : 128 * (1 - half) + 128]
            send_ref[to, 128:160, :] = jnp.concatenate(
                [far[32 * c : 32 * c + 32] for c in range(4)], 1
            )
            extra_s[CODE_ROW : CODE_ROW + 1, 0:128] = own_code[:, here]
            extra_s[CODE_ROW : CODE_ROW + 1, 128:256] = cross_code[:, here]
            send_ref[to, EX_AT : EX_AT + 16, :] = extra_s[...].astype(BF)


def self_fwd_kernel(ready, ids_ref, recv_ref, *refs):
    wa_own, wa_oth, kvw_own, kvw_oth = refs[:4], refs[4:8], refs[8], refs[9]
    h1_ref, g1_ref, mixed_e, mixed_d, log_e, log_d, meta_ref = refs[10:17]
    wq, wo, wkv, kv_s, k2, v2, sems = refs[17:]
    sec, m = ids_ref[0], ids_ref[1]
    loads = Loads(sems)
    kv_waits = [loads.start(sec == i, kvw_own, kvw_oth, wkv.at[i]) for i in range(2)]
    waits = []
    for layer in range(2):
        waits += loads.rows(sec == layer, wa_own, wa_oth, 0, wq.at[layer], m)
        waits += loads.rows(sec == layer, wa_own, wa_oth, 128, wo.at[layer], m)
    ready()
    meta_ref[...] = recv_ref[:, EX_AT : EX_AT + 16, :]
    wait_all(kv_waits)
    for layer in range(2):
        own_self_kv(recv_ref, layer, sec, wkv[layer], kv_s)
        widen_kv(kv_s, k2.at[layer], v2.at[layer])
    wait_all(waits)
    ends = [ends_of(extra_of(recv_ref, layer, 0).astype(F32)) for layer in range(2)]

    def tile(t, carry):
        for layer, after_ref, mixed_ref, log_ref in (
            (0, h1_ref, mixed_e, log_e),
            (1, g1_ref, mixed_d, log_d),
        ):
            rows = rows_of(recv_ref, layer, t)
            first = norm_of(rows, gain_of(recv_ref, layer, 0))[0].astype(BF)
            route = routing(first, extra_of(recv_ref, layer, 0), codes_of(recv_ref, layer, t, 0))
            allowed = allowed_rows(t, sec, ends[layer], ends[layer], layer == 1)
            out, mixed, row_log = attend_tile(
                first, route, wq[layer], wo[layer], k2[layer], v2[layer], allowed
            )
            after_ref[t] = rows + out
            mixed_ref[t] = mixed
            log_ref[t] = row_log
        return carry

    lax.fori_loop(0, 2, tile, 0)


def enc_ffn_kernel(ready, ids_ref, recv_ref, h1_ref, kvc_ref, *refs):
    f_own, f_oth = refs[:4], refs[4:8]
    h2_ref, mem_ref, kvm_ref, w_in, w_out, third_s, sems = refs[8:]
    low, m = ids_ref[0] == 0, ids_ref[1]
    loads = Loads(sems)
    waits = loads.pieces(low, f_own, f_oth, w_in, m) + loads.pieces(low, f_oth, f_own, w_out, m)
    ready()
    for t in range(2):
        h2_ref[t] = h1_ref[t]
        third_s[t] = norm_of(h1_ref[t], gain_of(recv_ref, 0, 2))[0].astype(BF)
    wait_all(waits)

    def chunk(c, carry):
        pre = nn(flat(third_s), w_in[c])
        hidden = (0.5 * pre * (1.0 + lax.erf(pre * 0.7071067811865476))).astype(BF)
        h2_ref[...] += nn(hidden, w_out[c]).reshape(2, TILE, 512)
        return carry

    lax.fori_loop(0, 4, chunk, 0)
    for t in range(2):
        memory = norm_of(h2_ref[t], gain_of(recv_ref, 0, 1))[0].astype(BF)
        mem_ref[t] = memory
        kv = nn(memory, kvc_ref[...]).astype(BF)
        kvm_ref[2 * t] = kv[0:128]
        kvm_ref[2 * t + 1] = kv[128:256]


def cross_fwd_kernel(
    ready, ids_ref, recv_ref, g1_ref, kvm_ref, kvo_ref, rc_ref, *refs
):
    wa_own, wa_oth = refs[:4], refs[4:8]
    g2_ref, mixed_ref, log_ref, wq, wo, kv_s, k2, v2, sems = refs[8:]
    sec, m = ids_ref[0], ids_ref[1]
    loads = Loads(sems)
    waits = loads.rows(sec == 0, wa_own, wa_oth, 256, wq, m)
    waits += loads.rows(sec == 0, wa_oth, wa_own, 256, wo, m)
    ready()
    cross_kv(kvm_ref, kvo_ref, sec, kv_s)
    widen_kv(kv_s, k2, v2)
    wait_all(waits)
    ends_k = ends_of(extra_of(recv_ref, 0, 0).astype(F32))
    ends_q = ends_of(extra_of(recv_ref, 1, 0).astype(F32))

    def tile(t, carry):
        before = g1_ref[t]
        second = norm_of(before, gain_of(recv_ref, 1, 1))[0].astype(BF)
        route = routing(second, rc_ref[...], codes_of(recv_ref, 1, t, 128))
        allowed = allowed_rows(t, sec, ends_q, ends_k, False)
        out, mixed, row_log = attend_tile(second, route, wq[...], wo[...], k2[...], v2[...], allowed)
        g2_ref[t] = before + out
        mixed_ref[t] = mixed
        log_ref[t] = row_log
        return carry

    lax.fori_loop(0, 2, tile, 0)


def ffn_both(c, third_s, third_t, dy_s, dy_t, w_in, w_out, dthird, sec, keep_ref, send_ref):
    pre = nn(flat(third_s), w_in[c])
    hidden, slope = gelu_parts(pre)
    hidden = hidden.astype(BF)
    dpre = (nt(flat(dy_s), w_out[c]) * slope).astype(BF)
    dthird[...] += nt(dpre, w_in[c])
    split_halves(nn(third_t[...], dpre), sec, keep_ref, send_ref, c, 0)
    split_halves(nn(dy_t[...], hidden), sec, keep_ref, send_ref, c, 512)
    return hidden


def dec_ffn_kernel(ready, ids_ref, recv_ref, g2_ref, mem_ref, cot_in, *refs):
    f_own, f_oth = refs[:5], refs[5:10]
    outs_ref, dg2_ref, gain_ref, keep_ref, send_ref = refs[10:15]
    w_in, w_out, cot_s, third_s, third_t, cot_t, acc, dthird, sems = refs[15:]
    sec, m = ids_ref[0], ids_ref[1]
    low = sec == 0
    loads = Loads(sems)
    cot_waits = [loads.plain(cot_in.at[i], cot_s.at[i]) for i in range(4)]
    waits = loads.pieces(low, f_own, f_oth, w_in, m) + loads.pieces(low, f_oth, f_own, w_out, m)
    ready()
    for t in range(2):
        acc[t] = g2_ref[t]
        third_s[t] = norm_of(g2_ref[t], gain_of(recv_ref, 1, 2))[0].astype(BF)
        outs_ref[2 * t : 2 * t + 2] = mem_ref[t].reshape(2, 128, 512)
    third_t[...] = turned_rows(flat(third_s))
    wait_all(cot_waits)
    cot_t[...] = turned_rows(flat(cot_s))
    dthird[...] = jnp.zeros_like(dthird)
    wait_all(waits)

    def chunk(c, carry):
        hidden = ffn_both(
            c, third_s, third_t, cot_s, cot_t, w_in, w_out, dthird, sec, keep_ref, send_ref
        )
        acc[...] += nn(hidden, w_out[c]).reshape(2, TILE, 512)
        return carry

    lax.fori_loop(0, 4, chunk, 0)
    total = jnp.zeros((1, 512), F32)
    gain = gain_of(recv_ref, 1, 2)
    for t in range(2):
        outs_ref[4 + 2 * t : 6 + 2 * t] = acc[t].astype(BF).reshape(2, 128, 512)
        unused_out, unit, scaled = norm_of(g2_ref[t], gain)
        back, gain_grad = norm_back(dthird[TILE * t : TILE * t + TILE, :], unit, scaled, gain)
        dg2_ref[t] = cot_s[2 * t : 2 * t + 2].reshape(TILE, 512).astype(F32) + back
        total = total + gain_grad
    gain_ref[...] = total


def cross_back_kernel(
    ready, ids_ref, recv_ref, g1_ref, dg2_ref, mixed_ref, log_ref, kvm_ref, kvo_ref, rc_ref, *refs
):
    wa_own, wa_oth = refs[:4], refs[4:8]
    dg1_ref, gain_ref, own_ref, send_ref, router_ref, keepw_ref, sendw_ref = refs[8:15]
    wq, wo, kv_s, k2, v2, segk, grad_k, grad_v, second_s, gated_s, dz_s, dq_s, dlog_s, sems = refs[15:]
    sec, m = ids_ref[0], ids_ref[1]
    loads = Loads(sems)
    waits = loads.rows(sec == 0, wa_own, wa_oth, 256, wq, m)
    waits += loads.rows(sec == 0, wa_oth, wa_own, 256, wo, m)
    ready()
    cross_kv(kvm_ref, kvo_ref, sec, kv_s)
    widen_kv(kv_s, k2, v2)
    ends_k = ends_of(extra_of(recv_ref, 0, 0).astype(F32))
    ends_q = ends_of(extra_of(recv_ref, 1, 0).astype(F32))
    key_segments_t(ends_k, segk)
    grad_k[...] = jnp.zeros_like(grad_k)
    grad_v[...] = jnp.zeros_like(grad_v)
    wait_all(waits)

    def tile(t, total):
        gain = gain_of(recv_ref, 1, 1)
        second, unit, scaled = norm_of(g1_ref[t], gain)
        second = second.astype(BF)
        second_s[t] = second
        route = routing(second, rc_ref[...], codes_of(recv_ref, 1, t, 128))
        allowed = allowed_cols(t, sec, ends_q, segk, False)
        grad_rows = attend_back_tile(
            t, dg2_ref[t], second, route, mixed_ref[t], log_ref[t], wq[...], wo[...], rc_ref[...],
            ROUTER_LANES[2], k2[...], v2[...], allowed, grad_k, grad_v, gated_s, dz_s, dq_s, dlog_s,
        )
        back, gain_grad = norm_back(grad_rows, unit, scaled, gain)
        dg1_ref[t] = dg2_ref[t] + back
        return total + gain_grad

    gain_ref[...] = lax.fori_loop(0, 2, tile, jnp.zeros((1, 512), F32))
    fold_kv(grad_k, grad_v, sec, own_ref, send_ref)
    router_ref[...] = router_grads(dlog_s, second_s)
    attention_weight_grads(
        turned_rows(flat(second_s)), gated_s, dz_s, dq_s, sec, keepw_ref, sendw_ref, 0
    )


def self_back_kernel(layer, ready, ids_ref, recv_ref, up_ref, mixed_ref, log_ref, *refs):
    wa_own, wa_oth, kvw_own, kvw_oth = refs[:4], refs[4:8], refs[8], refs[9]
    refs = refs[10:]
    if layer == 1:
        before, refs = refs[:2], refs[2:]
    dfirst_ref, own_ref, send_ref, router_ref, keepw_ref, sendw_ref = refs[:6]
    wq, wo, wkv, kv_s, k2, v2, segk, grad_k, grad_v = refs[6:15]
    first_s, gated_s, dz_s, dq_s, dlog_s, sems = refs[15:]
    sec, m = ids_ref[0], ids_ref[1]
    mine = sec == layer
    loads = Loads(sems)
    kv_wait = loads.start(mine, kvw_own, kvw_oth, wkv)
    waits = loads.rows(mine, wa_own, wa_oth, 0, wq, m) + loads.rows(mine, wa_own, wa_oth, 128, wo, m)
    lane = 0
    if layer == 1:
        lane = 256
        for src, dst in zip(before, (keepw_ref, sendw_ref)):
            waits.append(loads.plain(src, dst.at[:, :, pl.ds(0, 256)]))
    ready()
    ends = ends_of(extra_of(recv_ref, layer, 0).astype(F32))
    key_segments_t(ends, segk)
    grad_k[...] = jnp.zeros_like(grad_k)
    grad_v[...] = jnp.zeros_like(grad_v)
    kv_wait()
    own_self_kv(recv_ref, layer, sec, wkv[...], kv_s)
    widen_kv(kv_s, k2, v2)
    wait_all(waits)
    router_block = extra_of(recv_ref, layer, 0)

    def tile(t, carry):
        first = norm_of(rows_of(recv_ref, layer, t), gain_of(recv_ref, layer, 0))[0].astype(BF)
        first_s[t] = first
        route = routing(first, router_block, codes_of(recv_ref, layer, t, 0))
        allowed = allowed_cols(t, sec, ends, segk, layer == 1)
        dfirst_ref[t] = attend_back_tile(
            t, up_ref[t], first, route, mixed_ref[t], log_ref[t], wq[...], wo[...], router_block,
            ROUTER_LANES[layer], k2[...], v2[...], allowed, grad_k, grad_v, gated_s, dz_s, dq_s,
            dlog_s,
        )
        return carry

    lax.fori_loop(0, 2, tile, 0)
    fold_kv(grad_k, grad_v, sec, own_ref, send_ref)
    router_ref[...] = router_grads(dlog_s, first_s)
    attention_weight_grads(
        turned_rows(flat(first_s)), gated_s, dz_s, dq_s, sec, keepw_ref, sendw_ref, lane
    )


def enc_ffn_back_kernel(
    ready, ids_ref, recv_ref, h1_ref, h2_ref, own_ref, come_ref, kvc_ref, *refs
):
    f_own, f_oth = refs[:4], refs[4:8]
    dh1_ref, gain_ref, gain2_ref, keep_ref, send_ref = refs[8:13]
    w_in, w_out, third_s, third_t, dy_s, dy_t, dthird, sems = refs[13:]
    sec, m = ids_ref[0], ids_ref[1]
    low = sec == 0
    loads = Loads(sems)
    waits = loads.pieces(low, f_own, f_oth, w_in, m) + loads.pieces(low, f_oth, f_own, w_out, m)
    ready()
    total = jnp.zeros((1, 512), F32)
    gain = gain_of(recv_ref, 0, 1)
    for t in range(2):
        dkv = (own_ref[2 * t : 2 * t + 2] + come_ref[2 * t : 2 * t + 2].astype(F32)).astype(BF)
        dmem = rounded(nt(dkv.reshape(TILE, 128), kvc_ref[...]))
        unused_out, unit, scaled = norm_of(h2_ref[t], gain)
        back, gain_grad = norm_back(dmem, unit, scaled, gain)
        dh1_ref[t] = back
        dy_s[t] = back.astype(BF)
        third_s[t] = norm_of(h1_ref[t], gain_of(recv_ref, 0, 2))[0].astype(BF)
        total = total + gain_grad
    gain_ref[...] = total
    third_t[...] = turned_rows(flat(third_s))
    dy_t[...] = turned_rows(flat(dy_s))
    dthird[...] = jnp.zeros_like(dthird)
    wait_all(waits)

    def chunk(c, carry):
        ffn_both(c, third_s, third_t, dy_s, dy_t, w_in, w_out, dthird, sec, keep_ref, send_ref)
        return carry

    lax.fori_loop(0, 4, chunk, 0)
    total = jnp.zeros((1, 512), F32)
    gain = gain_of(recv_ref, 0, 2)
    for t in range(2):
        unused_out, unit, scaled = norm_of(h1_ref[t], gain)
        back, gain_grad = norm_back(dthird[TILE * t : TILE * t + TILE, :], unit, scaled, gain)
        dh1_ref[t] += back
        total = total + gain_grad
    gain2_ref[...] = total


def finish_rows(layer, recv_ref, up_ref, df_ref, own_ref, come_ref, wkv, first_s, out_ref, at):
    total = jnp.zeros((1, 512), F32)
    gain = gain_of(recv_ref, layer, 0)
    dkvs = []
    for t in range(2):
        first, unit, scaled = norm_of(rows_of(recv_ref, layer, t), gain)
        first_s[t] = first.astype(BF)
        dkv = (own_ref[2 * t : 2 * t + 2] + come_ref[2 * t : 2 * t + 2].astype(F32)).astype(BF)
        dkv = dkv.reshape(TILE, 128)
        dkvs.append(dkv)
        back, gain_grad = norm_back(df_ref[t] + nt(dkv, wkv), unit, scaled, gain)
        dx = (up_ref[t] + back).astype(BF)
        for i in range(2):
            out_ref[at + 2 * t + i, 0:128, :] = dx[128 * i : 128 * i + 128]
        total = total + gain_grad
    grad = nn(turned_rows(flat(first_s)), jnp.concatenate(dkvs, 0))
    return total, grad


def dec_finish_kernel(
    ready, ids_ref, recv_ref, up_ref, df_ref, own_ref, come_ref, own_c, come_c, mem_ref, kvw_own, kvw_oth,
    dx_ref, gain_ref, keep_ref, send_ref, wkv, first_s, sems,
):
    sec = ids_ref[0]
    wait = Loads(sems).start(sec == 1, kvw_own, kvw_oth, wkv)
    ready()
    dkv_c = (own_c[...] + come_c[...].astype(F32)).astype(BF).reshape(512, 128)
    split_flat(nn(turned_rows(flat(mem_ref)), dkv_c), sec, keep_ref, send_ref, 128)
    wait()
    gain_ref[...], grad = finish_rows(
        1, recv_ref, up_ref, df_ref, own_ref, come_ref, wkv[...], first_s, dx_ref, 0
    )
    split_flat(grad, sec, keep_ref, send_ref, 0)


def enc_finish_kernel(
    ready, ids_ref, recv_ref, up_ref, df_ref, own_ref, come_ref, dx1_ref, r0, r1, rc,
    gain_e1, gain_e2, gain_d0, gain_d1, gain_d2, kvw_own, kvw_oth,
    out_ref, wkv, first_s, misc, sems,
):
    sec = ids_ref[0]
    wait = Loads(sems).start(sec == 0, kvw_own, kvw_oth, wkv)
    ready()
    misc[...] = r0[...] + r1[...] + rc[...]
    out_ref[4:8, 0:128, :] = dx1_ref[...]
    wait()
    gain_e0, grad = finish_rows(
        0, recv_ref, up_ref, df_ref, own_ref, come_ref, wkv[...], first_s, out_ref, 0
    )
    rows = (gain_e0, gain_e1[...], gain_e2[...], gain_d0[...], gain_d1[...], gain_d2[...])
    for i, row in enumerate(rows):
        misc[GAIN_ROW + i : GAIN_ROW + i + 1, :] = row
    both = misc[...]
    for half in range(2):
        cut = slice(256 * half, 256 * half + 256)
        part = grad[cut].astype(BF)
        small = both[:, cut].astype(BF)
        block = jnp.concatenate(
            [
                jnp.concatenate([part[64 * c : 64 * c + 64] for c in range(4)], 1),
                jnp.concatenate([small[0:16], small[16:32]], 1),
            ],
            0,
        )
        for i in range(4):
            out_ref[4 * half + i, 128:208, :] = block


def add_kernel(keep_ref, come_ref, *outs):
    lane = 0
    for out_ref in outs:
        cut = slice(lane, lane + out_ref.shape[-1])
        out_ref[...] = keep_ref[:, :, cut] + come_ref[:, :, cut]
        lane += out_ref.shape[-1]


def add_pieces_kernel(flats, ready, ids_ref, *refs):
    ready()
    n = len(flats)
    keeps, comes, outs = refs[:n], refs[n : 2 * n], refs[2 * n :]
    m = ids_ref[1]
    for b in range(4):
        lane = 0
        for is_flat, keep, come in zip(flats, keeps, comes):
            left = keep[...] if is_flat else keep[m ^ b]
            right = come[...] if is_flat else come[m ^ b]
            width = keep.shape[-1]
            outs[b][:, lane : lane + width] = left + right
            lane += width


def sum_middle_kernel(ready, ids_ref, dec_a, dec_b, enc_ref, *refs):
    att, outs = refs[:4], refs[4:]
    ready()
    rows = outs[0].shape[0]
    d = ids_ref[2]
    for k in range(len(outs)):
        cut = pl.ds(pl.multiple_of((d ^ k) * rows, rows), rows)
        for ref, lane in ((enc_ref, 0), (dec_a, 1024), (dec_b, 1536)):
            total = ref[0, cut, :].astype(F32)
            for i in range(1, 4):
                total = total + ref[i, cut, :].astype(F32)
            outs[k][:, lane : lane + ref.shape[-1]] = total.astype(BF)
        total = att[0][cut, :].astype(F32)
        for part in att[1:]:
            total = total + part[cut, :].astype(F32)
        outs[k][:, 2048:2560] = total.astype(BF)


def place_kernel(ready, dx_ref, dx_out):
    ready()
    for i in range(4):
        for half in range(2):
            dx_out[i, half] = dx_ref[4 * half + i, 0:128, :].astype(F32)


def tail_kernel(ready, dx_ref, *refs):
    att_e, (out_ref,) = refs[:4], refs[4:]
    ready()
    total = att_e[0][...].astype(F32)
    for part in att_e[1:]:
        total = total + part[...].astype(F32)
    out_ref[:, 0:512] = total.astype(BF)
    small = dx_ref[0, 128:208, :].astype(F32)
    for i in range(1, 8):
        small = small + dx_ref[i, 128:208, :].astype(F32)
    for c in range(4):
        out_ref[64 * c : 64 * c + 64, 512:640] = small[0:64, 128 * c : 128 * c + 128].astype(BF)
    misc = jnp.concatenate([small[64:80, 0:256], small[64:80, 256:512]], 0)
    misc = jnp.concatenate([misc, jnp.zeros((96, 256), F32)], 0)
    out_ref[:, 640:768] = misc.T.astype(BF)


def final_kernel(ready, come_ref, *refs):
    middle, outs = refs[:4], refs[4:]
    ready()
    gains, router, query, keyval, output, inner, outer, router_c, query_c, keyval_c, output_c = outs
    small = come_ref[0].astype(F32)
    for i in range(1, 4):
        small = small + come_ref[i].astype(F32)
    wide = middle[0][...].astype(F32)
    for part in middle[1:]:
        wide = wide + part[...].astype(F32)
    for layer in range(2):
        inner[layer] = wide[:, 1024 * layer : 1024 * layer + 512]
        outer[layer] = wide[:, 1024 * layer + 512 : 1024 * layer + 1024]
    keyval[0], keyval[1] = small[:, 512:640], small[:, 256:384]
    keyval_c[...] = small[:, 384:512]
    for source, at, put_q, put_o in (
        (wide, 2048, query_c, output_c),
        (wide, 2304, query.at[1], output.at[1]),
        (small, 0, query.at[0], output.at[0]),
    ):
        turned = source[:, at + 128 : at + 256].T
        for e in range(2):
            put_q[e] = source[:, at + 64 * e : at + 64 * e + 64]
            put_o[e] = turned[64 * e : 64 * e + 64]
    misc = small[:, 640:768].T
    router[0], router[1], router_c[...] = misc[0:8], misc[8:16], misc[16:24]
    for i in range(3):
        gains[i, 0:1] = misc[24 + i : 25 + i]
        gains[i, 1:2] = misc[27 + i : 28 + i]


def shaped(dims, kind):
    return jax.ShapeDtypeStruct(dims, kind)


def cost_of(micros):
    return pl.CostEstimate(
        flops=int(micros * 1.1535e9), bytes_accessed=int(micros * 3.0e6), transcendentals=0
    )


def run(kernel, args, places, outs, scratch, micros, after=()):
    space = {
        "s": pl.BlockSpec(memory_space=pltpu.SMEM),
        "v": pl.BlockSpec(memory_space=pltpu.VMEM),
        "a": pl.BlockSpec(memory_space=pl.ANY),
    }
    large = [
        i for i, (p, a) in enumerate(zip(places, args)) if p == "v" and a.size * a.dtype.itemsize > LARGE
    ]
    places = ["a" if i in large else p for i, p in enumerate(places)]
    count, extra = len(args), len(after)
    copies = [pltpu.VMEM(args[i].shape, args[i].dtype) for i in large]

    def body(*refs):
        given, rest = list(refs[:count]), refs[count + extra :]
        if large:
            rest, held, sems = rest[: -len(large) - 1], rest[-len(large) - 1 : -1], rest[-1]
            moves = []
            for n, i in enumerate(large):
                moves.append(pltpu.make_async_copy(given[i], held[n], sems.at[n]))
                given[i] = held[n]
            for move in moves:
                move.start()
        else:
            moves = []

        def ready():
            for move in moves:
                move.wait()

        kernel(ready, *given, *rest)

    return pl.pallas_call(
        body,
        out_shape=outs,
        in_specs=[space[p] for p in places] + [space["a"]] * extra,
        out_specs=jax.tree.map(lambda _: space["v"], outs),
        scratch_shapes=scratch + copies + ([dma(len(large))] if large else []),
        compiler_params=pltpu.CompilerParams(vmem_limit_bytes=VMEM_LIMIT),
        cost_estimate=cost_of(micros),
    )(*args, *after)


def vm(*dims, kind=BF):
    return pltpu.VMEM(dims, kind)


def dma(count):
    return pltpu.SemaphoreType.DMA((count,))


def across(value, axes, size, by):
    return lax.ppermute(value, axes, [(i, i ^ by) for i in range(size)])


def swapped(value):
    return across(value, "section", 2, 1)


def gathered(value):
    return [value] + [across(value, "mp", 4, b) for b in range(1, 4)]


def to_all(value, axes):
    return lax.all_to_all(value, axes, split_axis=0, concat_axis=0, tiled=True)


def add_shares(keep, come, micros, after, parts=1):
    blocks, rows, width = keep.shape
    whole = pl.BlockSpec((1, rows, width), lambda i: (i, 0, 0))
    part = pl.BlockSpec((1, rows, width // parts), lambda i: (i, 0, 0))
    extra = len(after)
    return pl.pallas_call(
        lambda k, c, *rest: add_kernel(k, c, *rest[extra:]),
        out_shape=[shaped((blocks, rows, width // parts), BF)] * parts,
        grid=(blocks,),
        in_specs=[whole, whole] + [pl.BlockSpec(memory_space=pl.ANY)] * extra,
        out_specs=[part] * parts,
        cost_estimate=cost_of(micros),
    )(keep, come, *after)


def add_pieces(ids, keeps, comes, micros, after=()):
    flats = tuple(keep.ndim == 2 for keep in keeps)
    width = sum(keep.shape[-1] for keep in keeps)
    return run(
        functools.partial(add_pieces_kernel, flats),
        (ids, *keeps, *comes),
        "s" + "v" * (2 * len(keeps)),
        [shaped((256, width), BF)] * 4,
        [],
        micros,
        after=after,
    )


def mp_exchange(pieces):
    return [pieces[0]] + [across(pieces[b], "mp", 4, b) for b in range(1, 4)]


def dp_exchange(pieces):
    return [pieces[0]] + [across(pieces[k], "dp", 4, k) for k in range(1, 4)]


def gated(values, after):
    anywhere = pl.BlockSpec(memory_space=pl.ANY)
    count = len(values)
    return pl.pallas_call(
        lambda *refs: None,
        out_shape=[shaped(v.shape, v.dtype) for v in values],
        in_specs=[anywhere] * (count + len(after)),
        out_specs=[anywhere] * count,
        input_output_aliases={i: i for i in range(count)},
        cost_estimate=cost_of(0.2),
    )(*values, *after)


def per_device(
    inputs,
    lengths,
    routes_self,
    routes_cross,
    gains,
    router_self,
    query_self,
    keyval_self,
    output_self,
    ffn_in,
    ffn_out,
    router_cross,
    query_cross,
    keyval_cross,
    output_cross,
    cotangent,
):
    sec, m, d = lax.axis_index("section"), lax.axis_index("mp"), lax.axis_index("dp")
    low = sec == 0
    ids = jnp.stack([sec, m, d]).astype(jnp.int32)
    sem = dma(24)
    rowgroup = ("section", "mp")

    q_rows = query_self[0].transpose(0, 2, 1).reshape(128, 512)
    o_rows = output_self[0].reshape(128, 512)
    c_rows = jnp.where(
        low, query_cross.transpose(0, 2, 1).reshape(128, 512), output_cross.reshape(128, 512)
    )
    wa = jnp.concatenate([q_rows, o_rows, c_rows], 0)
    wa_own = gathered(wa)
    w_in, w_out = ffn_in[0], ffn_out[0]
    half_come = swapped(jnp.where(low, w_out, w_in))
    enc_half = jnp.where(low, w_in, half_come)
    dec_half = jnp.where(low, half_come, w_out)
    kvw_own = keyval_self[0]
    kvw_oth = swapped(kvw_own)
    router_c = jnp.concatenate([jnp.zeros((8, 512), BF), router_cross.T], 0)

    packed = run(
        pack_kernel,
        (
            lengths[0, :, 0],
            inputs[0, :, 0],
            gains[0],
            keyval_self[0],
            routes_self[0, :, 0].transpose(0, 2, 1),
            routes_cross[:, 0].transpose(0, 2, 1),
            router_self[0].T,
        ),
        "svvvvvv",
        shaped((8, 176, 512), BF),
        [vm(16, 512, kind=F32)],
        3.4,
        after=(wa, enc_half, dec_half),
    )
    (packed,) = gated([packed], wa_own[1:])
    recv = to_all(packed, rowgroup)
    wa_oth = [swapped(piece) for piece in wa_own]
    (enc_half,) = gated([enc_half], [packed])
    enc_own = gathered(enc_half)
    cot_in = lax.dynamic_index_in_dim(cotangent[:, 0].reshape(4, 2, 128, 512), sec, 1, False)

    act = shaped((2, TILE, 512), F32)
    actb = shaped((2, TILE, 512), BF)
    mixed_s = shaped((2, 2 * TILE, 128), F32)
    log_s = shaped((2, 1, 2 * TILE), F32)
    kv_b = shaped((4, 128, 128), BF)
    kv_f = shaped((4, 128, 128), F32)
    row_s = shaped((1, 512), F32)
    ffn_g = shaped((4, 256, 1024), BF)
    router_s = shaped((32, 512), F32)
    wide = [vm(512, 512), vm(512, 512)]
    kv_scratch = [vm(4, 2, 128, 128), vm(1024, 128), vm(1024, 128)]
    back_scratch = [
        vm(1024, TILE, kind=F32), vm(1024, 128, kind=F32), vm(1024, 128, kind=F32),
        vm(2, TILE, 512), vm(2, TILE, 512), vm(2, TILE, 512), vm(2, TILE, 512), vm(2, TILE, 128),
    ]
    ffn_w = [vm(4, 512, 512), vm(4, 512, 512)]

    h1, g1, mixed_e, mixed_d, log_e, log_d, meta = run(
        self_fwd_kernel,
        (ids, recv, *wa_own, *wa_oth, kvw_own, kvw_oth),
        "sv" + "a" * 10,
        (act, act, mixed_s, mixed_s, log_s, log_s, shaped((8, 16, 512), BF)),
        [vm(2, 512, 512), vm(2, 512, 512), vm(2, 512, 128), vm(4, 2, 128, 128)]
        + [vm(2, 1024, 128), vm(2, 1024, 128), sem],
        0.3,
    )
    enc_own[1:] = gated(enc_own[1:], [h1])
    enc_oth = [swapped(piece) for piece in enc_own]
    (dec_half,) = gated([dec_half], [enc_own[1]])
    dec_near = [across(dec_half, "mp", 4, b) for b in (1, 2)]
    (cot_in,) = gated([cot_in], [enc_own[1]])
    cot = to_all(cot_in, "mp")
    h2, memory, kvm = run(
        enc_ffn_kernel,
        (ids, meta, h1, keyval_cross, *enc_own, *enc_oth),
        "svvv" + "a" * 8,
        (act, actb, kv_b),
        ffn_w + [vm(2, TILE, 512), sem],
        4.0,
        after=(dec_half, cot_in),
    )
    kvm_oth = swapped(kvm)
    dec_near = gated(dec_near, [h2])
    dec_far = [
        across(dec_near[1][0:256], "mp", 4, 1),
        across(dec_near[0][256:512], "mp", 4, 2),
    ]
    g2, mixed_c, log_c = run(
        cross_fwd_kernel,
        (ids, meta, g1, kvm, kvm_oth, router_c, *wa_own, *wa_oth),
        "svvvvv" + "a" * 8,
        (act, mixed_s, log_s),
        wide + kv_scratch + [sem],
        0.3,
        after=(cot,),
    )
    dec_far = gated(dec_far, [g2])
    dec_own = [dec_half, *dec_near, *dec_far]
    dec_oth = [swapped(piece) for piece in dec_own]
    outs, dg2, gain_d2, keep_d, send_d = run(
        dec_ffn_kernel,
        (ids, meta, g2, memory, cot, *dec_own, *dec_oth),
        "svvva" + "a" * 10,
        (shaped((8, 128, 512), BF), act, row_s, ffn_g, ffn_g),
        ffn_w
        + [vm(4, 128, 512), vm(2, TILE, 512), vm(512, 512), vm(512, 512)]
        + [vm(2, TILE, 512, kind=F32), vm(512, 512, kind=F32), sem],
        15.0,
    )
    come_d = swapped(send_d)
    outs_come = to_all(outs, rowgroup)
    att_g = shaped((4, 256, 256), BF)
    flat_g = shaped((256, 256), BF)
    dg1, gain_d1, own_c, sendkv_c, router_cg, keep_wc, send_wc = run(
        cross_back_kernel,
        (ids, meta, g1, dg2, mixed_c, log_c, kvm, kvm_oth, router_c, *wa_own, *wa_oth),
        "svvvvvvvv" + "a" * 8,
        (act, row_s, kv_f, kv_b, router_s, att_g, att_g),
        wide + kv_scratch + back_scratch + [sem],
        13.0,
    )
    comekv_c = swapped(sendkv_c)
    dec_a, dec_b = add_shares(keep_d, come_d, 4.0, (dg1, outs_come), 2)
    dh1, gain_e1, gain_e2, keep_e, send_e = run(
        enc_ffn_back_kernel,
        (ids, meta, h1, h2, own_c, comekv_c, keyval_cross, *enc_own, *enc_oth),
        "svvvvvv" + "a" * 8,
        (act, row_s, row_s, ffn_g, ffn_g),
        ffn_w
        + [vm(2, TILE, 512), vm(512, 512), vm(2, TILE, 512), vm(512, 512)]
        + [vm(512, 512, kind=F32), sem],
        13.4,
        after=(dec_a,),
    )
    dec_a = to_all(dec_a, "mp")
    (dec_b,) = gated([dec_b], [dec_a])
    dec_b = to_all(dec_b, "mp")
    come_e = swapped(send_e)
    self_scratch = wide + [vm(512, 128)] + kv_scratch + back_scratch + [sem]
    att_dg = shaped((4, 256, 512), BF)
    df1, own_1, sendkv_1, router_1g, keep_w1, send_w1 = run(
        functools.partial(self_back_kernel, 1),
        (
            ids, recv, dg1, mixed_d, log_d, *wa_own, *wa_oth, kvw_own, kvw_oth, keep_wc, send_wc,
        ),
        "svvvv" + "a" * 12,
        (act, kv_f, kv_b, router_s, att_dg, att_dg),
        self_scratch,
        12.2,
        after=(dh1, dec_a),
    )
    comekv_1 = swapped(sendkv_1)
    come_w1 = swapped(send_w1)
    (ffn_e,) = add_shares(keep_e, come_e, 4.0, (df1, dec_b))
    att_d = add_pieces(ids, [keep_w1], [come_w1], 3.6, (ffn_e,))
    df0, own_0, sendkv_0, router_0g, keep_w0, send_w0 = run(
        functools.partial(self_back_kernel, 0),
        (ids, recv, dh1, mixed_e, log_e, *wa_own, *wa_oth, kvw_own, kvw_oth),
        "svvvv" + "a" * 10,
        (act, kv_f, kv_b, router_s, att_g, att_g),
        self_scratch,
        11.8,
        after=(ffn_e, *att_d),
    )
    comekv_0 = swapped(sendkv_0)
    come_w0 = swapped(send_w0)
    ffn_e = to_all(ffn_e, "mp")
    att_d = mp_exchange(att_d)
    dx1, gain_d0, keep_s1, send_s1 = run(
        dec_finish_kernel,
        (ids, recv, dg1, df1, own_1, comekv_1, own_c, comekv_c, memory, kvw_own, kvw_oth),
        "svvvvvvvvaa",
        (shaped((4, 128, 512), BF), row_s, flat_g, flat_g),
        [vm(512, 128), vm(2, TILE, 512), sem],
        0.3,
        after=(df0,),
    )
    come_s1 = swapped(send_s1)
    finished = run(
        enc_finish_kernel,
        (
            ids, recv, dh1, df0, own_0, comekv_0, dx1, router_0g, router_1g, router_cg,
            gain_e1, gain_e2, gain_d0, gain_d1, gain_d2, kvw_own, kvw_oth,
        ),
        "s" + "v" * 14 + "aa",
        shaped((8, 208, 512), BF),
        [vm(512, 128), vm(2, TILE, 512), vm(32, 512, kind=F32), sem],
        0.3,
        after=att_d[1:],
    )
    att_e = add_pieces(
        ids, [keep_w0, keep_s1], [come_w0, come_s1], 3.6, (finished,)
    )
    att_e = mp_exchange(att_e)
    dp = lax.axis_size("dp")
    share = 256 // dp
    if dp == 4:
        ffn = dp_exchange(
            run(
                sum_middle_kernel,
                (ids, dec_a, dec_b, ffn_e, *att_d),
                "s" + "v" * 7,
                [shaped((64, 2560), BF)] * 4,
                [],
                4.0,
                after=(att_e[0],),
            )
        )
        after = ffn[1:]
    else:
        after = ()
    finished = to_all(finished, rowgroup)
    small = run(
        tail_kernel,
        (finished, *att_e),
        "v" * 5,
        shaped((256, 768), BF),
        [],
        3.0,
        after=after,
    )
    dx = run(
        place_kernel,
        (finished,),
        "v",
        shaped((4, 2, 128, 512), F32),
        [],
        3.0,
        after=(small,),
    )
    small = to_all(small.reshape(dp, share, 768), "dp")
    outs_come = outs_come.reshape(2, 4, 128, 512).transpose(1, 0, 2, 3)
    results = (outs_come.reshape(1, 4, 1, 256, 512), dx.reshape(1, 4, 1, 256, 512))
    if dp == 4:
        made = run(
            final_kernel,
            (small, *ffn),
            "v" * 5,
            (
                shaped((3, 2, 64), F32),
                shaped((2, 8, 64), F32),
                shaped((2, 2, 64, 64), F32),
                shaped((2, 64, 128), F32),
                shaped((2, 2, 64, 64), F32),
                shaped((2, 64, 512), F32),
                shaped((2, 64, 512), F32),
                shaped((8, 64), F32),
                shaped((2, 64, 64), F32),
                shaped((64, 128), F32),
                shaped((2, 64, 64), F32),
            ),
            [],
            3.0,
        )
        made = list(made)
        made[0] = made[0].transpose(1, 0, 2)
        made[1] = made[1].transpose(0, 2, 1)
        made[6] = made[6].transpose(0, 2, 1)
        made[7] = made[7].T
        return (*results, *made)

    small = jnp.sum(small.astype(F32), 0)
    middle = jnp.concatenate(
        [jnp.sum(part.astype(F32), 0) for part in (ffn_e, dec_a, dec_b)]
        + [sum(part.astype(F32) for part in att_d)],
        1,
    )
    middle = to_all(middle.astype(BF).reshape(dp, share, 2560), "dp")
    middle = jnp.sum(middle.astype(F32), 0)

    def query_of(value, at):
        return value[:, at : at + 128].reshape(share, 2, 64).transpose(1, 0, 2)

    def output_of(value, at):
        return value[:, at + 128 : at + 256].T.reshape(2, 64, share)

    misc = small[:, 640:768].T

    def router_of(layer):
        return misc[ROUTER_LANES[layer] : ROUTER_LANES[layer] + 8].T

    return (
        *results,
        misc[GAIN_ROW : GAIN_ROW + 6].reshape(2, 3, share),
        jnp.stack([router_of(0), router_of(1)]),
        jnp.stack([query_of(small, 0), query_of(middle, 2304)]),
        jnp.stack([small[:, 512:640], small[:, 256:384]]),
        jnp.stack([output_of(small, 0), output_of(middle, 2304)]),
        jnp.stack([middle[:, :512], middle[:, 1024:1536]]),
        jnp.stack([middle[:, 512:1024].T, middle[:, 1536:2048].T]),
        router_of(2),
        query_of(middle, 2048),
        small[:, 384:512],
        output_of(middle, 2048),
    )


def solution(mesh):
    placed = (
        P("section", None, "dp", "mp", None),
        P("section", None, "dp", None),
        P("section", None, "dp", "mp", None),
        P(None, "dp", "mp", None),
        P("section", None, None),
        P("section", None, None),
        P("section", "mp", None, None),
        P("section", None, None),
        P("section", "mp", None, None),
        P("section", None, "mp"),
        P("section", "mp", None),
        P(),
        P("mp", None, None),
        P(),
        P("mp", None, None),
        P(None, "dp", "mp", None),
    )
    return jax.shard_map(
        per_device,
        mesh=mesh,
        in_specs=placed,
        out_specs=(
            P("section", None, "dp", "mp", None),
            P("section", None, "dp", "mp", None),
            P(None, None, ("section", "dp")),
            P(None, ("section", "dp"), None),
            P(None, "mp", ("section", "dp"), None),
            P(None, ("section", "dp"), None),
            P(None, "mp", None, ("section", "dp")),
            P(None, ("section", "dp"), "mp"),
            P(None, "mp", ("section", "dp")),
            P(("section", "dp"), None),
            P("mp", ("section", "dp"), None),
            P(("section", "dp"), None),
            P("mp", None, ("section", "dp")),
        ),
        check_vma=False,
    )
```

```python
import functools

import jax
import jax.numpy as jnp
from jax import lax
from jax.experimental import pallas as pl
from jax.experimental.pallas import tpu as pltpu
from jax.sharding import PartitionSpec as P

EPS = 1e-05
MASK_VALUE = -1000000000.0
BF = jnp.bfloat16
F32 = jnp.float32
TILE = 256
EX_AT = 160
CODE_ROW = 3
LEN_ROW = 4
ROUTER_AT = 8
GAIN_ROW = 24
ROUTER_LANES = (0, 8, 16)
VMEM_LIMIT = 63 * 1024 * 1024
LARGE = 1 << 40


def nn(left, right):
    return lax.dot_general(left, right, (((1,), (0,)), ((), ())), preferred_element_type=F32)


def nt(left, right):
    return lax.dot_general(left, right, (((1,), (1,)), ((), ())), preferred_element_type=F32)


def tn(left, right):
    return lax.dot_general(left, right, (((0,), (0,)), ((), ())), preferred_element_type=F32)


def norm_of(values, gain_row):
    center = values - jnp.mean(values, 1, keepdims=True)
    scaled = lax.rsqrt(jnp.mean(center * center, 1, keepdims=True) + EPS)
    unit_rows = center * scaled
    return unit_rows * gain_row, unit_rows, scaled


def norm_back(upstream, unit_rows, scaled, gain_row):
    inner = upstream * gain_row
    result = scaled * (
        inner
        - jnp.mean(inner, 1, keepdims=True)
        - unit_rows * jnp.mean(inner * unit_rows, 1, keepdims=True)
    )
    return result, jnp.sum(upstream * unit_rows, 0, keepdims=True)


def eye_of(size):
    return lax.broadcasted_iota(jnp.int32, (size, size), 0) == lax.broadcasted_iota(
        jnp.int32, (size, size), 1
    )


def row_to_col(row):
    return jnp.sum(jnp.where(eye_of(128), row, 0.0), 1, keepdims=True)


def col_to_row(col):
    parts = []
    for at in range(0, col.shape[0], 128):
        part = jnp.where(eye_of(128), col[at : at + 128], 0.0)
        parts.append(jnp.sum(part, 0, keepdims=True))
    return jnp.concatenate(parts, 1)


def ends_of(extra):
    lengths = extra[LEN_ROW : LEN_ROW + 1, 0:8] * 32.0 + extra[LEN_ROW : LEN_ROW + 1, 128:136]
    ends = [lengths[:, 0:1]]
    for k in range(1, 8):
        ends.append(ends[-1] + lengths[:, k : k + 1])
    return ends


def segments(places, ends):
    total = jnp.where(places >= ends[0], 1.0, 0.0)
    for end in ends[1:]:
        total = total + jnp.where(places >= end, 1.0, 0.0)
    return total


def extra_of(recv_ref, layer, quarter):
    at = EX_AT if recv_ref.shape[1] > 16 else 0
    return recv_ref[4 * layer + quarter, at : at + 16, :]


def gain_of(recv_ref, layer, which):
    return extra_of(recv_ref, layer, 0).astype(F32)[which : which + 1, :]


def rows_of(recv_ref, layer, t):
    return recv_ref[pl.ds(4 * layer + 2 * t, 2), 0:128, :].reshape(TILE, 512).astype(F32)


def codes_of(recv_ref, layer, t, lane):
    cols = []
    for i in range(2):
        extra = extra_of(recv_ref, layer, 2 * t + i).astype(F32)
        cols.append(row_to_col(extra[CODE_ROW : CODE_ROW + 1, lane : lane + 128]))
    return jnp.concatenate(cols, 0)


def other_kv(recv_ref, layer, quarter):
    packed = recv_ref[4 * layer + quarter, 128:160, :]
    return jnp.concatenate([packed[:, 128 * c : 128 * c + 128] for c in range(4)], 0)


def routing(query_rows, router_block, code):
    second = jnp.floor(code * 0.125)
    first = code - 8.0 * second
    e0, e1 = first.astype(jnp.int32), second.astype(jnp.int32)
    logits = nt(query_rows, router_block)
    lanes = lax.broadcasted_iota(jnp.int32, logits.shape, 1)
    l0 = jnp.sum(jnp.where(lanes == e0 + ROUTER_AT, logits, 0.0), 1, keepdims=True)
    l1 = jnp.sum(jnp.where(lanes == e1 + ROUTER_AT, logits, 0.0), 1, keepdims=True)
    top = jnp.maximum(l0, l1)
    x0, x1 = jnp.exp(l0 - top), jnp.exp(l1 - top)
    total = x0 + x1
    owners = lax.broadcasted_iota(jnp.int32, (code.shape[0], 512), 1) >> 6
    return e0, e1, x0 / total, x1 / total, owners == e0, owners == e1


def fold(wide, mask):
    kept = jnp.where(mask, wide, 0.0)
    return kept[:, 0:128] + kept[:, 128:256] + kept[:, 256:384] + kept[:, 384:512]


def spread(a0, a1, m0, m1):
    parts = []
    for c in range(4):
        cut = slice(128 * c, 128 * c + 128)
        parts.append(jnp.where(m0[:, cut], a0, jnp.where(m1[:, cut], a1, 0.0)))
    return jnp.concatenate(parts, 1).astype(BF)


def rounded(value):
    return value.astype(BF).astype(F32)


def start_pick(cond, yes, no, dst, sem):
    @pl.when(cond)
    def _():
        pltpu.make_async_copy(yes, dst, sem).start()

    @pl.when(jnp.logical_not(cond))
    def _():
        pltpu.make_async_copy(no, dst, sem).start()


class Loads:
    def __init__(self, sems):
        self.sems, self.used = sems, 0

    def start(self, cond, yes, no, dst):
        sem = self.sems.at[self.used]
        self.used += 1
        start_pick(cond, yes, no, dst, sem)
        return functools.partial(lambda a, b, c: pltpu.make_async_copy(a, b, c).wait(), yes, dst, sem)

    def plain(self, src, dst):
        sem = self.sems.at[self.used]
        self.used += 1
        copy = pltpu.make_async_copy(src, dst, sem)
        copy.start()
        return copy.wait

    def rows(self, cond, yes, no, at, dst, m):
        cut = pl.ds(at, 128)
        return [
            self.start(cond, yes[b].at[cut], no[b].at[cut], dst.at[pl.ds(128 * (m ^ b), 128)])
            for b in range(4)
        ]

    def pieces(self, cond, yes, no, dst, m):
        waits = []
        for b, (one, other) in enumerate(zip(yes, no)):
            to = dst.at[m ^ b] if b < 3 else dst.at[m ^ 3, pl.ds(256 * (b - 3), 256)]
            if len(yes) == 4:
                to = dst.at[m ^ b]
            waits.append(self.start(cond, one, other, to))
        return waits


def wait_all(waits):
    for wait in waits:
        wait()


def widen_kv(kv_ref, k2_ref, v2_ref):
    for j in range(4):
        kv = kv_ref[j].reshape(256, 128).astype(F32)
        turned = pltpu.roll(kv, 64, 1)
        low = lax.broadcasted_iota(jnp.int32, kv.shape, 1) < 64
        k2_ref[256 * j : 256 * j + 256, :] = jnp.where(low, kv, turned).astype(BF)
        v2_ref[256 * j : 256 * j + 256, :] = jnp.where(low, turned, kv).astype(BF)


def attend_tile(query_rows, route, w_qt, w_o, k2, v2, allowed):
    e0, e1, g0, g1, m0, m1 = route
    q_all = nt(query_rows, w_qt) * 0.125
    queries = jnp.concatenate([fold(q_all, m0), fold(q_all, m1)], 0).astype(BF)
    scores = nt(queries, k2)
    scores = jnp.concatenate(
        [
            jnp.where(allowed, scores[0:TILE], MASK_VALUE),
            jnp.where(allowed, scores[TILE:], MASK_VALUE),
        ],
        0,
    )
    top = jnp.max(scores, 1, keepdims=True)
    weights = jnp.exp(scores - top)
    total = jnp.sum(weights, 1, keepdims=True)
    mixed = nn(weights.astype(BF), v2) / total
    log_total = top + jnp.log(total)
    gated = spread(rounded(g0) * mixed[0:TILE], rounded(g1) * mixed[TILE:], m0, m1)
    return nn(gated, w_o), mixed, col_to_row(log_total)


def attend_back_tile(
    t, upstream, query_rows, route, mixed, log_row, w_qt, w_o, router_block, router_lane, k2, v2,
    allowed_t, grad_k, grad_v, gated_ref, dz_ref, dq_ref, dlog_ref,
):
    e0, e1, g0, g1, m0, m1 = route
    q_all = nt(query_rows, w_qt) * 0.125
    queries = jnp.concatenate([fold(q_all, m0), fold(q_all, m1)], 0).astype(BF)
    dz = upstream.astype(BF)
    dg_all = nt(dz, w_o)
    dgated0, dgated1 = fold(dg_all, m0), fold(dg_all, m1)
    r0, r1 = rounded(g0), rounded(g1)
    mixed0, mixed1 = mixed[0:TILE], mixed[TILE:]
    gated_ref[t] = spread(r0 * mixed0, r1 * mixed1, m0, m1)
    dz_ref[t] = dz
    dgate0 = rounded(jnp.sum(mixed0 * dgated0, 1, keepdims=True))
    dgate1 = rounded(jnp.sum(mixed1 * dgated1, 1, keepdims=True))
    do0, do1 = (r0 * dgated0).astype(BF), (r1 * dgated1).astype(BF)
    grad_mixed = jnp.concatenate([do0, do1], 0)
    inner_row = jnp.concatenate(
        [
            col_to_row(jnp.sum(do0.astype(F32) * mixed0, 1, keepdims=True)),
            col_to_row(jnp.sum(do1.astype(F32) * mixed1, 1, keepdims=True)),
        ],
        1,
    )
    scores = nt(k2, queries)
    scores = jnp.concatenate(
        [
            jnp.where(allowed_t, scores[:, 0:TILE], MASK_VALUE),
            jnp.where(allowed_t, scores[:, TILE:], MASK_VALUE),
        ],
        1,
    )
    probs = jnp.exp(scores - log_row)
    grad_probs = nt(v2, grad_mixed)
    grad_scores = (probs * (grad_probs - inner_row)).astype(BF)
    grad_v[...] += nn(probs.astype(BF), grad_mixed)
    grad_k[...] += nn(grad_scores, queries)
    grad_q = rounded(tn(grad_scores, k2) * 0.125)
    dq_all = spread(grad_q[0:TILE], grad_q[TILE:], m0, m1)
    dq_ref[t] = dq_all
    grad_rows = nn(dq_all, w_qt)
    mean_grad = g0 * dgate0 + g1 * dgate1
    dc0, dc1 = g0 * (dgate0 - mean_grad), g1 * (dgate1 - mean_grad)
    lanes = lax.broadcasted_iota(jnp.int32, (TILE, 16), 1)
    dlog = jnp.where(lanes == e0 + ROUTER_AT, dc0, 0.0) + jnp.where(
        lanes == e1 + ROUTER_AT, dc1, 0.0
    )
    wide = lax.broadcasted_iota(jnp.int32, (TILE, 128), 1)
    dlog_ref[t] = (
        jnp.where(wide == e0 + router_lane, dc0, 0.0)
        + jnp.where(wide == e1 + router_lane, dc1, 0.0)
    ).astype(BF)
    return grad_rows + nn(dlog.astype(BF), router_block)


def query_places(t, sec, dims, along):
    local = lax.broadcasted_iota(jnp.int32, dims, along)
    return (512 * t + 128 * sec + local + (local & ~127)).astype(F32)


def allowed_rows(t, sec, ends_q, ends_k, causal):
    query_at = query_places(t, sec, (TILE, 1), 0)
    key_at = lax.broadcasted_iota(jnp.int32, (1, 1024), 1).astype(F32)
    allowed = segments(query_at, ends_q) == segments(key_at, ends_k)
    if causal:
        allowed = allowed & (key_at <= query_at)
    return allowed


def key_segments_t(ends_k, segk_ref):
    for j in range(8):
        at = lax.broadcasted_iota(jnp.int32, (128, TILE), 0).astype(F32) + 128.0 * j
        segk_ref[128 * j : 128 * j + 128, :] = segments(at, ends_k)


def allowed_cols(t, sec, ends_q, segk_ref, causal):
    query_at = query_places(t, sec, (1, TILE), 1)
    allowed = segk_ref[...] == segments(query_at, ends_q)
    if causal:
        key_at = lax.broadcasted_iota(jnp.int32, (1024, TILE), 0).astype(F32)
        allowed = allowed & (key_at <= query_at)
    return allowed


def fold_kv(grad_k, grad_v, sec, own_ref, send_ref):
    for j in range(4):
        k = grad_k[256 * j : 256 * j + 256, :]
        v = grad_v[256 * j : 256 * j + 256, :]
        k = k + pltpu.roll(k, 64, 1)
        v = v + pltpu.roll(v, 64, 1)
        low = lax.broadcasted_iota(jnp.int32, k.shape, 1) < 64
        both = jnp.where(low, k, v)
        first, second = both[0:128], both[128:256]
        own_ref[j] = jnp.where(sec == 0, first, second)
        send_ref[j] = jnp.where(sec == 0, second, first).astype(send_ref.dtype)


def split_halves(value, sec, keep_ref, send_ref, m, lane):
    upper, lower = value[0:256], value[256:512]
    cut = slice(lane, lane + value.shape[1])
    keep_ref[m, :, cut] = jnp.where(sec == 0, upper, lower).astype(BF)
    send_ref[m, :, cut] = jnp.where(sec == 0, lower, upper).astype(BF)


def split_flat(value, sec, keep_ref, send_ref, lane):
    upper, lower = value[0:256], value[256:512]
    cut = slice(lane, lane + value.shape[1])
    keep_ref[:, cut] = jnp.where(sec == 0, upper, lower).astype(BF)
    send_ref[:, cut] = jnp.where(sec == 0, lower, upper).astype(BF)


def turned_rows(value):
    return value.astype(F32).T.astype(BF)


def flat(ref):
    return ref[...].reshape(512, ref.shape[-1])


def attention_weight_grads(first_t, gated_ref, dz_ref, dq_ref, sec, keep_ref, send_ref, lane):
    grad_q = nn(first_t, flat(dq_ref))
    grad_o = nn(turned_rows(flat(dz_ref)), flat(gated_ref))
    for b in range(4):
        cut = slice(128 * b, 128 * b + 128)
        split_halves(grad_q[:, cut], sec, keep_ref, send_ref, b, lane)
        split_halves(grad_o[:, cut], sec, keep_ref, send_ref, b, lane + 128)


def router_grads(dlog_ref, rows_ref):
    turned = flat(dlog_ref).astype(F32).T.astype(BF)
    return nn(turned, flat(rows_ref))[0:32]


def gelu_parts(pre):
    cdf = 0.5 * (1.0 + lax.erf(pre * 0.7071067811865476))
    slope = cdf + pre * (jnp.exp(-0.5 * pre * pre) * 0.3989422804014327)
    return pre * cdf, slope


def own_self_kv(recv_ref, layer, sec, w_kv, kv_ref):
    gain = gain_of(recv_ref, layer, 0)
    for t in range(2):
        first = norm_of(rows_of(recv_ref, layer, t), gain)[0].astype(BF)
        kv = nn(first, w_kv).astype(BF)
        for i in range(2):
            j = 2 * t + i
            kv_ref[j, sec] = kv[128 * i : 128 * i + 128]
            kv_ref[j, 1 - sec] = other_kv(recv_ref, layer, j)


def cross_kv(kvm_ref, kvo_ref, sec, kv_s):
    for j in range(4):
        kv_s[j, sec] = kvm_ref[j]
        kv_s[j, 1 - sec] = kvo_ref[j]


def pack_kernel(
    ready, len_ref, x_ref, gain_ref, w_kv_ref, own_ref, cross_ref, router_ref, send_ref, extra_s
):
    ready()
    gain = gain_ref[0:1, :].astype(F32)
    w_kv = w_kv_ref[...]
    extra_s[...] = jnp.zeros_like(extra_s)
    extra_s[0:3, :] = gain_ref[...].astype(F32)
    extra_s[ROUTER_AT : ROUTER_AT + 8, :] = router_ref[...].astype(F32)
    lanes = lax.broadcasted_iota(jnp.int32, (1, 512), 1)
    for i in range(4):
        first = norm_of(x_ref[i].astype(F32), gain)[0].astype(BF)
        kv = nn(first, w_kv).astype(BF)
        row = jnp.zeros((1, 512), jnp.int32)
        for k in range(8):
            length = len_ref[i, k]
            row = jnp.where(lanes == k, length >> 5, row)
            row = jnp.where(lanes == 128 + k, length & 31, row)
        extra_s[LEN_ROW : LEN_ROW + 1, :] = row.astype(F32)
        own, cross = own_ref[i], cross_ref[i]
        own_code = (own[0:1] + 8 * own[1:2]).astype(F32)
        cross_code = (cross[0:1] + 8 * cross[1:2]).astype(F32)
        for half in range(2):
            to = 4 * half + i
            here = slice(128 * half, 128 * half + 128)
            send_ref[to, 0:128, :] = x_ref[i, here, :]
            far = kv[128 * (1 - half) : 128 * (1 - half) + 128]
            send_ref[to, 128:160, :] = jnp.concatenate(
                [far[32 * c : 32 * c + 32] for c in range(4)], 1
            )
            extra_s[CODE_ROW : CODE_ROW + 1, 0:128] = own_code[:, here]
            extra_s[CODE_ROW : CODE_ROW + 1, 128:256] = cross_code[:, here]
            send_ref[to, EX_AT : EX_AT + 16, :] = extra_s[...].astype(BF)


def self_fwd_kernel(ready, ids_ref, recv_ref, *refs):
    wa_own, wa_oth, kvw_own, kvw_oth = refs[:4], refs[4:8], refs[8], refs[9]
    h1_ref, g1_ref, mixed_e, mixed_d, log_e, log_d, meta_ref = refs[10:17]
    wq, wo, wkv, kv_s, k2, v2, sems = refs[17:]
    sec, m = ids_ref[0], ids_ref[1]
    loads = Loads(sems)
    kv_waits = [loads.start(sec == i, kvw_own, kvw_oth, wkv.at[i]) for i in range(2)]
    waits = []
    for layer in range(2):
        waits += loads.rows(sec == layer, wa_own, wa_oth, 0, wq.at[layer], m)
        waits += loads.rows(sec == layer, wa_own, wa_oth, 128, wo.at[layer], m)
    ready()
    meta_ref[...] = recv_ref[:, EX_AT : EX_AT + 16, :]
    wait_all(kv_waits)
    for layer in range(2):
        own_self_kv(recv_ref, layer, sec, wkv[layer], kv_s)
        widen_kv(kv_s, k2.at[layer], v2.at[layer])
    wait_all(waits)
    ends = [ends_of(extra_of(recv_ref, layer, 0).astype(F32)) for layer in range(2)]

    def tile(t, carry):
        for layer, after_ref, mixed_ref, log_ref in (
            (0, h1_ref, mixed_e, log_e),
            (1, g1_ref, mixed_d, log_d),
        ):
            rows = rows_of(recv_ref, layer, t)
            first = norm_of(rows, gain_of(recv_ref, layer, 0))[0].astype(BF)
            route = routing(first, extra_of(recv_ref, layer, 0), codes_of(recv_ref, layer, t, 0))
            allowed = allowed_rows(t, sec, ends[layer], ends[layer], layer == 1)
            out, mixed, row_log = attend_tile(
                first, route, wq[layer], wo[layer], k2[layer], v2[layer], allowed
            )
            after_ref[t] = rows + out
            mixed_ref[t] = mixed
            log_ref[t] = row_log
        return carry

    lax.fori_loop(0, 2, tile, 0)


def enc_ffn_kernel(ready, ids_ref, recv_ref, h1_ref, kvc_ref, *refs):
    f_own, f_oth = refs[:5], refs[5:10]
    h2_ref, mem_ref, kvm_ref, w_in, w_out, third_s, sems = refs[10:]
    low, m = ids_ref[0] == 0, ids_ref[1]
    loads = Loads(sems)
    waits = loads.pieces(low, f_own, f_oth, w_in, m) + loads.pieces(low, f_oth, f_own, w_out, m)
    ready()
    for t in range(2):
        h2_ref[t] = h1_ref[t]
        third_s[t] = norm_of(h1_ref[t], gain_of(recv_ref, 0, 2))[0].astype(BF)
    wait_all(waits)

    def chunk(c, carry):
        pre = nn(flat(third_s), w_in[c])
        hidden = (0.5 * pre * (1.0 + lax.erf(pre * 0.7071067811865476))).astype(BF)
        h2_ref[...] += nn(hidden, w_out[c]).reshape(2, TILE, 512)
        return carry

    lax.fori_loop(0, 4, chunk, 0)
    for t in range(2):
        memory = norm_of(h2_ref[t], gain_of(recv_ref, 0, 1))[0].astype(BF)
        mem_ref[t] = memory
        kv = nn(memory, kvc_ref[...]).astype(BF)
        kvm_ref[2 * t] = kv[0:128]
        kvm_ref[2 * t + 1] = kv[128:256]


def cross_fwd_kernel(
    ready, ids_ref, recv_ref, g1_ref, kvm_ref, kvo_ref, rc_ref, *refs
):
    wa_own, wa_oth = refs[:4], refs[4:8]
    g2_ref, mixed_ref, log_ref, wq, wo, kv_s, k2, v2, sems = refs[8:]
    sec, m = ids_ref[0], ids_ref[1]
    loads = Loads(sems)
    waits = loads.rows(sec == 0, wa_own, wa_oth, 256, wq, m)
    waits += loads.rows(sec == 0, wa_oth, wa_own, 256, wo, m)
    ready()
    cross_kv(kvm_ref, kvo_ref, sec, kv_s)
    widen_kv(kv_s, k2, v2)
    wait_all(waits)
    ends_k = ends_of(extra_of(recv_ref, 0, 0).astype(F32))
    ends_q = ends_of(extra_of(recv_ref, 1, 0).astype(F32))

    def tile(t, carry):
        before = g1_ref[t]
        second = norm_of(before, gain_of(recv_ref, 1, 1))[0].astype(BF)
        route = routing(second, rc_ref[...], codes_of(recv_ref, 1, t, 128))
        allowed = allowed_rows(t, sec, ends_q, ends_k, False)
        out, mixed, row_log = attend_tile(second, route, wq[...], wo[...], k2[...], v2[...], allowed)
        g2_ref[t] = before + out
        mixed_ref[t] = mixed
        log_ref[t] = row_log
        return carry

    lax.fori_loop(0, 2, tile, 0)


def ffn_both(c, third_s, third_t, dy_s, dy_t, w_in, w_out, dthird, sec, keep_ref, send_ref):
    pre = nn(flat(third_s), w_in[c])
    hidden, slope = gelu_parts(pre)
    hidden = hidden.astype(BF)
    dpre = (nt(flat(dy_s), w_out[c]) * slope).astype(BF)
    dthird[...] += nt(dpre, w_in[c])
    split_halves(nn(third_t[...], dpre), sec, keep_ref, send_ref, c, 0)
    split_halves(nn(dy_t[...], hidden), sec, keep_ref, send_ref, c, 512)
    return hidden


def dec_ffn_kernel(ready, ids_ref, recv_ref, g2_ref, mem_ref, cot_in, *refs):
    f_own, f_oth = refs[:5], refs[5:10]
    outs_ref, dg2_ref, gain_ref, keep_ref, send_ref = refs[10:15]
    w_in, w_out, cot_s, third_s, third_t, cot_t, acc, dthird, sems = refs[15:]
    sec, m = ids_ref[0], ids_ref[1]
    low = sec == 0
    loads = Loads(sems)
    cot_waits = [loads.plain(cot_in.at[i], cot_s.at[i]) for i in range(4)]
    waits = loads.pieces(low, f_own, f_oth, w_in, m) + loads.pieces(low, f_oth, f_own, w_out, m)
    ready()
    for t in range(2):
        acc[t] = g2_ref[t]
        third_s[t] = norm_of(g2_ref[t], gain_of(recv_ref, 1, 2))[0].astype(BF)
        outs_ref[2 * t : 2 * t + 2] = mem_ref[t].reshape(2, 128, 512)
    third_t[...] = turned_rows(flat(third_s))
    wait_all(cot_waits)
    cot_t[...] = turned_rows(flat(cot_s))
    dthird[...] = jnp.zeros_like(dthird)
    wait_all(waits)

    def chunk(c, carry):
        hidden = ffn_both(
            c, third_s, third_t, cot_s, cot_t, w_in, w_out, dthird, sec, keep_ref, send_ref
        )
        acc[...] += nn(hidden, w_out[c]).reshape(2, TILE, 512)
        return carry

    lax.fori_loop(0, 4, chunk, 0)
    total = jnp.zeros((1, 512), F32)
    gain = gain_of(recv_ref, 1, 2)
    for t in range(2):
        outs_ref[4 + 2 * t : 6 + 2 * t] = acc[t].astype(BF).reshape(2, 128, 512)
        unused_out, unit, scaled = norm_of(g2_ref[t], gain)
        back, gain_grad = norm_back(dthird[TILE * t : TILE * t + TILE, :], unit, scaled, gain)
        dg2_ref[t] = cot_s[2 * t : 2 * t + 2].reshape(TILE, 512).astype(F32) + back
        total = total + gain_grad
    gain_ref[...] = total


def cross_back_kernel(
    ready, ids_ref, recv_ref, g1_ref, dg2_ref, mixed_ref, log_ref, kvm_ref, kvo_ref, rc_ref, *refs
):
    wa_own, wa_oth = refs[:4], refs[4:8]
    dg1_ref, gain_ref, own_ref, send_ref, router_ref, keepw_ref, sendw_ref = refs[8:15]
    wq, wo, kv_s, k2, v2, segk, grad_k, grad_v, second_s, gated_s, dz_s, dq_s, dlog_s, sems = refs[15:]
    sec, m = ids_ref[0], ids_ref[1]
    loads = Loads(sems)
    waits = loads.rows(sec == 0, wa_own, wa_oth, 256, wq, m)
    waits += loads.rows(sec == 0, wa_oth, wa_own, 256, wo, m)
    ready()
    cross_kv(kvm_ref, kvo_ref, sec, kv_s)
    widen_kv(kv_s, k2, v2)
    ends_k = ends_of(extra_of(recv_ref, 0, 0).astype(F32))
    ends_q = ends_of(extra_of(recv_ref, 1, 0).astype(F32))
    key_segments_t(ends_k, segk)
    grad_k[...] = jnp.zeros_like(grad_k)
    grad_v[...] = jnp.zeros_like(grad_v)
    wait_all(waits)

    def tile(t, total):
        gain = gain_of(recv_ref, 1, 1)
        second, unit, scaled = norm_of(g1_ref[t], gain)
        second = second.astype(BF)
        second_s[t] = second
        route = routing(second, rc_ref[...], codes_of(recv_ref, 1, t, 128))
        allowed = allowed_cols(t, sec, ends_q, segk, False)
        grad_rows = attend_back_tile(
            t, dg2_ref[t], second, route, mixed_ref[t], log_ref[t], wq[...], wo[...], rc_ref[...],
            ROUTER_LANES[2], k2[...], v2[...], allowed, grad_k, grad_v, gated_s, dz_s, dq_s, dlog_s,
        )
        back, gain_grad = norm_back(grad_rows, unit, scaled, gain)
        dg1_ref[t] = dg2_ref[t] + back
        return total + gain_grad

    gain_ref[...] = lax.fori_loop(0, 2, tile, jnp.zeros((1, 512), F32))
    fold_kv(grad_k, grad_v, sec, own_ref, send_ref)
    router_ref[...] = router_grads(dlog_s, second_s)
    attention_weight_grads(
        turned_rows(flat(second_s)), gated_s, dz_s, dq_s, sec, keepw_ref, sendw_ref, 0
    )


def self_back_kernel(layer, ready, ids_ref, recv_ref, up_ref, mixed_ref, log_ref, *refs):
    wa_own, wa_oth, kvw_own, kvw_oth = refs[:4], refs[4:8], refs[8], refs[9]
    refs = refs[10:]
    if layer == 1:
        before, refs = refs[:2], refs[2:]
    dfirst_ref, own_ref, send_ref, router_ref, keepw_ref, sendw_ref = refs[:6]
    wq, wo, wkv, kv_s, k2, v2, segk, grad_k, grad_v = refs[6:15]
    first_s, gated_s, dz_s, dq_s, dlog_s, sems = refs[15:]
    sec, m = ids_ref[0], ids_ref[1]
    mine = sec == layer
    loads = Loads(sems)
    kv_wait = loads.start(mine, kvw_own, kvw_oth, wkv)
    waits = loads.rows(mine, wa_own, wa_oth, 0, wq, m) + loads.rows(mine, wa_own, wa_oth, 128, wo, m)
    lane = 0
    if layer == 1:
        lane = 256
        for src, dst in zip(before, (keepw_ref, sendw_ref)):
            waits.append(loads.plain(src, dst.at[:, :, pl.ds(0, 256)]))
    ready()
    ends = ends_of(extra_of(recv_ref, layer, 0).astype(F32))
    key_segments_t(ends, segk)
    grad_k[...] = jnp.zeros_like(grad_k)
    grad_v[...] = jnp.zeros_like(grad_v)
    kv_wait()
    own_self_kv(recv_ref, layer, sec, wkv[...], kv_s)
    widen_kv(kv_s, k2, v2)
    wait_all(waits)
    router_block = extra_of(recv_ref, layer, 0)

    def tile(t, carry):
        first = norm_of(rows_of(recv_ref, layer, t), gain_of(recv_ref, layer, 0))[0].astype(BF)
        first_s[t] = first
        route = routing(first, router_block, codes_of(recv_ref, layer, t, 0))
        allowed = allowed_cols(t, sec, ends, segk, layer == 1)
        dfirst_ref[t] = attend_back_tile(
            t, up_ref[t], first, route, mixed_ref[t], log_ref[t], wq[...], wo[...], router_block,
            ROUTER_LANES[layer], k2[...], v2[...], allowed, grad_k, grad_v, gated_s, dz_s, dq_s,
            dlog_s,
        )
        return carry

    lax.fori_loop(0, 2, tile, 0)
    fold_kv(grad_k, grad_v, sec, own_ref, send_ref)
    router_ref[...] = router_grads(dlog_s, first_s)
    attention_weight_grads(
        turned_rows(flat(first_s)), gated_s, dz_s, dq_s, sec, keepw_ref, sendw_ref, lane
    )


def enc_ffn_back_kernel(
    ready, ids_ref, recv_ref, h1_ref, h2_ref, own_ref, come_ref, kvc_ref, *refs
):
    f_own, f_oth = refs[:5], refs[5:10]
    dh1_ref, gain_ref, gain2_ref, keep_ref, send_ref = refs[10:15]
    w_in, w_out, third_s, third_t, dy_s, dy_t, dthird, sems = refs[15:]
    sec, m = ids_ref[0], ids_ref[1]
    low = sec == 0
    loads = Loads(sems)
    waits = loads.pieces(low, f_own, f_oth, w_in, m) + loads.pieces(low, f_oth, f_own, w_out, m)
    ready()
    total = jnp.zeros((1, 512), F32)
    gain = gain_of(recv_ref, 0, 1)
    for t in range(2):
        dkv = (own_ref[2 * t : 2 * t + 2] + come_ref[2 * t : 2 * t + 2].astype(F32)).astype(BF)
        dmem = rounded(nt(dkv.reshape(TILE, 128), kvc_ref[...]))
        unused_out, unit, scaled = norm_of(h2_ref[t], gain)
        back, gain_grad = norm_back(dmem, unit, scaled, gain)
        dh1_ref[t] = back
        dy_s[t] = back.astype(BF)
        third_s[t] = norm_of(h1_ref[t], gain_of(recv_ref, 0, 2))[0].astype(BF)
        total = total + gain_grad
    gain_ref[...] = total
    third_t[...] = turned_rows(flat(third_s))
    dy_t[...] = turned_rows(flat(dy_s))
    dthird[...] = jnp.zeros_like(dthird)
    wait_all(waits)

    def chunk(c, carry):
        ffn_both(c, third_s, third_t, dy_s, dy_t, w_in, w_out, dthird, sec, keep_ref, send_ref)
        return carry

    lax.fori_loop(0, 4, chunk, 0)
    total = jnp.zeros((1, 512), F32)
    gain = gain_of(recv_ref, 0, 2)
    for t in range(2):
        unused_out, unit, scaled = norm_of(h1_ref[t], gain)
        back, gain_grad = norm_back(dthird[TILE * t : TILE * t + TILE, :], unit, scaled, gain)
        dh1_ref[t] += back
        total = total + gain_grad
    gain2_ref[...] = total


def finish_rows(layer, recv_ref, up_ref, df_ref, own_ref, come_ref, wkv, first_s, out_ref, at):
    total = jnp.zeros((1, 512), F32)
    gain = gain_of(recv_ref, layer, 0)
    dkvs = []
    for t in range(2):
        first, unit, scaled = norm_of(rows_of(recv_ref, layer, t), gain)
        first_s[t] = first.astype(BF)
        dkv = (own_ref[2 * t : 2 * t + 2] + come_ref[2 * t : 2 * t + 2].astype(F32)).astype(BF)
        dkv = dkv.reshape(TILE, 128)
        dkvs.append(dkv)
        back, gain_grad = norm_back(df_ref[t] + nt(dkv, wkv), unit, scaled, gain)
        dx = (up_ref[t] + back).astype(BF)
        for i in range(2):
            out_ref[at + 2 * t + i, 0:128, :] = dx[128 * i : 128 * i + 128]
        total = total + gain_grad
    grad = nn(turned_rows(flat(first_s)), jnp.concatenate(dkvs, 0))
    return total, grad


def dec_finish_kernel(
    ready, ids_ref, recv_ref, up_ref, df_ref, own_ref, come_ref, own_c, come_c, mem_ref, kvw_own, kvw_oth,
    dx_ref, gain_ref, keep_ref, send_ref, wkv, first_s, sems,
):
    sec = ids_ref[0]
    wait = Loads(sems).start(sec == 1, kvw_own, kvw_oth, wkv)
    ready()
    dkv_c = (own_c[...] + come_c[...].astype(F32)).astype(BF).reshape(512, 128)
    split_flat(nn(turned_rows(flat(mem_ref)), dkv_c), sec, keep_ref, send_ref, 128)
    wait()
    gain_ref[...], grad = finish_rows(
        1, recv_ref, up_ref, df_ref, own_ref, come_ref, wkv[...], first_s, dx_ref, 0
    )
    split_flat(grad, sec, keep_ref, send_ref, 0)


def enc_finish_kernel(
    ready, ids_ref, recv_ref, up_ref, df_ref, own_ref, come_ref, dx1_ref, r0, r1, rc,
    gain_e1, gain_e2, gain_d0, gain_d1, gain_d2, kvw_own, kvw_oth,
    out_ref, wkv, first_s, misc, sems,
):
    sec = ids_ref[0]
    wait = Loads(sems).start(sec == 0, kvw_own, kvw_oth, wkv)
    ready()
    misc[...] = r0[...] + r1[...] + rc[...]
    out_ref[4:8, 0:128, :] = dx1_ref[...]
    wait()
    gain_e0, grad = finish_rows(
        0, recv_ref, up_ref, df_ref, own_ref, come_ref, wkv[...], first_s, out_ref, 0
    )
    rows = (gain_e0, gain_e1[...], gain_e2[...], gain_d0[...], gain_d1[...], gain_d2[...])
    for i, row in enumerate(rows):
        misc[GAIN_ROW + i : GAIN_ROW + i + 1, :] = row
    both = misc[...]
    for half in range(2):
        cut = slice(256 * half, 256 * half + 256)
        part = grad[cut].astype(BF)
        small = both[:, cut].astype(BF)
        block = jnp.concatenate(
            [
                jnp.concatenate([part[64 * c : 64 * c + 64] for c in range(4)], 1),
                jnp.concatenate([small[0:16], small[16:32]], 1),
            ],
            0,
        )
        for i in range(4):
            out_ref[4 * half + i, 128:208, :] = block


def add_kernel(keep_ref, come_ref, *outs):
    lane = 0
    for out_ref in outs:
        cut = slice(lane, lane + out_ref.shape[-1])
        out_ref[...] = keep_ref[:, :, cut] + come_ref[:, :, cut]
        lane += out_ref.shape[-1]


def add_pieces_kernel(flats, ready, ids_ref, *refs):
    ready()
    n = len(flats)
    keeps, comes, outs = refs[:n], refs[n : 2 * n], refs[2 * n :]
    m = ids_ref[1]
    for b in range(4):
        lane = 0
        for is_flat, keep, come in zip(flats, keeps, comes):
            left = keep[...] if is_flat else keep[m ^ b]
            right = come[...] if is_flat else come[m ^ b]
            width = keep.shape[-1]
            outs[b][:, lane : lane + width] = left + right
            lane += width


def sum_middle_kernel(ready, ids_ref, dec_a, dec_b, enc_ref, *refs):
    att, outs = refs[:4], refs[4:]
    ready()
    rows = outs[0].shape[0]
    d = ids_ref[2]
    for k in range(len(outs)):
        cut = pl.ds(pl.multiple_of((d ^ k) * rows, rows), rows)
        for ref, lane in ((enc_ref, 0), (dec_a, 1024), (dec_b, 1536)):
            total = ref[0, cut, :].astype(F32)
            for i in range(1, 4):
                total = total + ref[i, cut, :].astype(F32)
            outs[k][:, lane : lane + ref.shape[-1]] = total.astype(BF)
        total = att[0][cut, :].astype(F32)
        for part in att[1:]:
            total = total + part[cut, :].astype(F32)
        outs[k][:, 2048:2560] = total.astype(BF)


def place_kernel(ready, dx_ref, dx_out):
    ready()
    for i in range(4):
        for half in range(2):
            dx_out[i, half] = dx_ref[4 * half + i, 0:128, :].astype(F32)


def tail_kernel(ready, dx_ref, *refs):
    att_e, (out_ref,) = refs[:4], refs[4:]
    ready()
    total = att_e[0][...].astype(F32)
    for part in att_e[1:]:
        total = total + part[...].astype(F32)
    out_ref[:, 0:512] = total.astype(BF)
    small = dx_ref[0, 128:208, :].astype(F32)
    for i in range(1, 8):
        small = small + dx_ref[i, 128:208, :].astype(F32)
    for c in range(4):
        out_ref[64 * c : 64 * c + 64, 512:640] = small[0:64, 128 * c : 128 * c + 128].astype(BF)
    misc = jnp.concatenate([small[64:80, 0:256], small[64:80, 256:512]], 0)
    misc = jnp.concatenate([misc, jnp.zeros((96, 256), F32)], 0)
    out_ref[:, 640:768] = misc.T.astype(BF)


def final_kernel(ready, come_ref, *refs):
    middle, outs = refs[:4], refs[4:]
    ready()
    gains, router, query, keyval, output, inner, outer, router_c, query_c, keyval_c, output_c = outs
    small = come_ref[0].astype(F32)
    for i in range(1, 4):
        small = small + come_ref[i].astype(F32)
    wide = middle[0][...].astype(F32)
    for part in middle[1:]:
        wide = wide + part[...].astype(F32)
    for layer in range(2):
        inner[layer] = wide[:, 1024 * layer : 1024 * layer + 512]
        outer[layer] = wide[:, 1024 * layer + 512 : 1024 * layer + 1024]
    keyval[0], keyval[1] = small[:, 512:640], small[:, 256:384]
    keyval_c[...] = small[:, 384:512]
    for source, at, put_q, put_o in (
        (wide, 2048, query_c, output_c),
        (wide, 2304, query.at[1], output.at[1]),
        (small, 0, query.at[0], output.at[0]),
    ):
        turned = source[:, at + 128 : at + 256].T
        for e in range(2):
            put_q[e] = source[:, at + 64 * e : at + 64 * e + 64]
            put_o[e] = turned[64 * e : 64 * e + 64]
    misc = small[:, 640:768].T
    router[0], router[1], router_c[...] = misc[0:8], misc[8:16], misc[16:24]
    for i in range(3):
        gains[i, 0:1] = misc[24 + i : 25 + i]
        gains[i, 1:2] = misc[27 + i : 28 + i]


def shaped(dims, kind):
    return jax.ShapeDtypeStruct(dims, kind)


def cost_of(micros):
    return pl.CostEstimate(
        flops=int(micros * 1.1535e9), bytes_accessed=int(micros * 3.0e6), transcendentals=0
    )


def run(kernel, args, places, outs, scratch, micros, after=()):
    space = {
        "s": pl.BlockSpec(memory_space=pltpu.SMEM),
        "v": pl.BlockSpec(memory_space=pltpu.VMEM),
        "a": pl.BlockSpec(memory_space=pl.ANY),
    }
    large = [
        i for i, (p, a) in enumerate(zip(places, args)) if p == "v" and a.size * a.dtype.itemsize > LARGE
    ]
    places = ["a" if i in large else p for i, p in enumerate(places)]
    count, extra = len(args), len(after)
    copies = [pltpu.VMEM(args[i].shape, args[i].dtype) for i in large]

    def body(*refs):
        given, rest = list(refs[:count]), refs[count + extra :]
        if large:
            rest, held, sems = rest[: -len(large) - 1], rest[-len(large) - 1 : -1], rest[-1]
            moves = []
            for n, i in enumerate(large):
                moves.append(pltpu.make_async_copy(given[i], held[n], sems.at[n]))
                given[i] = held[n]
            for move in moves:
                move.start()
        else:
            moves = []

        def ready():
            for move in moves:
                move.wait()

        kernel(ready, *given, *rest)

    return pl.pallas_call(
        body,
        out_shape=outs,
        in_specs=[space[p] for p in places] + [space["a"]] * extra,
        out_specs=jax.tree.map(lambda _: space["v"], outs),
        scratch_shapes=scratch + copies + ([dma(len(large))] if large else []),
        compiler_params=pltpu.CompilerParams(vmem_limit_bytes=VMEM_LIMIT),
        cost_estimate=cost_of(micros),
    )(*args, *after)


def vm(*dims, kind=BF):
    return pltpu.VMEM(dims, kind)


def dma(count):
    return pltpu.SemaphoreType.DMA((count,))


def across(value, axes, size, by):
    return lax.ppermute(value, axes, [(i, i ^ by) for i in range(size)])


def swapped(value):
    return across(value, "section", 2, 1)


def gathered(value):
    return [value] + [across(value, "mp", 4, b) for b in range(1, 4)]


def to_all(value, axes):
    return lax.all_to_all(value, axes, split_axis=0, concat_axis=0, tiled=True)


def add_shares(keep, come, micros, after, parts=1):
    blocks, rows, width = keep.shape
    whole = pl.BlockSpec((1, rows, width), lambda i: (i, 0, 0))
    part = pl.BlockSpec((1, rows, width // parts), lambda i: (i, 0, 0))
    extra = len(after)
    return pl.pallas_call(
        lambda k, c, *rest: add_kernel(k, c, *rest[extra:]),
        out_shape=[shaped((blocks, rows, width // parts), BF)] * parts,
        grid=(blocks,),
        in_specs=[whole, whole] + [pl.BlockSpec(memory_space=pl.ANY)] * extra,
        out_specs=[part] * parts,
        cost_estimate=cost_of(micros),
    )(keep, come, *after)


def add_pieces(ids, keeps, comes, micros, after=()):
    flats = tuple(keep.ndim == 2 for keep in keeps)
    width = sum(keep.shape[-1] for keep in keeps)
    return run(
        functools.partial(add_pieces_kernel, flats),
        (ids, *keeps, *comes),
        "s" + "v" * (2 * len(keeps)),
        [shaped((256, width), BF)] * 4,
        [],
        micros,
        after=after,
    )


def mp_exchange(pieces):
    return [pieces[0]] + [across(pieces[b], "mp", 4, b) for b in range(1, 4)]


def dp_exchange(pieces):
    return [pieces[0]] + [across(pieces[k], "dp", 4, k) for k in range(1, 4)]


def gated(values, after):
    anywhere = pl.BlockSpec(memory_space=pl.ANY)
    count = len(values)
    return pl.pallas_call(
        lambda *refs: None,
        out_shape=[shaped(v.shape, v.dtype) for v in values],
        in_specs=[anywhere] * (count + len(after)),
        out_specs=[anywhere] * count,
        input_output_aliases={i: i for i in range(count)},
        cost_estimate=cost_of(0.2),
    )(*values, *after)


def per_device(
    inputs,
    lengths,
    routes_self,
    routes_cross,
    gains,
    router_self,
    query_self,
    keyval_self,
    output_self,
    ffn_in,
    ffn_out,
    router_cross,
    query_cross,
    keyval_cross,
    output_cross,
    cotangent,
):
    sec, m, d = lax.axis_index("section"), lax.axis_index("mp"), lax.axis_index("dp")
    low = sec == 0
    ids = jnp.stack([sec, m, d]).astype(jnp.int32)
    sem = dma(24)
    rowgroup = ("section", "mp")

    q_rows = query_self[0].transpose(0, 2, 1).reshape(128, 512)
    o_rows = output_self[0].reshape(128, 512)
    c_rows = jnp.where(
        low, query_cross.transpose(0, 2, 1).reshape(128, 512), output_cross.reshape(128, 512)
    )
    wa = jnp.concatenate([q_rows, o_rows, c_rows], 0)
    wa_own = gathered(wa)
    w_in, w_out = ffn_in[0], ffn_out[0]
    half_come = swapped(jnp.where(low, w_out, w_in))
    enc_half = jnp.where(low, w_in, half_come)
    dec_half = jnp.where(low, half_come, w_out)
    kvw_own = keyval_self[0]
    kvw_oth = swapped(kvw_own)
    router_c = jnp.concatenate([jnp.zeros((8, 512), BF), router_cross.T], 0)

    packed = run(
        pack_kernel,
        (
            lengths[0, :, 0],
            inputs[0, :, 0],
            gains[0],
            keyval_self[0],
            routes_self[0, :, 0].transpose(0, 2, 1),
            routes_cross[:, 0].transpose(0, 2, 1),
            router_self[0].T,
        ),
        "svvvvvv",
        shaped((8, 176, 512), BF),
        [vm(16, 512, kind=F32)],
        3.4,
        after=(wa, enc_half, dec_half),
    )
    (packed,) = gated([packed], wa_own[1:])
    recv = to_all(packed, rowgroup)
    wa_oth = [swapped(piece) for piece in wa_own]
    (enc_half,) = gated([enc_half], [packed])
    enc_near = [across(enc_half, "mp", 4, b) for b in (1, 2)]
    enc_near = gated(enc_near, [recv])
    enc_far = [
        across(enc_near[1][0:256], "mp", 4, 1),
        across(enc_near[0][256:512], "mp", 4, 2),
    ]
    cot_in = lax.dynamic_index_in_dim(cotangent[:, 0].reshape(4, 2, 128, 512), sec, 1, False)

    act = shaped((2, TILE, 512), F32)
    actb = shaped((2, TILE, 512), BF)
    mixed_s = shaped((2, 2 * TILE, 128), F32)
    log_s = shaped((2, 1, 2 * TILE), F32)
    kv_b = shaped((4, 128, 128), BF)
    kv_f = shaped((4, 128, 128), F32)
    row_s = shaped((1, 512), F32)
    ffn_g = shaped((4, 256, 1024), BF)
    router_s = shaped((32, 512), F32)
    wide = [vm(512, 512), vm(512, 512)]
    kv_scratch = [vm(4, 2, 128, 128), vm(1024, 128), vm(1024, 128)]
    back_scratch = [
        vm(1024, TILE, kind=F32), vm(1024, 128, kind=F32), vm(1024, 128, kind=F32),
        vm(2, TILE, 512), vm(2, TILE, 512), vm(2, TILE, 512), vm(2, TILE, 512), vm(2, TILE, 128),
    ]
    ffn_w = [vm(4, 512, 512), vm(4, 512, 512)]

    h1, g1, mixed_e, mixed_d, log_e, log_d, meta = run(
        self_fwd_kernel,
        (ids, recv, *wa_own, *wa_oth, kvw_own, kvw_oth),
        "sv" + "a" * 10,
        (act, act, mixed_s, mixed_s, log_s, log_s, shaped((8, 16, 512), BF)),
        [vm(2, 512, 512), vm(2, 512, 512), vm(2, 512, 128), vm(4, 2, 128, 128)]
        + [vm(2, 1024, 128), vm(2, 1024, 128), sem],
        0.3,
    )
    enc_far = gated(enc_far, [h1])
    enc_own = [enc_half, *enc_near, *enc_far]
    enc_oth = [swapped(piece) for piece in enc_own]
    (dec_half,) = gated([dec_half], [enc_far[0]])
    dec_near = [across(dec_half, "mp", 4, b) for b in (1, 2)]
    (cot_in,) = gated([cot_in], [enc_far[0]])
    cot = to_all(cot_in, "mp")
    h2, memory, kvm = run(
        enc_ffn_kernel,
        (ids, meta, h1, keyval_cross, *enc_own, *enc_oth),
        "svvv" + "a" * 10,
        (act, actb, kv_b),
        ffn_w + [vm(2, TILE, 512), sem],
        4.0,
        after=(dec_half, cot_in),
    )
    kvm_oth = swapped(kvm)
    dec_near = gated(dec_near, [h2])
    dec_far = [
        across(dec_near[1][0:256], "mp", 4, 1),
        across(dec_near[0][256:512], "mp", 4, 2),
    ]
    g2, mixed_c, log_c = run(
        cross_fwd_kernel,
        (ids, meta, g1, kvm, kvm_oth, router_c, *wa_own, *wa_oth),
        "svvvvv" + "a" * 8,
        (act, mixed_s, log_s),
        wide + kv_scratch + [sem],
        0.3,
        after=(cot,),
    )
    dec_far = gated(dec_far, [g2])
    dec_own = [dec_half, *dec_near, *dec_far]
    dec_oth = [swapped(piece) for piece in dec_own]
    outs, dg2, gain_d2, keep_d, send_d = run(
        dec_ffn_kernel,
        (ids, meta, g2, memory, cot, *dec_own, *dec_oth),
        "svvva" + "a" * 10,
        (shaped((8, 128, 512), BF), act, row_s, ffn_g, ffn_g),
        ffn_w
        + [vm(4, 128, 512), vm(2, TILE, 512), vm(512, 512), vm(512, 512)]
        + [vm(2, TILE, 512, kind=F32), vm(512, 512, kind=F32), sem],
        15.0,
    )
    come_d = swapped(send_d)
    outs_come = to_all(outs, rowgroup)
    att_g = shaped((4, 256, 256), BF)
    flat_g = shaped((256, 256), BF)
    dg1, gain_d1, own_c, sendkv_c, router_cg, keep_wc, send_wc = run(
        cross_back_kernel,
        (ids, meta, g1, dg2, mixed_c, log_c, kvm, kvm_oth, router_c, *wa_own, *wa_oth),
        "svvvvvvvv" + "a" * 8,
        (act, row_s, kv_f, kv_b, router_s, att_g, att_g),
        wide + kv_scratch + back_scratch + [sem],
        13.0,
    )
    comekv_c = swapped(sendkv_c)
    dec_a, dec_b = add_shares(keep_d, come_d, 4.0, (dg1, outs_come), 2)
    dh1, gain_e1, gain_e2, keep_e, send_e = run(
        enc_ffn_back_kernel,
        (ids, meta, h1, h2, own_c, comekv_c, keyval_cross, *enc_own, *enc_oth),
        "svvvvvv" + "a" * 10,
        (act, row_s, row_s, ffn_g, ffn_g),
        ffn_w
        + [vm(2, TILE, 512), vm(512, 512), vm(2, TILE, 512), vm(512, 512)]
        + [vm(512, 512, kind=F32), sem],
        13.4,
        after=(dec_a,),
    )
    dec_a = to_all(dec_a, "mp")
    (dec_b,) = gated([dec_b], [dec_a])
    dec_b = to_all(dec_b, "mp")
    come_e = swapped(send_e)
    self_scratch = wide + [vm(512, 128)] + kv_scratch + back_scratch + [sem]
    att_dg = shaped((4, 256, 512), BF)
    df1, own_1, sendkv_1, router_1g, keep_w1, send_w1 = run(
        functools.partial(self_back_kernel, 1),
        (
            ids, recv, dg1, mixed_d, log_d, *wa_own, *wa_oth, kvw_own, kvw_oth, keep_wc, send_wc,
        ),
        "svvvv" + "a" * 12,
        (act, kv_f, kv_b, router_s, att_dg, att_dg),
        self_scratch,
        12.2,
        after=(dh1, dec_a),
    )
    comekv_1 = swapped(sendkv_1)
    come_w1 = swapped(send_w1)
    (ffn_e,) = add_shares(keep_e, come_e, 4.0, (df1, dec_b))
    att_d = add_pieces(ids, [keep_w1], [come_w1], 3.6, (ffn_e,))
    df0, own_0, sendkv_0, router_0g, keep_w0, send_w0 = run(
        functools.partial(self_back_kernel, 0),
        (ids, recv, dh1, mixed_e, log_e, *wa_own, *wa_oth, kvw_own, kvw_oth),
        "svvvv" + "a" * 10,
        (act, kv_f, kv_b, router_s, att_g, att_g),
        self_scratch,
        11.8,
        after=(ffn_e, *att_d),
    )
    comekv_0 = swapped(sendkv_0)
    come_w0 = swapped(send_w0)
    ffn_e = to_all(ffn_e, "mp")
    att_d = mp_exchange(att_d)
    dx1, gain_d0, keep_s1, send_s1 = run(
        dec_finish_kernel,
        (ids, recv, dg1, df1, own_1, comekv_1, own_c, comekv_c, memory, kvw_own, kvw_oth),
        "svvvvvvvvaa",
        (shaped((4, 128, 512), BF), row_s, flat_g, flat_g),
        [vm(512, 128), vm(2, TILE, 512), sem],
        0.3,
        after=(df0,),
    )
    come_s1 = swapped(send_s1)
    finished = run(
        enc_finish_kernel,
        (
            ids, recv, dh1, df0, own_0, comekv_0, dx1, router_0g, router_1g, router_cg,
            gain_e1, gain_e2, gain_d0, gain_d1, gain_d2, kvw_own, kvw_oth,
        ),
        "s" + "v" * 14 + "aa",
        shaped((8, 208, 512), BF),
        [vm(512, 128), vm(2, TILE, 512), vm(32, 512, kind=F32), sem],
        0.3,
        after=att_d[1:],
    )
    att_e = add_pieces(
        ids, [keep_w0, keep_s1], [come_w0, come_s1], 3.6, (finished,)
    )
    att_e = mp_exchange(att_e)
    dp = lax.axis_size("dp")
    share = 256 // dp
    if dp == 4:
        ffn = dp_exchange(
            run(
                sum_middle_kernel,
                (ids, dec_a, dec_b, ffn_e, *att_d),
                "s" + "v" * 7,
                [shaped((64, 2560), BF)] * 4,
                [],
                4.0,
                after=(att_e[0],),
            )
        )
        after = ffn[1:]
    else:
        after = ()
    finished = to_all(finished, rowgroup)
    small = run(
        tail_kernel,
        (finished, *att_e),
        "v" * 5,
        shaped((256, 768), BF),
        [],
        3.0,
        after=after,
    )
    dx = run(
        place_kernel,
        (finished,),
        "v",
        shaped((4, 2, 128, 512), F32),
        [],
        3.0,
        after=(small,),
    )
    small = to_all(small.reshape(dp, share, 768), "dp")
    outs_come = outs_come.reshape(2, 4, 128, 512).transpose(1, 0, 2, 3)
    results = (outs_come.reshape(1, 4, 1, 256, 512), dx.reshape(1, 4, 1, 256, 512))
    if dp == 4:
        made = run(
            final_kernel,
            (small, *ffn),
            "v" * 5,
            (
                shaped((3, 2, 64), F32),
                shaped((2, 8, 64), F32),
                shaped((2, 2, 64, 64), F32),
                shaped((2, 64, 128), F32),
                shaped((2, 2, 64, 64), F32),
                shaped((2, 64, 512), F32),
                shaped((2, 64, 512), F32),
                shaped((8, 64), F32),
                shaped((2, 64, 64), F32),
                shaped((64, 128), F32),
                shaped((2, 64, 64), F32),
            ),
            [],
            3.0,
        )
        made = list(made)
        made[0] = made[0].transpose(1, 0, 2)
        made[1] = made[1].transpose(0, 2, 1)
        made[6] = made[6].transpose(0, 2, 1)
        made[7] = made[7].T
        return (*results, *made)

    small = jnp.sum(small.astype(F32), 0)
    middle = jnp.concatenate(
        [jnp.sum(part.astype(F32), 0) for part in (ffn_e, dec_a, dec_b)]
        + [sum(part.astype(F32) for part in att_d)],
        1,
    )
    middle = to_all(middle.astype(BF).reshape(dp, share, 2560), "dp")
    middle = jnp.sum(middle.astype(F32), 0)

    def query_of(value, at):
        return value[:, at : at + 128].reshape(share, 2, 64).transpose(1, 0, 2)

    def output_of(value, at):
        return value[:, at + 128 : at + 256].T.reshape(2, 64, share)

    misc = small[:, 640:768].T

    def router_of(layer):
        return misc[ROUTER_LANES[layer] : ROUTER_LANES[layer] + 8].T

    return (
        *results,
        misc[GAIN_ROW : GAIN_ROW + 6].reshape(2, 3, share),
        jnp.stack([router_of(0), router_of(1)]),
        jnp.stack([query_of(small, 0), query_of(middle, 2304)]),
        jnp.stack([small[:, 512:640], small[:, 256:384]]),
        jnp.stack([output_of(small, 0), output_of(middle, 2304)]),
        jnp.stack([middle[:, :512], middle[:, 1024:1536]]),
        jnp.stack([middle[:, 512:1024].T, middle[:, 1536:2048].T]),
        router_of(2),
        query_of(middle, 2048),
        small[:, 384:512],
        output_of(middle, 2048),
    )


def solution(mesh):
    placed = (
        P("section", None, "dp", "mp", None),
        P("section", None, "dp", None),
        P("section", None, "dp", "mp", None),
        P(None, "dp", "mp", None),
        P("section", None, None),
        P("section", None, None),
        P("section", "mp", None, None),
        P("section", None, None),
        P("section", "mp", None, None),
        P("section", None, "mp"),
        P("section", "mp", None),
        P(),
        P("mp", None, None),
        P(),
        P("mp", None, None),
        P(None, "dp", "mp", None),
    )
    return jax.shard_map(
        per_device,
        mesh=mesh,
        in_specs=placed,
        out_specs=(
            P("section", None, "dp", "mp", None),
            P("section", None, "dp", "mp", None),
            P(None, None, ("section", "dp")),
            P(None, ("section", "dp"), None),
            P(None, "mp", ("section", "dp"), None),
            P(None, ("section", "dp"), None),
            P(None, "mp", None, ("section", "dp")),
            P(None, ("section", "dp"), "mp"),
            P(None, "mp", ("section", "dp")),
            P(("section", "dp"), None),
            P("mp", ("section", "dp"), None),
            P(("section", "dp"), None),
            P("mp", None, ("section", "dp")),
        ),
        check_vma=False,
    )
```

```python
import functools

import jax
import jax.numpy as jnp
from jax import lax
from jax.experimental import pallas as pl
from jax.experimental.pallas import tpu as pltpu
from jax.sharding import PartitionSpec as P

EPS = 1e-05
MASK_VALUE = -1000000000.0
BF = jnp.bfloat16
F32 = jnp.float32
TILE = 256
EX_AT = 160
CODE_ROW = 3
LEN_ROW = 4
ROUTER_AT = 8
GAIN_ROW = 24
ROUTER_LANES = (0, 8, 16)
VMEM_LIMIT = 63 * 1024 * 1024
LARGE = 1 << 40


def nn(left, right):
    return lax.dot_general(left, right, (((1,), (0,)), ((), ())), preferred_element_type=F32)


def nt(left, right):
    return lax.dot_general(left, right, (((1,), (1,)), ((), ())), preferred_element_type=F32)


def tn(left, right):
    return lax.dot_general(left, right, (((0,), (0,)), ((), ())), preferred_element_type=F32)


def norm_of(values, gain_row):
    center = values - jnp.mean(values, 1, keepdims=True)
    scaled = lax.rsqrt(jnp.mean(center * center, 1, keepdims=True) + EPS)
    unit_rows = center * scaled
    return unit_rows * gain_row, unit_rows, scaled


def norm_back(upstream, unit_rows, scaled, gain_row):
    inner = upstream * gain_row
    result = scaled * (
        inner
        - jnp.mean(inner, 1, keepdims=True)
        - unit_rows * jnp.mean(inner * unit_rows, 1, keepdims=True)
    )
    return result, jnp.sum(upstream * unit_rows, 0, keepdims=True)


def eye_of(size):
    return lax.broadcasted_iota(jnp.int32, (size, size), 0) == lax.broadcasted_iota(
        jnp.int32, (size, size), 1
    )


def row_to_col(row):
    return jnp.sum(jnp.where(eye_of(128), row, 0.0), 1, keepdims=True)


def col_to_row(col):
    parts = []
    for at in range(0, col.shape[0], 128):
        part = jnp.where(eye_of(128), col[at : at + 128], 0.0)
        parts.append(jnp.sum(part, 0, keepdims=True))
    return jnp.concatenate(parts, 1)


def ends_of(extra):
    lengths = extra[LEN_ROW : LEN_ROW + 1, 0:8] * 32.0 + extra[LEN_ROW : LEN_ROW + 1, 128:136]
    ends = [lengths[:, 0:1]]
    for k in range(1, 8):
        ends.append(ends[-1] + lengths[:, k : k + 1])
    return ends


def segments(places, ends):
    total = jnp.where(places >= ends[0], 1.0, 0.0)
    for end in ends[1:]:
        total = total + jnp.where(places >= end, 1.0, 0.0)
    return total


def extra_of(recv_ref, layer, quarter):
    at = EX_AT if recv_ref.shape[1] > 16 else 0
    return recv_ref[4 * layer + quarter, at : at + 16, :]


def gain_of(recv_ref, layer, which):
    return extra_of(recv_ref, layer, 0).astype(F32)[which : which + 1, :]


def rows_of(recv_ref, layer, t):
    return recv_ref[pl.ds(4 * layer + 2 * t, 2), 0:128, :].reshape(TILE, 512).astype(F32)


def codes_of(recv_ref, layer, t, lane):
    cols = []
    for i in range(2):
        extra = extra_of(recv_ref, layer, 2 * t + i).astype(F32)
        cols.append(row_to_col(extra[CODE_ROW : CODE_ROW + 1, lane : lane + 128]))
    return jnp.concatenate(cols, 0)


def other_kv(recv_ref, layer, quarter):
    packed = recv_ref[4 * layer + quarter, 128:160, :]
    return jnp.concatenate([packed[:, 128 * c : 128 * c + 128] for c in range(4)], 0)


def routing(query_rows, router_block, code):
    second = jnp.floor(code * 0.125)
    first = code - 8.0 * second
    e0, e1 = first.astype(jnp.int32), second.astype(jnp.int32)
    logits = nt(query_rows, router_block)
    lanes = lax.broadcasted_iota(jnp.int32, logits.shape, 1)
    l0 = jnp.sum(jnp.where(lanes == e0 + ROUTER_AT, logits, 0.0), 1, keepdims=True)
    l1 = jnp.sum(jnp.where(lanes == e1 + ROUTER_AT, logits, 0.0), 1, keepdims=True)
    top = jnp.maximum(l0, l1)
    x0, x1 = jnp.exp(l0 - top), jnp.exp(l1 - top)
    total = x0 + x1
    owners = lax.broadcasted_iota(jnp.int32, (code.shape[0], 512), 1) >> 6
    return e0, e1, x0 / total, x1 / total, owners == e0, owners == e1


def fold(wide, mask):
    kept = jnp.where(mask, wide, 0.0)
    return kept[:, 0:128] + kept[:, 128:256] + kept[:, 256:384] + kept[:, 384:512]


def spread(a0, a1, m0, m1):
    parts = []
    for c in range(4):
        cut = slice(128 * c, 128 * c + 128)
        parts.append(jnp.where(m0[:, cut], a0, jnp.where(m1[:, cut], a1, 0.0)))
    return jnp.concatenate(parts, 1).astype(BF)


def rounded(value):
    return value.astype(BF).astype(F32)


def start_pick(cond, yes, no, dst, sem):
    @pl.when(cond)
    def _():
        pltpu.make_async_copy(yes, dst, sem).start()

    @pl.when(jnp.logical_not(cond))
    def _():
        pltpu.make_async_copy(no, dst, sem).start()


class Loads:
    def __init__(self, sems):
        self.sems, self.used = sems, 0

    def start(self, cond, yes, no, dst):
        sem = self.sems.at[self.used]
        self.used += 1
        start_pick(cond, yes, no, dst, sem)
        return functools.partial(lambda a, b, c: pltpu.make_async_copy(a, b, c).wait(), yes, dst, sem)

    def plain(self, src, dst):
        sem = self.sems.at[self.used]
        self.used += 1
        copy = pltpu.make_async_copy(src, dst, sem)
        copy.start()
        return copy.wait

    def rows(self, cond, yes, no, at, dst, m):
        cut = pl.ds(at, 128)
        return [
            self.start(cond, yes[b].at[cut], no[b].at[cut], dst.at[pl.ds(128 * (m ^ b), 128)])
            for b in range(4)
        ]

    def pieces(self, cond, yes, no, dst, m):
        waits = []
        for b, (one, other) in enumerate(zip(yes, no)):
            to = dst.at[m ^ b] if b < 3 else dst.at[m ^ 3, pl.ds(256 * (b - 3), 256)]
            if len(yes) == 4:
                to = dst.at[m ^ b]
            waits.append(self.start(cond, one, other, to))
        return waits


def wait_all(waits):
    for wait in waits:
        wait()


def widen_kv(kv_ref, k2_ref, v2_ref):
    for j in range(4):
        kv = kv_ref[j].reshape(256, 128).astype(F32)
        turned = pltpu.roll(kv, 64, 1)
        low = lax.broadcasted_iota(jnp.int32, kv.shape, 1) < 64
        k2_ref[256 * j : 256 * j + 256, :] = jnp.where(low, kv, turned).astype(BF)
        v2_ref[256 * j : 256 * j + 256, :] = jnp.where(low, turned, kv).astype(BF)


def attend_tile(query_rows, route, w_qt, w_o, k2, v2, allowed):
    e0, e1, g0, g1, m0, m1 = route
    q_all = nt(query_rows, w_qt) * 0.125
    queries = jnp.concatenate([fold(q_all, m0), fold(q_all, m1)], 0).astype(BF)
    scores = nt(queries, k2)
    scores = jnp.concatenate(
        [
            jnp.where(allowed, scores[0:TILE], MASK_VALUE),
            jnp.where(allowed, scores[TILE:], MASK_VALUE),
        ],
        0,
    )
    top = jnp.max(scores, 1, keepdims=True)
    weights = jnp.exp(scores - top)
    total = jnp.sum(weights, 1, keepdims=True)
    mixed = nn(weights.astype(BF), v2) / total
    log_total = top + jnp.log(total)
    gated = spread(rounded(g0) * mixed[0:TILE], rounded(g1) * mixed[TILE:], m0, m1)
    return nn(gated, w_o), mixed, col_to_row(log_total)


def attend_back_tile(
    t, upstream, query_rows, route, mixed, log_row, w_qt, w_o, router_block, router_lane, k2, v2,
    allowed_t, grad_k, grad_v, gated_ref, dz_ref, dq_ref, dlog_ref,
):
    e0, e1, g0, g1, m0, m1 = route
    q_all = nt(query_rows, w_qt) * 0.125
    queries = jnp.concatenate([fold(q_all, m0), fold(q_all, m1)], 0).astype(BF)
    dz = upstream.astype(BF)
    dg_all = nt(dz, w_o)
    dgated0, dgated1 = fold(dg_all, m0), fold(dg_all, m1)
    r0, r1 = rounded(g0), rounded(g1)
    mixed0, mixed1 = mixed[0:TILE], mixed[TILE:]
    gated_ref[t] = spread(r0 * mixed0, r1 * mixed1, m0, m1)
    dz_ref[t] = dz
    dgate0 = rounded(jnp.sum(mixed0 * dgated0, 1, keepdims=True))
    dgate1 = rounded(jnp.sum(mixed1 * dgated1, 1, keepdims=True))
    do0, do1 = (r0 * dgated0).astype(BF), (r1 * dgated1).astype(BF)
    grad_mixed = jnp.concatenate([do0, do1], 0)
    inner_row = jnp.concatenate(
        [
            col_to_row(jnp.sum(do0.astype(F32) * mixed0, 1, keepdims=True)),
            col_to_row(jnp.sum(do1.astype(F32) * mixed1, 1, keepdims=True)),
        ],
        1,
    )
    scores = nt(k2, queries)
    scores = jnp.concatenate(
        [
            jnp.where(allowed_t, scores[:, 0:TILE], MASK_VALUE),
            jnp.where(allowed_t, scores[:, TILE:], MASK_VALUE),
        ],
        1,
    )
    probs = jnp.exp(scores - log_row)
    grad_probs = nt(v2, grad_mixed)
    grad_scores = (probs * (grad_probs - inner_row)).astype(BF)
    grad_v[...] += nn(probs.astype(BF), grad_mixed)
    grad_k[...] += nn(grad_scores, queries)
    grad_q = rounded(tn(grad_scores, k2) * 0.125)
    dq_all = spread(grad_q[0:TILE], grad_q[TILE:], m0, m1)
    dq_ref[t] = dq_all
    grad_rows = nn(dq_all, w_qt)
    mean_grad = g0 * dgate0 + g1 * dgate1
    dc0, dc1 = g0 * (dgate0 - mean_grad), g1 * (dgate1 - mean_grad)
    lanes = lax.broadcasted_iota(jnp.int32, (TILE, 16), 1)
    dlog = jnp.where(lanes == e0 + ROUTER_AT, dc0, 0.0) + jnp.where(
        lanes == e1 + ROUTER_AT, dc1, 0.0
    )
    wide = lax.broadcasted_iota(jnp.int32, (TILE, 128), 1)
    dlog_ref[t] = (
        jnp.where(wide == e0 + router_lane, dc0, 0.0)
        + jnp.where(wide == e1 + router_lane, dc1, 0.0)
    ).astype(BF)
    return grad_rows + nn(dlog.astype(BF), router_block)


def query_places(t, sec, dims, along):
    local = lax.broadcasted_iota(jnp.int32, dims, along)
    return (512 * t + 128 * sec + local + (local & ~127)).astype(F32)


def allowed_rows(t, sec, ends_q, ends_k, causal):
    query_at = query_places(t, sec, (TILE, 1), 0)
    key_at = lax.broadcasted_iota(jnp.int32, (1, 1024), 1).astype(F32)
    allowed = segments(query_at, ends_q) == segments(key_at, ends_k)
    if causal:
        allowed = allowed & (key_at <= query_at)
    return allowed


def key_segments_t(ends_k, segk_ref):
    for j in range(8):
        at = lax.broadcasted_iota(jnp.int32, (128, TILE), 0).astype(F32) + 128.0 * j
        segk_ref[128 * j : 128 * j + 128, :] = segments(at, ends_k)


def allowed_cols(t, sec, ends_q, segk_ref, causal):
    query_at = query_places(t, sec, (1, TILE), 1)
    allowed = segk_ref[...] == segments(query_at, ends_q)
    if causal:
        key_at = lax.broadcasted_iota(jnp.int32, (1024, TILE), 0).astype(F32)
        allowed = allowed & (key_at <= query_at)
    return allowed


def fold_kv(grad_k, grad_v, sec, own_ref, send_ref):
    for j in range(4):
        k = grad_k[256 * j : 256 * j + 256, :]
        v = grad_v[256 * j : 256 * j + 256, :]
        k = k + pltpu.roll(k, 64, 1)
        v = v + pltpu.roll(v, 64, 1)
        low = lax.broadcasted_iota(jnp.int32, k.shape, 1) < 64
        both = jnp.where(low, k, v)
        first, second = both[0:128], both[128:256]
        own_ref[j] = jnp.where(sec == 0, first, second)
        send_ref[j] = jnp.where(sec == 0, second, first).astype(send_ref.dtype)


def split_halves(value, sec, keep_ref, send_ref, m, lane):
    upper, lower = value[0:256], value[256:512]
    cut = slice(lane, lane + value.shape[1])
    keep_ref[m, :, cut] = jnp.where(sec == 0, upper, lower).astype(BF)
    send_ref[m, :, cut] = jnp.where(sec == 0, lower, upper).astype(BF)


def split_flat(value, sec, keep_ref, send_ref, lane):
    upper, lower = value[0:256], value[256:512]
    cut = slice(lane, lane + value.shape[1])
    keep_ref[:, cut] = jnp.where(sec == 0, upper, lower).astype(BF)
    send_ref[:, cut] = jnp.where(sec == 0, lower, upper).astype(BF)


def turned_rows(value):
    return value.astype(F32).T.astype(BF)


def flat(ref):
    return ref[...].reshape(512, ref.shape[-1])


def attention_weight_grads(first_t, gated_ref, dz_ref, dq_ref, sec, keep_ref, send_ref, lane):
    grad_q = nn(first_t, flat(dq_ref))
    grad_o = nn(turned_rows(flat(dz_ref)), flat(gated_ref))
    for b in range(4):
        cut = slice(128 * b, 128 * b + 128)
        split_halves(grad_q[:, cut], sec, keep_ref, send_ref, b, lane)
        split_halves(grad_o[:, cut], sec, keep_ref, send_ref, b, lane + 128)


def router_grads(dlog_ref, rows_ref):
    turned = flat(dlog_ref).astype(F32).T.astype(BF)
    return nn(turned, flat(rows_ref))[0:32]


def gelu_parts(pre):
    cdf = 0.5 * (1.0 + lax.erf(pre * 0.7071067811865476))
    slope = cdf + pre * (jnp.exp(-0.5 * pre * pre) * 0.3989422804014327)
    return pre * cdf, slope


def own_self_kv(recv_ref, layer, sec, w_kv, kv_ref):
    gain = gain_of(recv_ref, layer, 0)
    for t in range(2):
        first = norm_of(rows_of(recv_ref, layer, t), gain)[0].astype(BF)
        kv = nn(first, w_kv).astype(BF)
        for i in range(2):
            j = 2 * t + i
            kv_ref[j, sec] = kv[128 * i : 128 * i + 128]
            kv_ref[j, 1 - sec] = other_kv(recv_ref, layer, j)


def cross_kv(kvm_ref, kvo_ref, sec, kv_s):
    for j in range(4):
        kv_s[j, sec] = kvm_ref[j]
        kv_s[j, 1 - sec] = kvo_ref[j]


def pack_kernel(
    ready, len_ref, x_ref, gain_ref, w_kv_ref, own_ref, cross_ref, router_ref, send_ref, extra_s
):
    ready()
    gain = gain_ref[0:1, :].astype(F32)
    w_kv = w_kv_ref[...]
    extra_s[...] = jnp.zeros_like(extra_s)
    extra_s[0:3, :] = gain_ref[...].astype(F32)
    extra_s[ROUTER_AT : ROUTER_AT + 8, :] = router_ref[...].astype(F32)
    lanes = lax.broadcasted_iota(jnp.int32, (1, 512), 1)
    for i in range(4):
        first = norm_of(x_ref[i].astype(F32), gain)[0].astype(BF)
        kv = nn(first, w_kv).astype(BF)
        row = jnp.zeros((1, 512), jnp.int32)
        for k in range(8):
            length = len_ref[i, k]
            row = jnp.where(lanes == k, length >> 5, row)
            row = jnp.where(lanes == 128 + k, length & 31, row)
        extra_s[LEN_ROW : LEN_ROW + 1, :] = row.astype(F32)
        own, cross = own_ref[i], cross_ref[i]
        own_code = (own[0:1] + 8 * own[1:2]).astype(F32)
        cross_code = (cross[0:1] + 8 * cross[1:2]).astype(F32)
        for half in range(2):
            to = 4 * half + i
            here = slice(128 * half, 128 * half + 128)
            send_ref[to, 0:128, :] = x_ref[i, here, :]
            far = kv[128 * (1 - half) : 128 * (1 - half) + 128]
            send_ref[to, 128:160, :] = jnp.concatenate(
                [far[32 * c : 32 * c + 32] for c in range(4)], 1
            )
            extra_s[CODE_ROW : CODE_ROW + 1, 0:128] = own_code[:, here]
            extra_s[CODE_ROW : CODE_ROW + 1, 128:256] = cross_code[:, here]
            send_ref[to, EX_AT : EX_AT + 16, :] = extra_s[...].astype(BF)


def self_fwd_kernel(ready, ids_ref, recv_ref, *refs):
    wa_own, wa_oth, kvw_own, kvw_oth = refs[:4], refs[4:8], refs[8], refs[9]
    h1_ref, g1_ref, mixed_e, mixed_d, log_e, log_d, meta_ref, kv_ref = refs[10:18]
    wq, wo, wkv, k2, v2, sems = refs[18:]
    sec, m = ids_ref[0], ids_ref[1]
    loads = Loads(sems)
    kv_waits = [loads.start(sec == i, kvw_own, kvw_oth, wkv.at[i]) for i in range(2)]
    waits = []
    for layer in range(2):
        waits += loads.rows(sec == layer, wa_own, wa_oth, 0, wq.at[layer], m)
        waits += loads.rows(sec == layer, wa_own, wa_oth, 128, wo.at[layer], m)
    ready()
    meta_ref[...] = recv_ref[:, EX_AT : EX_AT + 16, :]
    wait_all(kv_waits)
    for layer in range(2):
        own_self_kv(recv_ref, layer, sec, wkv[layer], kv_ref.at[layer])
        widen_kv(kv_ref.at[layer], k2.at[layer], v2.at[layer])
    wait_all(waits)
    ends = [ends_of(extra_of(recv_ref, layer, 0).astype(F32)) for layer in range(2)]

    def tile(t, carry):
        for layer, after_ref, mixed_ref, log_ref in (
            (0, h1_ref, mixed_e, log_e),
            (1, g1_ref, mixed_d, log_d),
        ):
            rows = rows_of(recv_ref, layer, t)
            first = norm_of(rows, gain_of(recv_ref, layer, 0))[0].astype(BF)
            route = routing(first, extra_of(recv_ref, layer, 0), codes_of(recv_ref, layer, t, 0))
            allowed = allowed_rows(t, sec, ends[layer], ends[layer], layer == 1)
            out, mixed, row_log = attend_tile(
                first, route, wq[layer], wo[layer], k2[layer], v2[layer], allowed
            )
            after_ref[t] = rows + out
            mixed_ref[t] = mixed
            log_ref[t] = row_log
        return carry

    lax.fori_loop(0, 2, tile, 0)


def enc_ffn_kernel(ready, ids_ref, recv_ref, h1_ref, kvc_ref, *refs):
    f_own, f_oth = refs[:4], refs[4:8]
    h2_ref, mem_ref, kvm_ref, w_in, w_out, third_s, sems = refs[8:]
    low, m = ids_ref[0] == 0, ids_ref[1]
    loads = Loads(sems)
    waits = loads.pieces(low, f_own, f_oth, w_in, m) + loads.pieces(low, f_oth, f_own, w_out, m)
    ready()
    for t in range(2):
        h2_ref[t] = h1_ref[t]
        third_s[t] = norm_of(h1_ref[t], gain_of(recv_ref, 0, 2))[0].astype(BF)
    wait_all(waits)

    def chunk(c, carry):
        pre = nn(flat(third_s), w_in[c])
        hidden = (0.5 * pre * (1.0 + lax.erf(pre * 0.7071067811865476))).astype(BF)
        h2_ref[...] += nn(hidden, w_out[c]).reshape(2, TILE, 512)
        return carry

    lax.fori_loop(0, 4, chunk, 0)
    for t in range(2):
        memory = norm_of(h2_ref[t], gain_of(recv_ref, 0, 1))[0].astype(BF)
        mem_ref[t] = memory
        kv = nn(memory, kvc_ref[...]).astype(BF)
        kvm_ref[2 * t] = kv[0:128]
        kvm_ref[2 * t + 1] = kv[128:256]


def cross_fwd_kernel(
    ready, ids_ref, recv_ref, g1_ref, kvm_ref, kvo_ref, rc_ref, *refs
):
    wa_own, wa_oth = refs[:4], refs[4:8]
    g2_ref, mixed_ref, log_ref, wq, wo, kv_s, k2, v2, sems = refs[8:]
    sec, m = ids_ref[0], ids_ref[1]
    loads = Loads(sems)
    waits = loads.rows(sec == 0, wa_own, wa_oth, 256, wq, m)
    waits += loads.rows(sec == 0, wa_oth, wa_own, 256, wo, m)
    ready()
    cross_kv(kvm_ref, kvo_ref, sec, kv_s)
    widen_kv(kv_s, k2, v2)
    wait_all(waits)
    ends_k = ends_of(extra_of(recv_ref, 0, 0).astype(F32))
    ends_q = ends_of(extra_of(recv_ref, 1, 0).astype(F32))

    def tile(t, carry):
        before = g1_ref[t]
        second = norm_of(before, gain_of(recv_ref, 1, 1))[0].astype(BF)
        route = routing(second, rc_ref[...], codes_of(recv_ref, 1, t, 128))
        allowed = allowed_rows(t, sec, ends_q, ends_k, False)
        out, mixed, row_log = attend_tile(second, route, wq[...], wo[...], k2[...], v2[...], allowed)
        g2_ref[t] = before + out
        mixed_ref[t] = mixed
        log_ref[t] = row_log
        return carry

    lax.fori_loop(0, 2, tile, 0)


def ffn_both(c, third_s, third_t, dy_s, dy_t, w_in, w_out, dthird, sec, keep_ref, send_ref):
    pre = nn(flat(third_s), w_in[c])
    hidden, slope = gelu_parts(pre)
    hidden = hidden.astype(BF)
    dpre = (nt(flat(dy_s), w_out[c]) * slope).astype(BF)
    dthird[...] += nt(dpre, w_in[c])
    split_halves(nn(third_t[...], dpre), sec, keep_ref, send_ref, c, 0)
    split_halves(nn(dy_t[...], hidden), sec, keep_ref, send_ref, c, 512)
    return hidden


def dec_ffn_kernel(ready, ids_ref, recv_ref, g2_ref, mem_ref, cot_in, *refs):
    f_own, f_oth = refs[:5], refs[5:10]
    outs_ref, dg2_ref, gain_ref, keep_ref, send_ref = refs[10:15]
    w_in, w_out, cot_s, third_s, third_t, cot_t, acc, dthird, sems = refs[15:]
    sec, m = ids_ref[0], ids_ref[1]
    low = sec == 0
    loads = Loads(sems)
    cot_waits = [loads.plain(cot_in.at[i], cot_s.at[i]) for i in range(4)]
    waits = loads.pieces(low, f_own, f_oth, w_in, m) + loads.pieces(low, f_oth, f_own, w_out, m)
    ready()
    for t in range(2):
        acc[t] = g2_ref[t]
        third_s[t] = norm_of(g2_ref[t], gain_of(recv_ref, 1, 2))[0].astype(BF)
        outs_ref[2 * t : 2 * t + 2] = mem_ref[t].reshape(2, 128, 512)
    third_t[...] = turned_rows(flat(third_s))
    wait_all(cot_waits)
    cot_t[...] = turned_rows(flat(cot_s))
    dthird[...] = jnp.zeros_like(dthird)
    wait_all(waits)

    def chunk(c, carry):
        hidden = ffn_both(
            c, third_s, third_t, cot_s, cot_t, w_in, w_out, dthird, sec, keep_ref, send_ref
        )
        acc[...] += nn(hidden, w_out[c]).reshape(2, TILE, 512)
        return carry

    lax.fori_loop(0, 4, chunk, 0)
    total = jnp.zeros((1, 512), F32)
    gain = gain_of(recv_ref, 1, 2)
    for t in range(2):
        outs_ref[4 + 2 * t : 6 + 2 * t] = acc[t].astype(BF).reshape(2, 128, 512)
        unused_out, unit, scaled = norm_of(g2_ref[t], gain)
        back, gain_grad = norm_back(dthird[TILE * t : TILE * t + TILE, :], unit, scaled, gain)
        dg2_ref[t] = cot_s[2 * t : 2 * t + 2].reshape(TILE, 512).astype(F32) + back
        total = total + gain_grad
    gain_ref[...] = total


def cross_back_kernel(
    ready, ids_ref, recv_ref, g1_ref, dg2_ref, mixed_ref, log_ref, kvm_ref, kvo_ref, rc_ref, *refs
):
    wa_own, wa_oth = refs[:4], refs[4:8]
    dg1_ref, gain_ref, own_ref, send_ref, router_ref, keepw_ref, sendw_ref = refs[8:15]
    wq, wo, kv_s, k2, v2, segk, grad_k, grad_v, second_s, gated_s, dz_s, dq_s, dlog_s, sems = refs[15:]
    sec, m = ids_ref[0], ids_ref[1]
    loads = Loads(sems)
    waits = loads.rows(sec == 0, wa_own, wa_oth, 256, wq, m)
    waits += loads.rows(sec == 0, wa_oth, wa_own, 256, wo, m)
    ready()
    cross_kv(kvm_ref, kvo_ref, sec, kv_s)
    widen_kv(kv_s, k2, v2)
    ends_k = ends_of(extra_of(recv_ref, 0, 0).astype(F32))
    ends_q = ends_of(extra_of(recv_ref, 1, 0).astype(F32))
    key_segments_t(ends_k, segk)
    grad_k[...] = jnp.zeros_like(grad_k)
    grad_v[...] = jnp.zeros_like(grad_v)
    wait_all(waits)

    def tile(t, total):
        gain = gain_of(recv_ref, 1, 1)
        second, unit, scaled = norm_of(g1_ref[t], gain)
        second = second.astype(BF)
        second_s[t] = second
        route = routing(second, rc_ref[...], codes_of(recv_ref, 1, t, 128))
        allowed = allowed_cols(t, sec, ends_q, segk, False)
        grad_rows = attend_back_tile(
            t, dg2_ref[t], second, route, mixed_ref[t], log_ref[t], wq[...], wo[...], rc_ref[...],
            ROUTER_LANES[2], k2[...], v2[...], allowed, grad_k, grad_v, gated_s, dz_s, dq_s, dlog_s,
        )
        back, gain_grad = norm_back(grad_rows, unit, scaled, gain)
        dg1_ref[t] = dg2_ref[t] + back
        return total + gain_grad

    gain_ref[...] = lax.fori_loop(0, 2, tile, jnp.zeros((1, 512), F32))
    fold_kv(grad_k, grad_v, sec, own_ref, send_ref)
    router_ref[...] = router_grads(dlog_s, second_s)
    attention_weight_grads(
        turned_rows(flat(second_s)), gated_s, dz_s, dq_s, sec, keepw_ref, sendw_ref, 0
    )


def self_back_kernel(layer, ready, ids_ref, recv_ref, up_ref, mixed_ref, log_ref, *refs):
    wa_own, wa_oth, kv_self = refs[:4], refs[4:8], refs[8]
    refs = refs[9:]
    if layer == 1:
        before, refs = refs[:2], refs[2:]
    dfirst_ref, own_ref, send_ref, router_ref, keepw_ref, sendw_ref = refs[:6]
    wq, wo, kv_s, k2, v2, segk, grad_k, grad_v = refs[6:14]
    first_s, gated_s, dz_s, dq_s, dlog_s, sems = refs[14:]
    sec, m = ids_ref[0], ids_ref[1]
    mine = sec == layer
    loads = Loads(sems)
    kv_wait = loads.plain(kv_self.at[layer], kv_s)
    waits = loads.rows(mine, wa_own, wa_oth, 0, wq, m) + loads.rows(mine, wa_own, wa_oth, 128, wo, m)
    lane = 0
    if layer == 1:
        lane = 256
        for src, dst in zip(before, (keepw_ref, sendw_ref)):
            waits.append(loads.plain(src, dst.at[:, :, pl.ds(0, 256)]))
    ready()
    ends = ends_of(extra_of(recv_ref, layer, 0).astype(F32))
    key_segments_t(ends, segk)
    grad_k[...] = jnp.zeros_like(grad_k)
    grad_v[...] = jnp.zeros_like(grad_v)
    kv_wait()
    widen_kv(kv_s, k2, v2)
    wait_all(waits)
    router_block = extra_of(recv_ref, layer, 0)

    def tile(t, carry):
        first = norm_of(rows_of(recv_ref, layer, t), gain_of(recv_ref, layer, 0))[0].astype(BF)
        first_s[t] = first
        route = routing(first, router_block, codes_of(recv_ref, layer, t, 0))
        allowed = allowed_cols(t, sec, ends, segk, layer == 1)
        dfirst_ref[t] = attend_back_tile(
            t, up_ref[t], first, route, mixed_ref[t], log_ref[t], wq[...], wo[...], router_block,
            ROUTER_LANES[layer], k2[...], v2[...], allowed, grad_k, grad_v, gated_s, dz_s, dq_s,
            dlog_s,
        )
        return carry

    lax.fori_loop(0, 2, tile, 0)
    fold_kv(grad_k, grad_v, sec, own_ref, send_ref)
    router_ref[...] = router_grads(dlog_s, first_s)
    attention_weight_grads(
        turned_rows(flat(first_s)), gated_s, dz_s, dq_s, sec, keepw_ref, sendw_ref, lane
    )


def enc_ffn_back_kernel(
    ready, ids_ref, recv_ref, h1_ref, h2_ref, own_ref, come_ref, kvc_ref, *refs
):
    f_own, f_oth = refs[:4], refs[4:8]
    dh1_ref, gain_ref, gain2_ref, keep_ref, send_ref = refs[8:13]
    w_in, w_out, third_s, third_t, dy_s, dy_t, dthird, sems = refs[13:]
    sec, m = ids_ref[0], ids_ref[1]
    low = sec == 0
    loads = Loads(sems)
    waits = loads.pieces(low, f_own, f_oth, w_in, m) + loads.pieces(low, f_oth, f_own, w_out, m)
    ready()
    total = jnp.zeros((1, 512), F32)
    gain = gain_of(recv_ref, 0, 1)
    for t in range(2):
        dkv = (own_ref[2 * t : 2 * t + 2] + come_ref[2 * t : 2 * t + 2].astype(F32)).astype(BF)
        dmem = rounded(nt(dkv.reshape(TILE, 128), kvc_ref[...]))
        unused_out, unit, scaled = norm_of(h2_ref[t], gain)
        back, gain_grad = norm_back(dmem, unit, scaled, gain)
        dh1_ref[t] = back
        dy_s[t] = back.astype(BF)
        third_s[t] = norm_of(h1_ref[t], gain_of(recv_ref, 0, 2))[0].astype(BF)
        total = total + gain_grad
    gain_ref[...] = total
    third_t[...] = turned_rows(flat(third_s))
    dy_t[...] = turned_rows(flat(dy_s))
    dthird[...] = jnp.zeros_like(dthird)
    wait_all(waits)

    def chunk(c, carry):
        ffn_both(c, third_s, third_t, dy_s, dy_t, w_in, w_out, dthird, sec, keep_ref, send_ref)
        return carry

    lax.fori_loop(0, 4, chunk, 0)
    total = jnp.zeros((1, 512), F32)
    gain = gain_of(recv_ref, 0, 2)
    for t in range(2):
        unused_out, unit, scaled = norm_of(h1_ref[t], gain)
        back, gain_grad = norm_back(dthird[TILE * t : TILE * t + TILE, :], unit, scaled, gain)
        dh1_ref[t] += back
        total = total + gain_grad
    gain2_ref[...] = total


def finish_rows(layer, recv_ref, up_ref, df_ref, own_ref, come_ref, wkv, first_s, out_ref, at):
    total = jnp.zeros((1, 512), F32)
    gain = gain_of(recv_ref, layer, 0)
    dkvs = []
    for t in range(2):
        first, unit, scaled = norm_of(rows_of(recv_ref, layer, t), gain)
        first_s[t] = first.astype(BF)
        dkv = (own_ref[2 * t : 2 * t + 2] + come_ref[2 * t : 2 * t + 2].astype(F32)).astype(BF)
        dkv = dkv.reshape(TILE, 128)
        dkvs.append(dkv)
        back, gain_grad = norm_back(df_ref[t] + nt(dkv, wkv), unit, scaled, gain)
        dx = (up_ref[t] + back).astype(BF)
        for i in range(2):
            out_ref[at + 2 * t + i, 0:128, :] = dx[128 * i : 128 * i + 128]
        total = total + gain_grad
    grad = nn(turned_rows(flat(first_s)), jnp.concatenate(dkvs, 0))
    return total, grad


def dec_finish_kernel(
    ready, ids_ref, recv_ref, up_ref, df_ref, own_ref, come_ref, own_c, come_c, mem_ref, kvw_own, kvw_oth,
    dx_ref, gain_ref, keep_ref, send_ref, wkv, first_s, sems,
):
    sec = ids_ref[0]
    wait = Loads(sems).start(sec == 1, kvw_own, kvw_oth, wkv)
    ready()
    dkv_c = (own_c[...] + come_c[...].astype(F32)).astype(BF).reshape(512, 128)
    split_flat(nn(turned_rows(flat(mem_ref)), dkv_c), sec, keep_ref, send_ref, 128)
    wait()
    gain_ref[...], grad = finish_rows(
        1, recv_ref, up_ref, df_ref, own_ref, come_ref, wkv[...], first_s, dx_ref, 0
    )
    split_flat(grad, sec, keep_ref, send_ref, 0)


def enc_finish_kernel(
    ready, ids_ref, recv_ref, up_ref, df_ref, own_ref, come_ref, dx1_ref, r0, r1, rc,
    gain_e1, gain_e2, gain_d0, gain_d1, gain_d2, kvw_own, kvw_oth,
    out_ref, wkv, first_s, misc, sems,
):
    sec = ids_ref[0]
    wait = Loads(sems).start(sec == 0, kvw_own, kvw_oth, wkv)
    ready()
    misc[...] = r0[...] + r1[...] + rc[...]
    out_ref[4:8, 0:128, :] = dx1_ref[...]
    wait()
    gain_e0, grad = finish_rows(
        0, recv_ref, up_ref, df_ref, own_ref, come_ref, wkv[...], first_s, out_ref, 0
    )
    rows = (gain_e0, gain_e1[...], gain_e2[...], gain_d0[...], gain_d1[...], gain_d2[...])
    for i, row in enumerate(rows):
        misc[GAIN_ROW + i : GAIN_ROW + i + 1, :] = row
    both = misc[...]
    for half in range(2):
        cut = slice(256 * half, 256 * half + 256)
        part = grad[cut].astype(BF)
        small = both[:, cut].astype(BF)
        block = jnp.concatenate(
            [
                jnp.concatenate([part[64 * c : 64 * c + 64] for c in range(4)], 1),
                jnp.concatenate([small[0:16], small[16:32]], 1),
            ],
            0,
        )
        for i in range(4):
            out_ref[4 * half + i, 128:208, :] = block


def add_kernel(keep_ref, come_ref, *outs):
    lane = 0
    for out_ref in outs:
        cut = slice(lane, lane + out_ref.shape[-1])
        out_ref[...] = keep_ref[:, :, cut] + come_ref[:, :, cut]
        lane += out_ref.shape[-1]


def add_pieces_kernel(flats, ready, ids_ref, *refs):
    ready()
    n = len(flats)
    keeps, comes, outs = refs[:n], refs[n : 2 * n], refs[2 * n :]
    m = ids_ref[1]
    for b in range(4):
        lane = 0
        for is_flat, keep, come in zip(flats, keeps, comes):
            left = keep[...] if is_flat else keep[m ^ b]
            right = come[...] if is_flat else come[m ^ b]
            width = keep.shape[-1]
            outs[b][:, lane : lane + width] = left + right
            lane += width


def sum_middle_kernel(ready, ids_ref, dec_a, dec_b, enc_ref, *refs):
    att, outs = refs[:4], refs[4:]
    ready()
    rows = outs[0].shape[0]
    d = ids_ref[2]
    for k in range(len(outs)):
        cut = pl.ds(pl.multiple_of((d ^ k) * rows, rows), rows)
        for ref, lane in ((enc_ref, 0), (dec_a, 1024), (dec_b, 1536)):
            total = ref[0, cut, :].astype(F32)
            for i in range(1, 4):
                total = total + ref[i, cut, :].astype(F32)
            outs[k][:, lane : lane + ref.shape[-1]] = total.astype(BF)
        total = att[0][cut, :].astype(F32)
        for part in att[1:]:
            total = total + part[cut, :].astype(F32)
        outs[k][:, 2048:2560] = total.astype(BF)


def place_kernel(ready, dx_ref, dx_out):
    ready()
    for i in range(4):
        for half in range(2):
            dx_out[i, half] = dx_ref[4 * half + i, 0:128, :].astype(F32)


def tail_kernel(ready, dx_ref, *refs):
    att_e, (out_ref,) = refs[:4], refs[4:]
    ready()
    total = att_e[0][...].astype(F32)
    for part in att_e[1:]:
        total = total + part[...].astype(F32)
    out_ref[:, 0:512] = total.astype(BF)
    small = dx_ref[0, 128:208, :].astype(F32)
    for i in range(1, 8):
        small = small + dx_ref[i, 128:208, :].astype(F32)
    for c in range(4):
        out_ref[64 * c : 64 * c + 64, 512:640] = small[0:64, 128 * c : 128 * c + 128].astype(BF)
    misc = jnp.concatenate([small[64:80, 0:256], small[64:80, 256:512]], 0)
    misc = jnp.concatenate([misc, jnp.zeros((96, 256), F32)], 0)
    out_ref[:, 640:768] = misc.T.astype(BF)


def final_kernel(ready, come_ref, *refs):
    middle, outs = refs[:4], refs[4:]
    ready()
    gains, router, query, keyval, output, inner, outer, router_c, query_c, keyval_c, output_c = outs
    small = come_ref[0].astype(F32)
    for i in range(1, 4):
        small = small + come_ref[i].astype(F32)
    wide = middle[0][...].astype(F32)
    for part in middle[1:]:
        wide = wide + part[...].astype(F32)
    for layer in range(2):
        inner[layer] = wide[:, 1024 * layer : 1024 * layer + 512]
        outer[layer] = wide[:, 1024 * layer + 512 : 1024 * layer + 1024]
    keyval[0], keyval[1] = small[:, 512:640], small[:, 256:384]
    keyval_c[...] = small[:, 384:512]
    for source, at, put_q, put_o in (
        (wide, 2048, query_c, output_c),
        (wide, 2304, query.at[1], output.at[1]),
        (small, 0, query.at[0], output.at[0]),
    ):
        turned = source[:, at + 128 : at + 256].T
        for e in range(2):
            put_q[e] = source[:, at + 64 * e : at + 64 * e + 64]
            put_o[e] = turned[64 * e : 64 * e + 64]
    misc = small[:, 640:768].T
    router[0], router[1], router_c[...] = misc[0:8], misc[8:16], misc[16:24]
    for i in range(3):
        gains[i, 0:1] = misc[24 + i : 25 + i]
        gains[i, 1:2] = misc[27 + i : 28 + i]


def shaped(dims, kind):
    return jax.ShapeDtypeStruct(dims, kind)


def cost_of(micros):
    return pl.CostEstimate(
        flops=int(micros * 1.1535e9), bytes_accessed=int(micros * 3.0e6), transcendentals=0
    )


def run(kernel, args, places, outs, scratch, micros, after=()):
    space = {
        "s": pl.BlockSpec(memory_space=pltpu.SMEM),
        "v": pl.BlockSpec(memory_space=pltpu.VMEM),
        "a": pl.BlockSpec(memory_space=pl.ANY),
    }
    large = [
        i for i, (p, a) in enumerate(zip(places, args)) if p == "v" and a.size * a.dtype.itemsize > LARGE
    ]
    places = ["a" if i in large else p for i, p in enumerate(places)]
    count, extra = len(args), len(after)
    copies = [pltpu.VMEM(args[i].shape, args[i].dtype) for i in large]

    def body(*refs):
        given, rest = list(refs[:count]), refs[count + extra :]
        if large:
            rest, held, sems = rest[: -len(large) - 1], rest[-len(large) - 1 : -1], rest[-1]
            moves = []
            for n, i in enumerate(large):
                moves.append(pltpu.make_async_copy(given[i], held[n], sems.at[n]))
                given[i] = held[n]
            for move in moves:
                move.start()
        else:
            moves = []

        def ready():
            for move in moves:
                move.wait()

        kernel(ready, *given, *rest)

    return pl.pallas_call(
        body,
        out_shape=outs,
        in_specs=[space[p] for p in places] + [space["a"]] * extra,
        out_specs=jax.tree.map(lambda _: space["v"], outs),
        scratch_shapes=scratch + copies + ([dma(len(large))] if large else []),
        compiler_params=pltpu.CompilerParams(vmem_limit_bytes=VMEM_LIMIT),
        cost_estimate=cost_of(micros),
    )(*args, *after)


def vm(*dims, kind=BF):
    return pltpu.VMEM(dims, kind)


def dma(count):
    return pltpu.SemaphoreType.DMA((count,))


def across(value, axes, size, by):
    return lax.ppermute(value, axes, [(i, i ^ by) for i in range(size)])


def swapped(value):
    return across(value, "section", 2, 1)


def gathered(value):
    return [value] + [across(value, "mp", 4, b) for b in range(1, 4)]


def to_all(value, axes):
    return lax.all_to_all(value, axes, split_axis=0, concat_axis=0, tiled=True)


def add_shares(keep, come, micros, after, parts=1):
    blocks, rows, width = keep.shape
    whole = pl.BlockSpec((1, rows, width), lambda i: (i, 0, 0))
    part = pl.BlockSpec((1, rows, width // parts), lambda i: (i, 0, 0))
    extra = len(after)
    return pl.pallas_call(
        lambda k, c, *rest: add_kernel(k, c, *rest[extra:]),
        out_shape=[shaped((blocks, rows, width // parts), BF)] * parts,
        grid=(blocks,),
        in_specs=[whole, whole] + [pl.BlockSpec(memory_space=pl.ANY)] * extra,
        out_specs=[part] * parts,
        cost_estimate=cost_of(micros),
    )(keep, come, *after)


def add_pieces(ids, keeps, comes, micros, after=()):
    flats = tuple(keep.ndim == 2 for keep in keeps)
    width = sum(keep.shape[-1] for keep in keeps)
    return run(
        functools.partial(add_pieces_kernel, flats),
        (ids, *keeps, *comes),
        "s" + "v" * (2 * len(keeps)),
        [shaped((256, width), BF)] * 4,
        [],
        micros,
        after=after,
    )


def mp_exchange(pieces):
    return [pieces[0]] + [across(pieces[b], "mp", 4, b) for b in range(1, 4)]


def dp_exchange(pieces):
    return [pieces[0]] + [across(pieces[k], "dp", 4, k) for k in range(1, 4)]


def gated(values, after):
    anywhere = pl.BlockSpec(memory_space=pl.ANY)
    count = len(values)
    return pl.pallas_call(
        lambda *refs: None,
        out_shape=[shaped(v.shape, v.dtype) for v in values],
        in_specs=[anywhere] * (count + len(after)),
        out_specs=[anywhere] * count,
        input_output_aliases={i: i for i in range(count)},
        cost_estimate=cost_of(0.2),
    )(*values, *after)


def per_device(
    inputs,
    lengths,
    routes_self,
    routes_cross,
    gains,
    router_self,
    query_self,
    keyval_self,
    output_self,
    ffn_in,
    ffn_out,
    router_cross,
    query_cross,
    keyval_cross,
    output_cross,
    cotangent,
):
    sec, m, d = lax.axis_index("section"), lax.axis_index("mp"), lax.axis_index("dp")
    low = sec == 0
    ids = jnp.stack([sec, m, d]).astype(jnp.int32)
    sem = dma(24)
    rowgroup = ("section", "mp")

    q_rows = query_self[0].transpose(0, 2, 1).reshape(128, 512)
    o_rows = output_self[0].reshape(128, 512)
    c_rows = jnp.where(
        low, query_cross.transpose(0, 2, 1).reshape(128, 512), output_cross.reshape(128, 512)
    )
    wa = jnp.concatenate([q_rows, o_rows, c_rows], 0)
    wa_own = gathered(wa)
    w_in, w_out = ffn_in[0], ffn_out[0]
    half_come = swapped(jnp.where(low, w_out, w_in))
    enc_half = jnp.where(low, w_in, half_come)
    dec_half = jnp.where(low, half_come, w_out)
    kvw_own = keyval_self[0]
    kvw_oth = swapped(kvw_own)
    router_c = jnp.concatenate([jnp.zeros((8, 512), BF), router_cross.T], 0)

    packed = run(
        pack_kernel,
        (
            lengths[0, :, 0],
            inputs[0, :, 0],
            gains[0],
            keyval_self[0],
            routes_self[0, :, 0].transpose(0, 2, 1),
            routes_cross[:, 0].transpose(0, 2, 1),
            router_self[0].T,
        ),
        "svvvvvv",
        shaped((8, 176, 512), BF),
        [vm(16, 512, kind=F32)],
        3.4,
        after=(wa, enc_half, dec_half),
    )
    (packed,) = gated([packed], wa_own[1:])
    recv = to_all(packed, rowgroup)
    wa_oth = [swapped(piece) for piece in wa_own]
    (enc_half,) = gated([enc_half], [packed])
    enc_own = gathered(enc_half)
    cot_in = lax.dynamic_index_in_dim(cotangent[:, 0].reshape(4, 2, 128, 512), sec, 1, False)

    act = shaped((2, TILE, 512), F32)
    actb = shaped((2, TILE, 512), BF)
    mixed_s = shaped((2, 2 * TILE, 128), F32)
    log_s = shaped((2, 1, 2 * TILE), F32)
    kv_b = shaped((4, 128, 128), BF)
    kv_f = shaped((4, 128, 128), F32)
    row_s = shaped((1, 512), F32)
    ffn_g = shaped((4, 256, 1024), BF)
    router_s = shaped((32, 512), F32)
    wide = [vm(512, 512), vm(512, 512)]
    kv_scratch = [vm(4, 2, 128, 128), vm(1024, 128), vm(1024, 128)]
    back_scratch = [
        vm(1024, TILE, kind=F32), vm(1024, 128, kind=F32), vm(1024, 128, kind=F32),
        vm(2, TILE, 512), vm(2, TILE, 512), vm(2, TILE, 512), vm(2, TILE, 512), vm(2, TILE, 128),
    ]
    ffn_w = [vm(4, 512, 512), vm(4, 512, 512)]

    h1, g1, mixed_e, mixed_d, log_e, log_d, meta, kv_self = run(
        self_fwd_kernel,
        (ids, recv, *wa_own, *wa_oth, kvw_own, kvw_oth),
        "sv" + "a" * 10,
        (act, act, mixed_s, mixed_s, log_s, log_s, shaped((8, 16, 512), BF))
        + (shaped((2, 4, 2, 128, 128), BF),),
        [vm(2, 512, 512), vm(2, 512, 512), vm(2, 512, 128)]
        + [vm(2, 1024, 128), vm(2, 1024, 128), sem],
        0.3,
    )
    enc_own[1:] = gated(enc_own[1:], [h1])
    enc_oth = [swapped(piece) for piece in enc_own]
    (dec_half,) = gated([dec_half], [enc_own[1]])
    dec_near = [across(dec_half, "mp", 4, b) for b in (1, 2)]
    (cot_in,) = gated([cot_in], [enc_own[1]])
    cot = to_all(cot_in, "mp")
    h2, memory, kvm = run(
        enc_ffn_kernel,
        (ids, meta, h1, keyval_cross, *enc_own, *enc_oth),
        "svvv" + "a" * 8,
        (act, actb, kv_b),
        ffn_w + [vm(2, TILE, 512), sem],
        4.0,
        after=(dec_half, cot_in),
    )
    kvm_oth = swapped(kvm)
    dec_near = gated(dec_near, [h2])
    dec_far = [
        across(dec_near[1][0:256], "mp", 4, 1),
        across(dec_near[0][256:512], "mp", 4, 2),
    ]
    g2, mixed_c, log_c = run(
        cross_fwd_kernel,
        (ids, meta, g1, kvm, kvm_oth, router_c, *wa_own, *wa_oth),
        "svvvvv" + "a" * 8,
        (act, mixed_s, log_s),
        wide + kv_scratch + [sem],
        0.3,
        after=(cot,),
    )
    dec_far = gated(dec_far, [g2])
    dec_own = [dec_half, *dec_near, *dec_far]
    dec_oth = [swapped(piece) for piece in dec_own]
    outs, dg2, gain_d2, keep_d, send_d = run(
        dec_ffn_kernel,
        (ids, meta, g2, memory, cot, *dec_own, *dec_oth),
        "svvva" + "a" * 10,
        (shaped((8, 128, 512), BF), act, row_s, ffn_g, ffn_g),
        ffn_w
        + [vm(4, 128, 512), vm(2, TILE, 512), vm(512, 512), vm(512, 512)]
        + [vm(2, TILE, 512, kind=F32), vm(512, 512, kind=F32), sem],
        15.0,
    )
    come_d = swapped(send_d)
    outs_come = to_all(outs, rowgroup)
    att_g = shaped((4, 256, 256), BF)
    flat_g = shaped((256, 256), BF)
    dg1, gain_d1, own_c, sendkv_c, router_cg, keep_wc, send_wc = run(
        cross_back_kernel,
        (ids, meta, g1, dg2, mixed_c, log_c, kvm, kvm_oth, router_c, *wa_own, *wa_oth),
        "svvvvvvvv" + "a" * 8,
        (act, row_s, kv_f, kv_b, router_s, att_g, att_g),
        wide + kv_scratch + back_scratch + [sem],
        13.0,
    )
    comekv_c = swapped(sendkv_c)
    dec_a, dec_b = add_shares(keep_d, come_d, 4.0, (dg1, outs_come), 2)
    dh1, gain_e1, gain_e2, keep_e, send_e = run(
        enc_ffn_back_kernel,
        (ids, meta, h1, h2, own_c, comekv_c, keyval_cross, *enc_own, *enc_oth),
        "svvvvvv" + "a" * 8,
        (act, row_s, row_s, ffn_g, ffn_g),
        ffn_w
        + [vm(2, TILE, 512), vm(512, 512), vm(2, TILE, 512), vm(512, 512)]
        + [vm(512, 512, kind=F32), sem],
        13.4,
        after=(dec_a,),
    )
    dec_a = to_all(dec_a, "mp")
    (dec_b,) = gated([dec_b], [dec_a])
    dec_b = to_all(dec_b, "mp")
    come_e = swapped(send_e)
    self_scratch = wide + kv_scratch + back_scratch + [sem]
    att_dg = shaped((4, 256, 512), BF)
    df1, own_1, sendkv_1, router_1g, keep_w1, send_w1 = run(
        functools.partial(self_back_kernel, 1),
        (
            ids, recv, dg1, mixed_d, log_d, *wa_own, *wa_oth, kv_self, keep_wc, send_wc,
        ),
        "svvvv" + "a" * 11,
        (act, kv_f, kv_b, router_s, att_dg, att_dg),
        self_scratch,
        12.2,
        after=(dh1, dec_a),
    )
    comekv_1 = swapped(sendkv_1)
    come_w1 = swapped(send_w1)
    (ffn_e,) = add_shares(keep_e, come_e, 4.0, (df1, dec_b))
    att_d = add_pieces(ids, [keep_w1], [come_w1], 3.6, (ffn_e,))
    df0, own_0, sendkv_0, router_0g, keep_w0, send_w0 = run(
        functools.partial(self_back_kernel, 0),
        (ids, recv, dh1, mixed_e, log_e, *wa_own, *wa_oth, kv_self),
        "svvvv" + "a" * 9,
        (act, kv_f, kv_b, router_s, att_g, att_g),
        self_scratch,
        11.8,
        after=(ffn_e, *att_d),
    )
    comekv_0 = swapped(sendkv_0)
    come_w0 = swapped(send_w0)
    ffn_e = to_all(ffn_e, "mp")
    att_d = mp_exchange(att_d)
    dx1, gain_d0, keep_s1, send_s1 = run(
        dec_finish_kernel,
        (ids, recv, dg1, df1, own_1, comekv_1, own_c, comekv_c, memory, kvw_own, kvw_oth),
        "svvvvvvvvaa",
        (shaped((4, 128, 512), BF), row_s, flat_g, flat_g),
        [vm(512, 128), vm(2, TILE, 512), sem],
        0.3,
        after=(df0,),
    )
    come_s1 = swapped(send_s1)
    finished = run(
        enc_finish_kernel,
        (
            ids, recv, dh1, df0, own_0, comekv_0, dx1, router_0g, router_1g, router_cg,
            gain_e1, gain_e2, gain_d0, gain_d1, gain_d2, kvw_own, kvw_oth,
        ),
        "s" + "v" * 14 + "aa",
        shaped((8, 208, 512), BF),
        [vm(512, 128), vm(2, TILE, 512), vm(32, 512, kind=F32), sem],
        0.3,
        after=att_d[1:],
    )
    att_e = add_pieces(
        ids, [keep_w0, keep_s1], [come_w0, come_s1], 3.6, (finished,)
    )
    att_e = mp_exchange(att_e)
    dp = lax.axis_size("dp")
    share = 256 // dp
    if dp == 4:
        ffn = dp_exchange(
            run(
                sum_middle_kernel,
                (ids, dec_a, dec_b, ffn_e, *att_d),
                "s" + "v" * 7,
                [shaped((64, 2560), BF)] * 4,
                [],
                4.0,
                after=(att_e[0],),
            )
        )
        after = ffn[1:]
    else:
        after = ()
    finished = to_all(finished, rowgroup)
    small = run(
        tail_kernel,
        (finished, *att_e),
        "v" * 5,
        shaped((256, 768), BF),
        [],
        3.0,
        after=after,
    )
    dx = run(
        place_kernel,
        (finished,),
        "v",
        shaped((4, 2, 128, 512), F32),
        [],
        3.0,
        after=(small,),
    )
    small = to_all(small.reshape(dp, share, 768), "dp")
    outs_come = outs_come.reshape(2, 4, 128, 512).transpose(1, 0, 2, 3)
    results = (outs_come.reshape(1, 4, 1, 256, 512), dx.reshape(1, 4, 1, 256, 512))
    if dp == 4:
        made = run(
            final_kernel,
            (small, *ffn),
            "v" * 5,
            (
                shaped((3, 2, 64), F32),
                shaped((2, 8, 64), F32),
                shaped((2, 2, 64, 64), F32),
                shaped((2, 64, 128), F32),
                shaped((2, 2, 64, 64), F32),
                shaped((2, 64, 512), F32),
                shaped((2, 64, 512), F32),
                shaped((8, 64), F32),
                shaped((2, 64, 64), F32),
                shaped((64, 128), F32),
                shaped((2, 64, 64), F32),
            ),
            [],
            3.0,
        )
        made = list(made)
        made[0] = made[0].transpose(1, 0, 2)
        made[1] = made[1].transpose(0, 2, 1)
        made[6] = made[6].transpose(0, 2, 1)
        made[7] = made[7].T
        return (*results, *made)

    small = jnp.sum(small.astype(F32), 0)
    middle = jnp.concatenate(
        [jnp.sum(part.astype(F32), 0) for part in (ffn_e, dec_a, dec_b)]
        + [sum(part.astype(F32) for part in att_d)],
        1,
    )
    middle = to_all(middle.astype(BF).reshape(dp, share, 2560), "dp")
    middle = jnp.sum(middle.astype(F32), 0)

    def query_of(value, at):
        return value[:, at : at + 128].reshape(share, 2, 64).transpose(1, 0, 2)

    def output_of(value, at):
        return value[:, at + 128 : at + 256].T.reshape(2, 64, share)

    misc = small[:, 640:768].T

    def router_of(layer):
        return misc[ROUTER_LANES[layer] : ROUTER_LANES[layer] + 8].T

    return (
        *results,
        misc[GAIN_ROW : GAIN_ROW + 6].reshape(2, 3, share),
        jnp.stack([router_of(0), router_of(1)]),
        jnp.stack([query_of(small, 0), query_of(middle, 2304)]),
        jnp.stack([small[:, 512:640], small[:, 256:384]]),
        jnp.stack([output_of(small, 0), output_of(middle, 2304)]),
        jnp.stack([middle[:, :512], middle[:, 1024:1536]]),
        jnp.stack([middle[:, 512:1024].T, middle[:, 1536:2048].T]),
        router_of(2),
        query_of(middle, 2048),
        small[:, 384:512],
        output_of(middle, 2048),
    )


def solution(mesh):
    placed = (
        P("section", None, "dp", "mp", None),
        P("section", None, "dp", None),
        P("section", None, "dp", "mp", None),
        P(None, "dp", "mp", None),
        P("section", None, None),
        P("section", None, None),
        P("section", "mp", None, None),
        P("section", None, None),
        P("section", "mp", None, None),
        P("section", None, "mp"),
        P("section", "mp", None),
        P(),
        P("mp", None, None),
        P(),
        P("mp", None, None),
        P(None, "dp", "mp", None),
    )
    return jax.shard_map(
        per_device,
        mesh=mesh,
        in_specs=placed,
        out_specs=(
            P("section", None, "dp", "mp", None),
            P("section", None, "dp", "mp", None),
            P(None, None, ("section", "dp")),
            P(None, ("section", "dp"), None),
            P(None, "mp", ("section", "dp"), None),
            P(None, ("section", "dp"), None),
            P(None, "mp", None, ("section", "dp")),
            P(None, ("section", "dp"), "mp"),
            P(None, "mp", ("section", "dp")),
            P(("section", "dp"), None),
            P("mp", ("section", "dp"), None),
            P(("section", "dp"), None),
            P("mp", None, ("section", "dp")),
        ),
        check_vma=False,
    )
```
